32 devices in a mesh: dp: 8 (over z, y), fsdp: 4 (over x, core).
Axes of the slice: x: 2, y: 2, z: 4, core: 2. Of those that a mesh axis runs over, the one named last changes fastest.
Arguments:
- tokens: bfloat16 [8, 8, 128, 768], P('dp', 'fsdp'), may hold values from -6 to 6
- cotangent: bfloat16 [8, 8, 128, 768], P('dp', 'fsdp'), may hold values from -6 to 6
- seq_ids: int32 [8, 8], P('dp'), may hold values from 0 to 2, as said below
- col_ids: int32 [8, 128], P('dp'), may hold values from 0 to 3, as said below
- gain_row: bfloat16 [768], P(('dp', 'fsdp')), may hold values from 0.5 to 1.5
- qkv_row: bfloat16 [768, 2304], P(('dp', 'fsdp')), may hold values from -0.21875 to 0.21875
- out_row: bfloat16 [768, 768], P(('dp', 'fsdp')), may hold values from -1.25 to 1.25
- gain_col: bfloat16 [768], P(('dp', 'fsdp')), may hold values from 0.5 to 1.5
- qkv_col: bfloat16 [768, 2304], P(('dp', 'fsdp')), may hold values from -0.21875 to 0.21875
- out_col: bfloat16 [768, 768], P(('dp', 'fsdp')), may hold values from -0.4375 to 0.4375
- gain_ffn: bfloat16 [768], P(('dp', 'fsdp')), may hold values from 0.5 to 1.5
- up_ffn: bfloat16 [768, 3072], P(('dp', 'fsdp')), may hold values from -0.21875 to 0.21875
- down_ffn: bfloat16 [3072, 768], P(('dp', 'fsdp')), may hold values from -0.109375 to 0.109375
Outputs:
- mixed: bfloat16 [8, 8, 128, 768], P('dp', 'fsdp')
- input_grad: float32 [8, 8, 128, 768], P('dp', 'fsdp')
- grad_gain_row: float32 [768], P(('dp', 'fsdp'))
- grad_qkv_row: float32 [768, 2304], P(('dp', 'fsdp'))
- grad_out_row: float32 [768, 768], P(('dp', 'fsdp'))
- grad_gain_col: float32 [768], P(('dp', 'fsdp'))
- grad_qkv_col: float32 [768, 2304], P(('dp', 'fsdp'))
- grad_out_col: float32 [768, 768], P(('dp', 'fsdp'))
- grad_gain_ffn: float32 [768], P(('dp', 'fsdp'))
- grad_up_ffn: float32 [768, 3072], P(('dp', 'fsdp'))
- grad_down_ffn: float32 [3072, 768], P(('dp', 'fsdp'))
The draws below stay inside these ranges and needn't reach their ends.
Inputs may be any that keep to these rules, and one draw needn't show every extreme that they name: `seq_ids`: ids never fall along a grid's rows; block 1 runs from row 0 or row 1 to row 6, and the last row is block 2. `col_ids`: A grid's columns form four runs of consecutive columns with ids 0, 1, 2, 3 in order.
All inputs are finite; a program needn't handle non-finite values.
Results may differ from the reference program's by a relative error of at most 0.018.
Values may be sent and summed in bfloat16 or wider, within the bound.
A program may use at most 192 MiB of HBM per device.

```python
import jax
import jax.numpy as jnp
from jax import lax

D = 768
HEADS = 12
HEAD_DIM = 64
FF = 3072
COLS = 128
SEQ_BLOCKS = 3
ROWS = 8
GRIDS = 8


def draw_seq_ids(key, part):
    key = jax.random.fold_in(key, 11)
    starts = jax.random.randint(key, (GRIDS, 1), 0, 2)
    row_index = jnp.arange(ROWS, dtype=jnp.int32)[None, :]
    return (row_index >= starts).astype(jnp.int32) + (row_index >= ROWS - 1).astype(jnp.int32)


def draw_col_ids(key, part):
    key = jax.random.fold_in(key, 12)
    jitter = jax.random.randint(key, (GRIDS, 3), -(COLS // 16), COLS // 16 + 1)
    cuts = (jnp.arange(1, 4, dtype=jnp.int32) * (COLS // 4))[None, :] + jitter
    col_index = jnp.arange(COLS, dtype=jnp.int32)[None, :, None]
    return jnp.sum((col_index >= cuts[:, None, :]).astype(jnp.int32), axis=2)


def strengthened(entries, rng, source, target, parts, factor):
    owner, partner = [(jnp.arange(entries.shape[axis_at]) // (entries.shape[axis_at] // parts)).reshape([-1 if axis == axis_at else 1 for axis in range(entries.ndim)]) for axis_at in (source, target)]
    chosen = jax.random.permutation(rng, parts)[partner]
    strong = (owner == chosen) | (owner == (partner + parts // 2) % parts)
    return jnp.where(strong, factor * entries, entries)


def level_of(own_key, dims, split, smallest, top_value):
    loudness, own = 1.0, jax.random.fold_in(own_key, 6)
    for position, parts in split:
        steps = jnp.exp(jax.random.uniform(jax.random.fold_in(own, position), (parts,), jnp.float32, smallest / len(split), top_value / len(split)))
        loudness = loudness * jnp.repeat(steps, dims[position] // parts).reshape([-1 if axis == position else 1 for axis in range(len(dims))])
    return loudness


def bell_draw(rng, dims, deviation, reach, split=(), held_as=jnp.bfloat16):
    loudness = level_of(rng, dims, split, -0.22, 0.18) if split else 1.0
    entries = jax.random.normal(rng, dims, jnp.float32) * deviation * loudness
    return jnp.minimum(jnp.maximum(entries, -reach), reach).astype(held_as)


def heavy_noise(own_key, dims, deviation, reach, pieces, heavy, kind=jnp.bfloat16):
    values = deviation * jax.random.normal(own_key, dims, jnp.float32)
    if pieces:
        values = values * level_of(own_key, dims, pieces, -0.22, 0.18)
    return jnp.clip(strengthened(values, jax.random.fold_in(own_key, 3), *heavy), -reach, reach).astype(kind)


def setup_inputs(seed: int = 0) -> dict:
    keys = jax.random.split(jax.random.key(seed), 14)
    tokens = bell_draw(keys[0], (GRIDS, ROWS, COLS, D), 1.0, 6.0, ((0, 8), (1, 4)))
    cotangent = heavy_noise(keys[1], (GRIDS, ROWS, COLS, D), 1.0, 6.0, ((0, 8), (1, 4)), (0, 3, 8, 2.0))
    seq_ids = draw_seq_ids(jax.random.fold_in(keys[13], 71), 0)
    col_ids = draw_col_ids(jax.random.fold_in(keys[13], 71), 0)
    gain_row = jnp.clip(1.0 + 0.1 * jax.random.normal(keys[4], (D,), jnp.float32), 0.5, 1.5).astype(jnp.bfloat16)
    qkv_row = bell_draw(keys[5], (D, 3 * D), D ** -0.5, 0.21875, ((0, 32),))
    out_row = bell_draw(keys[6], (D, D), (4 * D // COLS) ** -0.5, 1.25, ((0, 32),))
    gain_col = jnp.clip(1.0 + 0.1 * jax.random.normal(keys[7], (D,), jnp.float32), 0.5, 1.5).astype(jnp.bfloat16)
    qkv_col = bell_draw(keys[8], (D, 3 * D), D ** -0.5, 0.21875, ((0, 32),))
    out_col = bell_draw(keys[9], (D, D), (2 * D // ROWS) ** -0.5, 0.4375, ((0, 32),))
    gain_ffn = jnp.clip(1.0 + 0.1 * jax.random.normal(keys[10], (D,), jnp.float32), 0.5, 1.5).astype(jnp.bfloat16)
    up_ffn = bell_draw(keys[11], (D, FF), D ** -0.5, 0.21875, ((0, 32),))
    down_ffn = bell_draw(keys[12], (FF, D), FF ** -0.5, 0.109375, ((0, 32),))
    return dict(tokens=tokens, cotangent=cotangent, seq_ids=seq_ids, col_ids=col_ids, gain_row=gain_row, qkv_row=qkv_row, out_row=out_row, gain_col=gain_col, qkv_col=qkv_col, out_col=out_col, gain_ffn=gain_ffn, up_ffn=up_ffn, down_ffn=down_ffn)


EPSILON = 1e-05
NEGATIVE = -1000000000.0
HIGHEST = lax.Precision.HIGHEST

@jax.custom_vjp
def low(v):
    return lax.optimization_barrier(v.astype(jnp.bfloat16)).astype(jnp.float32)

@jax.custom_vjp
def low_back(v):
    return v

def low_keep(v):
    return (low(v), None)

def low_pass(kept, grad):
    return (grad,)

def back_keep(v):
    return (v, None)

def back_low(kept, grad):
    return (low(grad),)
low.defvjp(low_keep, low_pass)
low_back.defvjp(back_keep, back_low)

def normalize(values, norm_gain):
    mean_value = lax.optimization_barrier(jnp.mean(values, axis=-1, keepdims=True))
    centred = values - mean_value
    variance = lax.optimization_barrier(jnp.mean(centred * centred, axis=-1, keepdims=True))
    return centred * lax.rsqrt(variance + EPSILON) * norm_gain

def grid_forward(grid_tokens, row_ids, column_ids, params):
    gain_row, qkv_row, out_row, gain_col, qkv_col, out_col, gain_ffn, up_ffn, down_ffn = params
    model_width = grid_tokens.shape[-1]

    def split_heads(values):
        return values.reshape(values.shape[:-1] + (HEADS, HEAD_DIM))

    def join_heads(values):
        return values.reshape(values.shape[:-2] + (model_width,))

    def project(values, weight):
        return jnp.einsum('rcd,de->rce', values, weight, precision=HIGHEST)
    normed = low(normalize(grid_tokens, gain_row))
    projected = low_back(low(project(normed, qkv_row)))
    queries = split_heads(projected[..., :model_width])
    key_rows = split_heads(projected[..., model_width:2 * model_width])
    value_rows = split_heads(projected[..., 2 * model_width:])
    blocks = jnp.arange(SEQ_BLOCKS, dtype=jnp.int32)
    member = (row_ids[None, :] == blocks[:, None]).astype(jnp.float32)
    counts = lax.optimization_barrier(jnp.sum(member, axis=1))
    scales = HEAD_DIM ** (-0.5) * lax.rsqrt(jnp.maximum(counts, 1.0))
    col_mask = column_ids[:, None] == column_ids[None, :]
    raw_scores = jnp.einsum('tr,rihd,rjhd->thij', member, queries, key_rows, precision=HIGHEST)
    raw_scores = raw_scores * scales[:, None, None, None]
    scores = jnp.where(col_mask, low_back(raw_scores), NEGATIVE)
    chances = low(jax.nn.softmax(scores, axis=-1))
    row_chances = jnp.einsum('tr,thij->rhij', member, chances, precision=HIGHEST)
    attended = jnp.einsum('rhij,rjhd->rihd', row_chances, value_rows, precision=HIGHEST)
    attended = low_back(low(join_heads(attended)))
    residual = grid_tokens + low_back(project(attended, out_row))
    normed = low(normalize(residual, gain_col))
    projected = low_back(low(project(normed, qkv_col)))
    queries = split_heads(projected[..., :model_width])
    key_rows = split_heads(projected[..., model_width:2 * model_width])
    value_rows = split_heads(projected[..., 2 * model_width:])
    raw_scores = jnp.einsum('rchd,schd->chrs', queries, key_rows, precision=HIGHEST) * HEAD_DIM ** (-0.5)
    row_mask = row_ids[:, None] == row_ids[None, :]
    scores = jnp.where(row_mask, low_back(raw_scores), NEGATIVE)
    chances = low(jax.nn.softmax(scores, axis=-1))
    attended = jnp.einsum('chrs,schd->rchd', chances, value_rows, precision=HIGHEST)
    attended = low_back(low(join_heads(attended)))
    residual = residual + low_back(project(attended, out_col))
    normed = low(normalize(residual, gain_ffn))
    upper_proj = low_back(project(normed, up_ffn))
    active = low(jax.nn.gelu(upper_proj, approximate=False))
    residual = residual + low_back(project(active, down_ffn))
    return residual

def reference(tokens, cotangent, seq_ids, col_ids, gain_row, qkv_row, out_row, gain_col, qkv_col, out_col, gain_ffn, up_ffn, down_ffn):
    params = tuple((weight.astype(jnp.float32) for weight in (gain_row, qkv_row, out_row, gain_col, qkv_col, out_col, gain_ffn, up_ffn, down_ffn)))
    zero_grads = tuple((jnp.zeros_like(weight) for weight in params))

    def grid_step(summed_grads, inputs):
        grid_tokens, grid_cot, row_ids, column_ids = inputs

        def forward(grid_values, weights):
            return grid_forward(grid_values, row_ids, column_ids, weights)
        result, pullback = jax.vjp(forward, grid_tokens.astype(jnp.float32), params)
        grad_grid, grad_weights = pullback(grid_cot.astype(jnp.float32))
        summed_grads = tuple((earlier + later for earlier, later in zip(summed_grads, grad_weights)))
        return (summed_grads, (result.astype(jnp.bfloat16), grad_grid))
    totals, outputs = lax.scan(grid_step, zero_grads, (tokens, cotangent, seq_ids, col_ids))
    mixed, input_grad = outputs
    return (mixed, input_grad, totals[0], totals[1], totals[2], totals[3], totals[4], totals[5], totals[6], totals[7], totals[8])
```

```python
from functools import partial

import jax
import jax.numpy as jnp
from jax import lax
from jax.experimental import pallas as pl
from jax.experimental.pallas import tpu as pltpu
from jax.sharding import PartitionSpec as P

HEADS = 12
EPSILON = 1e-05
NEGATIVE = -1000000000.0
MESH = pl.DeviceIdType.MESH
BF16 = jnp.bfloat16
F32 = jnp.float32
CELL = 8
AXES = ("dp", "fsdp")


class Place:
    def __init__(self):
        dp = lax.axis_index("dp")
        self.f = lax.axis_index("fsdp")
        self.base = dp // CELL * CELL
        low = dp - self.base
        self.z, self.y = low // 2, low % 2
        self.x, self.c = self.f // 2, self.f % 2

    def dev(self, z, y, x, c):
        return (self.base + z * 2 + y, x * 2 + c)

    def sib(self):
        return self.dev(self.z, self.y, self.x, 1 - self.c)

    def xn(self):
        return self.dev(self.z, self.y, 1 - self.x, self.c)

    def yn(self):
        return self.dev(self.z, 1 - self.y, self.x, self.c)

    def first(self):
        return self.dev(self.z, self.y + self.c * (1 - 2 * self.y), self.x + (1 - self.c) * (1 - 2 * self.x), self.c)

    def second(self):
        return self.dev(self.z, self.y + (1 - self.c) * (1 - 2 * self.y), self.x + self.c * (1 - 2 * self.x), self.c)

    def zup(self, d):
        return self.dev((self.z + d) % 4, self.y, self.x, self.c)


def greet(partners):
    bar = pltpu.get_barrier_semaphore()
    for t in partners:
        pl.semaphore_signal(bar, inc=1, device_id=t, device_id_type=MESH)
    pl.semaphore_wait(bar, len(partners))


def rcopy(src, dst, ss, rs, to):
    return pltpu.make_async_remote_copy(
        src_ref=src, dst_ref=dst, send_sem=ss, recv_sem=rs, device_id=to, device_id_type=MESH
    )


def block(w, rowed, h, z, y, x):
    return w.at[z, y, x, h] if rowed else w.at[h, z, y, x]


ALL = slice(None)


class Gather:
    def __init__(self, me, src, land, w, rowed, ssem, rsem):
        self.me, self.src, self.land, self.w, self.rowed = me, src, land, w, rowed
        self.ss, self.rs = ssem, rsem
        self.sent = []

    def go(self, i, src, dst, to):
        c = rcopy(src, dst, self.ss.at[i], self.rs.at[i], to)
        c.start()
        self.sent.append(c)

    def got(self, i, ref):
        rcopy(ref, ref, self.ss.at[i], self.rs.at[i], self.me.sib()).wait_recv()

    def s0(self):
        if not self.rowed:
            me = self.me
            self.go(0, self.src.at[1 - me.c], self.land, me.sib())

    def s1(self):
        me = self.me
        own = block(self.w, self.rowed, me.c, me.z, me.y, me.x)
        if self.rowed:
            own[...] = self.src[...]
        else:
            self.got(0, self.land)
            mine = self.src[me.c].astype(F32)
            other = self.land[...].astype(F32)
            flag = (me.c == 0).astype(F32)
            top = flag * mine + (1 - flag) * other
            low = flag * other + (1 - flag) * mine
            own[...] = jnp.concatenate([top, low], axis=0).astype(BF16)
        for d in (1, 2, 3):
            self.go(d, own, own, me.zup(d))

    def s2(self):
        me = self.me
        own = block(self.w, self.rowed, me.c, 0, me.y, me.x)
        for d in (1, 2, 3):
            self.got(d, own)
        col = block(self.w, self.rowed, me.c, ALL, me.y, me.x)
        self.go(4, col, col, me.first())
        self.go(6, col, col, me.sib())

    def s3(self):
        me = self.me
        col = block(self.w, self.rowed, me.c, ALL, me.y, me.x)
        self.got(4, col)

        @pl.when(me.c == 0)
        def _():
            r = block(self.w, self.rowed, me.c, ALL, me.y, ALL)
            rcopy(r, r, self.ss.at[5], self.rs.at[5], me.second()).start()
            r = block(self.w, self.rowed, me.c, ALL, me.y, 1 - me.x)
            rcopy(r, r, self.ss.at[7], self.rs.at[7], me.sib()).start()

        @pl.when(me.c == 1)
        def _():
            r = block(self.w, self.rowed, me.c, ALL, ALL, me.x)
            rcopy(r, r, self.ss.at[5], self.rs.at[5], me.second()).start()
            r = block(self.w, self.rowed, me.c, ALL, 1 - me.y, me.x)
            rcopy(r, r, self.ss.at[7], self.rs.at[7], me.sib()).start()

    def s4(self):
        me = self.me
        two = block(self.w, self.rowed, me.c, ALL, me.y, ALL)
        self.got(5, two)

        @pl.when(me.c == 0)
        def _():
            r = block(self.w, self.rowed, me.c, ALL, 1 - me.y, ALL)
            rcopy(r, r, self.ss.at[8], self.rs.at[8], me.sib()).start()

        @pl.when(me.c == 1)
        def _():
            r = block(self.w, self.rowed, me.c, ALL, ALL, 1 - me.x)
            rcopy(r, r, self.ss.at[8], self.rs.at[8], me.sib()).start()

    def s5(self):
        me = self.me
        col = block(self.w, self.rowed, me.c, ALL, me.y, me.x)
        two = block(self.w, self.rowed, me.c, ALL, me.y, ALL)
        self.got(6, col)
        self.got(7, col)
        self.got(8, two)

    def drain(self):
        me = self.me
        for c in self.sent:
            c.wait_send()
        col = block(self.w, self.rowed, me.c, ALL, me.y, me.x)
        two = block(self.w, self.rowed, me.c, ALL, me.y, ALL)
        for i, r in ((5, two), (7, col), (8, two)):
            rcopy(r, r, self.ss.at[i], self.rs.at[i], me.sib()).wait_send()


def gather_kernel(i0, i1, i2, i3, w0, w1, w2, w3, l0, l1, l2, ssem, rsem):
    me = Place()
    greet([me.sib(), me.xn(), me.yn(), me.zup(1), me.zup(2), me.zup(3)])
    gs = [
        Gather(me, i, l, w, r, ssem.at[k], rsem.at[k])
        for k, (i, l, w, r) in enumerate(
            ((i0, l0, w0, False), (i1, l1, w1, False), (i2, l2, w2, False), (i3, None, w3, True))
        )
    ]
    for g in gs:
        g.s0()
    for g in gs:
        g.s1()
    for k in range(len(gs) + 3):
        for s, step in enumerate(("s2", "s3", "s4", "s5")):
            if 0 <= k - s < len(gs):
                getattr(gs[k - s], step)()
    for g in gs:
        g.drain()


def gather_all(shards):
    shapes, lands = [], []
    for s in shards[:3]:
        shapes.append(jax.ShapeDtypeStruct((2, 4, 2, 2, 2 * s.shape[1], s.shape[2]), BF16))
        lands.append(pltpu.VMEM(s.shape[1:], BF16))
    s = shards[3]
    shapes.append(jax.ShapeDtypeStruct((4, 2, 2, 2) + s.shape, BF16))
    vm = pl.BlockSpec(memory_space=pltpu.VMEM)
    return pl.pallas_call(
        gather_kernel,
        out_shape=shapes,
        in_specs=[vm] * 4,
        out_specs=[vm] * 4,
        scratch_shapes=lands + [pltpu.SemaphoreType.DMA((4, 9)), pltpu.SemaphoreType.DMA((4, 9))],
        name="gather",
        compiler_params=pltpu.CompilerParams(
            collective_id=0, has_side_effects=True, vmem_limit_bytes=40 * 2**20
        ),
    )(*shards)


def add_rows(dst, a, b, n):
    def body(i, _):
        dst[i] = (a[i].astype(F32) + b[i].astype(F32)).astype(BF16)
        return 0

    lax.fori_loop(0, n, body, 0)


class Reduce:
    def __init__(self, me, g, acc, l0, l1, l2, l3, l4, out, rowed, ssem, rsem):
        self.me, self.g, self.acc, self.rowed, self.out = me, g, acc, rowed, out
        self.l0, self.l1, self.l2, self.l3, self.l4 = l0, l1, l2, l3, l4
        self.ss, self.rs = ssem, rsem

    def copy(self, i, src, dst, to):
        return rcopy(src, dst, self.ss.at[i], self.rs.at[i], to)

    def done(self, i, ref):
        c = self.copy(i, ref, ref, self.me.sib())
        c.wait_send()
        c.wait_recv()

    def r0(self):
        me = self.me
        self.copy(0, block(self.g, self.rowed, 1 - me.c, ALL, ALL, ALL), self.l0, me.sib()).start()

    def r1(self):
        me = self.me
        self.done(0, self.l0)
        for z in range(4):
            for y in range(2):
                for x in range(2):
                    mine = block(self.g, self.rowed, me.c, z, y, x)
                    self.acc[z, y, x] = (mine[...].astype(F32) + self.l0[z, y, x].astype(F32)).astype(BF16)

        @pl.when(me.c == 0)
        def _():
            self.copy(1, self.acc.at[:, 1 - me.y], self.l1, me.second()).start()

        @pl.when(me.c == 1)
        def _():
            self.copy(1, self.acc.at[:, :, 1 - me.x], self.l1, me.second()).start()

    def r2(self):
        me = self.me
        self.done(1, self.l1)
        for k in range(4):
            for m in range(2):
                y = me.y + me.c * (m - me.y)
                x = me.x + (1 - me.c) * (m - me.x)
                self.acc[k, y, x] = (self.acc[k, y, x].astype(F32) + self.l1[k, m].astype(F32)).astype(BF16)
        oy = me.y + me.c * (1 - 2 * me.y)
        ox = me.x + (1 - me.c) * (1 - 2 * me.x)
        self.copy(2, self.acc.at[:, oy, ox], self.l2, me.first()).start()

    def r3(self):
        me = self.me
        self.done(2, self.l2)
        for k in range(4):
            self.acc[k, me.y, me.x] = (
                self.acc[k, me.y, me.x].astype(F32) + self.l2[k].astype(F32)
            ).astype(BF16)
        for d in (1, 2, 3):
            self.copy(2 + d, self.acc.at[(me.z + d) % 4, me.y, me.x], self.l3.at[d - 1], me.zup(d)).start()

    def r4(self):
        me = self.me
        for d in (1, 2, 3):
            self.done(2 + d, self.l3.at[d - 1])
        total = self.acc[me.z, me.y, me.x].astype(F32)
        for d in (1, 2, 3):
            total = total + self.l3[d - 1].astype(F32)
        if self.rowed:
            self.out[...] = total
        else:
            half = total.shape[0] // 2
            flag = (me.c == 0).astype(F32)
            top, low = total[:half], total[half:]
            self.out[me.c] = flag * top + (1 - flag) * low
            self.l4[0] = flag * low + (1 - flag) * top
            self.copy(6, self.l4.at[0], self.l4.at[1], me.sib()).start()

    def r5(self):
        if not self.rowed:
            self.done(6, self.l4.at[0])
            self.out[1 - self.me.c] = self.l4[1]


def reduce_kernel(*refs):
    me = Place()
    greet([me.sib(), me.xn(), me.yn(), me.zup(1), me.zup(2), me.zup(3)])
    ins, outs, rest = refs[:4], refs[4:8], refs[8:]
    ssem, rsem = rest[-2:]
    groups = []
    at = 0
    for k in range(4):
        rowed = k == 3
        n = 5 if rowed else 6
        s = list(rest[at : at + n])
        at += n
        if rowed:
            s.append(None)
        groups.append(Reduce(me, ins[k], *s, outs[k], rowed, ssem.at[k], rsem.at[k]))
    steps = ("r0", "r1", "r2", "r3", "r4", "r5")
    for k in range(len(groups) + len(steps) - 1):
        for s, step in enumerate(steps):
            if 0 <= k - s < len(groups):
                getattr(groups[k - s], step)()


def reduce_all(parts):
    shapes, scratch = [], []
    for k, p in enumerate(parts):
        rows, cols = p.shape[-2:]
        scratch += [
            pltpu.VMEM((4, 2, 2, rows, cols), BF16),
            pltpu.VMEM((4, 2, 2, rows, cols), BF16),
            pltpu.VMEM((4, 2, rows, cols), BF16),
            pltpu.VMEM((4, rows, cols), BF16),
            pltpu.VMEM((3, rows, cols), BF16),
        ]
        if k < 3:
            scratch.append(pltpu.VMEM((2, rows // 2, cols), F32))
            shapes.append(jax.ShapeDtypeStruct((2, rows // 2, cols), F32))
        else:
            shapes.append(jax.ShapeDtypeStruct((rows, cols), F32))
    vm = pl.BlockSpec(memory_space=pltpu.VMEM)
    return pl.pallas_call(
        reduce_kernel,
        out_shape=shapes,
        in_specs=[vm] * 4,
        out_specs=[vm] * 4,
        scratch_shapes=scratch + [pltpu.SemaphoreType.DMA((4, 7)), pltpu.SemaphoreType.DMA((4, 7))],
        name="reduce",
        compiler_params=pltpu.CompilerParams(
            collective_id=1, has_side_effects=True, vmem_limit_bytes=60 * 2**20
        ),
    )(*parts)


def normalize(values, norm_gain):
    mean_value = jnp.mean(values, axis=-1, keepdims=True)
    centred = values - mean_value
    variance = jnp.mean(centred * centred, axis=-1, keepdims=True)
    return centred * lax.rsqrt(variance + EPSILON) * norm_gain


def exact_gelu(values):
    return jax.nn.gelu(values, approximate=False)


def split_heads(values, head_count):
    return values.reshape(values.shape[:-1] + (head_count, values.shape[-1] // head_count))


def heads_first(values, head_count):
    return jnp.moveaxis(split_heads(values, head_count), -2, 0)


def heads_last(values):
    joined = jnp.moveaxis(values, 0, -2)
    return joined.reshape(joined.shape[:-2] + (joined.shape[-2] * joined.shape[-1],))


def matmul(left_side, right_side):
    return jnp.dot(left_side, right_side, preferred_element_type=jnp.float32)


def left_grad(left_side, right_side):
    return jnp.einsum("tk,tn->kn", left_side, right_side, preferred_element_type=jnp.float32)


def right_grad(gradient, weight):
    return jnp.einsum("tn,kn->tk", gradient, weight, preferred_element_type=jnp.float32)
def tied_scores(query_all, key_all, member_low, scales, col_mask):
    masked = member_low[:, :, None, None] * query_all[None]
    raw_scores = jnp.einsum("lrid,rjd->lij", masked, key_all, preferred_element_type=jnp.float32)
    return jnp.where(col_mask[None], raw_scores * scales[:, None, None], NEGATIVE)


def row_head_forward(pieces, member_low, scales, col_mask):
    query_all, key_all, value_own = pieces
    scores = tied_scores(query_all, key_all, member_low, scales, col_mask)
    largest = jnp.max(scores, axis=-1, keepdims=True)
    exponent = jnp.exp(scores - largest)
    summed = jnp.sum(exponent, axis=-1, keepdims=True)
    chances = (exponent / summed).astype(jnp.bfloat16)
    attended = jnp.einsum("lij,ljd->lid", chances, value_own, preferred_element_type=jnp.float32)
    return (attended, (largest + jnp.log(summed))[..., 0])


def row_head_backward(pieces, member_low, scales, col_mask, first_row):
    query_all, key_all, value_all, dout_all, log_total = pieces
    local_rows = member_low.shape[0]
    scores = tied_scores(query_all, key_all, member_low, scales, col_mask)
    chances = jnp.exp(scores - log_total[..., None])
    chances_low = chances.astype(jnp.bfloat16)
    masked_dout = member_low[:, :, None, None] * dout_all[None]
    grad_chances = jnp.einsum(
        "lrid,rjd->lij", masked_dout, value_all, preferred_element_type=jnp.float32
    )
    centred_grad = grad_chances - jnp.sum(grad_chances * chances, axis=-1, keepdims=True)
    grad_scores = (chances * centred_grad).astype(jnp.bfloat16)
    query_own = lax.dynamic_slice_in_dim(query_all, first_row, local_rows, 0)
    key_own = lax.dynamic_slice_in_dim(key_all, first_row, local_rows, 0)
    dout_own = lax.dynamic_slice_in_dim(dout_all, first_row, local_rows, 0)
    grad_query = (
        jnp.einsum("lij,ljd->lid", grad_scores, key_own, preferred_element_type=jnp.float32)
        * scales[:, None, None]
    )
    grad_key = (
        jnp.einsum("lij,lid->ljd", grad_scores, query_own, preferred_element_type=jnp.float32)
        * scales[:, None, None]
    )
    grad_value = jnp.einsum(
        "lij,lid->ljd", chances_low, dout_own, preferred_element_type=jnp.float32
    )
    return (grad_query, grad_key, grad_value)


def column_chances(queries, key_rows, row_mask, head_count):
    query_heads = split_heads(queries, head_count)
    key_heads = split_heads(key_rows, head_count)
    factor = query_heads.shape[-1] ** (-0.5)
    scores = (
        jnp.einsum("lchd,schd->chls", query_heads, key_heads, preferred_element_type=jnp.float32)
        * factor
    )
    scores = jnp.where(row_mask[None, None], scores, NEGATIVE)
    return jax.nn.softmax(scores, axis=-1)


def column_forward(queries, key_rows, value_rows, row_mask, head_count):
    chances = column_chances(queries, key_rows, row_mask, head_count).astype(jnp.bfloat16)
    attended = jnp.einsum(
        "chls,schd->lchd",
        chances,
        split_heads(value_rows, head_count),
        preferred_element_type=jnp.float32,
    )
    return attended.reshape(queries.shape).astype(jnp.bfloat16)


def column_backward(queries, key_rows, value_rows, row_mask, grad_out, head_count):
    chances = column_chances(queries, key_rows, row_mask, head_count)
    query_heads = split_heads(queries, head_count)
    key_heads = split_heads(key_rows, head_count)
    value_heads = split_heads(value_rows, head_count)
    grad_heads = split_heads(grad_out, head_count)
    factor = query_heads.shape[-1] ** (-0.5)
    grad_chances = jnp.einsum(
        "lchd,schd->chls", grad_heads, value_heads, preferred_element_type=jnp.float32
    )
    centred_grad = grad_chances - jnp.sum(grad_chances * chances, axis=-1, keepdims=True)
    grad_scores = (chances * centred_grad).astype(jnp.bfloat16)
    grad_query = (
        jnp.einsum("chls,schd->lchd", grad_scores, key_heads, preferred_element_type=jnp.float32)
        * factor
    )
    grad_key = (
        jnp.einsum("chls,lchd->schd", grad_scores, query_heads, preferred_element_type=jnp.float32)
        * factor
    )
    grad_value = jnp.einsum(
        "chls,lchd->schd",
        chances.astype(jnp.bfloat16),
        grad_heads,
        preferred_element_type=jnp.float32,
    )
    return (
        grad_query.reshape(queries.shape),
        grad_key.reshape(key_rows.shape),
        grad_value.reshape(key_rows.shape),
    )


def on_device(
    tokens,
    cotangent,
    seq_ids,
    col_ids,
    gain_row,
    qkv_row,
    out_row,
    gain_col,
    qkv_col,
    out_col,
    gain_ffn,
    up_ffn,
    down_ffn,
    cells,
):
    head_count = HEADS
    local_rows = tokens.shape[1]
    col_count = tokens.shape[2]
    model_width = tokens.shape[3]
    token_count = local_rows * col_count
    members = CELL * lax.axis_size("fsdp")
    low_index = (lax.axis_index("dp") % CELL) * lax.axis_size("fsdp") + lax.axis_index("fsdp")

    def in_cell(shard):
        if cells == 1:
            return shard
        whole = lax.all_gather(shard, AXES, axis=0, tiled=True)
        rows = whole.shape[0] // members
        return lax.dynamic_slice_in_dim(whole, low_index * rows, rows, 0)

    def from_cell(summed):
        if cells == 1:
            return summed
        rows = summed.shape[0]
        whole = jnp.zeros((rows * members,) + summed.shape[1:], summed.dtype)
        whole = lax.dynamic_update_slice_in_dim(whole, summed, low_index * rows, 0)
        return lax.psum_scatter(whole, AXES, scatter_dimension=0, tiled=True)

    def halves(shard):
        return jnp.stack(jnp.split(shard, 2, axis=1))

    residual = tokens[0].astype(jnp.float32).reshape(token_count, model_width)
    row_ids = seq_ids[0]
    column_ids = col_ids[0]
    first_row = lax.axis_index("fsdp") * local_rows
    own_ids = lax.dynamic_slice_in_dim(row_ids, first_row, local_rows, 0)
    member = own_ids[:, None] == row_ids[None, :]
    member_low = member.astype(jnp.bfloat16)
    counts = jnp.sum(member.astype(jnp.float32), axis=1)
    scales = (model_width // head_count) ** (-0.5) * lax.rsqrt(jnp.maximum(counts, 1.0))
    col_mask = column_ids[:, None] == column_ids[None, :]

    shards = (
        halves(jnp.concatenate([in_cell(qkv_row), in_cell(out_row)], axis=1)),
        halves(jnp.concatenate([in_cell(qkv_col), in_cell(out_col)], axis=1)),
        halves(in_cell(up_ffn)),
        in_cell(down_ffn),
    )
    w_row, w_col, w_up, w_down = gather_all(shards)
    gains = lax.all_gather(jnp.stack([gain_row, gain_col, gain_ffn]), AXES, axis=1, tiled=True)
    gains = gains.astype(F32)

    def join(w):
        w = w.reshape(2, -1, w.shape[-1])
        return jnp.concatenate([w[0], w[1]], axis=1)

    w_row, w_col, w_up = join(w_row), join(w_col), join(w_up)
    w_down = w_down.reshape(-1, w_down.shape[-1])
    split = 3 * model_width

    def to_grid(values):
        return values.reshape(local_rows, col_count, values.shape[-1])

    normed_row, pull_row = jax.vjp(normalize, residual, gains[0])
    low_row = normed_row.astype(jnp.bfloat16)
    projected = matmul(low_row, w_row[:, :split]).astype(jnp.bfloat16)
    all_rows = lax.all_gather(to_grid(projected), "fsdp", axis=0, tiled=True)
    query_all, key_all, value_all = jnp.split(all_rows, 3, axis=-1)
    value_rows = to_grid(projected[:, 2 * model_width :])
    row_forward = partial(row_head_forward, member_low=member_low, scales=scales, col_mask=col_mask)
    attended_heads, log_totals = lax.map(
        row_forward,
        (
            heads_first(query_all, head_count),
            heads_first(key_all, head_count),
            heads_first(value_rows, head_count),
        ),
    )
    attended_row = heads_last(attended_heads).reshape(token_count, model_width).astype(jnp.bfloat16)
    residual_one = residual + matmul(attended_row, w_row[:, split:])
    normed_col, pull_col = jax.vjp(normalize, residual_one, gains[1])
    low_col = normed_col.astype(jnp.bfloat16)
    projected_col = matmul(low_col, w_col[:, :split]).astype(jnp.bfloat16)
    col_queries = to_grid(projected_col[:, :model_width])
    both = lax.all_gather(to_grid(projected_col[:, model_width:]), "fsdp", axis=0, tiled=True)
    keys_all, values_all = jnp.split(both, 2, axis=-1)
    attended_col = column_forward(col_queries, keys_all, values_all, member, head_count)
    attended_col = attended_col.reshape(token_count, model_width)
    residual_two = residual_one + matmul(attended_col, w_col[:, split:])
    normed_ffn, pull_ffn = jax.vjp(normalize, residual_two, gains[2])
    low_ffn = normed_ffn.astype(jnp.bfloat16)
    upper_proj = matmul(low_ffn, w_up)
    activated, pull_gelu = jax.vjp(exact_gelu, upper_proj)
    active_low = activated.astype(jnp.bfloat16)
    residual_three = residual_two + matmul(active_low, w_down)
    mixed = residual_three.reshape(1, local_rows, col_count, model_width).astype(jnp.bfloat16)
    gradient = cotangent[0].astype(jnp.float32).reshape(token_count, model_width)
    grad_low = gradient.astype(jnp.bfloat16)
    grad_down = left_grad(active_low, grad_low)
    grad_upper = pull_gelu(right_grad(grad_low, w_down))[0].astype(jnp.bfloat16)
    grad_up = left_grad(low_ffn, grad_upper)
    grad_input, gain_f = pull_ffn(right_grad(grad_upper, w_up))
    gradient = gradient + grad_input
    grad_low = gradient.astype(jnp.bfloat16)
    grad_out_c = left_grad(attended_col, grad_low)
    grad_attended = to_grid(right_grad(grad_low, w_col[:, split:]).astype(jnp.bfloat16))
    grad_query, grad_key_part, grad_value_part = column_backward(
        col_queries, keys_all, values_all, member, grad_attended, head_count
    )
    parts = jnp.concatenate([grad_key_part, grad_value_part], axis=-1)
    grad_pair = lax.psum_scatter(parts.astype(BF16), "fsdp", scatter_dimension=0, tiled=True)
    grad_projected = jnp.concatenate([grad_query.astype(BF16), grad_pair], axis=-1)
    grad_projected = grad_projected.reshape(token_count, 3 * model_width)
    grad_qkv_c = left_grad(low_col, grad_projected)
    grad_input, gain_c = pull_col(right_grad(grad_projected, w_col[:, :split]))
    gradient = gradient + grad_input
    grad_low = gradient.astype(jnp.bfloat16)
    grad_out_r = left_grad(attended_row, grad_low)
    grad_attended = to_grid(right_grad(grad_low, w_row[:, split:]).astype(jnp.bfloat16))
    dout_all = lax.all_gather(grad_attended, "fsdp", axis=0, tiled=True)
    row_backward = partial(
        row_head_backward,
        member_low=member_low,
        scales=scales,
        col_mask=col_mask,
        first_row=first_row,
    )
    grad_query_h, grad_key_h, grad_value_h = lax.map(
        row_backward,
        (
            heads_first(query_all, head_count),
            heads_first(key_all, head_count),
            heads_first(value_all, head_count),
            heads_first(dout_all, head_count),
            log_totals,
        ),
    )
    grad_projected = jnp.concatenate(
        [heads_last(grad_query_h), heads_last(grad_key_h), heads_last(grad_value_h)], axis=-1
    )
    grad_projected = grad_projected.reshape(token_count, 3 * model_width).astype(jnp.bfloat16)
    grad_qkv_r = left_grad(low_row, grad_projected)
    grad_input, gain_r = pull_row(right_grad(grad_projected, w_row[:, :split]))
    gradient = gradient + grad_input
    input_grad = gradient.reshape(1, local_rows, col_count, model_width)
    gain_grads = lax.psum_scatter(
        jnp.stack([gain_r, gain_c, gain_f]), AXES, scatter_dimension=1, tiled=True
    )

    def parted(whole):
        whole = jnp.stack(jnp.split(whole.astype(BF16), 2, axis=1))
        return whole.reshape(2, 4, 2, 2, -1, whole.shape[-1])

    sums = reduce_all(
        (
            parted(jnp.concatenate([grad_qkv_r, grad_out_r], axis=1)),
            parted(jnp.concatenate([grad_qkv_c, grad_out_c], axis=1)),
            parted(grad_up),
            grad_down.astype(BF16).reshape(4, 2, 2, 2, -1, model_width),
        )
    )
    s_row, s_col, s_up = (from_cell(jnp.concatenate([s[0], s[1]], axis=1)) for s in sums[:3])
    s_down = from_cell(sums[3])
    return (
        mixed,
        input_grad,
        gain_grads[0],
        s_row[:, :split],
        s_row[:, split:],
        gain_grads[1],
        s_col[:, :split],
        s_col[:, split:],
        gain_grads[2],
        s_up,
        s_down,
    )


def solution(mesh):
    rows = P(AXES, None)
    vector = P(AXES)
    grid = P("dp", "fsdp", None, None)
    ids = P("dp", None)
    return jax.shard_map(
        partial(on_device, cells=mesh.shape["dp"] // CELL),
        mesh=mesh,
        in_specs=(grid, grid, ids, ids) + (vector, rows, rows) * 3,
        out_specs=(grid, grid) + (vector, rows, rows) * 3,
        check_vma=False,
    )
```

```python
from functools import partial

import jax
import jax.numpy as jnp
from jax import lax
from jax.experimental import pallas as pl
from jax.experimental.pallas import tpu as pltpu
from jax.sharding import PartitionSpec as P

HEADS = 12
EPSILON = 1e-05
NEGATIVE = -1000000000.0
MESH = pl.DeviceIdType.MESH
BF16 = jnp.bfloat16
F32 = jnp.float32
CELL = 8
AXES = ("dp", "fsdp")


class Place:
    def __init__(self):
        dp = lax.axis_index("dp")
        self.f = lax.axis_index("fsdp")
        self.base = dp // CELL * CELL
        low = dp - self.base
        self.z, self.y = low // 2, low % 2
        self.x, self.c = self.f // 2, self.f % 2

    def dev(self, z, y, x, c):
        return (self.base + z * 2 + y, x * 2 + c)

    def sib(self):
        return self.dev(self.z, self.y, self.x, 1 - self.c)

    def xn(self):
        return self.dev(self.z, self.y, 1 - self.x, self.c)

    def yn(self):
        return self.dev(self.z, 1 - self.y, self.x, self.c)

    def first(self):
        return self.dev(self.z, self.y + self.c * (1 - 2 * self.y), self.x + (1 - self.c) * (1 - 2 * self.x), self.c)

    def second(self):
        return self.dev(self.z, self.y + (1 - self.c) * (1 - 2 * self.y), self.x + self.c * (1 - 2 * self.x), self.c)

    def zup(self, d):
        return self.dev((self.z + d) % 4, self.y, self.x, self.c)


def greet(partners):
    bar = pltpu.get_barrier_semaphore()
    for t in partners:
        pl.semaphore_signal(bar, inc=1, device_id=t, device_id_type=MESH)
    pl.semaphore_wait(bar, len(partners))


def rcopy(src, dst, ss, rs, to):
    return pltpu.make_async_remote_copy(
        src_ref=src, dst_ref=dst, send_sem=ss, recv_sem=rs, device_id=to, device_id_type=MESH
    )


def block(w, rowed, h, z, y, x):
    return w.at[z, y, x, h] if rowed else w.at[h, z, y, x]


ALL = slice(None)


class Gather:
    def __init__(self, me, src, land, w, rowed, ssem, rsem):
        self.me, self.src, self.land, self.w, self.rowed = me, src, land, w, rowed
        self.ss, self.rs = ssem, rsem
        self.sent = []

    def go(self, i, src, dst, to):
        c = rcopy(src, dst, self.ss.at[i], self.rs.at[i], to)
        c.start()
        self.sent.append(c)

    def got(self, i, ref):
        rcopy(ref, ref, self.ss.at[i], self.rs.at[i], self.me.sib()).wait_recv()

    def s0(self):
        if not self.rowed:
            me = self.me
            self.go(0, self.src.at[1 - me.c], self.land, me.sib())

    def s1(self):
        me = self.me
        own = block(self.w, self.rowed, me.c, me.z, me.y, me.x)
        if self.rowed:
            own[...] = self.src[...]
        else:
            self.got(0, self.land)
            mine = self.src[me.c].astype(F32)
            other = self.land[...].astype(F32)
            flag = (me.c == 0).astype(F32)
            top = flag * mine + (1 - flag) * other
            low = flag * other + (1 - flag) * mine
            own[...] = jnp.concatenate([top, low], axis=0).astype(BF16)
        for d in (1, 2, 3):
            self.go(d, own, own, me.zup(d))

    def s2(self):
        me = self.me
        own = block(self.w, self.rowed, me.c, 0, me.y, me.x)
        for d in (1, 2, 3):
            self.got(d, own)
        col = block(self.w, self.rowed, me.c, ALL, me.y, me.x)
        self.go(4, col, col, me.first())
        self.go(6, col, col, me.sib())

    def s3(self):
        me = self.me
        col = block(self.w, self.rowed, me.c, ALL, me.y, me.x)
        self.got(4, col)

        @pl.when(me.c == 0)
        def _():
            r = block(self.w, self.rowed, me.c, ALL, me.y, ALL)
            rcopy(r, r, self.ss.at[5], self.rs.at[5], me.second()).start()
            r = block(self.w, self.rowed, me.c, ALL, me.y, 1 - me.x)
            rcopy(r, r, self.ss.at[7], self.rs.at[7], me.sib()).start()

        @pl.when(me.c == 1)
        def _():
            r = block(self.w, self.rowed, me.c, ALL, ALL, me.x)
            rcopy(r, r, self.ss.at[5], self.rs.at[5], me.second()).start()
            r = block(self.w, self.rowed, me.c, ALL, 1 - me.y, me.x)
            rcopy(r, r, self.ss.at[7], self.rs.at[7], me.sib()).start()

    def s4(self):
        me = self.me
        two = block(self.w, self.rowed, me.c, ALL, me.y, ALL)
        self.got(5, two)

        @pl.when(me.c == 0)
        def _():
            r = block(self.w, self.rowed, me.c, ALL, 1 - me.y, ALL)
            rcopy(r, r, self.ss.at[8], self.rs.at[8], me.sib()).start()

        @pl.when(me.c == 1)
        def _():
            r = block(self.w, self.rowed, me.c, ALL, ALL, 1 - me.x)
            rcopy(r, r, self.ss.at[8], self.rs.at[8], me.sib()).start()

    def s5(self):
        me = self.me
        col = block(self.w, self.rowed, me.c, ALL, me.y, me.x)
        two = block(self.w, self.rowed, me.c, ALL, me.y, ALL)
        self.got(6, col)
        self.got(7, col)
        self.got(8, two)

    def drain(self):
        me = self.me
        for c in self.sent:
            c.wait_send()
        col = block(self.w, self.rowed, me.c, ALL, me.y, me.x)
        two = block(self.w, self.rowed, me.c, ALL, me.y, ALL)
        for i, r in ((5, two), (7, col), (8, two)):
            rcopy(r, r, self.ss.at[i], self.rs.at[i], me.sib()).wait_send()


class Reduce:
    def __init__(self, me, g, lands, out, rowed, ssem, rsem):
        self.me, self.g, self.rowed, self.out = me, g, rowed, out
        self.l0, self.l1, self.l2, self.l3, self.l4 = lands
        self.ss, self.rs = ssem, rsem

    def at(self, z, y, x):
        return block(self.g, self.rowed, self.me.c, z, y, x)

    def copy(self, i, src, dst, to):
        return rcopy(src, dst, self.ss.at[i], self.rs.at[i], to)

    def done(self, i, ref):
        c = self.copy(i, ref, ref, self.me.sib())
        c.wait_send()
        c.wait_recv()

    def r0(self):
        me = self.me
        self.copy(0, block(self.g, self.rowed, 1 - me.c, ALL, ALL, ALL), self.l0, me.sib()).start()

    def r1(self):
        me = self.me
        self.done(0, self.l0)

        def add(k, _):
            z, y, x = k // 4, k // 2 % 2, k % 2
            mine = self.at(z, y, x)
            mine[...] = (mine[...].astype(F32) + self.l0[z, y, x].astype(F32)).astype(BF16)
            return 0

        lax.fori_loop(0, 16, add, 0)

        @pl.when(me.c == 0)
        def _():
            self.copy(1, self.at(ALL, 1 - me.y, ALL), self.l1, me.second()).start()

        @pl.when(me.c == 1)
        def _():
            self.copy(1, self.at(ALL, ALL, 1 - me.x), self.l1, me.second()).start()

    def r2(self):
        me = self.me
        self.done(1, self.l1)

        def add(k, _):
            z, m = k // 2, k % 2
            y = me.y + me.c * (m - me.y)
            x = me.x + (1 - me.c) * (m - me.x)
            mine = self.at(z, y, x)
            mine[...] = (mine[...].astype(F32) + self.l1[z, m].astype(F32)).astype(BF16)
            return 0

        lax.fori_loop(0, 8, add, 0)
        oy = me.y + me.c * (1 - 2 * me.y)
        ox = me.x + (1 - me.c) * (1 - 2 * me.x)
        self.copy(2, self.at(ALL, oy, ox), self.l2, me.first()).start()

    def r3(self):
        me = self.me
        self.done(2, self.l2)

        def add(k, _):
            mine = self.at(k, me.y, me.x)
            mine[...] = (mine[...].astype(F32) + self.l2[k].astype(F32)).astype(BF16)
            return 0

        lax.fori_loop(0, 4, add, 0)
        for d in (1, 2, 3):
            self.copy(2 + d, self.at((me.z + d) % 4, me.y, me.x), self.l3.at[d - 1], me.zup(d)).start()

    def r4(self):
        me = self.me
        for d in (1, 2, 3):
            self.done(2 + d, self.l3.at[d - 1])
        total = self.at(me.z, me.y, me.x)[...].astype(F32)
        for d in (1, 2, 3):
            total = total + self.l3[d - 1].astype(F32)
        if self.rowed:
            self.out[...] = total
        else:
            half = total.shape[0] // 2
            flag = (me.c == 0).astype(F32)
            top, low = total[:half], total[half:]
            self.out[me.c] = flag * top + (1 - flag) * low
            self.l4[0] = flag * low + (1 - flag) * top
            self.copy(6, self.l4.at[0], self.l4.at[1], me.sib()).start()

    def r5(self):
        if not self.rowed:
            self.done(6, self.l4.at[0])
            self.out[1 - self.me.c] = self.l4[1]


class Swap:
    def __init__(self, me, ssem, rsem):
        self.me, self.ss, self.rs, self.sent = me, ssem, rsem, []

    def other(self, d):
        return (self.me.f + d) % 4

    def go(self, src_of, dst):
        me = self.me
        for d in (1, 2, 3):
            t = self.other(d)
            c = rcopy(src_of(t), dst, self.ss.at[d - 1], self.rs.at[d - 1], me.dev(me.z, me.y, t // 2, t % 2))
            c.start()
            self.sent.append(c)

    def wait(self):
        for c in self.sent:
            c.wait_send()
            c.wait_recv()


def nn(a, b):
    return lax.dot_general(a, b, (((1,), (0,)), ((), ())), preferred_element_type=F32)


def nt(a, b):
    return lax.dot_general(a, b, (((1,), (1,)), ((), ())), preferred_element_type=F32)


def tn(a, b):
    return lax.dot_general(a, b, (((0,), (0,)), ((), ())), preferred_element_type=F32)


def standard(values):
    centred = values - jnp.mean(values, axis=-1, keepdims=True)
    scale = lax.rsqrt(jnp.mean(centred * centred, axis=-1, keepdims=True) + EPSILON)
    return centred * scale, scale


def norm_back(values, gain, grad):
    unit, scale = standard(values)
    inner = grad * gain
    low = jnp.mean(inner, axis=-1, keepdims=True)
    high = jnp.mean(inner * unit, axis=-1, keepdims=True)
    return scale * (inner - low - unit * high)


def softmax(scores):
    e = jnp.exp(scores - jnp.max(scores, axis=-1, keepdims=True))
    return e / jnp.sum(e, axis=-1, keepdims=True)


def low_half(shape):
    return lax.broadcasted_iota(jnp.int32, shape, 1) % 128 < 64


D, FF, ROWS, COLS, HEAD = 768, 3072, 8, 128, 64
HALF = D // 2
OWN = COLS // 4
TOK = ROWS * OWN
WIDE = 640
FACTOR = HEAD**-0.5


def layer_kernel(
    tok, cot, seq, cid, i_q, i_o, i_c, i_u, i_d,
    mixed, igrad, o_q, o_o, o_c, o_u, o_d,
    w_q, w_o, w_c, w_u, w_d, f_q, f_o, f_c, f_u,
    l_o0, l_o1, l_o2, l_o3, l_o4,
    l_c0, l_c1, l_c2, l_c3, l_c4,
    l_u0, l_u1, l_u2, l_u3, l_u4,
    l_d0, l_d1, l_d2, l_d3,
    l_q1, l_q2, t_q, l_h0, l_h1,
    tok_all, h1, qkv, p_row, o1f, o1c, x1, h2, qkv2, p_col, o2, x2, h3, x3, dh, e3, g, do2, dqkv2,
    e1, dost, do1, dqkv, dh1, mix_c, mix_r, e1r, gains, cmask, tmask,
    gs, gr, rs, rr, ms, mr,
):
    me = Place()
    f = me.f
    scope = jax.named_scope
    diag = me.dev(me.z, me.y, 1 - me.x, 1 - me.c)
    greet([me.sib(), me.xn(), diag, me.yn(), me.zup(1), me.zup(2), me.zup(3)])
    go = Gather(me, i_o, f_o, w_o, False, gs.at[0], gr.at[0])
    gc = Gather(me, i_c, f_c, w_c, False, gs.at[1], gr.at[1])
    gu = Gather(me, i_u, f_u, w_u, False, gs.at[2], gr.at[2])
    gd = Gather(me, i_d, None, w_d, True, gs.at[3], gr.at[3])
    ro = Reduce(me, w_o, (l_o0, l_o1, l_o2, l_o3, l_o4), o_o, False, rs.at[0], rr.at[0])
    rc = Reduce(me, w_c, (l_c0, l_c1, l_c2, l_c3, l_c4), o_c, False, rs.at[1], rr.at[1])
    ru = Reduce(me, w_u, (l_u0, l_u1, l_u2, l_u3, l_u4), o_u, False, rs.at[2], rr.at[2])
    rd = Reduce(me, w_d, (l_d0, l_d1, l_d2, l_d3, None), o_d, True, rs.at[3], rr.at[3])

    def misc(i):
        return ms.at[i], mr.at[i]

    own_cols = pl.ds(pl.multiple_of(f * OWN, OWN), OWN)

    def cols_of(t):
        return pl.ds(pl.multiple_of(t * OWN, OWN), OWN)

    def swap(i):
        return Swap(me, ms.at[pl.ds(i, 3)], mr.at[pl.ds(i, 3)])

    s_q = swap(0)
    s_q.go(lambda t: i_q.at[t], f_q.at[f])
    go.s0()
    t_sib = rcopy(tok, tok_all.at[pl.ds(2 * f, 2)], *misc(3), me.sib())
    t_x = rcopy(tok, tok_all.at[pl.ds(2 * f, 2)], *misc(4), me.xn())
    t_sib.start()
    t_x.start()
    gc.s0()
    gu.s0()
    with scope("masks"):
        tok_all[pl.ds(2 * f, 2)] = tok[...]
        f_q[f] = i_q[f]
        first = seq[0, 0]
        ids = jnp.broadcast_to(cid[...], (COLS, COLS)).astype(F32)
        cmask[...] = jnp.where(ids == ids.T, 1.0, 0.0)
        i = lax.broadcasted_iota(jnp.int32, (TOK, TOK), 0)
        j = lax.broadcasted_iota(jnp.int32, (TOK, TOK), 1)

        def block_of(k):
            r = k // OWN
            return jnp.where(r == 0, first, jnp.where(r == ROWS - 1, 2, 1))

        tmask[...] = jnp.where((i % OWN == j % OWN) & (block_of(i) == block_of(j)), 1.0, 0.0)

    with scope("q_f"):
        s_q.wait()
        w_q[me.z, me.y] = jnp.concatenate([f_q[k].astype(F32) for k in range(4)], axis=0).astype(BF16)
    q_z = [rcopy(w_q.at[me.z, me.y], w_q.at[me.z, me.y], *misc(4 + d), me.zup(d)) for d in (1, 2, 3)]
    for c in q_z:
        c.start()
    with scope("go1"):
        go.s1()
    far = pl.ds(2 * (2 * (1 - me.x) + me.c), 2)
    t_far = rcopy(tok_all.at[far], tok_all.at[far], *misc(8), me.sib())
    with scope("tok"):
        t_x.wait_recv()
    t_far.start()
    s_e = swap(9)
    s_e.go(lambda t: cot.at[:, cols_of(t)], e3.at[pl.ds(2 * f, 2)])
    e3[pl.ds(2 * f, 2)] = cot[:, own_cols]
    gc.s1()
    with scope("q_z"):
        for c in q_z:
            c.wait_recv()
    q_y = rcopy(w_q.at[:, me.y], w_q.at[:, me.y], *misc(12), me.yn())
    q_y.start()
    with scope("go2"):
        go.s2()
    with scope("go3"):
        go.s3()
    gu.s1()
    with scope("go4"):
        go.s4()
        go.s5()
    with scope("gains"):
        for k in range(D // 128):
            part = w_o[0, :, :, :, :, HALF : HALF + 128].reshape(D, 128)[k * 128 : (k + 1) * 128]
            gains[:, k * 128 : (k + 1) * 128] = part.astype(F32).T[:8]
    with scope("gc2"):
        gc.s2()
    with scope("tok2"):
        t_sib.wait()
        t_x.wait_send()
        t_far.wait()

    with scope("norm_row"):

        def norm_rows(k, _):
            unit, _s = standard(tok_all[k].astype(F32))
            h1[k] = (unit * gains[0:1]).astype(BF16)
            return 0

        lax.fori_loop(0, ROWS, norm_rows, 0)
    with scope("gc3"):
        gc.s3()
    gd.s1()
    with scope("q_y"):
        q_y.wait()
        for c in q_z:
            c.wait_send()
    with scope("qkv_row"):
        wide = w_q[...].reshape(D, WIDE)

        def project(k, _):
            pair = h1[pl.ds(2 * k, 2)].reshape(2 * COLS, D)
            qkv[pl.ds(2 * k, 2)] = nn(pair, wide).astype(BF16).reshape(2, COLS, WIDE)
            return 0

        lax.fori_loop(0, ROWS // 2, project, 0)

    joined = (jnp.full((1, 1), first, jnp.int32) == 1)
    tied = jnp.where(joined, 1.0, 0.0)
    s_mid = jnp.where(joined, FACTOR / 7**0.5, FACTOR / 6**0.5)
    lower = low_half((COLS, 128))
    zero = jnp.zeros((COLS, 128), BF16)

    def tile(ref, r, k):
        return ref[r, :, k * 128 : (k + 1) * 128]

    def head_tiles(r):
        q01, q2k2, k01 = tile(qkv, r, 0), tile(qkv, r, 1), tile(qkv, r, 2)
        k2 = pltpu.roll(q2k2.astype(F32), 64, 1).astype(BF16)
        return (
            (jnp.where(lower, q01, zero), k01),
            (jnp.where(lower, zero, q01), k01),
            (jnp.where(lower, q2k2, zero), k2),
        )

    with scope("row_fwd"):
        sums = [[None] * 3 for _ in range(3)]
        for r in range(ROWS):
            for h, (a, b) in enumerate(head_tiles(r)):
                s = nt(a, b)
                t = 0 if r == 0 else 2 if r == ROWS - 1 else 1
                sums[h][t] = s if sums[h][t] is None else sums[h][t] + s
        for h in range(3):
            s0, s1, s2 = sums[h]
            for t, s in enumerate((s0 * FACTOR, (s1 + tied * s0) * s_mid, s2 * FACTOR)):
                p_row[h, t] = softmax(jnp.where(cmask[...] > 0.5, s, NEGATIVE))

    def chances(h, r):
        if r == 0:
            return jnp.where(joined, p_row[h, 1], p_row[h, 0])
        return p_row[h, 2 if r == ROWS - 1 else 1]

    with scope("row_out"):
        for r in range(ROWS):
            v01, v2 = tile(qkv, r, 3), tile(qkv, r, 4)
            p = [chances(h, r).astype(BF16) for h in range(3)]
            o1f[r, :, :128] = jnp.where(lower, nn(p[0], v01), nn(p[1], v01)).astype(BF16)
            o1f[r, :, 128:] = nn(p[2], v2).astype(BF16)
    s_o = swap(13)
    s_o.go(lambda t: o1f.at[:, cols_of(t)], o1c.at[f])
    o1c[f] = o1f[:, own_cols]
    with scope("gc4"):
        gc.s4()
    with scope("gu2"):
        gu.s2()
    with scope("o1"):
        s_o.wait()

    def o1_of(k):
        return o1c[k].reshape(TOK, 256)[:, :192]

    def w_out(h, k):
        return w_o[h, k].reshape(192, 512)[:, :HALF]

    with scope("out_row"):
        for h in range(2):
            cols = slice(h * HALF, (h + 1) * HALF)
            total = tok_all[:, own_cols, cols].reshape(TOK, HALF).astype(F32)
            for k in range(4):
                total = total + nn(o1_of(k), w_out(h, k))
            x1[:, cols] = total

    def in_pieces(step, rows=64, total=TOK):
        def body(k, _):
            step(pl.ds(pl.multiple_of(k * rows, rows), rows))
            return 0

        lax.fori_loop(0, total // rows, body, 0)

    def norm_to(dst, src, gain):
        def step(at):
            dst[at] = (standard(src[at])[0] * gains[gain : gain + 1]).astype(BF16)

        in_pieces(step)

    with scope("norm_col"):
        norm_to(h2, x1, 1)
    with scope("gc5"):
        gc.s5()
        gc.drain()

    def w_col(part, k):
        off = part % 2 * D
        at = pl.ds(pl.multiple_of(off + k * 256, 256), 256)
        return w_c.at[part // 2, :, :, :, :, at]

    with scope("qkv_col"):
        for part in range(3):

            def project2(k, _, part=part):
                at = pl.ds(pl.multiple_of(k * 256, 256), 256)
                qkv2[part, :, at] = nn(h2[...], w_col(part, k)[...].reshape(D, 256)).astype(BF16)
                return 0

            lax.fori_loop(0, 3, project2, 0)
    with scope("gu3"):
        gu.s3()
    with scope("gd2"):
        gd.s2()
    lower2 = low_half((TOK, 128))
    zero2 = jnp.zeros((TOK, 128), BF16)

    def pairs(step):
        def body(k, _):
            step(k, pl.ds(pl.multiple_of(k * 128, 128), 128))
            return 0

        lax.fori_loop(0, HEADS // 2, body, 0)

    with scope("col_fwd"):

        def col_pair(k, at):
            q, kk, v = (qkv2[n, :, at] for n in range(3))
            out = []
            for e in range(2):
                mine = jnp.where(lower2, q, zero2) if e == 0 else jnp.where(lower2, zero2, q)
                s = nt(mine, kk) * FACTOR
                p = softmax(jnp.where(tmask[...] > 0.5, s, NEGATIVE))
                p_col[2 * k + e] = p
                out.append(nn(p.astype(BF16), v))
            o2[:, at] = jnp.where(lower2, out[0], out[1]).astype(BF16)

        pairs(col_pair)
    with scope("gu4"):
        gu.s4()
    with scope("gd3"):
        gd.s3()
    with scope("out_col"):

        def close(k, _):
            at = pl.ds(pl.multiple_of(k * 256, 256), 256)
            x2[:, at] = x1[:, at] + nn(o2[...], w_col(3, k)[...].reshape(D, 256))
            return 0

        lax.fori_loop(0, 3, close, 0)
    with scope("norm_ffn"):
        norm_to(h3, x2, 2)
    with scope("gu5"):
        gu.s5()
        gu.drain()
    with scope("gd4"):
        gd.s4()
        s_e.wait()
    with scope("gd5"):
        gd.s5()
        gd.drain()
    x3[...] = x2[...]
    dh[...] = jnp.zeros((TOK, D), F32)

    with scope("ffn"):

        def hidden(j, _):
            cols = pl.ds(pl.multiple_of(j % 4 * HALF, HALF), HALF)
            up = w_u.at[j // 4, :, :, :, :, cols]
            down = w_d.at[j // 2, j % 2]
            grad = e3[...].reshape(TOK, D)
            u = nn(h3[...], up[...].reshape(D, HALF))
            bell = jnp.exp(-0.5 * u * u) * (1 / (2 * jnp.pi) ** 0.5)
            upper = 0.5 + 0.5 * lax.erf(u * 0.5**0.5)
            a = (u * upper).astype(BF16)
            x3[...] += nn(a, down[...].reshape(HALF, D))
            du = (nt(grad, down[...].reshape(HALF, D)) * (upper + u * bell)).astype(BF16)
            dh[...] += nt(du, up[...].reshape(D, HALF))
            up[...] = tn(h3[...], du).astype(BF16).reshape(4, 2, 2, 48, HALF)
            down[...] = tn(a, grad).astype(BF16).reshape(2, 2, 96, D)
            return 0

        lax.fori_loop(0, 8, hidden, 0)
    ru.r0()
    rd.r0()
    with scope("mix"):
        mix_c[...] = x3[...].astype(BF16).reshape(ROWS, OWN, D)
    s_m = swap(16)
    s_m.go(lambda t: mix_c.at[pl.ds(2 * t, 2)], mix_r.at[:, own_cols])
    mix_r[:, own_cols] = mix_c[pl.ds(2 * f, 2)]
    with scope("ru1"):
        ru.r1()
    with scope("rd1"):
        rd.r1()

    with scope("back_ffn"):

        def back_ffn(at):
            g[at] = g[at] + norm_back(x2[at], gains[2:3], dh[at])

        g[...] = e3[...].reshape(TOK, D).astype(F32)
        in_pieces(back_ffn)
        e1[...] = g[...].astype(BF16)
    with scope("do2"):
        for n in range(3):
            at = slice(n * 256, (n + 1) * 256)
            w = w_c[1, :, :, :, :, D:].reshape(D, D)[at]
            do2[:, at] = nt(e1[...], w).astype(BF16)
        for n in range(3):
            w_col(3, n)[...] = tn(o2[...], e1[:, n * 256 : (n + 1) * 256]).astype(BF16).reshape(4, 2, 2, 48, 256)
    with scope("col_bwd"):

        def col_back(k, at):
            q, kk, v, d = qkv2[0, :, at], qkv2[1, :, at], qkv2[2, :, at], do2[:, at]
            got = []
            for e in range(2):
                mine = jnp.where(lower2, d, zero2) if e == 0 else jnp.where(lower2, zero2, d)
                dp = nt(mine, v)
                p = p_col[2 * k + e]
                ds = (p * (dp - jnp.sum(dp * p, axis=-1, keepdims=True))).astype(BF16)
                got.append((nn(ds, kk) * FACTOR, tn(ds, q) * FACTOR, tn(p.astype(BF16), d)))
            for n in range(3):
                dqkv2[n, :, at] = jnp.where(lower2, got[0][n], got[1][n]).astype(BF16)

        pairs(col_back)
    with scope("ru2"):
        ru.r2()
    with scope("rd2"):
        rd.r2()
    with scope("dh2"):
        for n in range(3):
            at = slice(n * 256, (n + 1) * 256)
            total = nt(dqkv2[0], w_c[0, :, :, :, :, :D].reshape(D, D)[at])
            total = total + nt(dqkv2[1], w_c[0, :, :, :, :, D:].reshape(D, D)[at])
            dh[:, at] = total + nt(dqkv2[2], w_c[1, :, :, :, :, :D].reshape(D, D)[at])
    with scope("g_qkv_col"):
        for part in range(3):

            def grad_col(k, _, part=part):
                at = pl.ds(pl.multiple_of(k * 256, 256), 256)
                w_col(part, k)[...] = tn(h2[...], dqkv2[part, :, at]).astype(BF16).reshape(4, 2, 2, 48, 256)
                return 0

            lax.fori_loop(0, 3, grad_col, 0)
    rc.r0()
    with scope("back_col"):

        def back_col(at):
            g[at] = g[at] + norm_back(x1[at], gains[1:2], dh[at])
            e1[at] = g[at].astype(BF16)

        in_pieces(back_col)

    with scope("do1"):
        for k in range(4):
            d = nt(e1[:, :HALF], w_out(0, k)) + nt(e1[:, HALF:], w_out(1, k))
            d = jnp.concatenate([d, jnp.zeros((TOK, 64), F32)], axis=1)
            dost[k] = d.astype(BF16).reshape(ROWS, OWN, 256)
    s_d = swap(19)
    s_d.go(lambda t: dost.at[t], do1.at[:, own_cols])
    do1[:, own_cols] = dost[f]
    s_g = swap(22)
    s_g.go(lambda t: e1.at[pl.ds(pl.multiple_of(2 * OWN * t, 2 * OWN), 2 * OWN)], e1r.at[f])
    e1r[f] = e1[pl.ds(pl.multiple_of(2 * OWN * f, 2 * OWN), 2 * OWN)]
    with scope("g_out_row"):
        go.drain()
        for h in range(2):
            for k in range(4):
                part = tn(o1_of(k), e1[:, h * HALF : (h + 1) * HALF])
                w_o[h, k, :, :, :, :HALF] = part.astype(BF16).reshape(2, 2, 48, HALF)
    ro.r0()
    with scope("rc1"):
        rc.r1()
    with scope("ru3"):
        ru.r3()
    with scope("rd3"):
        rd.r3()
    with scope("do1w"):
        s_d.wait()
    with scope("row_bwd"):
        d_sum = [[None] * 3 for _ in range(3)]
        for r in range(ROWS):
            d01, d2, v01, v2 = tile(do1, r, 0), tile(do1, r, 1), tile(qkv, r, 3), tile(qkv, r, 4)
            ops = ((jnp.where(lower, d01, zero), v01), (jnp.where(lower, zero, d01), v01), (d2, v2))
            for h, (a, b) in enumerate(ops):
                s = nt(a, b)
                t = 0 if r == 0 else 2 if r == ROWS - 1 else 1
                d_sum[h][t] = s if d_sum[h][t] is None else d_sum[h][t] + s
        da, dat, pt = [], [], []
        for h in range(3):
            s0, s1, s2 = d_sum[h]
            by = []
            for t, s in enumerate((s0, s1 + tied * s0, s2)):
                p = p_row[h, t]
                by.append(p * (s - jnp.sum(s * p, axis=-1, keepdims=True)))
            da.append((jnp.where(joined, by[1], by[0]), by[1], by[2]))
            dat.append([a.T.astype(BF16) for a in da[h]])
            pt.append([chances(h, r).T.astype(BF16) for r in (0, 1, ROWS - 1)])
            da[h] = [a.astype(BF16) for a in da[h]]
        s_first = jnp.where(joined, s_mid, FACTOR)
        for r in range(ROWS):
            t = 0 if r == 0 else 2 if r == ROWS - 1 else 1
            scale = (s_first, s_mid, FACTOR)[t]
            q01, q2k2, k01 = tile(qkv, r, 0), tile(qkv, r, 1), tile(qkv, r, 2)
            d01, d2 = tile(do1, r, 0), tile(do1, r, 1)
            dq = jnp.where(lower, nn(da[0][t], k01), nn(da[1][t], k01)) * scale
            dk = jnp.where(lower, nn(dat[0][t], q01), nn(dat[1][t], q01)) * scale
            mid = jnp.where(lower, nn(dat[2][t], q2k2), nn(da[2][t], q2k2)) * scale
            dv = jnp.where(lower, nn(pt[0][t], d01), nn(pt[1][t], d01))
            for n, val in enumerate((dq, pltpu.roll(mid, 64, 1), dk, dv, nn(pt[2][t], d2))):
                dqkv[r, :, n * 128 : (n + 1) * 128] = val.astype(BF16)
    with scope("dh1"):
        wide = w_q[...].reshape(D, WIDE)

        def partial_dh(k, _):
            pair = dqkv[pl.ds(2 * k, 2)].reshape(2 * COLS, WIDE)
            dh1[k // 2, k % 2] = nt(pair, wide).astype(BF16).reshape(2, COLS, D)
            return 0

        lax.fori_loop(0, 4, partial_dh, 0)
    h_sib = rcopy(dh1.at[:, 1 - me.c], l_h0, *misc(25), me.sib())
    h_sib.start()
    with scope("g_qkv_row"):
        for n in range(WIDE // 128):
            at = slice(n * 128, (n + 1) * 128)
            total = tn(h1[...].reshape(ROWS * COLS, D), dqkv[:, :, at].reshape(ROWS * COLS, 128))
            w_q[:, :, :, at] = total.astype(BF16).reshape(4, 2, 96, 128)
    y_q = rcopy(w_q.at[:, 1 - me.y], l_q1, *misc(26), me.yn())
    y_q.start()
    with scope("dh1_add"):
        h_sib.wait()

        def add_dh(k, _):
            mine = dh1.at[k // 2, me.c, k % 2]
            mine[...] = (mine[...].astype(F32) + l_h0[k // 2, k % 2].astype(F32)).astype(BF16)
            return 0

        lax.fori_loop(0, 4, add_dh, 0)
    h_x = rcopy(dh1.at[1 - me.x, me.c], l_h1, *misc(27), me.xn())
    h_x.start()
    with scope("ro1"):
        ro.r1()
    with scope("rc2"):
        rc.r2()
    with scope("q1"):
        y_q.wait()

        def add_q(k, _):
            w_q[k, me.y] = (w_q[k, me.y].astype(F32) + l_q1[k].astype(F32)).astype(BF16)
            return 0

        lax.fori_loop(0, 4, add_q, 0)
    z_q = [rcopy(w_q.at[(me.z + d) % 4, me.y], l_q2.at[d - 1], *misc(27 + d), me.zup(d)) for d in (1, 2, 3)]
    for c in z_q:
        c.start()
    with scope("ro2"):
        ro.r2()
    with scope("rc3"):
        rc.r3()
    with scope("ro3"):
        ro.r3()
    with scope("u4d4"):
        ru.r4()
        rd.r4()
    with scope("in_grad"):
        h_x.wait()
        s_g.wait()
        for r in range(2):
            for k in range(4):
                at = slice(k * OWN, (k + 1) * OWN)
                grad = dh1[me.x, me.c, r, at].astype(F32) + l_h1[r, at].astype(F32)
                back = norm_back(tok[r, at].astype(F32), gains[0:1], grad)
                igrad[r, at] = e1r[k, r * OWN : (r + 1) * OWN].astype(F32) + back
        s_m.wait()
        mixed[...] = mix_r[...]
    with scope("q2"):
        for c in z_q:
            c.wait()
        total = w_q[me.z, me.y].astype(F32)
        for d in range(3):
            total = total + l_q2[d].astype(F32)
        t_q[...] = total.reshape(4, 24, WIDE)
    s_t = swap(31)
    s_t.go(lambda t: t_q.at[t], o_q.at[f])
    o_q[f] = t_q[f]
    with scope("c4"):
        rc.r4()
    with scope("o4"):
        ro.r4()
    for k in (ru, rc, ro):
        k.r5()
    s_t.wait()


def run_layer(tok, cot, seq, cid, i_q, i_o, i_c, i_u, i_d):
    sds = jax.ShapeDtypeStruct
    rows = i_c.shape[1]
    shapes = [
        sds(tok.shape, BF16),
        sds(tok.shape, F32),
        sds((4, rows, WIDE), F32),
        sds(i_o.shape, F32),
        sds(i_c.shape, F32),
        sds(i_u.shape, F32),
        sds(i_d.shape, F32),
    ]

    def vmem(*shape, dtype=BF16):
        return pltpu.VMEM(shape, dtype)

    def lands(r, c, last=True):
        out = [vmem(4, 2, 2, r, c), vmem(4, 2, r, c), vmem(4, r, c), vmem(3, r, c)]
        return out + ([vmem(2, r // 2, c, dtype=F32)] if last else [])

    r2 = 2 * rows
    wo, wc, wu = i_o.shape[2], i_c.shape[2], i_u.shape[2]
    scratch = [
        vmem(4, 2, 4 * rows, WIDE),
        vmem(2, 4, 2, 2, r2, wo),
        vmem(2, 4, 2, 2, r2, wc),
        vmem(2, 4, 2, 2, r2, wu),
        vmem(4, 2, 2, 2, *i_d.shape),
        vmem(4, rows, WIDE),
        vmem(rows, wo),
        vmem(rows, wc),
        vmem(rows, wu),
        *lands(r2, wo),
        *lands(r2, wc),
        *lands(r2, wu),
        *lands(*i_d.shape, last=False),
        vmem(4, 4 * rows, WIDE),
        vmem(3, 4 * rows, WIDE),
        vmem(4, rows, WIDE, dtype=F32),
        vmem(2, 2, COLS, D),
        vmem(2, COLS, D),
        vmem(ROWS, COLS, D),
        vmem(ROWS, COLS, D),
        vmem(ROWS, COLS, WIDE),
        vmem(3, 3, COLS, COLS, dtype=F32),
        vmem(ROWS, COLS, 256),
        vmem(4, ROWS, OWN, 256),
        vmem(TOK, D, dtype=F32),
        vmem(TOK, D),
        vmem(3, TOK, D),
        vmem(HEADS, TOK, TOK, dtype=F32),
        vmem(TOK, D),
        vmem(TOK, D, dtype=F32),
        vmem(TOK, D),
        vmem(TOK, D, dtype=F32),
        vmem(TOK, D, dtype=F32),
        vmem(ROWS, OWN, D),
        vmem(TOK, D, dtype=F32),
        vmem(TOK, D),
        vmem(3, TOK, D),
        vmem(TOK, D),
        vmem(4, ROWS, OWN, 256),
        vmem(ROWS, COLS, 256),
        vmem(ROWS, COLS, WIDE),
        vmem(2, 2, 2, COLS, D),
        vmem(ROWS, OWN, D),
        vmem(2, COLS, D),
        vmem(4, 2 * OWN, D),
        vmem(8, D, dtype=F32),
        vmem(COLS, COLS, dtype=F32),
        vmem(TOK, TOK, dtype=F32),
        pltpu.SemaphoreType.DMA((4, 9)),
        pltpu.SemaphoreType.DMA((4, 9)),
        pltpu.SemaphoreType.DMA((4, 7)),
        pltpu.SemaphoreType.DMA((4, 7)),
        pltpu.SemaphoreType.DMA((34,)),
        pltpu.SemaphoreType.DMA((34,)),
    ]
    vm = pl.BlockSpec(memory_space=pltpu.VMEM)
    return pl.pallas_call(
        layer_kernel,
        out_shape=shapes,
        in_specs=[vm, vm, pl.BlockSpec(memory_space=pltpu.SMEM)] + [vm] * 6,
        out_specs=[vm] * 7,
        scratch_shapes=scratch,
        name="layer",
        compiler_params=pltpu.CompilerParams(
            collective_id=0, has_side_effects=True, vmem_limit_bytes=VMEM_LIMIT
        ),
    )(tok, cot, seq, cid, i_q, i_o, i_c, i_u, i_d)


VMEM_LIMIT = 63 * 2**20


def on_device(
    tokens, cotangent, seq_ids, col_ids,
    gain_row, qkv_row, out_row, gain_col, qkv_col, out_col, gain_ffn, up_ffn, down_ffn,
    cells,
):
    members = CELL * lax.axis_size("fsdp")
    low_index = (lax.axis_index("dp") % CELL) * lax.axis_size("fsdp") + lax.axis_index("fsdp")

    def in_cell(shard):
        if cells == 1:
            return shard
        whole = lax.all_gather(shard, AXES, axis=0, tiled=True)
        rows = whole.shape[0] // members
        return lax.dynamic_slice_in_dim(whole, low_index * rows, rows, 0)

    def from_cell(summed):
        if cells == 1:
            return summed
        rows = summed.shape[0]
        whole = jnp.zeros((rows * members,) + summed.shape[1:], summed.dtype)
        whole = lax.dynamic_update_slice_in_dim(whole, summed, low_index * rows, 0)
        return lax.psum_scatter(whole, AXES, scatter_dimension=0, tiled=True)

    def halves(shard):
        return jnp.stack(jnp.split(shard, 2, axis=1))

    def unhalved(pair):
        return jnp.concatenate([pair[0], pair[1]], axis=1)

    wq = in_cell(qkv_row)
    rows = wq.shape[0]
    per = wq.reshape(rows, 3, 4, 3, HEAD)
    q, k, v = per[:, 0], per[:, 1], per[:, 2]
    i_q = jnp.concatenate([q, k[:, :, 2:], k[:, :, :2], v, jnp.zeros_like(v[:, :, :1])], axis=2)
    i_q = jnp.moveaxis(i_q.reshape(rows, 4, WIDE), 1, 0)
    gain = in_cell(jnp.stack([gain_row, gain_col, gain_ffn], axis=1))
    gain = jnp.pad(gain, ((0, 0), (0, 125)))
    wo = in_cell(out_row)
    i_o = jnp.stack([jnp.concatenate([wo[:, :HALF], gain], axis=1), jnp.concatenate([wo[:, HALF:], gain], axis=1)])
    i_c = halves(jnp.concatenate([in_cell(qkv_col), in_cell(out_col)], axis=1))
    i_u = halves(in_cell(up_ffn))
    i_d = in_cell(down_ffn)
    mixed, igrad, o_q, o_o, o_c, o_u, o_d = run_layer(
        tokens[0], cotangent[0], seq_ids, col_ids, i_q, i_o, i_c, i_u, i_d
    )
    o_q = jnp.moveaxis(o_q, 0, 1).reshape(rows, 4, WIDE // HEAD, HEAD)
    back = jnp.stack(
        [o_q[:, :, 0:3], jnp.concatenate([o_q[:, :, 4:6], o_q[:, :, 3:4]], axis=2), o_q[:, :, 6:9]], axis=1
    )
    g_q = from_cell(back.reshape(rows, 3 * D))
    g_o = from_cell(unhalved(o_o[:, :, :HALF]))
    g_c = from_cell(unhalved(o_c))
    g_u = from_cell(unhalved(o_u))
    g_d = from_cell(o_d)

    def gain_grad(weight, grad, gain):
        return jnp.sum(weight.astype(F32) * grad, axis=1) / gain.astype(F32)

    return (
        mixed[None],
        igrad[None],
        gain_grad(qkv_row, g_q, gain_row),
        g_q,
        g_o,
        gain_grad(qkv_col, g_c[:, : 3 * D], gain_col),
        g_c[:, : 3 * D],
        g_c[:, 3 * D :],
        gain_grad(up_ffn, g_u, gain_ffn),
        g_u,
        g_d,
    )


def solution(mesh):
    rows = P(AXES, None)
    vector = P(AXES)
    grid = P("dp", "fsdp", None, None)
    ids = P("dp", None)
    return jax.shard_map(
        partial(on_device, cells=mesh.shape["dp"] // CELL),
        mesh=mesh,
        in_specs=(grid, grid, ids, ids) + (vector, rows, rows) * 3,
        out_specs=(grid, grid) + (vector, rows, rows) * 3,
        check_vma=False,
    )
```

```python
from functools import partial

import jax
import jax.numpy as jnp
from jax import lax
from jax.experimental import pallas as pl
from jax.experimental.pallas import tpu as pltpu
from jax.sharding import PartitionSpec as P

HEADS = 12
EPSILON = 1e-05
NEGATIVE = -1000000000.0
MESH = pl.DeviceIdType.MESH
BF16 = jnp.bfloat16
F32 = jnp.float32
CELL = 8
AXES = ("dp", "fsdp")


class Place:
    def __init__(self):
        dp = lax.axis_index("dp")
        self.f = lax.axis_index("fsdp")
        self.base = dp // CELL * CELL
        low = dp - self.base
        self.z, self.y = low // 2, low % 2
        self.x, self.c = self.f // 2, self.f % 2

    def dev(self, z, y, x, c):
        return (self.base + z * 2 + y, x * 2 + c)

    def sib(self):
        return self.dev(self.z, self.y, self.x, 1 - self.c)

    def xn(self):
        return self.dev(self.z, self.y, 1 - self.x, self.c)

    def yn(self):
        return self.dev(self.z, 1 - self.y, self.x, self.c)

    def first(self):
        return self.dev(self.z, self.y + self.c * (1 - 2 * self.y), self.x + (1 - self.c) * (1 - 2 * self.x), self.c)

    def second(self):
        return self.dev(self.z, self.y + (1 - self.c) * (1 - 2 * self.y), self.x + self.c * (1 - 2 * self.x), self.c)

    def zup(self, d):
        return self.dev((self.z + d) % 4, self.y, self.x, self.c)


def greet(partners):
    bar = pltpu.get_barrier_semaphore()
    for t in partners:
        pl.semaphore_signal(bar, inc=1, device_id=t, device_id_type=MESH)
    pl.semaphore_wait(bar, len(partners))


def rcopy(src, dst, ss, rs, to):
    return pltpu.make_async_remote_copy(
        src_ref=src, dst_ref=dst, send_sem=ss, recv_sem=rs, device_id=to, device_id_type=MESH
    )


def block(w, rowed, h, z, y, x):
    return w.at[z, y, x, h] if rowed else w.at[h, z, y, x]


ALL = slice(None)


class Gather:
    def __init__(self, me, src, land, w, rowed, ssem, rsem):
        self.me, self.src, self.land, self.w, self.rowed = me, src, land, w, rowed
        self.ss, self.rs = ssem, rsem
        self.sent = []

    def go(self, i, src, dst, to):
        c = rcopy(src, dst, self.ss.at[i], self.rs.at[i], to)
        c.start()
        self.sent.append(c)

    def got(self, i, ref):
        rcopy(ref, ref, self.ss.at[i], self.rs.at[i], self.me.sib()).wait_recv()

    def s0(self):
        if not self.rowed:
            me = self.me
            self.go(0, self.src.at[1 - me.c], self.land, me.sib())

    def s1(self):
        me = self.me
        own = block(self.w, self.rowed, me.c, me.z, me.y, me.x)
        if self.rowed:
            own[...] = self.src[...]
        else:
            self.got(0, self.land)
            mine = self.src[me.c].astype(F32)
            other = self.land[...].astype(F32)
            flag = (me.c == 0).astype(F32)
            top = flag * mine + (1 - flag) * other
            low = flag * other + (1 - flag) * mine
            own[...] = jnp.concatenate([top, low], axis=0).astype(BF16)
        for d in (1, 2, 3):
            self.go(d, own, own, me.zup(d))

    def s2(self):
        me = self.me
        own = block(self.w, self.rowed, me.c, 0, me.y, me.x)
        for d in (1, 2, 3):
            self.got(d, own)
        col = block(self.w, self.rowed, me.c, ALL, me.y, me.x)
        self.go(4, col, col, me.first())
        self.go(6, col, col, me.sib())

    def s3(self):
        me = self.me
        col = block(self.w, self.rowed, me.c, ALL, me.y, me.x)
        self.got(4, col)

        @pl.when(me.c == 0)
        def _():
            r = block(self.w, self.rowed, me.c, ALL, me.y, ALL)
            rcopy(r, r, self.ss.at[5], self.rs.at[5], me.second()).start()
            r = block(self.w, self.rowed, me.c, ALL, me.y, 1 - me.x)
            rcopy(r, r, self.ss.at[7], self.rs.at[7], me.sib()).start()

        @pl.when(me.c == 1)
        def _():
            r = block(self.w, self.rowed, me.c, ALL, ALL, me.x)
            rcopy(r, r, self.ss.at[5], self.rs.at[5], me.second()).start()
            r = block(self.w, self.rowed, me.c, ALL, 1 - me.y, me.x)
            rcopy(r, r, self.ss.at[7], self.rs.at[7], me.sib()).start()

    def s4(self):
        me = self.me
        two = block(self.w, self.rowed, me.c, ALL, me.y, ALL)
        self.got(5, two)

        @pl.when(me.c == 0)
        def _():
            r = block(self.w, self.rowed, me.c, ALL, 1 - me.y, ALL)
            rcopy(r, r, self.ss.at[8], self.rs.at[8], me.sib()).start()

        @pl.when(me.c == 1)
        def _():
            r = block(self.w, self.rowed, me.c, ALL, ALL, 1 - me.x)
            rcopy(r, r, self.ss.at[8], self.rs.at[8], me.sib()).start()

    def s5(self):
        me = self.me
        col = block(self.w, self.rowed, me.c, ALL, me.y, me.x)
        two = block(self.w, self.rowed, me.c, ALL, me.y, ALL)
        self.got(6, col)
        self.got(7, col)
        self.got(8, two)

    def drain(self):
        me = self.me
        for c in self.sent:
            c.wait_send()
        col = block(self.w, self.rowed, me.c, ALL, me.y, me.x)
        two = block(self.w, self.rowed, me.c, ALL, me.y, ALL)
        for i, r in ((5, two), (7, col), (8, two)):
            rcopy(r, r, self.ss.at[i], self.rs.at[i], me.sib()).wait_send()


class Reduce:
    def __init__(self, me, g, lands, out, rowed, ssem, rsem):
        self.me, self.g, self.rowed, self.out = me, g, rowed, out
        self.l0, self.l1, self.l2, self.l3, self.l4 = lands
        self.ss, self.rs = ssem, rsem

    def at(self, z, y, x):
        return block(self.g, self.rowed, self.me.c, z, y, x)

    def copy(self, i, src, dst, to):
        return rcopy(src, dst, self.ss.at[i], self.rs.at[i], to)

    def done(self, i, ref):
        c = self.copy(i, ref, ref, self.me.sib())
        c.wait_send()
        c.wait_recv()

    def r0(self):
        me = self.me
        self.copy(0, block(self.g, self.rowed, 1 - me.c, ALL, ALL, ALL), self.l0, me.sib()).start()

    def r1(self):
        me = self.me
        self.done(0, self.l0)

        def add(k, _):
            z, y, x = k // 4, k // 2 % 2, k % 2
            mine = self.at(z, y, x)
            mine[...] = (mine[...].astype(F32) + self.l0[z, y, x].astype(F32)).astype(BF16)
            return 0

        lax.fori_loop(0, 16, add, 0)

        @pl.when(me.c == 0)
        def _():
            self.copy(1, self.at(ALL, 1 - me.y, ALL), self.l1, me.second()).start()

        @pl.when(me.c == 1)
        def _():
            self.copy(1, self.at(ALL, ALL, 1 - me.x), self.l1, me.second()).start()

    def r2(self):
        me = self.me
        self.done(1, self.l1)

        def add(k, _):
            z, m = k // 2, k % 2
            y = me.y + me.c * (m - me.y)
            x = me.x + (1 - me.c) * (m - me.x)
            mine = self.at(z, y, x)
            mine[...] = (mine[...].astype(F32) + self.l1[z, m].astype(F32)).astype(BF16)
            return 0

        lax.fori_loop(0, 8, add, 0)
        oy = me.y + me.c * (1 - 2 * me.y)
        ox = me.x + (1 - me.c) * (1 - 2 * me.x)
        self.copy(2, self.at(ALL, oy, ox), self.l2, me.first()).start()

    def r3(self):
        me = self.me
        self.done(2, self.l2)

        def add(k, _):
            mine = self.at(k, me.y, me.x)
            mine[...] = (mine[...].astype(F32) + self.l2[k].astype(F32)).astype(BF16)
            return 0

        lax.fori_loop(0, 4, add, 0)
        for d in (1, 2, 3):
            self.copy(2 + d, self.at((me.z + d) % 4, me.y, me.x), self.l3.at[d - 1], me.zup(d)).start()

    def r4(self):
        me = self.me
        for d in (1, 2, 3):
            self.done(2 + d, self.l3.at[d - 1])
        total = self.at(me.z, me.y, me.x)[...].astype(F32)
        for d in (1, 2, 3):
            total = total + self.l3[d - 1].astype(F32)
        if self.rowed:
            self.out[...] = total
        else:
            half = total.shape[0] // 2
            flag = (me.c == 0).astype(F32)
            top, low = total[:half], total[half:]
            self.out[me.c] = flag * top + (1 - flag) * low
            self.l4[0] = flag * low + (1 - flag) * top
            self.copy(6, self.l4.at[0], self.l4.at[1], me.sib()).start()

    def r5(self):
        if not self.rowed:
            self.done(6, self.l4.at[0])
            self.out[1 - self.me.c] = self.l4[1]


class Swap:
    def __init__(self, me, ssem, rsem):
        self.me, self.ss, self.rs, self.sent = me, ssem, rsem, []

    def other(self, d):
        return (self.me.f + d) % 4

    def go(self, src_of, dst):
        me = self.me
        for d in (1, 2, 3):
            t = self.other(d)
            c = rcopy(src_of(t), dst, self.ss.at[d - 1], self.rs.at[d - 1], me.dev(me.z, me.y, t // 2, t % 2))
            c.start()
            self.sent.append(c)

    def wait(self):
        for c in self.sent:
            c.wait_send()
            c.wait_recv()


class Slices:
    def __init__(self, me, w, l1, l2, sems):
        self.me, self.w, self.l1, self.l2, self.sems = me, w, l1, l2, sems

    def z_send(self):
        me = self.me
        own = self.w.at[me.z, me.y]
        self.zs = [rcopy(own, own, *self.sems(), me.zup(d)) for d in (1, 2, 3)]
        for c in self.zs:
            c.start()

    def y_send(self):
        for c in self.zs:
            c.wait_recv()
        col = self.w.at[:, self.me.y]
        self.ys = rcopy(col, col, *self.sems(), self.me.yn())
        self.ys.start()

    def finish(self):
        self.ys.wait()
        for c in self.zs:
            c.wait_send()

    def back_y(self):
        me = self.me
        self.by = rcopy(self.w.at[:, 1 - me.y], self.l1, *self.sems(), me.yn())
        self.by.start()

    def back_z(self):
        me = self.me
        self.by.wait()

        def add(k, _):
            self.w[k, me.y] = (self.w[k, me.y].astype(F32) + self.l1[k].astype(F32)).astype(BF16)
            return 0

        lax.fori_loop(0, 4, add, 0)
        self.bz = [
            rcopy(self.w.at[(me.z + d) % 4, me.y], self.l2.at[d - 1], *self.sems(), me.zup(d)) for d in (1, 2, 3)
        ]
        for c in self.bz:
            c.start()

    def back_sum(self):
        for c in self.bz:
            c.wait()
        total = self.w[self.me.z, self.me.y].astype(F32)
        for d in range(3):
            total = total + self.l2[d].astype(F32)
        return total


class Share:
    def __init__(self, me, whole, sems):
        self.me, self.sems = me, sems
        self.whole = whole

    def send(self):
        me = self.me
        own = self.whole(me.f)
        self.s = rcopy(own, own, *self.sems(), me.sib())
        self.x = rcopy(own, own, *self.sems(), me.xn())
        self.s.start()
        self.x.start()

    def near(self):
        self.s.wait()

    def forward(self):
        me = self.me
        self.x.wait_recv()
        got = self.whole(2 * (1 - me.x) + me.c)
        self.t = rcopy(got, got, *self.sems(), me.sib())
        self.t.start()

    def finish(self):
        self.x.wait_send()
        self.t.wait()


class Collect:
    def __init__(self, me, part, lands, sems):
        self.me, self.part, self.lands, self.sems = me, part, lands, sems

    def near(self):
        me = self.me
        self.n = rcopy(self.part.at[2 * me.x + 1 - me.c], self.lands.at[0], *self.sems(), me.sib())
        self.n.start()

    def pair(self):
        me = self.me
        self.p = rcopy(self.part.at[2 * (1 - me.x) + 1 - me.c], self.lands.at[1], *self.sems(), me.sib())
        self.p.start()

    def cross(self):
        me = self.me
        self.p.wait()
        f = 2 * (1 - me.x) + me.c

        def add(k, _):
            at = pl.ds(pl.multiple_of(k * 64, 64), 64)
            self.part[f, at] = (self.part[f, at].astype(F32) + self.lands[1, at].astype(F32)).astype(BF16)
            return 0

        lax.fori_loop(0, self.part.shape[1] // 64, add, 0)
        self.x = rcopy(self.part.at[f], self.lands.at[2], *self.sems(), me.xn())
        self.x.start()

    def finish(self):
        self.n.wait()
        self.x.wait()

    def total(self, at):
        own = self.part[self.me.f, at].astype(F32) + self.lands[0, at].astype(F32)
        return own + self.lands[2, at].astype(F32)


def nn(a, b):
    return lax.dot_general(a, b, (((1,), (0,)), ((), ())), preferred_element_type=F32)


def nt(a, b):
    return lax.dot_general(a, b, (((1,), (1,)), ((), ())), preferred_element_type=F32)


def tn(a, b):
    return lax.dot_general(a, b, (((0,), (0,)), ((), ())), preferred_element_type=F32)


def standard(values):
    centred = values - jnp.mean(values, axis=-1, keepdims=True)
    scale = lax.rsqrt(jnp.mean(centred * centred, axis=-1, keepdims=True) + EPSILON)
    return centred * scale, scale


def norm_back(values, gain, grad):
    unit, scale = standard(values)
    inner = grad * gain
    low = jnp.mean(inner, axis=-1, keepdims=True)
    high = jnp.mean(inner * unit, axis=-1, keepdims=True)
    return scale * (inner - low - unit * high)


def softmax(scores):
    e = jnp.exp(scores - jnp.max(scores, axis=-1, keepdims=True))
    return e / jnp.sum(e, axis=-1, keepdims=True)


def low_half(shape):
    return lax.broadcasted_iota(jnp.int32, shape, 1) % 128 < 64


D, FF, ROWS, COLS, HEAD = 768, 3072, 8, 128, 64
HALF = D // 2
OWN = COLS // 4
TOK = ROWS * OWN
WIDE = 640
FACTOR = HEAD**-0.5


def layer_kernel(
    tok, cot, seq, cid, i_q, i_o, i_c, i_u, i_d,
    mixed, igrad, o_q, o_o, o_c, o_u, o_d,
    w_q, w_o, w_c, w_u, w_d, f_q, f_o, f_c, f_u,
    l_o0, l_o1, l_o2, l_o3, l_o4,
    l_c0, l_c1, l_c2, l_c3, l_c4,
    l_q1, l_q2, t_q, l_u1, l_u2, t_u, l_d1, l_d2,
    tok_all, e_all, h1, qkv, p_row, o1f, o1c, x1, h2, qkv2, p_col, o2, x2, h3, act, du, yp, l_y, dp, l_p,
    g, do2, dqkv2, dh2, e1, dost, do1, dqkv, hp, l_h, mix_c, mix_r, e1r, gains, cmask, tmask,
    gs, gr, rs, rr, ms, mr,
):
    me = Place()
    f = me.f
    scope = jax.named_scope
    sib_f, x_f, diag_f = 2 * me.x + 1 - me.c, 2 * (1 - me.x) + me.c, 2 * (1 - me.x) + 1 - me.c
    diag = me.dev(me.z, me.y, 1 - me.x, 1 - me.c)
    greet([me.sib(), me.xn(), diag, me.yn(), me.zup(1), me.zup(2), me.zup(3)])
    used = [0]

    def sems():
        used[0] += 1
        return ms.at[used[0] - 1], mr.at[used[0] - 1]

    def swap():
        used[0] += 3
        at = pl.ds(used[0] - 3, 3)
        return Swap(me, ms.at[at], mr.at[at])

    go = Gather(me, i_o, f_o, w_o, False, gs.at[0], gr.at[0])
    gc = Gather(me, i_c, f_c, w_c, False, gs.at[1], gr.at[1])
    ro = Reduce(me, w_o, (l_o0, l_o1, l_o2, l_o3, l_o4), o_o, False, rs.at[0], rr.at[0])
    rc = Reduce(me, w_c, (l_c0, l_c1, l_c2, l_c3, l_c4), o_c, False, rs.at[1], rr.at[1])
    sq = Slices(me, w_q, l_q1, l_q2, sems)
    su = Slices(me, w_u, l_u1, l_u2, sems)
    sd = Slices(me, w_d, l_d1, l_d2, sems)

    def cols_of(t):
        return pl.ds(pl.multiple_of(t * OWN, OWN), OWN)

    own_cols = cols_of(f)

    def stacked(land):
        return jnp.concatenate([land[k].astype(F32) for k in range(4)], axis=0).astype(BF16)

    s_q = swap()
    s_q.go(lambda t: i_q.at[t], f_q.at[f])
    go.s0()
    tok_all[pl.ds(2 * f, 2)] = tok[...]
    shr_t = Share(me, lambda k: tok_all.at[pl.ds(2 * k, 2)], sems)
    shr_t.send()
    gc.s0()
    s_u = swap()
    s_u.go(lambda t: i_u.at[t], f_u.at[f])
    with scope("q_f"):
        f_q[f] = i_q[f]
        s_q.wait()
        w_q[me.z, me.y] = stacked(f_q)
    sq.z_send()
    with scope("go1"):
        go.s1()
    with scope("masks"):
        first = seq[0, 0]
        ids = jnp.broadcast_to(cid[...], (COLS, COLS)).astype(F32)
        cmask[...] = jnp.where(ids == ids.T, 1.0, 0.0)
        i = lax.broadcasted_iota(jnp.int32, (TOK, TOK), 0)
        j = lax.broadcasted_iota(jnp.int32, (TOK, TOK), 1)

        def block_of(k):
            r = k // OWN
            return jnp.where(r == 0, first, jnp.where(r == ROWS - 1, 2, 1))

        tmask[...] = jnp.where((i % OWN == j % OWN) & (block_of(i) == block_of(j)), 1.0, 0.0)
    with scope("tok"):
        shr_t.forward()
    gc.s1()
    with scope("q_z"):
        sq.y_send()
    with scope("go2"):
        go.s2()
    e_all[pl.ds(2 * f, 2)] = cot[...]
    with scope("go3"):
        go.s3()
    f_u[f] = i_u[f]
    s_u.wait()
    w_u[me.z, me.y] = stacked(f_u)
    su.z_send()
    with scope("go4"):
        go.s4()
        go.s5()
    with scope("gains"):
        for k in range(D // 128):
            part = w_o[0, :, :, :, :, HALF : HALF + 128].reshape(D, 128)[k * 128 : (k + 1) * 128]
            gains[:, k * 128 : (k + 1) * 128] = part.astype(F32).T[:8]
    with scope("gc2"):
        gc.s2()
    with scope("tok2"):
        shr_t.near()
        shr_t.finish()

    with scope("norm_row"):

        def norm_rows(k, _):
            unit, _s = standard(tok_all[k].astype(F32))
            h1[k] = (unit * gains[0:1]).astype(BF16)
            return 0

        lax.fori_loop(0, ROWS, norm_rows, 0)
    with scope("q_y"):
        sq.finish()
    with scope("qkv_row"):
        wide = w_q[...].reshape(D, WIDE)

        def project(k, _):
            pair = h1[pl.ds(2 * k, 2)].reshape(2 * COLS, D)
            qkv[pl.ds(2 * k, 2)] = nn(pair, wide).astype(BF16).reshape(2, COLS, WIDE)
            return 0

        lax.fori_loop(0, ROWS // 2, project, 0)
    with scope("gc3"):
        gc.s3()
    w_d[me.z, me.y] = i_d[...]
    sd.z_send()

    joined = (jnp.full((1, 1), first, jnp.int32) == 1)
    tied = jnp.where(joined, 1.0, 0.0)
    s_mid = jnp.where(joined, FACTOR / 7**0.5, FACTOR / 6**0.5)
    lower = low_half((COLS, 128))
    zero = jnp.zeros((COLS, 128), BF16)

    def tile(ref, r, k):
        return ref[r, :, k * 128 : (k + 1) * 128]

    def head_tiles(r):
        q01, q2k2, k01 = tile(qkv, r, 0), tile(qkv, r, 1), tile(qkv, r, 2)
        k2 = pltpu.roll(q2k2.astype(F32), 64, 1).astype(BF16)
        return (
            (jnp.where(lower, q01, zero), k01),
            (jnp.where(lower, zero, q01), k01),
            (jnp.where(lower, q2k2, zero), k2),
        )

    with scope("row_fwd"):
        sums = [[None] * 3 for _ in range(3)]
        for r in range(ROWS):
            for h, (a, b) in enumerate(head_tiles(r)):
                s = nt(a, b)
                t = 0 if r == 0 else 2 if r == ROWS - 1 else 1
                sums[h][t] = s if sums[h][t] is None else sums[h][t] + s
        for h in range(3):
            s0, s1, s2 = sums[h]
            for t, s in enumerate((s0 * FACTOR, (s1 + tied * s0) * s_mid, s2 * FACTOR)):
                p_row[h, t] = softmax(jnp.where(cmask[...] > 0.5, s, NEGATIVE))

    def chances(h, r):
        if r == 0:
            return jnp.where(joined, p_row[h, 1], p_row[h, 0])
        return p_row[h, 2 if r == ROWS - 1 else 1]

    with scope("row_out"):
        for r in range(ROWS):
            v01, v2 = tile(qkv, r, 3), tile(qkv, r, 4)
            p = [chances(h, r).astype(BF16) for h in range(3)]
            o1f[r, :, :128] = jnp.where(lower, nn(p[0], v01), nn(p[1], v01)).astype(BF16)
            o1f[r, :, 128:] = nn(p[2], v2).astype(BF16)
    s_o = swap()
    s_o.go(lambda t: o1f.at[:, cols_of(t)], o1c.at[f])
    o1c[f] = o1f[:, own_cols]
    shr_e = Share(me, lambda k: e_all.at[pl.ds(2 * k, 2)], sems)
    shr_e.send()
    with scope("su_y"):
        su.y_send()
    with scope("gc4"):
        gc.s4()
    with scope("o1"):
        s_o.wait()

    def o1_of(k):
        return o1c[k].reshape(TOK, 256)[:, :192]

    def w_out(h, k):
        return w_o[h, k].reshape(192, 512)[:, :HALF]

    with scope("out_row"):
        for h in range(2):
            cols = slice(h * HALF, (h + 1) * HALF)
            total = tok_all[:, own_cols, cols].reshape(TOK, HALF).astype(F32)
            for k in range(4):
                total = total + nn(o1_of(k), w_out(h, k))
            x1[:, cols] = total

    def in_pieces(step, rows=64, total=TOK):
        def body(k, _):
            step(pl.ds(pl.multiple_of(k * rows, rows), rows))
            return 0

        lax.fori_loop(0, total // rows, body, 0)

    with scope("norm_col"):

        def norm_col(at):
            h2[at] = (standard(x1[at])[0] * gains[1:2]).astype(BF16)

        in_pieces(norm_col)
    with scope("gc5"):
        gc.s5()
        gc.drain()

    def w_col(part, k):
        off = part % 2 * D
        at = pl.ds(pl.multiple_of(off + k * 256, 256), 256)
        return w_c.at[part // 2, :, :, :, :, at]

    with scope("qkv_col"):
        for part in range(3):

            def project2(k, _, part=part):
                at = pl.ds(pl.multiple_of(k * 256, 256), 256)
                qkv2[part, :, at] = nn(h2[...], w_col(part, k)[...].reshape(D, 256)).astype(BF16)
                return 0

            lax.fori_loop(0, 3, project2, 0)
    with scope("sd_y"):
        sd.y_send()
        shr_e.forward()
    lower2 = low_half((TOK, 128))
    zero2 = jnp.zeros((TOK, 128), BF16)

    def pairs(step):
        def body(k, _):
            step(k, pl.ds(pl.multiple_of(k * 128, 128), 128))
            return 0

        lax.fori_loop(0, HEADS // 2, body, 0)

    with scope("col_fwd"):

        def col_pair(k, at):
            q, kk, v = (qkv2[n, :, at] for n in range(3))
            out = []
            for e in range(2):
                mine = jnp.where(lower2, q, zero2) if e == 0 else jnp.where(lower2, zero2, q)
                s = nt(mine, kk) * FACTOR
                p = softmax(jnp.where(tmask[...] > 0.5, s, NEGATIVE))
                p_col[2 * k + e] = p
                out.append(nn(p.astype(BF16), v))
            o2[:, at] = jnp.where(lower2, out[0], out[1]).astype(BF16)

        pairs(col_pair)
    with scope("out_col"):

        def close(k, _):
            at = pl.ds(pl.multiple_of(k * 256, 256), 256)
            x2[:, at] = x1[:, at] + nn(o2[...], w_col(3, k)[...].reshape(D, 256))
            return 0

        lax.fori_loop(0, 3, close, 0)
    with scope("norm_ffn"):

        def norm_ffn(at):
            h3[f, at] = (standard(x2[at])[0] * gains[2:3]).astype(BF16)

        in_pieces(norm_ffn)
    shr_h = Share(me, lambda k: h3.at[k], sems)
    shr_h.send()
    with scope("su_f"):
        su.finish()
    with scope("sd_f"):
        sd.finish()
        shr_e.near()
        shr_e.finish()

    def grads_of(b):
        return e_all[:, cols_of(b)].reshape(TOK, D)

    def ffn_block(b):
        grad = grads_of(b)
        y_sum, d_sum = None, None
        for k in range(2):
            at = slice(k * HALF, (k + 1) * HALF)
            up = w_u[:, :, :, at].reshape(D, HALF)
            down = w_d[2 * k : 2 * k + 2].reshape(HALF, D)
            u = nn(h3[b], up)
            bell = jnp.exp(-0.5 * u * u) * (1 / (2 * jnp.pi) ** 0.5)
            upper = 0.5 + 0.5 * lax.erf(u * 0.5**0.5)
            a = (u * upper).astype(BF16)
            act[b, :, at] = a
            d = (nt(grad, down) * (upper + u * bell)).astype(BF16)
            du[b, :, at] = d
            y, dd = nn(a, down), nt(d, up)
            y_sum = y if y_sum is None else y_sum + y
            d_sum = dd if d_sum is None else d_sum + dd
        yp[b] = y_sum.astype(BF16)
        dp[b] = d_sum.astype(BF16)

    cy = Collect(me, yp, l_y, sems)
    cd = Collect(me, dp, l_p, sems)
    order = (f, sib_f, x_f, diag_f)

    def ffn_two(first_block):
        def body(k, _):
            ffn_block(jnp.where(k == 0, order[first_block], order[first_block + 1]))
            return 0

        lax.fori_loop(0, 2, body, 0)

    with scope("h3_near"):
        shr_h.near()
    with scope("ffn1"):
        ffn_two(0)
    with scope("h3_far"):
        shr_h.forward()
    cd.near()
    cy.near()
    with scope("h3_diag"):
        shr_h.finish()
    with scope("ffn2"):
        ffn_two(2)
    cd.pair()
    cy.pair()
    with scope("dh3"):
        cd.cross()
    with scope("g_down"):
        for k in range(3):
            at = slice(k * 256, (k + 1) * 256)
            part = sum(tn(act[b], grads_of(b)[:, at]) for b in range(4))
            w_d[:, :, :, at] = part.astype(BF16).reshape(4, 2, 96, 256)
    sd.back_y()
    with scope("g_up"):
        for k in range(3):
            at = slice(k * 256, (k + 1) * 256)
            part = sum(tn(h3[b], du[b, :, at]) for b in range(4))
            w_u[:, :, :, at] = part.astype(BF16).reshape(4, 2, 96, 256)
    su.back_y()

    with scope("cd_w"):
        cd.finish()
    with scope("back_ffn"):

        def back_ffn(k, _):
            at = pl.ds(pl.multiple_of(k * OWN, OWN), OWN)
            g[at] = e_all[k, own_cols].astype(F32) + norm_back(x2[at], gains[2:3], cd.total(at))
            e1[at] = g[at].astype(BF16)
            return 0

        lax.fori_loop(0, ROWS, back_ffn, 0)
    with scope("mix"):
        cy.cross()
    with scope("do2"):
        for n in range(3):
            at = slice(n * 256, (n + 1) * 256)
            w = w_c[1, :, :, :, :, D:].reshape(D, D)[at]
            do2[:, at] = nt(e1[...], w).astype(BF16)
        for n in range(3):
            w_col(3, n)[...] = tn(o2[...], e1[:, n * 256 : (n + 1) * 256]).astype(BF16).reshape(4, 2, 2, 48, 256)
    with scope("col_bwd"):

        def col_back(k, at):
            q, kk, v, d = qkv2[0, :, at], qkv2[1, :, at], qkv2[2, :, at], do2[:, at]
            got = []
            for e in range(2):
                mine = jnp.where(lower2, d, zero2) if e == 0 else jnp.where(lower2, zero2, d)
                dq = nt(mine, v)
                p = p_col[2 * k + e]
                ds = (p * (dq - jnp.sum(dq * p, axis=-1, keepdims=True))).astype(BF16)
                got.append((nn(ds, kk) * FACTOR, tn(ds, q) * FACTOR, tn(p.astype(BF16), d)))
            for n in range(3):
                dqkv2[n, :, at] = jnp.where(lower2, got[0][n], got[1][n]).astype(BF16)

        pairs(col_back)
    with scope("sd_z"):
        sd.back_z()
    with scope("dh2"):
        for n in range(3):
            at = slice(n * 256, (n + 1) * 256)
            total = nt(dqkv2[0], w_c[0, :, :, :, :, :D].reshape(D, D)[at])
            total = total + nt(dqkv2[1], w_c[0, :, :, :, :, D:].reshape(D, D)[at])
            dh2[:, at] = total + nt(dqkv2[2], w_c[1, :, :, :, :, :D].reshape(D, D)[at])
    with scope("g_qkv_col"):
        for part in range(3):

            def grad_col(k, _, part=part):
                at = pl.ds(pl.multiple_of(k * 256, 256), 256)
                w_col(part, k)[...] = tn(h2[...], dqkv2[part, :, at]).astype(BF16).reshape(4, 2, 2, 48, 256)
                return 0

            lax.fori_loop(0, 3, grad_col, 0)
    rc.r0()
    with scope("su_z"):
        su.back_z()
    with scope("back_col"):

        def back_col(at):
            g[at] = g[at] + norm_back(x1[at], gains[1:2], dh2[at])
            e1[at] = g[at].astype(BF16)

        in_pieces(back_col)

    with scope("do1"):
        for k in range(4):
            d = nt(e1[:, :HALF], w_out(0, k)) + nt(e1[:, HALF:], w_out(1, k))
            d = jnp.concatenate([d, jnp.zeros((TOK, 64), F32)], axis=1)
            dost[k] = d.astype(BF16).reshape(ROWS, OWN, 256)
    s_d = swap()
    s_d.go(lambda t: dost.at[t], do1.at[:, own_cols])
    do1[:, own_cols] = dost[f]
    s_g = swap()
    s_g.go(lambda t: e1.at[pl.ds(pl.multiple_of(2 * OWN * t, 2 * OWN), 2 * OWN)], e1r.at[f])
    e1r[f] = e1[pl.ds(pl.multiple_of(2 * OWN * f, 2 * OWN), 2 * OWN)]
    with scope("rc1"):
        rc.r1()
    with scope("g_out_row"):
        go.drain()
        for h in range(2):
            for k in range(4):
                part = tn(o1_of(k), e1[:, h * HALF : (h + 1) * HALF])
                w_o[h, k, :, :, :, :HALF] = part.astype(BF16).reshape(2, 2, 48, HALF)
    ro.r0()
    with scope("mix2"):
        cy.finish()

        def mix(k, _):
            at = pl.ds(pl.multiple_of(k * OWN, OWN), OWN)
            mix_c[k] = (x2[at] + cy.total(at)).astype(BF16)
            return 0

        lax.fori_loop(0, ROWS, mix, 0)
    s_m = swap()
    s_m.go(lambda t: mix_c.at[pl.ds(2 * t, 2)], mix_r.at[:, own_cols])
    mix_r[:, own_cols] = mix_c[pl.ds(2 * f, 2)]
    with scope("do1w"):
        s_d.wait()
    with scope("row_bwd"):
        d_sum = [[None] * 3 for _ in range(3)]
        for r in range(ROWS):
            d01, d2, v01, v2 = tile(do1, r, 0), tile(do1, r, 1), tile(qkv, r, 3), tile(qkv, r, 4)
            ops = ((jnp.where(lower, d01, zero), v01), (jnp.where(lower, zero, d01), v01), (d2, v2))
            for h, (a, b) in enumerate(ops):
                s = nt(a, b)
                t = 0 if r == 0 else 2 if r == ROWS - 1 else 1
                d_sum[h][t] = s if d_sum[h][t] is None else d_sum[h][t] + s
        da, dat, pt = [], [], []
        for h in range(3):
            s0, s1, s2 = d_sum[h]
            by = []
            for t, s in enumerate((s0, s1 + tied * s0, s2)):
                p = p_row[h, t]
                by.append(p * (s - jnp.sum(s * p, axis=-1, keepdims=True)))
            da.append((jnp.where(joined, by[1], by[0]), by[1], by[2]))
            dat.append([a.T.astype(BF16) for a in da[h]])
            pt.append([chances(h, r).T.astype(BF16) for r in (0, 1, ROWS - 1)])
            da[h] = [a.astype(BF16) for a in da[h]]
        s_first = jnp.where(joined, s_mid, FACTOR)
        for r in range(ROWS):
            t = 0 if r == 0 else 2 if r == ROWS - 1 else 1
            scale = (s_first, s_mid, FACTOR)[t]
            q01, q2k2, k01 = tile(qkv, r, 0), tile(qkv, r, 1), tile(qkv, r, 2)
            d01, d2 = tile(do1, r, 0), tile(do1, r, 1)
            dq = jnp.where(lower, nn(da[0][t], k01), nn(da[1][t], k01)) * scale
            dk = jnp.where(lower, nn(dat[0][t], q01), nn(dat[1][t], q01)) * scale
            mid = jnp.where(lower, nn(dat[2][t], q2k2), nn(da[2][t], q2k2)) * scale
            dv = jnp.where(lower, nn(pt[0][t], d01), nn(pt[1][t], d01))
            for n, val in enumerate((dq, pltpu.roll(mid, 64, 1), dk, dv, nn(pt[2][t], d2))):
                dqkv[r, :, n * 128 : (n + 1) * 128] = val.astype(BF16)
    with scope("dh1"):
        wide = w_q[...].reshape(D, WIDE)

        def partial_dh(k, _):
            pair = dqkv[pl.ds(2 * k, 2)].reshape(2 * COLS, WIDE)
            hp[k] = nt(pair, wide).astype(BF16)
            return 0

        lax.fori_loop(0, 4, partial_dh, 0)
    ch = Collect(me, hp, l_h, sems)
    ch.pair()
    ch.near()
    with scope("g_qkv_row"):
        for n in range(WIDE // 128):
            at = slice(n * 128, (n + 1) * 128)
            total = tn(h1[...].reshape(ROWS * COLS, D), dqkv[:, :, at].reshape(ROWS * COLS, 128))
            w_q[:, :, :, at] = total.astype(BF16).reshape(4, 2, 96, 128)
    sq.back_y()
    with scope("dh1_x"):
        ch.cross()
    with scope("rc2"):
        rc.r2()
    with scope("ro1"):
        ro.r1()
    with scope("d_sum"):
        o_d[...] = sd.back_sum()
    with scope("u_sum"):
        t_u[...] = su.back_sum().reshape(t_u.shape)
    s_v = swap()
    s_v.go(lambda t: t_u.at[t], o_u.at[f])
    o_u[f] = t_u[f]
    with scope("rc3"):
        rc.r3()
    with scope("q1"):
        sq.back_z()
    with scope("ro2"):
        ro.r2()
    with scope("ro3"):
        ro.r3()
    with scope("in_grad"):
        ch.finish()
        s_g.wait()
        for r in range(2):
            for k in range(4):
                at = slice(k * OWN, (k + 1) * OWN)
                grad = ch.total(slice(r * COLS + k * OWN, r * COLS + (k + 1) * OWN))
                back = norm_back(tok[r, at].astype(F32), gains[0:1], grad)
                igrad[r, at] = e1r[k, r * OWN : (r + 1) * OWN].astype(F32) + back
        s_m.wait()
        mixed[...] = mix_r[...]
    with scope("c4"):
        rc.r4()
    with scope("q2"):
        t_q[...] = sq.back_sum().reshape(t_q.shape)
    s_t = swap()
    s_t.go(lambda t: t_q.at[t], o_q.at[f])
    o_q[f] = t_q[f]
    with scope("o4"):
        ro.r4()
    for k in (rc, ro):
        k.r5()
    s_v.wait()
    s_t.wait()
    assert used[0] <= SEMS, used[0]


SEMS = 72


def run_layer(tok, cot, seq, cid, i_q, i_o, i_c, i_u, i_d):
    sds = jax.ShapeDtypeStruct
    rows = i_c.shape[1]
    shapes = [
        sds(tok.shape, BF16),
        sds(tok.shape, F32),
        sds(i_q.shape, F32),
        sds(i_o.shape, F32),
        sds(i_c.shape, F32),
        sds(i_u.shape, F32),
        sds(i_d.shape, F32),
    ]

    def vmem(*shape, dtype=BF16):
        return pltpu.VMEM(shape, dtype)

    def lands(r, c):
        return [
            vmem(4, 2, 2, r, c), vmem(4, 2, r, c), vmem(4, r, c), vmem(3, r, c), vmem(2, r // 2, c, dtype=F32)
        ]

    def slices(c):
        return [vmem(4, 4 * rows, c), vmem(3, 4 * rows, c)]

    r2 = 2 * rows
    wo, wc, wu = i_o.shape[2], i_c.shape[2], i_u.shape[2]
    scratch = [
        vmem(4, 2, 4 * rows, WIDE),
        vmem(2, 4, 2, 2, r2, wo),
        vmem(2, 4, 2, 2, r2, wc),
        vmem(4, 2, 4 * rows, wu),
        vmem(4, 2, *i_d.shape),
        vmem(*i_q.shape),
        vmem(rows, wo),
        vmem(rows, wc),
        vmem(*i_u.shape),
        *lands(r2, wo),
        *lands(r2, wc),
        *slices(WIDE),
        vmem(*i_q.shape, dtype=F32),
        *slices(wu),
        vmem(*i_u.shape, dtype=F32),
        *slices(D),
        vmem(ROWS, COLS, D),
        vmem(ROWS, COLS, D),
        vmem(ROWS, COLS, D),
        vmem(ROWS, COLS, WIDE),
        vmem(3, 3, COLS, COLS, dtype=F32),
        vmem(ROWS, COLS, 256),
        vmem(4, ROWS, OWN, 256),
        vmem(TOK, D, dtype=F32),
        vmem(TOK, D),
        vmem(3, TOK, D),
        vmem(HEADS, TOK, TOK, dtype=F32),
        vmem(TOK, D),
        vmem(TOK, D, dtype=F32),
        vmem(4, TOK, D),
        vmem(4, TOK, D),
        vmem(4, TOK, D),
        vmem(4, TOK, D),
        vmem(3, TOK, D),
        vmem(4, TOK, D),
        vmem(3, TOK, D),
        vmem(TOK, D, dtype=F32),
        vmem(TOK, D),
        vmem(3, TOK, D),
        vmem(TOK, D, dtype=F32),
        vmem(TOK, D),
        vmem(4, ROWS, OWN, 256),
        vmem(ROWS, COLS, 256),
        vmem(ROWS, COLS, WIDE),
        vmem(4, TOK, D),
        vmem(3, TOK, D),
        vmem(ROWS, OWN, D),
        vmem(2, COLS, D),
        vmem(4, 2 * OWN, D),
        vmem(8, D, dtype=F32),
        vmem(COLS, COLS, dtype=F32),
        vmem(TOK, TOK, dtype=F32),
        pltpu.SemaphoreType.DMA((2, 9)),
        pltpu.SemaphoreType.DMA((2, 9)),
        pltpu.SemaphoreType.DMA((2, 7)),
        pltpu.SemaphoreType.DMA((2, 7)),
        pltpu.SemaphoreType.DMA((SEMS,)),
        pltpu.SemaphoreType.DMA((SEMS,)),
    ]
    vm = pl.BlockSpec(memory_space=pltpu.VMEM)
    return pl.pallas_call(
        layer_kernel,
        out_shape=shapes,
        in_specs=[vm, vm, pl.BlockSpec(memory_space=pltpu.SMEM)] + [vm] * 6,
        out_specs=[vm] * 7,
        scratch_shapes=scratch,
        name="layer",
        compiler_params=pltpu.CompilerParams(
            collective_id=0, has_side_effects=True, vmem_limit_bytes=VMEM_LIMIT
        ),
    )(tok, cot, seq, cid, i_q, i_o, i_c, i_u, i_d)


VMEM_LIMIT = 63 * 2**20


def on_device(
    tokens, cotangent, seq_ids, col_ids,
    gain_row, qkv_row, out_row, gain_col, qkv_col, out_col, gain_ffn, up_ffn, down_ffn,
    cells,
):
    members = CELL * lax.axis_size("fsdp")
    low_index = (lax.axis_index("dp") % CELL) * lax.axis_size("fsdp") + lax.axis_index("fsdp")

    def in_cell(shard):
        if cells == 1:
            return shard
        whole = lax.all_gather(shard, AXES, axis=0, tiled=True)
        rows = whole.shape[0] // members
        return lax.dynamic_slice_in_dim(whole, low_index * rows, rows, 0)

    def from_cell(summed):
        if cells == 1:
            return summed
        rows = summed.shape[0]
        whole = jnp.zeros((rows * members,) + summed.shape[1:], summed.dtype)
        whole = lax.dynamic_update_slice_in_dim(whole, summed, low_index * rows, 0)
        return lax.psum_scatter(whole, AXES, scatter_dimension=0, tiled=True)

    def halves(shard):
        return jnp.stack(jnp.split(shard, 2, axis=1))

    def unhalved(pair):
        return jnp.concatenate([pair[0], pair[1]], axis=1)

    wq = in_cell(qkv_row)
    rows = wq.shape[0]
    per = wq.reshape(rows, 3, 4, 3, HEAD)
    q, k, v = per[:, 0], per[:, 1], per[:, 2]
    i_q = jnp.concatenate([q, k[:, :, 2:], k[:, :, :2], v, jnp.zeros_like(v[:, :, :1])], axis=2)
    i_q = jnp.moveaxis(i_q.reshape(rows, 4, WIDE), 1, 0)
    gain = in_cell(jnp.stack([gain_row, gain_col, gain_ffn], axis=1))
    gain = jnp.pad(gain, ((0, 0), (0, 125)))
    wo = in_cell(out_row)
    i_o = jnp.stack([jnp.concatenate([wo[:, :HALF], gain], axis=1), jnp.concatenate([wo[:, HALF:], gain], axis=1)])
    i_c = halves(jnp.concatenate([in_cell(qkv_col), in_cell(out_col)], axis=1))
    i_u = jnp.moveaxis(in_cell(up_ffn).reshape(rows, FF // 384, 4, 96), 2, 0).reshape(4, rows, D)
    i_d = in_cell(down_ffn)
    mixed, igrad, o_q, o_o, o_c, o_u, o_d = run_layer(
        tokens[0], cotangent[0], seq_ids, col_ids, i_q, i_o, i_c, i_u, i_d
    )
    o_q = jnp.moveaxis(o_q, 0, 1).reshape(rows, 4, WIDE // HEAD, HEAD)
    back = jnp.stack(
        [o_q[:, :, 0:3], jnp.concatenate([o_q[:, :, 4:6], o_q[:, :, 3:4]], axis=2), o_q[:, :, 6:9]], axis=1
    )
    g_q = from_cell(back.reshape(rows, 3 * D))
    g_o = from_cell(unhalved(o_o[:, :, :HALF]))
    g_c = from_cell(unhalved(o_c))
    g_u = from_cell(jnp.moveaxis(o_u.reshape(4, rows, FF // 384, 96), 0, 2).reshape(rows, FF))
    g_d = from_cell(o_d)

    def gain_grad(weight, grad, gain):
        return jnp.sum(weight.astype(F32) * grad, axis=1) / gain.astype(F32)

    return (
        mixed[None],
        igrad[None],
        gain_grad(qkv_row, g_q, gain_row),
        g_q,
        g_o,
        gain_grad(qkv_col, g_c[:, : 3 * D], gain_col),
        g_c[:, : 3 * D],
        g_c[:, 3 * D :],
        gain_grad(up_ffn, g_u, gain_ffn),
        g_u,
        g_d,
    )


def solution(mesh):
    rows = P(AXES, None)
    vector = P(AXES)
    grid = P("dp", "fsdp", None, None)
    ids = P("dp", None)
    return jax.shard_map(
        partial(on_device, cells=mesh.shape["dp"] // CELL),
        mesh=mesh,
        in_specs=(grid, grid, ids, ids) + (vector, rows, rows) * 3,
        out_specs=(grid, grid) + (vector, rows, rows) * 3,
        check_vma=False,
    )
```

```python
from functools import partial

import jax
import jax.numpy as jnp
from jax import lax
from jax.experimental import pallas as pl
from jax.experimental.pallas import tpu as pltpu
from jax.sharding import PartitionSpec as P

HEADS = 12
EPSILON = 1e-05
NEGATIVE = -1000000000.0
MESH = pl.DeviceIdType.MESH
BF16 = jnp.bfloat16
F32 = jnp.float32
CELL = 8
AXES = ("dp", "fsdp")


class Place:
    def __init__(self):
        dp = lax.axis_index("dp")
        self.f = lax.axis_index("fsdp")
        self.base = dp // CELL * CELL
        low = dp - self.base
        self.z, self.y = low // 2, low % 2
        self.hi, self.lo = self.z // 2, self.z % 2
        self.x, self.c = self.f // 2, self.f % 2

    def dev(self, z, y, x, c):
        return (self.base + z * 2 + y, x * 2 + c)

    def sib(self):
        return self.dev(self.z, self.y, self.x, 1 - self.c)

    def xn(self):
        return self.dev(self.z, self.y, 1 - self.x, self.c)

    def yn(self):
        return self.dev(self.z, 1 - self.y, self.x, self.c)

    def first(self):
        return self.dev(self.z, self.y + self.c * (1 - 2 * self.y), self.x + (1 - self.c) * (1 - 2 * self.x), self.c)

    def second(self):
        return self.dev(self.z, self.y + (1 - self.c) * (1 - 2 * self.y), self.x + self.c * (1 - 2 * self.x), self.c)

    def z1(self):
        return self.dev(2 * self.hi + 1 - self.lo, self.y, self.x, self.c)

    def z2(self):
        return self.dev(2 * (1 - self.hi) + self.lo, self.y, self.x, self.c)


def greet(partners):
    bar = pltpu.get_barrier_semaphore()
    for t in partners:
        pl.semaphore_signal(bar, inc=1, device_id=t, device_id_type=MESH)
    pl.semaphore_wait(bar, len(partners))


def rcopy(src, dst, ss, rs, to):
    return pltpu.make_async_remote_copy(
        src_ref=src, dst_ref=dst, send_sem=ss, recv_sem=rs, device_id=to, device_id_type=MESH
    )


ALL = slice(None)


class Part:
    def __init__(self, me, w, at):
        self.me, self.w, self.at = me, w, at

    def block(self, hi, lo, y, x, half=None):
        return self.w.at[self.me.c if half is None else half, hi, lo, y, x, :, self.at]


class Gather(Part):
    def __init__(self, me, src_of, land, w, at, sems):
        super().__init__(me, w, at)
        self.src_of, self.land, self.sems = src_of, land, sems

    def swap(self):
        me = self.me
        self.c0 = rcopy(self.src_of(1 - me.c), self.land.at[:, self.at], *self.sems(), me.sib())
        self.c0.start()

    def start(self, ref, to):
        c = rcopy(ref, ref, *self.sems(), to)
        c.start()
        self.sent.append(c)
        return c

    def own(self):
        me = self.me
        self.c0.wait()
        mine = self.src_of(me.c)[...].astype(F32)
        other = self.land[:, self.at].astype(F32)
        flag = (me.c == 0).astype(F32)
        top = flag * mine + (1 - flag) * other
        low = flag * other + (1 - flag) * mine
        own = self.block(me.hi, me.lo, me.y, me.x)
        own[...] = jnp.concatenate([top, low], axis=0).astype(BF16)
        self.sent = []

    def s0(self):
        me = self.me
        self.own()
        self.a = self.start(self.block(me.hi, me.lo, me.y, me.x), me.z2())

    def s1(self):
        me = self.me
        self.a.wait_recv()
        self.b = self.start(self.block(ALL, me.lo, me.y, me.x), me.z1())

    def s2(self):
        me = self.me
        self.b.wait_recv()
        col = self.block(ALL, ALL, me.y, me.x)
        self.e = self.start(col, me.first())
        self.to_sib = [self.start(col, me.sib())]

    def fork(self, ref0, ref1, to, like):
        me, m = self.me, self.sems()

        @pl.when(me.c == 0)
        def _():
            rcopy(ref0, ref0, *m, to).start()

        @pl.when(me.c == 1)
        def _():
            rcopy(ref1, ref1, *m, to).start()

        c = rcopy(like, like, *m, to)
        self.sent.append(c)
        return c

    def s3(self):
        me = self.me
        self.e.wait_recv()
        two, col = self.block(ALL, ALL, me.y, ALL), self.block(ALL, ALL, me.y, me.x)
        self.g = self.fork(
            self.block(ALL, ALL, me.y, ALL, 0), self.block(ALL, ALL, ALL, me.x, 1), me.second(), two
        )
        self.to_sib.append(
            self.fork(
                self.block(ALL, ALL, me.y, 1 - me.x, 0), self.block(ALL, ALL, 1 - me.y, me.x, 1), me.sib(), col
            )
        )

    def s4(self):
        me = self.me
        self.g.wait_recv()
        two = self.block(ALL, ALL, me.y, ALL)
        self.to_sib.append(
            self.fork(
                self.block(ALL, ALL, 1 - me.y, ALL, 0), self.block(ALL, ALL, ALL, 1 - me.x, 1), me.sib(), two
            )
        )

    def s5(self):
        for c in self.to_sib:
            c.wait_recv()

    def drain(self):
        for c in self.sent:
            c.wait_send()


class EarlyGather(Gather):
    def s0(self):
        me = self.me
        self.own()
        self.e = self.start(self.block(me.hi, me.lo, me.y, me.x), me.yn())

    def s1(self):
        me = self.me
        self.e.wait_recv()
        self.g = self.start(self.block(me.hi, me.lo, ALL, me.x), me.xn())

    def s2(self):
        me = self.me
        self.g.wait_recv()
        mine = self.block(me.hi, me.lo, ALL, ALL)
        self.a = self.start(mine, me.z2())
        self.to_sib = [self.start(mine, me.sib())]

    def s3(self):
        me = self.me
        self.a.wait_recv()
        self.b = self.start(self.block(ALL, me.lo, ALL, ALL), me.z1())
        self.to_sib.append(self.start(self.block(1 - me.hi, me.lo, ALL, ALL), me.sib()))

    def s4(self):
        me = self.me
        self.b.wait_recv()
        self.to_sib.append(self.start(self.block(ALL, 1 - me.lo, ALL, ALL), me.sib()))


class Reduce(Part):
    def __init__(self, me, w, at, lands, out_of, sems):
        super().__init__(me, w, at)
        self.l0, self.l1, self.l2, self.l3, self.l4 = lands
        self.out_of, self.sems = out_of, sems

    def add(self, n, mine_of, land_of):
        def body(k, _):
            mine = mine_of(k)
            mine[...] = (mine[...].astype(F32) + land_of(k)[...].astype(F32)).astype(BF16)
            return 0

        lax.fori_loop(0, n, body, 0)

    def r0(self):
        me = self.me
        self.c0 = rcopy(
            self.block(ALL, ALL, ALL, ALL, 1 - me.c), self.l0.at[:, :, :, :, :, self.at], *self.sems(), me.sib()
        )
        self.c0.start()

    def r1(self):
        me = self.me
        self.c0.wait()
        self.add(
            16,
            lambda k: self.block(k // 8, k // 4 % 2, k // 2 % 2, k % 2),
            lambda k: self.l0.at[k // 8, k // 4 % 2, k // 2 % 2, k % 2, :, self.at],
        )
        land, m = self.l1.at[:, :, :, :, self.at], self.sems()

        @pl.when(me.c == 0)
        def _():
            rcopy(self.block(ALL, ALL, 1 - me.y, ALL, 0), land, *m, me.second()).start()

        @pl.when(me.c == 1)
        def _():
            rcopy(self.block(ALL, ALL, ALL, 1 - me.x, 1), land, *m, me.second()).start()

        self.c1 = rcopy(land, land, *m, me.sib())

    def r2(self):
        me = self.me
        self.c1.wait()

        def mine(k):
            m = k % 2
            y, x = me.y + me.c * (m - me.y), me.x + (1 - me.c) * (m - me.x)
            return self.block(k // 4, k // 2 % 2, y, x)

        self.add(8, mine, lambda k: self.l1.at[k // 4, k // 2 % 2, k % 2, :, self.at])
        oy = me.y + me.c * (1 - 2 * me.y)
        ox = me.x + (1 - me.c) * (1 - 2 * me.x)
        self.c2 = rcopy(self.block(ALL, ALL, oy, ox), self.l2.at[:, :, :, self.at], *self.sems(), me.first())
        self.c2.start()

    def r3(self):
        me = self.me
        self.c2.wait()
        self.add(
            4, lambda k: self.block(k // 2, k % 2, me.y, me.x), lambda k: self.l2.at[k // 2, k % 2, :, self.at]
        )
        self.c3 = rcopy(
            self.block(ALL, 1 - me.lo, me.y, me.x), self.l3.at[pl.ds(0, 2), :, self.at], *self.sems(), me.z1()
        )
        self.c3.start()

    def r3b(self):
        me = self.me
        self.c3.wait()
        self.add(2, lambda k: self.block(k, me.lo, me.y, me.x), lambda k: self.l3.at[k, :, self.at])
        self.c3 = rcopy(
            self.block(1 - me.hi, me.lo, me.y, me.x), self.l3.at[2, :, self.at], *self.sems(), me.z2()
        )
        self.c3.start()

    def r4(self):
        me = self.me
        self.c3.wait()
        total = self.block(me.hi, me.lo, me.y, me.x)[...].astype(F32) + self.l3[2, :, self.at].astype(F32)
        half = total.shape[0] // 2
        flag = (me.c == 0).astype(F32)
        top, low = total[:half], total[half:]
        self.out_of(me.c)[...] = flag * top + (1 - flag) * low
        self.l4[0, :, self.at] = flag * low + (1 - flag) * top
        self.c4 = rcopy(self.l4.at[0, :, self.at], self.l4.at[1, :, self.at], *self.sems(), me.sib())
        self.c4.start()

    def r5(self):
        self.c4.wait()
        self.out_of(1 - self.me.c)[...] = self.l4[1, :, self.at]


class EarlyReduce(Reduce):
    def go(self, src, land, to):
        self.c = rcopy(src, land, *self.sems(), to)
        self.c.start()

    def r1(self):
        me = self.me
        self.c0.wait()
        self.add(
            16,
            lambda k: self.block(k // 8, k // 4 % 2, k // 2 % 2, k % 2),
            lambda k: self.l0.at[k // 8, k // 4 % 2, k // 2 % 2, k % 2, :, self.at],
        )
        self.go(self.block(ALL, 1 - me.lo, ALL, ALL), self.l1.at[:, :, :, :, self.at], me.z1())

    def r2(self):
        me = self.me
        self.c.wait()
        self.add(
            8,
            lambda k: self.block(k // 4, me.lo, k // 2 % 2, k % 2),
            lambda k: self.l1.at[k // 4, k // 2 % 2, k % 2, :, self.at],
        )
        self.go(self.block(1 - me.hi, me.lo, ALL, ALL), self.l2.at[:, :, :, self.at], me.z2())

    def r3(self):
        me = self.me
        self.c.wait()
        self.add(
            4,
            lambda k: self.block(me.hi, me.lo, k // 2, k % 2),
            lambda k: self.l2.at[k // 2, k % 2, :, self.at],
        )
        self.go(self.block(me.hi, me.lo, ALL, 1 - me.x), self.l3.at[pl.ds(0, 2), :, self.at], me.xn())

    def r3b(self):
        me = self.me
        self.c.wait()
        self.add(2, lambda k: self.block(me.hi, me.lo, k, me.x), lambda k: self.l3.at[k, :, self.at])
        self.go(self.block(me.hi, me.lo, 1 - me.y, me.x), self.l3.at[2, :, self.at], me.yn())
        self.c3 = self.c


class Swap:
    def __init__(self, me, ssem, rsem):
        self.me, self.ss, self.rs, self.sent = me, ssem, rsem, []

    def other(self, d):
        return (self.me.f + d) % 4

    def go(self, src_of, dst):
        me = self.me
        for d in (1, 2, 3):
            t = self.other(d)
            c = rcopy(src_of(t), dst, self.ss.at[d - 1], self.rs.at[d - 1], me.dev(me.z, me.y, t // 2, t % 2))
            c.start()
            self.sent.append(c)

    def wait(self):
        for c in self.sent:
            c.wait_send()
            c.wait_recv()


class Slices:
    def __init__(self, me, w, at, l1, l2, sems, early=False):
        self.me, self.w, self.at, self.l1, self.l2, self.sems, self.early = me, w, at, l1, l2, sems, early
        self.sent = []

    def part(self, hi, lo, y):
        return self.w.at[hi, lo, y, :, self.at]

    def steps(self):
        me = self.me
        if self.early:
            return (
                (self.part(me.hi, me.lo, me.y), me.yn()),
                (self.part(me.hi, me.lo, ALL), me.z2()),
                (self.part(ALL, me.lo, ALL), me.z1()),
            )
        return (
            (self.part(me.hi, me.lo, me.y), me.z2()),
            (self.part(ALL, me.lo, me.y), me.z1()),
            (self.part(ALL, ALL, me.y), me.yn()),
        )

    def send(self, n):
        if n:
            self.sent[-1].wait_recv()
        ref, to = self.steps()[n]
        c = rcopy(ref, ref, *self.sems(), to)
        c.start()
        self.sent.append(c)

    def finish(self):
        self.sent[-1].wait_recv()
        for c in self.sent:
            c.wait_send()

    def kept(self, n):
        me = self.me
        if self.early:
            return (
                (4, lambda k: self.part(k // 2, me.lo, k % 2)),
                (2, lambda k: self.part(me.hi, me.lo, k)),
            )[n]
        return (
            (4, lambda k: self.part(k // 2, k % 2, me.y)),
            (2, lambda k: self.part(k, me.lo, me.y)),
        )[n]

    def back(self, n):
        me = self.me
        if n:
            self.c.wait()
            count, mine_of = self.kept(n - 1)

            def body(k, _):
                mine = mine_of(k)
                land = self.l1[k // 2, k % 2, :, self.at] if n == 1 else self.l2[k, :, self.at]
                mine[...] = (mine[...].astype(F32) + land.astype(F32)).astype(BF16)
                return 0

            lax.fori_loop(0, count, body, 0)
        lands = (self.l1.at[:, :, :, self.at], self.l2.at[pl.ds(0, 2), :, self.at], self.l2.at[2, :, self.at])
        if self.early:
            src, to = (
                (self.part(ALL, 1 - me.lo, ALL), me.z1()),
                (self.part(1 - me.hi, me.lo, ALL), me.z2()),
                (self.part(me.hi, me.lo, 1 - me.y), me.yn()),
            )[n]
        else:
            src, to = (
                (self.part(ALL, ALL, 1 - me.y), me.yn()),
                (self.part(ALL, 1 - me.lo, me.y), me.z1()),
                (self.part(1 - me.hi, me.lo, me.y), me.z2()),
            )[n]
        self.c = rcopy(src, lands[n], *self.sems(), to)
        self.c.start()

    def back_sum(self):
        me = self.me
        self.c.wait()
        return self.part(me.hi, me.lo, me.y)[...].astype(F32) + self.l2[2, :, self.at].astype(F32)


class Share:
    def __init__(self, me, whole, sems):
        self.me, self.sems = me, sems
        self.whole = whole

    def send(self):
        me = self.me
        own = self.whole(me.f)
        self.s = rcopy(own, own, *self.sems(), me.sib())
        self.x = rcopy(own, own, *self.sems(), me.xn())
        self.s.start()
        self.x.start()

    def near(self):
        self.s.wait()

    def forward(self):
        me = self.me
        self.x.wait_recv()
        got = self.whole(2 * (1 - me.x) + me.c)
        self.t = rcopy(got, got, *self.sems(), me.sib())
        self.t.start()

    def finish(self):
        self.x.wait_send()
        self.t.wait()


class Collect:
    def __init__(self, me, part_of, lands, sems):
        self.me, self.part_of, self.lands, self.sems = me, part_of, lands, sems

    def near(self):
        me = self.me
        self.n = rcopy(self.part_of(2 * me.x + 1 - me.c), self.lands.at[0], *self.sems(), me.sib())
        self.n.start()

    def pair(self):
        me = self.me
        self.p = rcopy(self.part_of(2 * (1 - me.x) + 1 - me.c), self.lands.at[1], *self.sems(), me.sib())
        self.p.start()

    def cross(self):
        me = self.me
        self.p.wait()
        part = self.part_of(2 * (1 - me.x) + me.c)

        def add(k, _):
            mine = part.at[k]
            mine[...] = (mine[...].astype(F32) + self.lands[1, k].astype(F32)).astype(BF16)
            return 0

        lax.fori_loop(0, 4, add, 0)
        self.x = rcopy(part, self.lands.at[2], *self.sems(), me.xn())
        self.x.start()

    def finish(self):
        self.n.wait()
        self.x.wait()

    def total(self, k, at):
        own = self.part_of(self.me.f)[k, at].astype(F32) + self.lands[0, k, at].astype(F32)
        return own + self.lands[2, k, at].astype(F32)


def nn(a, b):
    return lax.dot_general(a, b, (((1,), (0,)), ((), ())), preferred_element_type=F32)


def nt(a, b):
    return lax.dot_general(a, b, (((1,), (1,)), ((), ())), preferred_element_type=F32)


def tn(a, b):
    return lax.dot_general(a, b, (((0,), (0,)), ((), ())), preferred_element_type=F32)


def standard(values):
    centred = values - jnp.mean(values, axis=-1, keepdims=True)
    scale = lax.rsqrt(jnp.mean(centred * centred, axis=-1, keepdims=True) + EPSILON)
    return centred * scale, scale


def norm_back(values, gain, grad):
    unit, scale = standard(values)
    inner = grad * gain
    low = jnp.mean(inner, axis=-1, keepdims=True)
    high = jnp.mean(inner * unit, axis=-1, keepdims=True)
    return scale * (inner - low - unit * high)


def softmax(scores):
    e = jnp.exp(scores - jnp.max(scores, axis=-1, keepdims=True))
    return e / jnp.sum(e, axis=-1, keepdims=True)


def low_half(shape):
    return lax.broadcasted_iota(jnp.int32, shape, 1) % 128 < 64


def by_halves(pieces):
    out = []
    for n, piece in enumerate(pieces):
        if piece is None:
            out.append(jnp.zeros_like(pieces[0][0][:, :128]))
            continue
        ref, k = piece
        part = ref[:, k // 2 * 128 : k // 2 * 128 + 128].astype(F32)
        out.append(part if k % 2 == n else pltpu.roll(part, 64, 1))
    return jnp.where(low_half(out[0].shape), out[0], out[1])


def head_order(f):
    q, k, v = (HEADS * n + 3 * f for n in range(3))
    return ((q, q + 1), (q + 2, k + 2), (k, k + 1), (v, v + 1), (v + 2, None))


def spread(parts, shifts):
    lane = lax.broadcasted_iota(jnp.int32, parts[0].shape, 1) // 96
    total = None
    for n in range(4):
        part = pltpu.roll(parts[n], shifts[n] % 4 * 96, 1) if shifts[n] % 4 else parts[n]
        total = part if total is None else jnp.where(lane == n, part, total)
    return total


def upright(row):
    n = row.shape[1]
    i, j = (lax.broadcasted_iota(jnp.int32, (n, n), k) for k in range(2))
    return jnp.sum(jnp.where(i == j, jnp.broadcast_to(row, (n, n)), 0.0), axis=1, keepdims=True)


def level(column):
    n = column.shape[0]
    i, j = (lax.broadcasted_iota(jnp.int32, (n, n), k) for k in range(2))
    return jnp.sum(jnp.where(i == j, jnp.broadcast_to(column, (n, n)), 0.0), axis=0, keepdims=True)


D, FF, ROWS, COLS, HEAD = 768, 3072, 8, 128, 64
HALF = D // 2
OWN = COLS // 4
TOK = ROWS * OWN
WIDE = 640
FACTOR = HEAD**-0.5


def layer_kernel(
    tok, cot, seq, cid, gain_row, r_q, r_o, gain_col, r_c, r_co, gain_ffn, r_u, r_d,
    mixed, igrad, o_q, d_o, d_c, d_co, o_u, d_d,
    i_q, i_u, i_g,
    w_q, w_o, w_c, w_u, w_d, f_q, f_o, f_c, f_u,
    l_o0, l_o1, l_o2, l_o3, l_o4,
    l_c0, l_c1, l_c2, l_c3, l_c4,
    l_q1, l_q2, t_q, l_u1, l_u2, t_u, l_d1, l_d2,
    tok_all, e_all, h1, qkv, p_row, o1f, o1c, x1, h2, qkv2, p_col, o2, x2, h3, act, du, yp, l_y, dp, l_p,
    g, do2, dqkv2, dh2, e1, dost, do1, dqkv, e1r, gains, cmask, tmask, ms, mr,
):
    me = Place()
    f = me.f
    scope = jax.named_scope
    sib_f, x_f, diag_f = 2 * me.x + 1 - me.c, 2 * (1 - me.x) + me.c, 2 * (1 - me.x) + 1 - me.c
    diag = me.dev(me.z, me.y, 1 - me.x, 1 - me.c)
    greet([me.sib(), me.xn(), diag, me.yn(), me.z1(), me.z2()])
    used = [0]

    def sems():
        used[0] += 1
        return ms.at[used[0] - 1], mr.at[used[0] - 1]

    def swap():
        used[0] += 3
        at = pl.ds(used[0] - 3, 3)
        return Swap(me, ms.at[at], mr.at[at])

    at_w, at_g = pl.ds(0, HALF), pl.ds(HALF, 128)
    at_qv, at_k, at_o = pl.ds(0, D), pl.ds(D, HALF), pl.ds(D + HALF, HALF)

    def lanes(ref, start, step, size):
        return lambda h: ref.at[:, pl.ds(pl.multiple_of(start + h * step, 128), size)]

    of_o = lanes(r_o, 0, HALF, HALF)
    of_qv, of_k, of_co = lanes(r_c, 0, 2 * D, D), lanes(r_c, D, HALF, HALF), lanes(r_co, 0, HALF, HALF)
    go = Gather(me, of_o, f_o, w_o, at_w, sems)
    gg = Gather(me, lambda h: i_g, f_o, w_o, at_g, sems)
    g_qv = Gather(me, of_qv, f_c, w_c, at_qv, sems)
    g_k = EarlyGather(me, of_k, f_c, w_c, at_k, sems)
    g_out = Gather(me, of_co, f_c, w_c, at_o, sems)
    ro = Reduce(me, w_o, at_w, (l_o0, l_o1, l_o2, l_o3, l_o4), lanes(d_o, 0, HALF, HALF), sems)
    r_qv, r_k, r_out = (
        kind(me, w_c, at, (l_c0, l_c1, l_c2, l_c3, l_c4), out, sems)
        for kind, at, out in (
            (Reduce, at_qv, lanes(d_c, 0, 2 * D, D)),
            (EarlyReduce, at_k, lanes(d_c, D, HALF, HALF)),
            (Reduce, at_o, lanes(d_co, 0, HALF, HALF)),
        )
    )
    sq = [Slices(me, w_q, pl.ds(*at), l_q1, l_q2, sems, at[0] > 0) for at in ((0, 384), (384, 256))]
    su = [Slices(me, w_u, pl.ds(k * HALF, HALF), l_u1, l_u2, sems) for k in range(2)]
    sd = [Slices(me, w_d, pl.ds(k * HALF, HALF), l_d1, l_d2, sems, k == 0) for k in range(2)]

    def cols_of(t):
        return pl.ds(pl.multiple_of(t * OWN, OWN), OWN)

    own_cols = cols_of(f)

    def stacked(land):
        return jnp.concatenate([land[k].astype(F32) for k in range(4)], axis=0).astype(BF16)

    for t in range(4):
        for n, pair in enumerate(head_order(t)):
            pieces = [None if k is None else (r_q, k) for k in pair]
            i_q[t, :, n * 128 : (n + 1) * 128] = by_halves(pieces).astype(BF16)
    s_q = swap()
    s_q.go(lambda t: i_q.at[t], f_q.at[f])
    columns = [upright(v[...].astype(F32)) for v in (gain_row, gain_col, gain_ffn)]
    lane = lax.broadcasted_iota(jnp.int32, i_g.shape, 1)
    i_g[...] = sum(jnp.where(lane == n, v, 0.0) for n, v in enumerate(columns)).astype(BF16)
    for k in (gg, g_k, g_qv, go, g_out):
        k.swap()
    tok_all[pl.ds(2 * f, 2)] = tok[...]
    shr_t = Share(me, lambda k: tok_all.at[pl.ds(2 * k, 2)], sems)
    shr_t.send()
    w_d[me.hi, me.lo, me.y] = r_d[...]
    sd[0].send(0)
    with scope("gg0"):
        gg.s0()
    with scope("k0"):
        g_k.s0()
    with scope("q_f"):
        f_q[f] = i_q[f]
        s_q.wait()
        w_q[me.hi, me.lo, me.y] = stacked(f_q)
    sq[1].send(0)
    sq[0].send(0)
    with scope("gg1"):
        gg.s1()
    with scope("i_u"):
        for t in range(4):
            for n in range(2):
                parts = [r_u[:, (4 * n + k) * 384 : (4 * n + k + 1) * 384].astype(F32) for k in range(4)]
                i_u[t, :, n * 384 : (n + 1) * 384] = spread(parts, [k - t for k in range(4)]).astype(BF16)
    s_u = swap()
    s_u.go(lambda t: i_u.at[t], f_u.at[f])
    with scope("masks"):
        first = seq[0, 0]
        ids = jnp.broadcast_to(cid[...], (COLS, COLS)).astype(F32)
        cmask[...] = jnp.where(ids == ids.T, 1.0, 0.0)
        i = lax.broadcasted_iota(jnp.int32, (TOK, TOK), 0)
        j = lax.broadcasted_iota(jnp.int32, (TOK, TOK), 1)

        def block_of(k):
            r = k // OWN
            return jnp.where(r == 0, first, jnp.where(r == ROWS - 1, 2, 1))

        tmask[...] = jnp.where((i % OWN == j % OWN) & (block_of(i) == block_of(j)), 1.0, 0.0)
        e_all[pl.ds(2 * f, 2)] = cot[...]
        f_u[f] = i_u[f]
    with scope("q_m1"):
        sq[1].send(1)
    with scope("gg2"):
        gg.s2()
    with scope("q_m0"):
        sq[0].send(1)
    g_qv.s0()
    with scope("k1"):
        g_k.s1()
    with scope("gg3"):
        gg.s3()
    with scope("q_n1"):
        sq[1].send(2)
    with scope("gg4"):
        gg.s4()
    with scope("q_n0"):
        sq[0].send(2)
    with scope("k2"):
        g_k.s2()
    with scope("qv1"):
        g_qv.s1()
    with scope("tok"):
        shr_t.forward()
    with scope("gg5"):
        gg.s5()
    with scope("gains"):
        for k in range(D // 128):
            part = w_o[0, :, :, :, :, :, HALF : HALF + 128].reshape(D, 128)[k * 128 : (k + 1) * 128]
            gains[:, k * 128 : (k + 1) * 128] = part.astype(F32).T[:8]
    go.s0()
    with scope("tok2"):
        shr_t.near()
        shr_t.finish()

    with scope("norm_row"):

        def norm_rows(k, _):
            unit, _s = standard(tok_all[k].astype(F32))
            h1[k] = (unit * gains[0:1]).astype(BF16)
            return 0

        lax.fori_loop(0, ROWS, norm_rows, 0)
    with scope("qv2"):
        g_qv.s2()
    with scope("k3"):
        g_k.s3()
    with scope("go1"):
        go.s1()
    with scope("q_fin"):
        sq[1].finish()
        sq[0].finish()
    with scope("qkv_row"):
        wide = w_q[...].reshape(D, WIDE)

        def project(k, _):
            pair = h1[pl.ds(2 * k, 2)].reshape(2 * COLS, D)
            qkv[pl.ds(2 * k, 2)] = nn(pair, wide).astype(BF16).reshape(2, COLS, WIDE)
            return 0

        lax.fori_loop(0, ROWS // 2, project, 0)
    with scope("qv3"):
        g_qv.s3()

    joined = (jnp.full((1, 1), first, jnp.int32) == 1)
    tied = jnp.where(joined, 1.0, 0.0)
    s_mid = jnp.where(joined, FACTOR / 7**0.5, FACTOR / 6**0.5)
    lower = low_half((COLS, 128))
    zero = jnp.zeros((COLS, 128), BF16)

    def tile(ref, r, k):
        return ref[r, :, k * 128 : (k + 1) * 128]

    def head_tiles(r):
        q01, q2k2, k01 = tile(qkv, r, 0), tile(qkv, r, 1), tile(qkv, r, 2)
        k2 = pltpu.roll(q2k2.astype(F32), 64, 1).astype(BF16)
        return (
            (jnp.where(lower, q01, zero), k01),
            (jnp.where(lower, zero, q01), k01),
            (jnp.where(lower, q2k2, zero), k2),
        )

    with scope("row_fwd"):
        sums = [[None] * 3 for _ in range(3)]
        for r in range(ROWS):
            for h, (a, b) in enumerate(head_tiles(r)):
                s = nt(a, b)
                t = 0 if r == 0 else 2 if r == ROWS - 1 else 1
                sums[h][t] = s if sums[h][t] is None else sums[h][t] + s
        for h in range(3):
            s0, s1, s2 = sums[h]
            for t, s in enumerate((s0 * FACTOR, (s1 + tied * s0) * s_mid, s2 * FACTOR)):
                p_row[h, t] = softmax(jnp.where(cmask[...] > 0.5, s, NEGATIVE))

    def chances(h, r):
        if r == 0:
            return jnp.where(joined, p_row[h, 1], p_row[h, 0])
        return p_row[h, 2 if r == ROWS - 1 else 1]

    with scope("row_out"):
        for r in range(ROWS):
            v01, v2 = tile(qkv, r, 3), tile(qkv, r, 4)
            p = [chances(h, r).astype(BF16) for h in range(3)]
            o1f[r, :, :128] = jnp.where(lower, nn(p[0], v01), nn(p[1], v01)).astype(BF16)
            o1f[r, :, 128:] = nn(p[2], v2).astype(BF16)
    s_o = swap()
    s_o.go(lambda t: o1f.at[:, cols_of(t)], o1c.at[f])
    o1c[f] = o1f[:, own_cols]
    with scope("go2"):
        go.s2()
    g_out.s0()
    with scope("sd_m0"):
        sd[0].send(1)
    s_u.wait()
    w_u[me.hi, me.lo, me.y] = stacked(f_u)
    su[0].send(0)
    with scope("go3"):
        go.s3()
    with scope("k4"):
        g_k.s4()
    with scope("out1"):
        g_out.s1()
    with scope("sd_n0"):
        sd[0].send(2)
    with scope("su_m0"):
        su[0].send(1)
    su[1].send(0)
    with scope("qv4"):
        g_qv.s4()
    with scope("o1"):
        s_o.wait()

    def o1_of(k):
        return o1c[k].reshape(TOK, 256)[:, :192]

    def w_out(h, k):
        return w_o[h, k // 2, k % 2].reshape(192, 512)[:, :HALF]

    shr_e = Share(me, lambda k: e_all.at[pl.ds(2 * k, 2)], sems)
    shr_e.send()
    with scope("out2"):
        g_out.s2()
    with scope("go4"):
        go.s4()
        go.s5()
    with scope("su_m1"):
        su[1].send(1)
    sd[1].send(0)
    with scope("out_row"):
        for h in range(2):
            cols = slice(h * HALF, (h + 1) * HALF)
            total = tok_all[:, own_cols, cols].reshape(TOK, HALF).astype(F32)
            for k in range(4):
                total = total + nn(o1_of(k), w_out(h, k))
            x1[:, cols] = total

    def in_pieces(step, rows=64, total=TOK):
        def body(k, _):
            step(pl.ds(pl.multiple_of(k * rows, rows), rows))
            return 0

        lax.fori_loop(0, total // rows, body, 0)

    with scope("norm_col"):

        def norm_col(at):
            h2[at] = (standard(x1[at])[0] * gains[1:2]).astype(BF16)

        in_pieces(norm_col)

    def w_col(part, k):
        half, off = ((0, k * HALF), (k, D), (1, k * HALF), (k, D + HALF))[part]
        return w_c.at[half, :, :, :, :, :, off : off + HALF]

    def project2(part):
        for k in range(2):
            at = slice(k * HALF, (k + 1) * HALF)
            qkv2[part, :, at] = nn(h2[...], w_col(part, k)[...].reshape(D, HALF)).astype(BF16)

    with scope("out3"):
        g_out.s3()
    with scope("qv5"):
        g_qv.s5()
    with scope("qkv_col"):
        project2(0)
        project2(2)
        g_k.s5()
        project2(1)
    with scope("su_y0"):
        su[0].send(2)
    with scope("sd_m1"):
        sd[1].send(1)
    with scope("out4"):
        g_out.s4()
    with scope("su_y1"):
        su[1].send(2)
    lower2 = low_half((TOK, 128))
    zero2 = jnp.zeros((TOK, 128), BF16)

    def pairs(step):
        def body(k, _):
            step(k, pl.ds(pl.multiple_of(k * 128, 128), 128))
            return 0

        lax.fori_loop(0, HEADS // 2, body, 0)

    with scope("col_fwd"):

        def col_pair(k, at):
            q, kk, v = (qkv2[n, :, at] for n in range(3))
            out = []
            for e in range(2):
                mine = jnp.where(lower2, q, zero2) if e == 0 else jnp.where(lower2, zero2, q)
                s = nt(mine, kk) * FACTOR
                p = softmax(jnp.where(tmask[...] > 0.5, s, NEGATIVE))
                p_col[2 * k + e] = p
                out.append(nn(p.astype(BF16), v))
            o2[:, at] = jnp.where(lower2, out[0], out[1]).astype(BF16)

        pairs(col_pair)
    with scope("sd_n1"):
        sd[1].send(2)
    with scope("e_f"):
        shr_e.forward()
    with scope("out_col"):
        g_out.s5()
        for k in range(2):
            at = slice(k * HALF, (k + 1) * HALF)
            x2[:, at] = x1[:, at] + nn(o2[...], w_col(3, k)[...].reshape(D, HALF))
    with scope("norm_ffn"):

        def norm_ffn(at):
            h3[f, at] = (standard(x2[at])[0] * gains[2:3]).astype(BF16)

        in_pieces(norm_ffn)
    shr_h = Share(me, lambda k: h3.at[k], sems)
    shr_h.send()
    for k in (gg, go, g_qv, g_k, g_out):
        k.drain()
    with scope("su_f"):
        for k in su:
            k.finish()
    with scope("e"):
        shr_e.near()
        shr_e.finish()
    with scope("sd_f"):
        for k in sd:
            k.finish()

    def grads_of(b):
        return e_all[:, cols_of(b)].reshape(TOK, D)

    def ffn_block(b):
        grad = grads_of(b)
        y_sum, d_sum = None, None
        for k in range(2):
            at = slice(k * HALF, (k + 1) * HALF)
            up = w_u[:, :, :, :, at].reshape(D, HALF)
            down = w_d[k].reshape(HALF, D)
            u = nn(h3[b], up)
            bell = jnp.exp(-0.5 * u * u) * (1 / (2 * jnp.pi) ** 0.5)
            upper = 0.5 + 0.5 * lax.erf(u * 0.5**0.5)
            a = (u * upper).astype(BF16)
            act[b, :, at] = a
            d = (nt(grad, down) * (upper + u * bell)).astype(BF16)
            du[b, :, at] = d
            y, dd = nn(a, down), nt(d, up)
            y_sum = y if y_sum is None else y_sum + y
            d_sum = dd if d_sum is None else d_sum + dd
        y_sum = y_sum + x2[...] * (b == f).astype(F32)
        yp[b] = y_sum.astype(BF16).reshape(4, 2 * OWN, D)
        dp[b] = d_sum.astype(BF16).reshape(4, 2 * OWN, D)

    cy = Collect(me, lambda k: yp.at[:, k], l_y, sems)
    cd = Collect(me, lambda k: dp.at[k], l_p, sems)

    with scope("h3_near"):
        shr_h.near()
    with scope("ffn1"):

        def near_two(k, _):
            ffn_block(jnp.where(k == 0, f, sib_f))
            return 0

        lax.fori_loop(0, 2, near_two, 0)
    with scope("h3_far"):
        shr_h.forward()
    cd.near()
    with scope("ffn2"):
        ffn_block(x_f)
    with scope("h3_diag"):
        shr_h.finish()
    with scope("ffn3"):
        ffn_block(diag_f)
    cd.pair()
    cy.near()
    cy.pair()
    with scope("dh3"):
        cd.cross()
    for k in range(2):
        at = slice(k * HALF, (k + 1) * HALF)
        with scope("g_down%d" % k):
            part = sum(tn(act[b], grads_of(b)[:, at]) for b in range(4))
            w_d[:, :, :, :, at] = part.astype(BF16).reshape(2, 2, 2, 96, HALF)
        sd[k].back(0)
    for k in range(2):
        at = slice(k * HALF, (k + 1) * HALF)
        with scope("g_up%d" % k):
            part = sum(tn(h3[b], du[b, :, at]) for b in range(4))
            w_u[:, :, :, :, at] = part.astype(BF16).reshape(2, 2, 2, 96, HALF)
        su[k].back(0)

    with scope("cd_w"):
        cd.finish()
    with scope("back_ffn"):

        def back_ffn(k, _):
            at = pl.ds(pl.multiple_of(k * OWN, OWN), OWN)
            grad = cd.total(k // 2, pl.ds(pl.multiple_of(k % 2 * OWN, OWN), OWN))
            g[at] = e_all[k, own_cols].astype(F32) + norm_back(x2[at], gains[2:3], grad)
            e1[at] = g[at].astype(BF16)
            return 0

        lax.fori_loop(0, ROWS, back_ffn, 0)
    with scope("mix"):
        cy.cross()
    with scope("do2"):
        total = sum(nt(e1[:, k * HALF : (k + 1) * HALF], w_col(3, k)[...].reshape(D, HALF)) for k in range(2))
        do2[...] = total.astype(BF16)
        for k in range(2):
            part = tn(o2[...], e1[:, k * HALF : (k + 1) * HALF])
            w_col(3, k)[...] = part.astype(BF16).reshape(2, 2, 2, 2, 48, HALF)
    r_out.r0()
    with scope("sd_b0"):
        sd[0].back(1)
    with scope("su_b0"):
        su[0].back(1)
    with scope("col_bwd"):

        def col_back(k, at):
            q, kk, v, d = qkv2[0, :, at], qkv2[1, :, at], qkv2[2, :, at], do2[:, at]
            got = []
            for e in range(2):
                mine = jnp.where(lower2, d, zero2) if e == 0 else jnp.where(lower2, zero2, d)
                dq = nt(mine, v)
                p = p_col[2 * k + e]
                ds = (p * (dq - jnp.sum(dq * p, axis=-1, keepdims=True))).astype(BF16)
                got.append((nn(ds, kk) * FACTOR, tn(ds, q) * FACTOR, tn(p.astype(BF16), d)))
            for n in range(3):
                dqkv2[n, :, at] = jnp.where(lower2, got[0][n], got[1][n]).astype(BF16)

        pairs(col_back)
    with scope("out_r1"):
        r_out.r1()
    with scope("sd_b1"):
        sd[1].back(1)
    with scope("su_b1"):
        su[1].back(1)
    with scope("dh2"):
        total = None
        for part in range(3):
            for k in range(2):
                one = nt(dqkv2[part, :, k * HALF : (k + 1) * HALF], w_col(part, k)[...].reshape(D, HALF))
                total = one if total is None else total + one
        dh2[...] = total

    def grad_col(part):
        for k in range(2):
            one = tn(h2[...], dqkv2[part, :, k * HALF : (k + 1) * HALF])
            w_col(part, k)[...] = one.astype(BF16).reshape(2, 2, 2, 2, 48, HALF)

    with scope("back_col"):

        def back_col(at):
            g[at] = g[at] + norm_back(x1[at], gains[1:2], dh2[at])
            e1[at] = g[at].astype(BF16)

        in_pieces(back_col)

    with scope("do1"):
        for k in range(4):
            d = nt(e1[:, :HALF], w_out(0, k)) + nt(e1[:, HALF:], w_out(1, k))
            d = jnp.concatenate([d, jnp.zeros((TOK, 64), F32)], axis=1)
            dost[k] = d.astype(BF16).reshape(ROWS, OWN, 256)
    s_d = swap()
    s_d.go(lambda t: dost.at[t], do1.at[:, own_cols])
    do1[:, own_cols] = dost[f]
    s_g = swap()
    s_g.go(lambda t: e1.at[pl.ds(pl.multiple_of(2 * OWN * t, 2 * OWN), 2 * OWN)], e1r.at[f])
    e1r[f] = e1[pl.ds(pl.multiple_of(2 * OWN * f, 2 * OWN), 2 * OWN)]
    with scope("g_qv"):
        grad_col(0)
        grad_col(2)
    r_qv.r0()
    with scope("g_k"):
        grad_col(1)
    r_k.r0()
    with scope("sd_c0"):
        sd[0].back(2)
    with scope("su_c0"):
        su[0].back(2)
    with scope("qv_r1"):
        r_qv.r1()
    with scope("k_r1"):
        r_k.r1()
    with scope("out_r2"):
        r_out.r2()
    with scope("g_out_row"):
        for h in range(2):
            for k in range(4):
                part = tn(o1_of(k), e1[:, h * HALF : (h + 1) * HALF])
                w_o[h, k // 2, k % 2, :, :, :, :HALF] = part.astype(BF16).reshape(2, 2, 48, HALF)
    ro.r0()
    with scope("sd_c1"):
        sd[1].back(2)
    with scope("su_c1"):
        su[1].back(2)
    with scope("do1w"):
        s_d.wait()
    with scope("row_bwd"):
        d_sum = [[None] * 3 for _ in range(3)]
        for r in range(ROWS):
            d01, d2, v01, v2 = tile(do1, r, 0), tile(do1, r, 1), tile(qkv, r, 3), tile(qkv, r, 4)
            ops = ((jnp.where(lower, d01, zero), v01), (jnp.where(lower, zero, d01), v01), (d2, v2))
            for h, (a, b) in enumerate(ops):
                s = nt(a, b)
                t = 0 if r == 0 else 2 if r == ROWS - 1 else 1
                d_sum[h][t] = s if d_sum[h][t] is None else d_sum[h][t] + s
        da, dat, pt = [], [], []
        for h in range(3):
            s0, s1, s2 = d_sum[h]
            by = []
            for t, s in enumerate((s0, s1 + tied * s0, s2)):
                p = p_row[h, t]
                by.append(p * (s - jnp.sum(s * p, axis=-1, keepdims=True)))
            da.append((jnp.where(joined, by[1], by[0]), by[1], by[2]))
            dat.append([a.T.astype(BF16) for a in da[h]])
            pt.append([chances(h, r).T.astype(BF16) for r in (0, 1, ROWS - 1)])
            da[h] = [a.astype(BF16) for a in da[h]]
        s_first = jnp.where(joined, s_mid, FACTOR)
        for r in range(ROWS):
            t = 0 if r == 0 else 2 if r == ROWS - 1 else 1
            scale = (s_first, s_mid, FACTOR)[t]
            q01, q2k2, k01 = tile(qkv, r, 0), tile(qkv, r, 1), tile(qkv, r, 2)
            d01, d2 = tile(do1, r, 0), tile(do1, r, 1)
            dq = jnp.where(lower, nn(da[0][t], k01), nn(da[1][t], k01)) * scale
            dk = jnp.where(lower, nn(dat[0][t], q01), nn(dat[1][t], q01)) * scale
            mid = jnp.where(lower, nn(dat[2][t], q2k2), nn(da[2][t], q2k2)) * scale
            dv = jnp.where(lower, nn(pt[0][t], d01), nn(pt[1][t], d01))
            for n, val in enumerate((dq, pltpu.roll(mid, 64, 1), dk, dv, nn(pt[2][t], d2))):
                dqkv[r, :, n * 128 : (n + 1) * 128] = val.astype(BF16)
    with scope("dh1"):
        wide = w_q[...].reshape(D, WIDE)

        def partial_dh(k, _):
            pair = dqkv[pl.ds(2 * k, 2)].reshape(2 * COLS, WIDE)
            dp[k] = nt(pair, wide).astype(BF16).reshape(4, 2 * OWN, D)
            return 0

        lax.fori_loop(0, 4, partial_dh, 0)
    ch = Collect(me, lambda k: dp.at[k], l_p, sems)
    ch.pair()
    ch.near()
    for k in range(2):
        at = slice(0, 384) if k == 0 else slice(384, WIDE)
        with scope("g_qkv%d" % k):
            total = tn(h1[...].reshape(ROWS * COLS, D), dqkv[:, :, at].reshape(ROWS * COLS, -1))
            w_q[:, :, :, :, at] = total.astype(BF16).reshape(2, 2, 2, 96, -1)
        sq[k].back(0)
    with scope("dh1_x"):
        ch.cross()
    with scope("out_r3"):
        r_out.r3()
    with scope("qv_r2"):
        r_qv.r2()
    with scope("k_r2"):
        r_k.r2()
    with scope("ro1"):
        ro.r1()
    with scope("out_r3b"):
        r_out.r3b()
    with scope("q_b0"):
        sq[0].back(1)
    with scope("qv_r3"):
        r_qv.r3()
    with scope("q_b1"):
        sq[1].back(1)
    with scope("k_r3"):
        r_k.r3()
    with scope("q_c0"):
        sq[0].back(2)
    with scope("ro2"):
        ro.r2()
    with scope("q_c1"):
        sq[1].back(2)
    with scope("qv_r3b"):
        r_qv.r3b()
    with scope("k_r3b"):
        r_k.r3b()
    with scope("d_sum"):
        for k in sd:
            d_d[:, k.at] = k.back_sum()
    with scope("u_sum"):
        for k in su:
            t_u[:, :, k.at] = k.back_sum().reshape(4, -1, HALF)
    s_v = swap()
    s_v.go(lambda t: t_u.at[t], o_u.at[f])
    o_u[f] = t_u[f]
    with scope("ro3"):
        ro.r3()
    with scope("mixed"):
        cy.finish()
        for r in range(2):
            for k in range(4):
                mixed[r, k * OWN : (k + 1) * OWN] = cy.total(k, slice(r * OWN, (r + 1) * OWN)).astype(BF16)
    with scope("in_grad"):
        ch.finish()
        s_g.wait()
        for r in range(2):
            for k in range(4):
                at = slice(k * OWN, (k + 1) * OWN)
                grad = ch.total(2 * r + k // 2, slice(k % 2 * OWN, (k % 2 + 1) * OWN))
                back = norm_back(tok[r, at].astype(F32), gains[0:1], grad)
                igrad[r, at] = e1r[k, r * OWN : (r + 1) * OWN].astype(F32) + back
    with scope("out_r4"):
        r_out.r4()
    with scope("ro3b"):
        ro.r3b()
    with scope("qv_r4"):
        r_qv.r4()
    with scope("k_r4"):
        r_k.r4()
    with scope("q_sum"):
        for k in sq:
            t_q[:, :, k.at] = k.back_sum().reshape(4, -1, k.at.size)
    s_t = swap()
    s_t.go(lambda t: t_q.at[t], o_q.at[f])
    o_q[f] = t_q[f]
    with scope("ro4"):
        ro.r4()
    with scope("last"):
        for k in (r_out, r_qv, r_k, ro):
            k.r5()
        s_v.wait()
        s_t.wait()
    assert used[0] <= SEMS, used[0]


SEMS = 160


def finish_kernel(
    mixed, igrad, o_q, e_o, e_c, e_co, o_u, e_d, gain_row, r_q, gain_col, r_c, gain_ffn, r_u,
    mixed_out, igrad_out, dg_row, d_q, d_o, dg_col, d_c, d_co, dg_ffn, d_u, d_d,
):
    for a, b in ((mixed, mixed_out), (igrad, igrad_out), (e_o, d_o), (e_c, d_c), (e_co, d_co), (e_d, d_d)):
        b[...] = a[...]
    for n in range(8):
        parts = [o_u[t, :, n // 4 * 384 : (n // 4 + 1) * 384] for t in range(4)]
        d_u[:, n * 384 : (n + 1) * 384] = spread(parts, [t - n % 4 for t in range(4)])
    where = {}
    for t in range(4):
        for n, pair in enumerate(head_order(t)):
            for k, piece in enumerate(pair):
                where[piece] = (o_q.at[t], 2 * n + k)
    for n in range(3 * D // 128):
        d_q[:, n * 128 : (n + 1) * 128] = by_halves([where[2 * n], where[2 * n + 1]])

    for out, weight, grad, gain in (
        (dg_row, r_q, d_q, gain_row), (dg_col, r_c, d_c, gain_col), (dg_ffn, r_u, d_u, gain_ffn)
    ):
        total = jnp.sum(weight[...].astype(F32) * grad[...], axis=1, keepdims=True)
        out[...] = level(total / upright(gain[...].astype(F32)))


def run_layer(tok, cot, seq, cid, *weights):
    sds = jax.ShapeDtypeStruct
    rows = weights[1].shape[0]
    i_d = weights[-1]
    first = [sds(tok.shape, BF16), sds(tok.shape, F32)]
    wide_q, wide_u = sds((4, rows, WIDE), F32), sds((4, rows, D), F32)
    plain = [sds(w.shape, F32) for w in weights]
    shapes = first + [wide_q, plain[2], plain[4], plain[5], wide_u, plain[8]]

    def vmem(*shape, dtype=BF16):
        return pltpu.VMEM(shape, dtype)

    def lands(r, c):
        return [
            vmem(2, 2, 2, 2, r, c), vmem(2, 2, 2, r, c), vmem(2, 2, r, c), vmem(3, r, c), vmem(2, r // 2, c, dtype=F32)
        ]

    def slices(c):
        return [vmem(2, 2, 4 * rows, c), vmem(3, 4 * rows, c)]

    r2 = 2 * rows
    wo, wc, wu = 512, 2 * D, D
    scratch = [
        vmem(4, rows, WIDE),
        vmem(4, rows, wu),
        vmem(rows, 128),
        vmem(2, 2, 2, 4 * rows, WIDE),
        vmem(2, 2, 2, 2, 2, r2, wo),
        vmem(2, 2, 2, 2, 2, r2, wc),
        vmem(2, 2, 2, 4 * rows, wu),
        vmem(2, 2, 2, *i_d.shape),
        vmem(4, rows, WIDE),
        vmem(rows, wo),
        vmem(rows, wc),
        vmem(4, rows, wu),
        *lands(r2, wo),
        *lands(r2, wc),
        *slices(WIDE),
        vmem(4, rows, WIDE, dtype=F32),
        *slices(wu),
        vmem(4, rows, wu, dtype=F32),
        *slices(D),
        vmem(ROWS, COLS, D),
        vmem(ROWS, COLS, D),
        vmem(ROWS, COLS, D),
        vmem(ROWS, COLS, WIDE),
        vmem(3, 3, COLS, COLS, dtype=F32),
        vmem(ROWS, COLS, 256),
        vmem(4, ROWS, OWN, 256),
        vmem(TOK, D, dtype=F32),
        vmem(TOK, D),
        vmem(3, TOK, D),
        vmem(HEADS, TOK, TOK, dtype=F32),
        vmem(TOK, D),
        vmem(TOK, D, dtype=F32),
        vmem(4, TOK, D),
        vmem(4, TOK, D),
        vmem(4, TOK, D),
        vmem(4, 4, 2 * OWN, D),
        vmem(3, 4, 2 * OWN, D),
        vmem(4, 4, 2 * OWN, D),
        vmem(3, 4, 2 * OWN, D),
        vmem(TOK, D, dtype=F32),
        vmem(TOK, D),
        vmem(3, TOK, D),
        vmem(TOK, D, dtype=F32),
        vmem(TOK, D),
        vmem(4, ROWS, OWN, 256),
        vmem(ROWS, COLS, 256),
        vmem(ROWS, COLS, WIDE),
        vmem(4, 2 * OWN, D),
        vmem(8, D, dtype=F32),
        vmem(COLS, COLS, dtype=F32),
        vmem(TOK, TOK, dtype=F32),
        pltpu.SemaphoreType.DMA((SEMS,)),
        pltpu.SemaphoreType.DMA((SEMS,)),
    ]
    vm = pl.BlockSpec(memory_space=pltpu.VMEM)
    outs = pl.pallas_call(
        layer_kernel,
        out_shape=shapes,
        in_specs=[vm, vm, pl.BlockSpec(memory_space=pltpu.SMEM)] + [vm] * 10,
        out_specs=[vm] * 8,
        scratch_shapes=scratch,
        name="layer",
        compiler_params=pltpu.CompilerParams(
            collective_id=0, has_side_effects=True, vmem_limit_bytes=VMEM_LIMIT
        ),
    )(tok, cot, seq, cid, *weights)
    return pl.pallas_call(
        finish_kernel,
        out_shape=first + plain,
        in_specs=[vm] * 14,
        out_specs=[vm] * 11,
        name="finish",
        compiler_params=pltpu.CompilerParams(vmem_limit_bytes=VMEM_LIMIT),
    )(*outs, weights[0], weights[1], weights[3], weights[4], weights[6], weights[7])


VMEM_LIMIT = 63 * 2**20


def on_device(
    tokens, cotangent, seq_ids, col_ids,
    gain_row, qkv_row, out_row, gain_col, qkv_col, out_col, gain_ffn, up_ffn, down_ffn,
    cells,
):
    members = CELL * lax.axis_size("fsdp")
    low_index = (lax.axis_index("dp") % CELL) * lax.axis_size("fsdp") + lax.axis_index("fsdp")

    def in_cell(shard):
        if cells == 1:
            return shard
        whole = lax.all_gather(shard, AXES, axis=0, tiled=True)
        rows = whole.shape[0] // members
        return lax.dynamic_slice_in_dim(whole, low_index * rows, rows, 0)

    def from_cell(summed):
        if cells == 1:
            return summed
        rows = summed.shape[0]
        whole = jnp.zeros((rows * members,) + summed.shape[1:], summed.dtype)
        whole = lax.dynamic_update_slice_in_dim(whole, summed, low_index * rows, 0)
        return lax.psum_scatter(whole, AXES, scatter_dimension=0, tiled=True)

    weights = [
        in_cell(w).reshape(1, -1) if w.ndim == 1 else in_cell(w)
        for w in (gain_row, qkv_row, out_row, gain_col, qkv_col, out_col, gain_ffn, up_ffn, down_ffn)
    ]
    mixed, igrad, *grads = run_layer(tokens[0], cotangent[0], seq_ids, col_ids, *weights)
    grads = [from_cell(v.reshape(-1) if v.shape[0] == 1 else v) for v in grads]
    return (mixed[None], igrad[None], *grads)


def solution(mesh):
    rows = P(AXES, None)
    vector = P(AXES)
    grid = P("dp", "fsdp", None, None)
    ids = P("dp", None)
    return jax.shard_map(
        partial(on_device, cells=mesh.shape["dp"] // CELL),
        mesh=mesh,
        in_specs=(grid, grid, ids, ids) + (vector, rows, rows) * 3,
        out_specs=(grid, grid) + (vector, rows, rows) * 3,
        check_vma=False,
    )
```

```python
from functools import partial

import jax
import jax.numpy as jnp
from jax import lax
from jax.experimental import pallas as pl
from jax.experimental.pallas import tpu as pltpu
from jax.sharding import PartitionSpec as P

HEADS = 12
EPSILON = 1e-05
NEGATIVE = -1000000000.0
MESH = pl.DeviceIdType.MESH
BF16 = jnp.bfloat16
F32 = jnp.float32
CELL = 8
AXES = ("dp", "fsdp")


class Place:
    def __init__(self):
        dp = lax.axis_index("dp")
        self.f = lax.axis_index("fsdp")
        self.base = dp // CELL * CELL
        low = dp - self.base
        self.z, self.y = low // 2, low % 2
        self.hi, self.lo = self.z // 2, self.z % 2
        self.x, self.c = self.f // 2, self.f % 2

    def dev(self, z, y, x, c):
        return (self.base + z * 2 + y, x * 2 + c)

    def sib(self):
        return self.dev(self.z, self.y, self.x, 1 - self.c)

    def xn(self):
        return self.dev(self.z, self.y, 1 - self.x, self.c)

    def yn(self):
        return self.dev(self.z, 1 - self.y, self.x, self.c)

    def first(self):
        return self.dev(self.z, self.y + self.c * (1 - 2 * self.y), self.x + (1 - self.c) * (1 - 2 * self.x), self.c)

    def second(self):
        return self.dev(self.z, self.y + (1 - self.c) * (1 - 2 * self.y), self.x + self.c * (1 - 2 * self.x), self.c)

    def z1(self):
        return self.dev(2 * self.hi + 1 - self.lo, self.y, self.x, self.c)

    def z2(self):
        return self.dev(2 * (1 - self.hi) + self.lo, self.y, self.x, self.c)


def greet(partners):
    bar = pltpu.get_barrier_semaphore()
    for t in partners:
        pl.semaphore_signal(bar, inc=1, device_id=t, device_id_type=MESH)
    pl.semaphore_wait(bar, len(partners))


def rcopy(src, dst, ss, rs, to):
    return pltpu.make_async_remote_copy(
        src_ref=src, dst_ref=dst, send_sem=ss, recv_sem=rs, device_id=to, device_id_type=MESH
    )


ALL = slice(None)


class Part:
    def __init__(self, me, w, at):
        self.me, self.w, self.at = me, w, at

    def block(self, hi, lo, y, x, half=None):
        return self.w.at[self.me.c if half is None else half, hi, lo, y, x, :, self.at]


class Gather(Part):
    def __init__(self, me, src_of, land, w, at, sems):
        super().__init__(me, w, at)
        self.src_of, self.land, self.sems = src_of, land, sems

    def swap(self):
        me = self.me
        self.c0 = rcopy(self.src_of(1 - me.c), self.land.at[:, self.at], *self.sems(), me.sib())
        self.c0.start()

    def start(self, ref, to):
        c = rcopy(ref, ref, *self.sems(), to)
        c.start()
        self.sent.append(c)
        return c

    def own(self):
        me = self.me
        self.c0.wait()
        mine = self.src_of(me.c)[...].astype(F32)
        other = self.land[:, self.at].astype(F32)
        flag = (me.c == 0).astype(F32)
        top = flag * mine + (1 - flag) * other
        low = flag * other + (1 - flag) * mine
        own = self.block(me.hi, me.lo, me.y, me.x)
        own[...] = jnp.concatenate([top, low], axis=0).astype(BF16)
        self.sent = []

    def s0(self):
        me = self.me
        self.own()
        self.a = self.start(self.block(me.hi, me.lo, me.y, me.x), me.z2())

    def s1(self):
        me = self.me
        self.a.wait_recv()
        self.b = self.start(self.block(ALL, me.lo, me.y, me.x), me.z1())

    def s2(self):
        me = self.me
        self.b.wait_recv()
        col = self.block(ALL, ALL, me.y, me.x)
        self.e = self.start(col, me.first())
        self.to_sib = [self.start(col, me.sib())]

    def fork(self, ref0, ref1, to, like):
        me, m = self.me, self.sems()

        @pl.when(me.c == 0)
        def _():
            rcopy(ref0, ref0, *m, to).start()

        @pl.when(me.c == 1)
        def _():
            rcopy(ref1, ref1, *m, to).start()

        c = rcopy(like, like, *m, to)
        self.sent.append(c)
        return c

    def s3(self):
        me = self.me
        self.e.wait_recv()
        two, col = self.block(ALL, ALL, me.y, ALL), self.block(ALL, ALL, me.y, me.x)
        self.g = self.fork(
            self.block(ALL, ALL, me.y, ALL, 0), self.block(ALL, ALL, ALL, me.x, 1), me.second(), two
        )
        self.to_sib.append(
            self.fork(
                self.block(ALL, ALL, me.y, 1 - me.x, 0), self.block(ALL, ALL, 1 - me.y, me.x, 1), me.sib(), col
            )
        )

    def s4(self):
        me = self.me
        self.g.wait_recv()
        two = self.block(ALL, ALL, me.y, ALL)
        self.to_sib.append(
            self.fork(
                self.block(ALL, ALL, 1 - me.y, ALL, 0), self.block(ALL, ALL, ALL, 1 - me.x, 1), me.sib(), two
            )
        )

    def s5(self):
        for c in self.to_sib:
            c.wait_recv()

    def drain(self):
        for c in self.sent:
            c.wait_send()


class Reduce(Part):
    def __init__(self, me, w, at, lands, out_of, sems):
        super().__init__(me, w, at)
        self.l0, self.l1, self.l2, self.l3, self.l4 = lands
        self.out_of, self.sems = out_of, sems

    def add(self, n, mine_of, land_of):
        def body(k, _):
            mine = mine_of(k)
            mine[...] = (mine[...].astype(F32) + land_of(k)[...].astype(F32)).astype(BF16)
            return 0

        lax.fori_loop(0, n, body, 0)

    def r0(self):
        me = self.me
        self.c0 = rcopy(
            self.block(ALL, ALL, ALL, ALL, 1 - me.c), self.l0.at[:, :, :, :, :, self.at], *self.sems(), me.sib()
        )
        self.c0.start()

    def r1(self):
        me = self.me
        self.c0.wait()
        self.add(
            16,
            lambda k: self.block(k // 8, k // 4 % 2, k // 2 % 2, k % 2),
            lambda k: self.l0.at[k // 8, k // 4 % 2, k // 2 % 2, k % 2, :, self.at],
        )
        land, m = self.l1.at[:, :, :, :, self.at], self.sems()

        @pl.when(me.c == 0)
        def _():
            rcopy(self.block(ALL, ALL, 1 - me.y, ALL, 0), land, *m, me.second()).start()

        @pl.when(me.c == 1)
        def _():
            rcopy(self.block(ALL, ALL, ALL, 1 - me.x, 1), land, *m, me.second()).start()

        self.c1 = rcopy(land, land, *m, me.sib())

    def r2(self):
        me = self.me
        self.c1.wait()

        def mine(k):
            m = k % 2
            y, x = me.y + me.c * (m - me.y), me.x + (1 - me.c) * (m - me.x)
            return self.block(k // 4, k // 2 % 2, y, x)

        self.add(8, mine, lambda k: self.l1.at[k // 4, k // 2 % 2, k % 2, :, self.at])
        oy = me.y + me.c * (1 - 2 * me.y)
        ox = me.x + (1 - me.c) * (1 - 2 * me.x)
        self.c2 = rcopy(self.block(ALL, ALL, oy, ox), self.l2.at[:, :, :, self.at], *self.sems(), me.first())
        self.c2.start()

    def r3(self):
        me = self.me
        self.c2.wait()
        self.add(
            4, lambda k: self.block(k // 2, k % 2, me.y, me.x), lambda k: self.l2.at[k // 2, k % 2, :, self.at]
        )
        self.c3 = rcopy(
            self.block(ALL, 1 - me.lo, me.y, me.x), self.l3.at[pl.ds(0, 2), :, self.at], *self.sems(), me.z1()
        )
        self.c3.start()

    def r3b(self):
        me = self.me
        self.c3.wait()
        self.add(2, lambda k: self.block(k, me.lo, me.y, me.x), lambda k: self.l3.at[k, :, self.at])
        self.c3 = rcopy(
            self.block(1 - me.hi, me.lo, me.y, me.x), self.l3.at[2, :, self.at], *self.sems(), me.z2()
        )
        self.c3.start()

    def r4(self):
        me = self.me
        self.c3.wait()
        total = self.block(me.hi, me.lo, me.y, me.x)[...].astype(F32) + self.l3[2, :, self.at].astype(F32)
        half = total.shape[0] // 2
        flag = (me.c == 0).astype(F32)
        top, low = total[:half], total[half:]
        self.out_of(me.c)[...] = flag * top + (1 - flag) * low
        self.l4[0, :, self.at] = flag * low + (1 - flag) * top
        self.c4 = rcopy(self.l4.at[0, :, self.at], self.l4.at[1, :, self.at], *self.sems(), me.sib())
        self.c4.start()

    def r5(self):
        self.c4.wait()
        self.out_of(1 - self.me.c)[...] = self.l4[1, :, self.at]


class EarlyReduce(Reduce):
    def go(self, src, land, to):
        self.c = rcopy(src, land, *self.sems(), to)
        self.c.start()

    def r1(self):
        me = self.me
        self.c0.wait()
        self.add(
            16,
            lambda k: self.block(k // 8, k // 4 % 2, k // 2 % 2, k % 2),
            lambda k: self.l0.at[k // 8, k // 4 % 2, k // 2 % 2, k % 2, :, self.at],
        )
        self.go(self.block(ALL, 1 - me.lo, ALL, ALL), self.l1.at[:, :, :, :, self.at], me.z1())

    def r2(self):
        me = self.me
        self.c.wait()
        self.add(
            8,
            lambda k: self.block(k // 4, me.lo, k // 2 % 2, k % 2),
            lambda k: self.l1.at[k // 4, k // 2 % 2, k % 2, :, self.at],
        )
        self.go(self.block(1 - me.hi, me.lo, ALL, ALL), self.l2.at[:, :, :, self.at], me.z2())

    def r3(self):
        me = self.me
        self.c.wait()
        self.add(
            4,
            lambda k: self.block(me.hi, me.lo, k // 2, k % 2),
            lambda k: self.l2.at[k // 2, k % 2, :, self.at],
        )
        self.go(self.block(me.hi, me.lo, ALL, 1 - me.x), self.l3.at[pl.ds(0, 2), :, self.at], me.xn())

    def r3b(self):
        me = self.me
        self.c.wait()
        self.add(2, lambda k: self.block(me.hi, me.lo, k, me.x), lambda k: self.l3.at[k, :, self.at])
        self.go(self.block(me.hi, me.lo, 1 - me.y, me.x), self.l3.at[2, :, self.at], me.yn())
        self.c3 = self.c


class Swap:
    def __init__(self, me, ssem, rsem):
        self.me, self.ss, self.rs, self.sent = me, ssem, rsem, []

    def other(self, d):
        return (self.me.f + d) % 4

    def go(self, src_of, dst):
        me = self.me
        for d in (1, 2, 3):
            t = self.other(d)
            c = rcopy(src_of(t), dst, self.ss.at[d - 1], self.rs.at[d - 1], me.dev(me.z, me.y, t // 2, t % 2))
            c.start()
            self.sent.append(c)

    def wait(self):
        for c in self.sent:
            c.wait_send()
            c.wait_recv()


class Slices:
    def __init__(self, me, w, at, l1, l2, sems, early=False):
        self.me, self.w, self.at, self.l1, self.l2, self.sems, self.early = me, w, at, l1, l2, sems, early
        self.sent = []

    def part(self, hi, lo, y):
        return self.w.at[hi, lo, y, :, self.at]

    def steps(self):
        me = self.me
        if self.early:
            return (
                (self.part(me.hi, me.lo, me.y), me.yn()),
                (self.part(me.hi, me.lo, ALL), me.z2()),
                (self.part(ALL, me.lo, ALL), me.z1()),
            )
        return (
            (self.part(me.hi, me.lo, me.y), me.z2()),
            (self.part(ALL, me.lo, me.y), me.z1()),
            (self.part(ALL, ALL, me.y), me.yn()),
        )

    def send(self, n):
        if n:
            self.sent[-1].wait_recv()
        ref, to = self.steps()[n]
        c = rcopy(ref, ref, *self.sems(), to)
        c.start()
        self.sent.append(c)

    def finish(self):
        self.sent[-1].wait_recv()
        for c in self.sent:
            c.wait_send()

    def kept(self, n):
        me = self.me
        if self.early:
            return (
                (4, lambda k: self.part(k // 2, me.lo, k % 2)),
                (2, lambda k: self.part(me.hi, me.lo, k)),
            )[n]
        return (
            (4, lambda k: self.part(k // 2, k % 2, me.y)),
            (2, lambda k: self.part(k, me.lo, me.y)),
        )[n]

    def back(self, n):
        me = self.me
        if n:
            self.c.wait()
            count, mine_of = self.kept(n - 1)

            def body(k, _):
                mine = mine_of(k)
                land = self.l1[k // 2, k % 2, :, self.at] if n == 1 else self.l2[k, :, self.at]
                mine[...] = (mine[...].astype(F32) + land.astype(F32)).astype(BF16)
                return 0

            lax.fori_loop(0, count, body, 0)
        lands = (self.l1.at[:, :, :, self.at], self.l2.at[pl.ds(0, 2), :, self.at], self.l2.at[2, :, self.at])
        if self.early:
            src, to = (
                (self.part(ALL, 1 - me.lo, ALL), me.z1()),
                (self.part(1 - me.hi, me.lo, ALL), me.z2()),
                (self.part(me.hi, me.lo, 1 - me.y), me.yn()),
            )[n]
        else:
            src, to = (
                (self.part(ALL, ALL, 1 - me.y), me.yn()),
                (self.part(ALL, 1 - me.lo, me.y), me.z1()),
                (self.part(1 - me.hi, me.lo, me.y), me.z2()),
            )[n]
        self.c = rcopy(src, lands[n], *self.sems(), to)
        self.c.start()

    def back_sum(self):
        me = self.me
        self.c.wait()
        return self.part(me.hi, me.lo, me.y)[...].astype(F32) + self.l2[2, :, self.at].astype(F32)


class Share:
    def __init__(self, me, whole, sems):
        self.me, self.sems = me, sems
        self.whole = whole

    def send(self):
        me = self.me
        own = self.whole(me.f)
        self.s = rcopy(own, own, *self.sems(), me.sib())
        self.x = rcopy(own, own, *self.sems(), me.xn())
        self.s.start()
        self.x.start()

    def near(self):
        self.s.wait()

    def forward(self):
        me = self.me
        self.x.wait_recv()
        got = self.whole(2 * (1 - me.x) + me.c)
        self.t = rcopy(got, got, *self.sems(), me.sib())
        self.t.start()

    def finish(self):
        self.x.wait_send()
        self.t.wait()


class Collect:
    def __init__(self, me, part_of, lands, sems, pieces=4):
        self.me, self.part_of, self.lands, self.sems, self.pieces = me, part_of, lands, sems, pieces

    def near(self):
        me = self.me
        self.n = rcopy(self.part_of(2 * me.x + 1 - me.c), self.lands.at[0], *self.sems(), me.sib())
        self.n.start()

    def pair(self):
        me = self.me
        self.p = rcopy(self.part_of(2 * (1 - me.x) + 1 - me.c), self.lands.at[1], *self.sems(), me.sib())
        self.p.start()

    def cross(self):
        me = self.me
        self.p.wait()
        part = self.part_of(2 * (1 - me.x) + me.c)

        def add(k, _):
            mine = part.at[k]
            mine[...] = (mine[...].astype(F32) + self.lands[1, k].astype(F32)).astype(BF16)
            return 0

        lax.fori_loop(0, self.pieces, add, 0)
        self.x = rcopy(part, self.lands.at[2], *self.sems(), me.xn())
        self.x.start()

    def finish(self):
        self.n.wait()
        self.x.wait()

    def total(self, k, at):
        own = self.part_of(self.me.f)[k, at].astype(F32) + self.lands[0, k, at].astype(F32)
        return own + self.lands[2, k, at].astype(F32)


def nn(a, b):
    return lax.dot_general(a, b, (((1,), (0,)), ((), ())), preferred_element_type=F32)


def nt(a, b):
    return lax.dot_general(a, b, (((1,), (1,)), ((), ())), preferred_element_type=F32)


def tn(a, b):
    return lax.dot_general(a, b, (((0,), (0,)), ((), ())), preferred_element_type=F32)


def standard(values):
    centred = values - jnp.mean(values, axis=-1, keepdims=True)
    scale = lax.rsqrt(jnp.mean(centred * centred, axis=-1, keepdims=True) + EPSILON)
    return centred * scale, scale


def norm_back(values, gain, grad):
    unit, scale = standard(values)
    inner = grad * gain
    low = jnp.mean(inner, axis=-1, keepdims=True)
    high = jnp.mean(inner * unit, axis=-1, keepdims=True)
    return scale * (inner - low - unit * high)


def softmax(scores):
    e = jnp.exp(scores - jnp.max(scores, axis=-1, keepdims=True))
    return e / jnp.sum(e, axis=-1, keepdims=True)


def low_half(shape):
    return lax.broadcasted_iota(jnp.int32, shape, 1) % 128 < 64


def by_halves(pieces):
    out = []
    for n, piece in enumerate(pieces):
        if piece is None:
            out.append(jnp.zeros_like(pieces[0][0][:, :128]))
            continue
        ref, k = piece
        part = ref[:, k // 2 * 128 : k // 2 * 128 + 128].astype(F32)
        out.append(part if k % 2 == n else pltpu.roll(part, 64, 1))
    return jnp.where(low_half(out[0].shape), out[0], out[1])


def head_order(f):
    q, k, v = (HEADS * n + 3 * f for n in range(3))
    return ((q, q + 1), (q + 2, k + 2), (k, k + 1), (v, v + 1), (v + 2, None))


def spread(parts, shifts):
    lane = lax.broadcasted_iota(jnp.int32, parts[0].shape, 1) // 96
    total = None
    for n in range(4):
        part = pltpu.roll(parts[n], shifts[n] % 4 * 96, 1) if shifts[n] % 4 else parts[n]
        total = part if total is None else jnp.where(lane == n, part, total)
    return total


def upright(row):
    n = row.shape[1]
    i, j = (lax.broadcasted_iota(jnp.int32, (n, n), k) for k in range(2))
    return jnp.sum(jnp.where(i == j, jnp.broadcast_to(row, (n, n)), 0.0), axis=1, keepdims=True)


def level(column):
    n = column.shape[0]
    i, j = (lax.broadcasted_iota(jnp.int32, (n, n), k) for k in range(2))
    return jnp.sum(jnp.where(i == j, jnp.broadcast_to(column, (n, n)), 0.0), axis=0, keepdims=True)


D, FF, ROWS, COLS, HEAD = 768, 3072, 8, 128, 64
HALF = D // 2
OWN = COLS // 4
TOK = ROWS * OWN
WIDE = 640
FACTOR = HEAD**-0.5


def layer_kernel(
    tok, cot, seq, cid, gain_row, r_q, r_o, gain_col, r_c, r_co, gain_ffn, r_u, r_d,
    mixed, igrad, o_q, d_o, d_c, d_co, o_u, d_d,
    i_q, i_u,
    w_q, w_o, w_c, w_u, w_d, f_q, f_o, f_c, f_u,
    l_o0, l_o1, l_o2, l_o3, l_o4,
    l_c0, l_c1, l_c2, l_c3, l_c4,
    l_q1, l_q2, t_q, l_u1, l_u2, t_u, l_d1, l_d2,
    tok_all, e_all, h1, qkv, p_row, o1f, o1c, x1, h2, qkv2, p_col, o2, x2, h3, act, du, yp, l_y, dp, l_p,
    g, do2, dqkv2, dh2, e1, dost, do1, dqkv, e1r, gains, cmask, tmask, ms, mr,
):
    me = Place()
    f = me.f
    scope = jax.named_scope
    sib_f, x_f, diag_f = 2 * me.x + 1 - me.c, 2 * (1 - me.x) + me.c, 2 * (1 - me.x) + 1 - me.c
    diag = me.dev(me.z, me.y, 1 - me.x, 1 - me.c)
    greet([me.sib(), me.xn(), diag, me.yn(), me.z1(), me.z2()])
    used = [0]

    def sems():
        used[0] += 1
        return ms.at[used[0] - 1], mr.at[used[0] - 1]

    def swap():
        used[0] += 3
        at = pl.ds(used[0] - 3, 3)
        return Swap(me, ms.at[at], mr.at[at])

    at_w = pl.ds(0, HALF)
    at_qv, at_k, at_o = pl.ds(0, D), pl.ds(D, HALF), pl.ds(D + HALF, HALF)

    def lanes(ref, start, step, size):
        return lambda h: ref.at[:, pl.ds(pl.multiple_of(start + h * step, 128), size)]

    of_o = lanes(r_o, 0, HALF, HALF)
    of_qv, of_k, of_co = lanes(r_c, 0, 2 * D, D), lanes(r_c, D, HALF, HALF), lanes(r_co, 0, HALF, HALF)
    go = Gather(me, of_o, f_o, w_o, at_w, sems)
    g_qv = Gather(me, of_qv, f_c, w_c, at_qv, sems)
    g_k = Gather(me, of_k, f_c, w_c, at_k, sems)
    g_out = Gather(me, of_co, f_c, w_c, at_o, sems)
    ro = Reduce(me, w_o, at_w, (l_o0, l_o1, l_o2, l_o3, l_o4), lanes(d_o, 0, HALF, HALF), sems)
    r_qv, r_k, r_out = (
        kind(me, w_c, at, (l_c0, l_c1, l_c2, l_c3, l_c4), out, sems)
        for kind, at, out in (
            (Reduce, at_qv, lanes(d_c, 0, 2 * D, D)),
            (EarlyReduce, at_k, lanes(d_c, D, HALF, HALF)),
            (Reduce, at_o, lanes(d_co, 0, HALF, HALF)),
        )
    )
    sq = [Slices(me, w_q, pl.ds(*at), l_q1, l_q2, sems, at[0] > 0) for at in ((0, 384), (384, 256))]
    su = [Slices(me, w_u, pl.ds(k * HALF, HALF), l_u1, l_u2, sems, k == 1) for k in range(2)]
    sd = [Slices(me, w_d, pl.ds(k * HALF, HALF), l_d1, l_d2, sems, k == 0) for k in range(2)]

    def cols_of(t):
        return pl.ds(pl.multiple_of(t * OWN, OWN), OWN)

    own_cols = cols_of(f)

    def stacked(land):
        return jnp.concatenate([land[k].astype(F32) for k in range(4)], axis=0).astype(BF16)

    lane = lax.broadcasted_iota(jnp.int32, (r_q.shape[0], 128), 1)
    columns = [upright(v[...].astype(F32)) for v in (gain_row, gain_col, gain_ffn)]
    spare = sum(jnp.where(lane == HEAD + n, v, 0.0) for n, v in enumerate(columns))
    for t in range(4):
        for n, pair in enumerate(head_order(t)):
            part = by_halves([None if k is None else (r_q, k) for k in pair])
            i_q[t, :, n * 128 : (n + 1) * 128] = (part + spare if n == 4 else part).astype(BF16)
    s_q = swap()
    s_q.go(lambda t: i_q.at[t], f_q.at[f])
    for k in (g_k, g_qv, go, g_out):
        k.swap()
    tok_all[pl.ds(2 * f, 2)] = tok[...]
    w_d[me.hi, me.lo, me.y] = r_d[...]
    sd[0].send(0)
    with scope("i_u"):
        for t in range(4):
            for n in range(2):
                parts = [r_u[:, (4 * n + k) * 384 : (4 * n + k + 1) * 384].astype(F32) for k in range(4)]
                i_u[t, :, n * 384 : (n + 1) * 384] = spread(parts, [k - t for k in range(4)]).astype(BF16)
    s_u = swap()
    s_u.go(lambda t: i_u.at[t], f_u.at[f])
    shr_t = Share(me, lambda k: tok_all.at[pl.ds(2 * k, 2)], sems)
    shr_t.send()
    with scope("q_f"):
        f_q[f] = i_q[f]
        s_q.wait()
        w_q[me.hi, me.lo, me.y] = stacked(f_q)
    sq[1].send(0)
    sq[0].send(0)
    with scope("masks"):
        first = seq[0, 0]
        ids = jnp.broadcast_to(cid[...], (COLS, COLS)).astype(F32)
        cmask[...] = jnp.where(ids == ids.T, 1.0, 0.0)
        i, j = (lax.broadcasted_iota(jnp.int32, tmask.shape, n) for n in range(2))
        wide = OWN // 2

        def block_of(k):
            r = k // wide
            return jnp.where(r == 0, first, jnp.where(r == ROWS - 1, 2, 1))

        tmask[...] = jnp.where((i % wide == j % wide) & (block_of(i) == block_of(j)), 1.0, 0.0)
        e_all[pl.ds(2 * f, 2)] = cot[...]
        f_u[f] = i_u[f]
    with scope("q_m1"):
        sq[1].send(1)
    s_u.wait()
    w_u[me.hi, me.lo, me.y] = stacked(f_u)
    su[1].send(0)
    with scope("q_m0"):
        sq[0].send(1)
    g_qv.s0()
    go.s0()
    with scope("q_n1"):
        sq[1].send(2)
    shr_e = Share(me, lambda k: e_all.at[pl.ds(2 * k, 2)], sems)
    shr_e.send()
    with scope("q_n0"):
        sq[0].send(2)
    g_k.s0()
    with scope("qv1"):
        g_qv.s1()
    with scope("tok"):
        shr_t.forward()
    with scope("go1"):
        go.s1()
    with scope("q_fin1"):
        sq[1].finish()
    with scope("gains"):
        wide = w_q[:, :, :, :, WIDE - 128 :].reshape(D, 128)
        for k in range(D // 128):
            part = wide[k * 128 : (k + 1) * 128].astype(F32).T
            gains[:, k * 128 : (k + 1) * 128] = part[HEAD : HEAD + 8]
    with scope("tok2"):
        shr_t.near()
        shr_t.finish()

    with scope("norm_row"):

        def norm_rows(k, _):
            unit, _s = standard(tok_all[k].astype(F32))
            h1[k] = (unit * gains[0:1]).astype(BF16)
            return 0

        lax.fori_loop(0, ROWS, norm_rows, 0)
    with scope("k1"):
        g_k.s1()
    with scope("qv2"):
        g_qv.s2()
    su[0].send(0)
    g_out.s0()
    with scope("go2"):
        go.s2()
    with scope("q_fin0"):
        sq[0].finish()
    with scope("qkv_row"):
        wide = w_q[...].reshape(D, WIDE)

        def project(k, _):
            pair = h1[pl.ds(2 * k, 2)].reshape(2 * COLS, D)
            qkv[pl.ds(2 * k, 2)] = nn(pair, wide).astype(BF16).reshape(2, COLS, WIDE)
            return 0

        lax.fori_loop(0, ROWS // 2, project, 0)
    with scope("k2"):
        g_k.s2()
    with scope("qv3"):
        g_qv.s3()
    with scope("su_m0"):
        su[0].send(1)

    joined = (jnp.full((1, 1), first, jnp.int32) == 1)
    tied = jnp.where(joined, 1.0, 0.0)
    s_mid = jnp.where(joined, FACTOR / 7**0.5, FACTOR / 6**0.5)
    lower = low_half((COLS, 128))
    zero = jnp.zeros((COLS, 128), BF16)

    def tile(ref, r, k):
        return ref[r, :, k * 128 : (k + 1) * 128]

    def head_tiles(r):
        q01, q2k2, k01 = tile(qkv, r, 0), tile(qkv, r, 1), tile(qkv, r, 2)
        k2 = pltpu.roll(q2k2.astype(F32), 64, 1).astype(BF16)
        return (
            (jnp.where(lower, q01, zero), k01),
            (jnp.where(lower, zero, q01), k01),
            (jnp.where(lower, q2k2, zero), k2),
        )

    with scope("row_fwd"):
        sums = [[None] * 3 for _ in range(3)]
        for r in range(ROWS):
            for h, (a, b) in enumerate(head_tiles(r)):
                s = nt(a, b)
                t = 0 if r == 0 else 2 if r == ROWS - 1 else 1
                sums[h][t] = s if sums[h][t] is None else sums[h][t] + s
        for h in range(3):
            s0, s1, s2 = sums[h]
            for t, s in enumerate((s0 * FACTOR, (s1 + tied * s0) * s_mid, s2 * FACTOR)):
                p_row[h, t] = softmax(jnp.where(cmask[...] > 0.5, s, NEGATIVE))

    def chances(h, r):
        if r == 0:
            return jnp.where(joined, p_row[h, 1], p_row[h, 0])
        return p_row[h, 2 if r == ROWS - 1 else 1]

    with scope("row_out"):
        for r in range(ROWS):
            v01, v2 = tile(qkv, r, 3), tile(qkv, r, 4)
            p = [chances(h, r).astype(BF16) for h in range(3)]
            o1f[r, :, :128] = jnp.where(lower, nn(p[0], v01), nn(p[1], v01)).astype(BF16)
            o1f[r, :, 128:] = nn(p[2], v2).astype(BF16)
    s_o = swap()
    s_o.go(lambda t: o1f.at[:, cols_of(t)], o1c.at[f])
    o1c[f] = o1f[:, own_cols]
    with scope("go3"):
        go.s3()
    with scope("out1"):
        g_out.s1()
    su[1].send(1)
    with scope("e_f"):
        shr_e.forward()
    with scope("k3"):
        g_k.s3()
    sd[1].send(0)
    with scope("qv4"):
        g_qv.s4()
    with scope("su_n1"):
        su[1].send(2)
    sd[0].send(1)
    with scope("sd_m1"):
        sd[1].send(1)
    with scope("go4"):
        go.s4()
    with scope("out2"):
        g_out.s2()
    with scope("k4"):
        g_k.s4()
    with scope("su_y0"):
        su[0].send(2)
    with scope("o1"):
        s_o.wait()

    def o1_of(k):
        return o1c[k].reshape(TOK, 256)[:, :192]

    def w_out(h, k):
        return w_o[h, k // 2, k % 2].reshape(192, HALF)

    with scope("go5"):
        go.s5()
    with scope("out_row"):
        for h in range(2):
            cols = slice(h * HALF, (h + 1) * HALF)
            total = tok_all[:, own_cols, cols].reshape(TOK, HALF).astype(F32)
            for k in range(4):
                total = total + nn(o1_of(k), w_out(h, k))
            x1[:, cols] = total

    def in_pieces(step, rows=64, total=TOK):
        def body(k, _):
            step(pl.ds(pl.multiple_of(k * rows, rows), rows))
            return 0

        lax.fori_loop(0, total // rows, body, 0)

    with scope("norm_col"):

        def norm_col(at):
            h2[at] = (standard(x1[at])[0] * gains[1:2]).astype(BF16)

        in_pieces(norm_col)

    def w_col(part, k):
        half, off = ((0, k * HALF), (k, D), (1, k * HALF), (k, D + HALF))[part]
        return w_c.at[half, :, :, :, :, :, off : off + HALF]

    def project2(part):
        for k in range(2):
            at = slice(k * HALF, (k + 1) * HALF)
            one = nn(h2[...], w_col(part, k)[...].reshape(D, HALF))
            qkv2[part, :, :, at] = one.astype(BF16).reshape(ROWS, OWN, HALF)

    with scope("qv5"):
        g_qv.s5()
    with scope("qkv_col"):
        project2(0)
        project2(2)
        g_k.s5()
        project2(1)
    with scope("sd_n0"):
        sd[0].send(2)
    with scope("sd_n1"):
        sd[1].send(2)
    part_cols = OWN // 2
    part_size = ROWS * part_cols
    lower2 = low_half((part_size, 128))
    zero2 = jnp.zeros((part_size, 128), BF16)

    def some(ref, m, at, *lead):
        return ref[(*lead, ALL, slice(m * part_cols, (m + 1) * part_cols), at)].reshape(part_size, 128)

    def put(ref, m, at, value, *lead):
        value = value.astype(BF16).reshape(ROWS, part_cols, 128)
        ref[(*lead, ALL, slice(m * part_cols, (m + 1) * part_cols), at)] = value

    def pairs(step):
        def body(k, _):
            step([(2 * k + n, m, pl.ds(pl.multiple_of((2 * k + n) * 128, 128), 128)) for n in range(2) for m in range(2)])
            return 0

        lax.fori_loop(0, HEADS // 4, body, 0)

    def one_head(e, value):
        return jnp.where(lower2, value, zero2) if e == 0 else jnp.where(lower2, zero2, value)

    with scope("col_fwd"):

        def col_pair(work):
            scores, chosen = [], []
            for _k, m, at in work:
                q, kk = some(qkv2, m, at, 0), some(qkv2, m, at, 1)
                scores.append([nt(one_head(e, q), kk) * FACTOR for e in range(2)])
            same = tmask[...] > 0.5
            for pair in scores:
                chosen.append([softmax(jnp.where(same, one, NEGATIVE)) for one in pair])
            out = []
            for (_k, m, at), pair in zip(work, chosen):
                v = some(qkv2, m, at, 2)
                out.append([nn(p.astype(BF16), v) for p in pair])
            for (k, m, at), pair, got in zip(work, chosen, out):
                put(o2, m, at, jnp.where(lower2, got[0], got[1]))
                for e in range(2):
                    p_col[2 * k + e, m] = pair[e]

        pairs(col_pair)
    with scope("out3"):
        g_out.s3()
    with scope("out4"):
        g_out.s4()
    with scope("out_col"):
        g_out.s5()
        for k in range(2):
            at = slice(k * HALF, (k + 1) * HALF)
            x2[:, at] = x1[:, at] + nn(o2[...].reshape(TOK, D), w_col(3, k)[...].reshape(D, HALF))
    half_size = TOK // 2
    shr_h = [Share(me, lambda k, u=u: h3.at[k, u], sems) for u in range(2)]
    for u in range(2):
        with scope("norm_ffn%d" % u):

            def norm_ffn(k, _, u=u):
                at = pl.ds(pl.multiple_of(k * 64, 64), 64)
                src = pl.ds(pl.multiple_of(u * half_size + k * 64, 64), 64)
                h3[f, u, at] = (standard(x2[src])[0] * gains[2:3]).astype(BF16)
                return 0

            lax.fori_loop(0, half_size // 64, norm_ffn, 0)
        shr_h[u].send()
    for k in (go, g_qv, g_k, g_out):
        k.drain()
    with scope("su_f"):
        for k in su:
            k.finish()
    with scope("e"):
        shr_e.near()
        shr_e.finish()
    with scope("sd_f"):
        for k in sd:
            k.finish()

    def grads_of(b):
        return e_all[:, cols_of(b)].reshape(TOK, D)

    def ffn_block(pair, mine=None):
        grad = jnp.concatenate(
            [e_all[4 * u : 4 * u + 4, cols_of(b)].reshape(half_size, D) for b, u in pair], axis=0
        )
        tokens = jnp.concatenate([h3[b, u] for b, u in pair], axis=0)
        y_sum, d_sum = None, None
        for k in range(2):
            at = slice(k * HALF, (k + 1) * HALF)
            up = w_u[:, :, :, :, at].reshape(D, HALF)
            down = w_d[k].reshape(HALF, D)
            u_k = nn(tokens, up)
            bell = jnp.exp(-0.5 * u_k * u_k) * (1 / (2 * jnp.pi) ** 0.5)
            upper = 0.5 + 0.5 * lax.erf(u_k * 0.5**0.5)
            a = (u_k * upper).astype(BF16)
            d = (nt(grad, down) * (upper + u_k * bell)).astype(BF16)
            for n, (b, u) in enumerate(pair):
                act[b, u, :, at] = a[n * half_size : (n + 1) * half_size]
                du[b, u, :, at] = d[n * half_size : (n + 1) * half_size]
            y, dd = nn(a, down), nt(d, up)
            y_sum = y if y_sum is None else y_sum + y
            d_sum = dd if d_sum is None else d_sum + dd
        if mine is not None:
            y_sum = y_sum + x2[...] * mine
        y_sum = y_sum.astype(BF16).reshape(4, 2 * OWN, D)
        d_sum = d_sum.astype(BF16).reshape(4, 2 * OWN, D)
        for n, (b, u) in enumerate(pair):
            yp[b, 2 * u : 2 * u + 2] = y_sum[2 * n : 2 * n + 2]
            dp[b, 2 * u : 2 * u + 2] = d_sum[2 * n : 2 * n + 2]

    cy = Collect(me, lambda k: yp.at[:, k], l_y, sems)
    cd = [
        Collect(me, lambda k, u=u: dp.at[k, pl.ds(2 * u, 2)], l_p.at[:, pl.ds(2 * u, 2)], sems, 2) for u in range(2)
    ]
    with scope("h3_near"):
        shr_h[0].near()
        shr_h[1].near()
    with scope("ffn1"):

        def near_two(k, _):
            b = jnp.where(k == 0, f, sib_f)
            ffn_block(((b, 0), (b, 1)), (k == 0).astype(F32))
            return 0

        lax.fori_loop(0, 2, near_two, 0)
    cd[0].near()
    cd[1].near()
    with scope("h3_far0"):
        shr_h[0].forward()
    with scope("h3_diag0"):
        shr_h[0].finish()
    with scope("ffn2"):
        ffn_block(((x_f, 0), (diag_f, 0)))
    cd[0].pair()
    with scope("h3_far1"):
        shr_h[1].forward()
    with scope("dh3_0"):
        cd[0].cross()
    with scope("h3_diag1"):
        shr_h[1].finish()
    with scope("ffn3"):
        ffn_block(((x_f, 1), (diag_f, 1)))
    cd[1].pair()
    cy.near()
    cy.pair()
    with scope("dh3_1"):
        cd[1].cross()
    for k in range(2):
        at = slice(k * HALF, (k + 1) * HALF)
        with scope("g_down%d" % k):
            part = sum(tn(act[b].reshape(TOK, D), grads_of(b)[:, at]) for b in range(4))
            w_d[:, :, :, :, at] = part.astype(BF16).reshape(2, 2, 2, 96, HALF)
        sd[k].back(0)
    for k in range(2):
        at = slice(k * HALF, (k + 1) * HALF)
        with scope("g_up%d" % k):
            part = sum(tn(h3[b].reshape(TOK, D), du[b, :, :, at].reshape(TOK, HALF)) for b in range(4))
            w_u[:, :, :, :, at] = part.astype(BF16).reshape(2, 2, 2, 96, HALF)
        su[k].back(0)

    for u in range(2):
        with scope("cd_w%d" % u):
            cd[u].finish()
        with scope("back_ffn%d" % u):

            def back_ffn(k, _, u=u):
                row = 4 * u + k
                at = pl.ds(pl.multiple_of(row * OWN, OWN), OWN)
                grad = cd[u].total(k // 2, pl.ds(pl.multiple_of(k % 2 * OWN, OWN), OWN))
                g[at] = e_all[row, own_cols].astype(F32) + norm_back(x2[at], gains[2:3], grad)
                e1[at] = g[at].astype(BF16)
                return 0

            lax.fori_loop(0, 4, back_ffn, 0)
    with scope("mix"):
        cy.cross()
    with scope("do2"):
        total = sum(nt(e1[:, k * HALF : (k + 1) * HALF], w_col(3, k)[...].reshape(D, HALF)) for k in range(2))
        do2[...] = total.astype(BF16).reshape(ROWS, OWN, D)
        for k in range(2):
            part = tn(o2[...].reshape(TOK, D), e1[:, k * HALF : (k + 1) * HALF])
            w_col(3, k)[...] = part.astype(BF16).reshape(2, 2, 2, 2, 48, HALF)
    r_out.r0()
    with scope("sd_b0"):
        sd[0].back(1)
    with scope("col_bwd"):

        def col_back(work):
            grads, back, out = [], [], []
            for _k, m, at in work:
                d, v = some(do2, m, at), some(qkv2, m, at, 2)
                grads.append([nt(one_head(e, d), v) for e in range(2)])
            for (k, m, at), pair in zip(work, grads):
                for e in range(2):
                    p, dq = p_col[2 * k + e, m], pair[e]
                    ds = p * (dq - jnp.sum(dq * p, axis=-1, keepdims=True))
                    back.append((ds.astype(BF16), ds.T.astype(BF16), p.T.astype(BF16)))
            for n, (_k, m, at) in enumerate(work):
                q, kk, d = some(qkv2, m, at, 0), some(qkv2, m, at, 1), some(do2, m, at)
                got = [
                    (nn(ds, kk) * FACTOR, nn(dst, q) * FACTOR, nn(pt, d)) for ds, dst, pt in back[2 * n : 2 * n + 2]
                ]
                out.append([jnp.where(lower2, got[0][i], got[1][i]) for i in range(3)])
            for (_k, m, at), got in zip(work, out):
                for n in range(3):
                    put(dqkv2, m, at, got[n], n)

        pairs(col_back)
    with scope("dh2"):
        total = None
        for part in range(3):
            for k in range(2):
                one = nt(dqkv2[part, :, :, k * HALF : (k + 1) * HALF].reshape(TOK, HALF), w_col(part, k)[...].reshape(D, HALF))
                total = one if total is None else total + one
        dh2[...] = total

    def grad_col(part):
        for k in range(2):
            one = tn(h2[...], dqkv2[part, :, :, k * HALF : (k + 1) * HALF].reshape(TOK, HALF))
            w_col(part, k)[...] = one.astype(BF16).reshape(2, 2, 2, 2, 48, HALF)

    with scope("back_col"):

        def back_col(at):
            g[at] = g[at] + norm_back(x1[at], gains[1:2], dh2[at])
            e1[at] = g[at].astype(BF16)

        in_pieces(back_col)

    with scope("do1"):
        for k in range(4):
            d = nt(e1[:, :HALF], w_out(0, k)) + nt(e1[:, HALF:], w_out(1, k))
            d = jnp.concatenate([d, jnp.zeros((TOK, 64), F32)], axis=1)
            dost[k] = d.astype(BF16).reshape(ROWS, OWN, 256)
    s_d = swap()
    s_d.go(lambda t: dost.at[t], do1.at[:, own_cols])
    do1[:, own_cols] = dost[f]
    s_g = swap()
    s_g.go(lambda t: e1.at[pl.ds(pl.multiple_of(2 * OWN * t, 2 * OWN), 2 * OWN)], e1r.at[f])
    e1r[f] = e1[pl.ds(pl.multiple_of(2 * OWN * f, 2 * OWN), 2 * OWN)]
    with scope("su_b0"):
        su[0].back(1)
    with scope("su_b1"):
        su[1].back(1)
    with scope("out_r1"):
        r_out.r1()
    with scope("sd_b1"):
        sd[1].back(1)
    with scope("g_qv"):
        grad_col(0)
        grad_col(2)
    r_qv.r0()
    with scope("sd_c0"):
        sd[0].back(2)
    with scope("g_k"):
        grad_col(1)
    r_k.r0()
    with scope("g_out_row"):
        for h in range(2):
            for k in range(4):
                part = tn(o1_of(k), e1[:, h * HALF : (h + 1) * HALF])
                w_o[h, k // 2, k % 2] = part.astype(BF16).reshape(2, 2, 48, HALF)
    ro.r0()
    with scope("qv_r1"):
        r_qv.r1()
    with scope("k_r1"):
        r_k.r1()
    with scope("ro1"):
        ro.r1()
    with scope("su_c0"):
        su[0].back(2)
    with scope("su_c1"):
        su[1].back(2)
    with scope("do1w"):
        s_d.wait()
    with scope("row_bwd"):
        d_sum = [[None] * 3 for _ in range(3)]
        for r in range(ROWS):
            d01, d2, v01, v2 = tile(do1, r, 0), tile(do1, r, 1), tile(qkv, r, 3), tile(qkv, r, 4)
            ops = ((jnp.where(lower, d01, zero), v01), (jnp.where(lower, zero, d01), v01), (d2, v2))
            for h, (a, b) in enumerate(ops):
                s = nt(a, b)
                t = 0 if r == 0 else 2 if r == ROWS - 1 else 1
                d_sum[h][t] = s if d_sum[h][t] is None else d_sum[h][t] + s
        da, dat, pt = [], [], []
        for h in range(3):
            s0, s1, s2 = d_sum[h]
            by = []
            for t, s in enumerate((s0, s1 + tied * s0, s2)):
                p = p_row[h, t]
                by.append(p * (s - jnp.sum(s * p, axis=-1, keepdims=True)))
            da.append((jnp.where(joined, by[1], by[0]), by[1], by[2]))
            dat.append([a.T.astype(BF16) for a in da[h]])
            pt.append([chances(h, r).T.astype(BF16) for r in (0, 1, ROWS - 1)])
            da[h] = [a.astype(BF16) for a in da[h]]
        s_first = jnp.where(joined, s_mid, FACTOR)
        for r in range(ROWS):
            t = 0 if r == 0 else 2 if r == ROWS - 1 else 1
            scale = (s_first, s_mid, FACTOR)[t]
            q01, q2k2, k01 = tile(qkv, r, 0), tile(qkv, r, 1), tile(qkv, r, 2)
            d01, d2 = tile(do1, r, 0), tile(do1, r, 1)
            dq = jnp.where(lower, nn(da[0][t], k01), nn(da[1][t], k01)) * scale
            dk = jnp.where(lower, nn(dat[0][t], q01), nn(dat[1][t], q01)) * scale
            mid = jnp.where(lower, nn(dat[2][t], q2k2), nn(da[2][t], q2k2)) * scale
            dv = jnp.where(lower, nn(pt[0][t], d01), nn(pt[1][t], d01))
            for n, val in enumerate((dq, pltpu.roll(mid, 64, 1), dk, dv, nn(pt[2][t], d2))):
                dqkv[r, :, n * 128 : (n + 1) * 128] = val.astype(BF16)
    with scope("dh1"):
        wide = w_q[...].reshape(D, WIDE)

        def partial_dh(k, _):
            pair = dqkv[pl.ds(2 * k, 2)].reshape(2 * COLS, WIDE)
            dp[k] = nt(pair, wide).astype(BF16).reshape(4, 2 * OWN, D)
            return 0

        lax.fori_loop(0, 4, partial_dh, 0)
    ch = Collect(me, lambda k: dp.at[k], l_p, sems)
    ch.pair()
    ch.near()
    for k in range(2):
        at = slice(0, 384) if k == 0 else slice(384, WIDE)
        with scope("g_qkv%d" % k):
            total = tn(h1[...].reshape(ROWS * COLS, D), dqkv[:, :, at].reshape(ROWS * COLS, -1))
            w_q[:, :, :, :, at] = total.astype(BF16).reshape(2, 2, 2, 96, -1)
        sq[k].back(0)
    with scope("out_r2"):
        r_out.r2()
    with scope("sd_c1"):
        sd[1].back(2)
    with scope("qv_r2"):
        r_qv.r2()
    with scope("out_r3"):
        r_out.r3()
    with scope("ro2"):
        ro.r2()
    with scope("k_r2"):
        r_k.r2()
    with scope("q_b1"):
        sq[1].back(1)
    with scope("q_b0"):
        sq[0].back(1)
    with scope("qv_r3"):
        r_qv.r3()
    with scope("dh1_x"):
        ch.cross()
    with scope("out_r3b"):
        r_out.r3b()
    with scope("q_c1"):
        sq[1].back(2)
    with scope("ro3"):
        ro.r3()
    with scope("k_r3"):
        r_k.r3()
    with scope("q_c0"):
        sq[0].back(2)
    with scope("qv_r3b"):
        r_qv.r3b()
    with scope("ro3b"):
        ro.r3b()
    with scope("k_r3b"):
        r_k.r3b()
    with scope("d_sum"):
        for k in sd:
            d_d[:, k.at] = k.back_sum()
    with scope("u_sum"):
        for k in su:
            t_u[:, :, k.at] = k.back_sum().astype(BF16).reshape(4, -1, HALF)
    s_v = swap()
    s_v.go(lambda t: t_u.at[t], o_u.at[f])
    o_u[f] = t_u[f]
    with scope("mixed"):
        cy.finish()
        for r in range(2):
            for k in range(4):
                mixed[r, k * OWN : (k + 1) * OWN] = cy.total(k, slice(r * OWN, (r + 1) * OWN)).astype(BF16)
    with scope("in_grad"):
        ch.finish()
        s_g.wait()
        for r in range(2):
            for k in range(4):
                at = slice(k * OWN, (k + 1) * OWN)
                grad = ch.total(2 * r + k // 2, slice(k % 2 * OWN, (k % 2 + 1) * OWN))
                back = norm_back(tok[r, at].astype(F32), gains[0:1], grad)
                igrad[r, at] = e1r[k, r * OWN : (r + 1) * OWN].astype(F32) + back
    with scope("out_r4"):
        r_out.r4()
    with scope("qv_r4"):
        r_qv.r4()
    with scope("k_r4"):
        r_k.r4()
    with scope("q_sum"):
        s_t = []
        for k in reversed(sq):
            t_q[:, :, k.at] = k.back_sum().astype(BF16).reshape(4, -1, k.at.size)
            o_q[f, :, k.at] = t_q[f, :, k.at]
            s_t.append(swap())
            s_t[-1].go(lambda t, at=k.at: t_q.at[t, :, at], o_q.at[f, :, k.at])
    with scope("ro4"):
        ro.r4()
    with scope("last"):
        for k in (r_out, r_qv, r_k, ro):
            k.r5()
        s_v.wait()
        for k in s_t:
            k.wait()
    assert used[0] <= SEMS, used[0]


SEMS = 160


def finish_kernel(
    mixed, igrad, o_q, e_o, e_c, e_co, o_u, e_d, gain_row, r_q, gain_col, r_c, gain_ffn, r_u,
    mixed_out, igrad_out, dg_row, d_q, d_o, dg_col, d_c, d_co, dg_ffn, d_u, d_d,
):
    for a, b in ((mixed, mixed_out), (igrad, igrad_out), (e_o, d_o), (e_c, d_c), (e_co, d_co), (e_d, d_d)):
        b[...] = a[...]
    for n in range(8):
        parts = [o_u[t, :, n // 4 * 384 : (n // 4 + 1) * 384].astype(F32) for t in range(4)]
        d_u[:, n * 384 : (n + 1) * 384] = spread(parts, [t - n % 4 for t in range(4)])
    where = {}
    for t in range(4):
        for n, pair in enumerate(head_order(t)):
            for k, piece in enumerate(pair):
                where[piece] = (o_q.at[t], 2 * n + k)
    for n in range(3 * D // 128):
        d_q[:, n * 128 : (n + 1) * 128] = by_halves([where[2 * n], where[2 * n + 1]])

    for out, weight, grad, gain in (
        (dg_row, r_q, d_q, gain_row), (dg_col, r_c, d_c, gain_col), (dg_ffn, r_u, d_u, gain_ffn)
    ):
        total = jnp.sum(weight[...].astype(F32) * grad[...], axis=1, keepdims=True)
        out[...] = level(total / upright(gain[...].astype(F32)))


def run_layer(tok, cot, seq, cid, *weights):
    sds = jax.ShapeDtypeStruct
    rows = weights[1].shape[0]
    i_d = weights[-1]
    first = [sds(tok.shape, BF16), sds(tok.shape, F32)]
    wide_q, wide_u = sds((4, rows, WIDE), BF16), sds((4, rows, D), BF16)
    plain = [sds(w.shape, F32) for w in weights]
    shapes = first + [wide_q, plain[2], plain[4], plain[5], wide_u, plain[8]]

    def vmem(*shape, dtype=BF16):
        return pltpu.VMEM(shape, dtype)

    def lands(r, c):
        return [
            vmem(2, 2, 2, 2, r, c), vmem(2, 2, 2, r, c), vmem(2, 2, r, c), vmem(3, r, c), vmem(2, r // 2, c, dtype=F32)
        ]

    def slices(c):
        return [vmem(2, 2, 4 * rows, c), vmem(3, 4 * rows, c)]

    r2 = 2 * rows
    wo, wc, wu = HALF, 2 * D, D
    scratch = [
        vmem(4, rows, WIDE),
        vmem(4, rows, wu),
        vmem(2, 2, 2, 4 * rows, WIDE),
        vmem(2, 2, 2, 2, 2, r2, wo),
        vmem(2, 2, 2, 2, 2, r2, wc),
        vmem(2, 2, 2, 4 * rows, wu),
        vmem(2, 2, 2, *i_d.shape),
        vmem(4, rows, WIDE),
        vmem(rows, wo),
        vmem(rows, wc),
        vmem(4, rows, wu),
        *lands(r2, wo),
        *lands(r2, wc),
        *slices(WIDE),
        vmem(4, rows, WIDE),
        *slices(wu),
        vmem(4, rows, wu),
        *slices(D),
        vmem(ROWS, COLS, D),
        vmem(ROWS, COLS, D),
        vmem(ROWS, COLS, D),
        vmem(ROWS, COLS, WIDE),
        vmem(3, 3, COLS, COLS, dtype=F32),
        vmem(ROWS, COLS, 256),
        vmem(4, ROWS, OWN, 256),
        vmem(TOK, D, dtype=F32),
        vmem(TOK, D),
        vmem(3, ROWS, OWN, D),
        vmem(HEADS, 2, TOK // 2, TOK // 2, dtype=F32),
        vmem(ROWS, OWN, D),
        vmem(TOK, D, dtype=F32),
        vmem(4, 2, TOK // 2, D),
        vmem(4, 2, TOK // 2, D),
        vmem(4, 2, TOK // 2, D),
        vmem(4, 4, 2 * OWN, D),
        vmem(3, 4, 2 * OWN, D),
        vmem(4, 4, 2 * OWN, D),
        vmem(3, 4, 2 * OWN, D),
        vmem(TOK, D, dtype=F32),
        vmem(ROWS, OWN, D),
        vmem(3, ROWS, OWN, D),
        vmem(TOK, D, dtype=F32),
        vmem(TOK, D),
        vmem(4, ROWS, OWN, 256),
        vmem(ROWS, COLS, 256),
        vmem(ROWS, COLS, WIDE),
        vmem(4, 2 * OWN, D),
        vmem(8, D, dtype=F32),
        vmem(COLS, COLS, dtype=F32),
        vmem(TOK // 2, TOK // 2, dtype=F32),
        pltpu.SemaphoreType.DMA((SEMS,)),
        pltpu.SemaphoreType.DMA((SEMS,)),
    ]
    vm = pl.BlockSpec(memory_space=pltpu.VMEM)
    outs = pl.pallas_call(
        layer_kernel,
        out_shape=shapes,
        in_specs=[vm, vm, pl.BlockSpec(memory_space=pltpu.SMEM)] + [vm] * 10,
        out_specs=[vm] * 8,
        scratch_shapes=scratch,
        name="layer",
        compiler_params=pltpu.CompilerParams(
            collective_id=0, has_side_effects=True, vmem_limit_bytes=VMEM_LIMIT
        ),
    )(tok, cot, seq, cid, *weights)
    return pl.pallas_call(
        finish_kernel,
        out_shape=first + plain,
        in_specs=[vm] * 14,
        out_specs=[vm] * 11,
        name="finish",
        compiler_params=pltpu.CompilerParams(vmem_limit_bytes=VMEM_LIMIT),
    )(*outs, weights[0], weights[1], weights[3], weights[4], weights[6], weights[7])


VMEM_LIMIT = 63 * 2**20


def on_device(
    tokens, cotangent, seq_ids, col_ids,
    gain_row, qkv_row, out_row, gain_col, qkv_col, out_col, gain_ffn, up_ffn, down_ffn,
    cells,
):
    members = CELL * lax.axis_size("fsdp")
    low_index = (lax.axis_index("dp") % CELL) * lax.axis_size("fsdp") + lax.axis_index("fsdp")

    def in_cell(shard):
        if cells == 1:
            return shard
        whole = lax.all_gather(shard, AXES, axis=0, tiled=True)
        rows = whole.shape[0] // members
        return lax.dynamic_slice_in_dim(whole, low_index * rows, rows, 0)

    def from_cell(summed):
        if cells == 1:
            return summed
        rows = summed.shape[0]
        whole = jnp.zeros((rows * members,) + summed.shape[1:], summed.dtype)
        whole = lax.dynamic_update_slice_in_dim(whole, summed, low_index * rows, 0)
        return lax.psum_scatter(whole, AXES, scatter_dimension=0, tiled=True)

    weights = [
        in_cell(w).reshape(1, -1) if w.ndim == 1 else in_cell(w)
        for w in (gain_row, qkv_row, out_row, gain_col, qkv_col, out_col, gain_ffn, up_ffn, down_ffn)
    ]
    mixed, igrad, *grads = run_layer(tokens[0], cotangent[0], seq_ids, col_ids, *weights)
    grads = [from_cell(v.reshape(-1) if v.shape[0] == 1 else v) for v in grads]
    return (mixed[None], igrad[None], *grads)


def solution(mesh):
    rows = P(AXES, None)
    vector = P(AXES)
    grid = P("dp", "fsdp", None, None)
    ids = P("dp", None)
    return jax.shard_map(
        partial(on_device, cells=mesh.shape["dp"] // CELL),
        mesh=mesh,
        in_specs=(grid, grid, ids, ids) + (vector, rows, rows) * 3,
        out_specs=(grid, grid) + (vector, rows, rows) * 3,
        check_vma=False,
    )
```

```python
from functools import partial

import jax
import jax.numpy as jnp
from jax import lax
from jax.experimental import pallas as pl
from jax.experimental.pallas import tpu as pltpu
from jax.sharding import PartitionSpec as P

HEADS = 12
EPSILON = 1e-05
NEGATIVE = -1000000000.0
MESH = pl.DeviceIdType.MESH
BF16 = jnp.bfloat16
F32 = jnp.float32
CELL = 8
AXES = ("dp", "fsdp")


class Place:
    def __init__(self):
        dp = lax.axis_index("dp")
        self.f = lax.axis_index("fsdp")
        self.base = dp // CELL * CELL
        low = dp - self.base
        self.z, self.y = low // 2, low % 2
        self.hi, self.lo = self.z // 2, self.z % 2
        self.x, self.c = self.f // 2, self.f % 2

    def dev(self, z, y, x, c):
        return (self.base + z * 2 + y, x * 2 + c)

    def sib(self):
        return self.dev(self.z, self.y, self.x, 1 - self.c)

    def xn(self):
        return self.dev(self.z, self.y, 1 - self.x, self.c)

    def yn(self):
        return self.dev(self.z, 1 - self.y, self.x, self.c)

    def first(self):
        return self.dev(self.z, self.y + self.c * (1 - 2 * self.y), self.x + (1 - self.c) * (1 - 2 * self.x), self.c)

    def second(self):
        return self.dev(self.z, self.y + (1 - self.c) * (1 - 2 * self.y), self.x + self.c * (1 - 2 * self.x), self.c)

    def z1(self):
        return self.dev(2 * self.hi + 1 - self.lo, self.y, self.x, self.c)

    def z2(self):
        return self.dev(2 * (1 - self.hi) + self.lo, self.y, self.x, self.c)


def greet(partners):
    bar = pltpu.get_barrier_semaphore()
    for t in partners:
        pl.semaphore_signal(bar, inc=1, device_id=t, device_id_type=MESH)
    pl.semaphore_wait(bar, len(partners))


def rcopy(src, dst, ss, rs, to):
    return pltpu.make_async_remote_copy(
        src_ref=src, dst_ref=dst, send_sem=ss, recv_sem=rs, device_id=to, device_id_type=MESH
    )


ALL = slice(None)


class Part:
    def __init__(self, me, w, at):
        self.me, self.w, self.at = me, w, at

    def block(self, hi, lo, y, x, half=None):
        return self.w.at[self.me.c if half is None else half, hi, lo, y, x, :, self.at]


class Gather(Part):
    def __init__(self, me, src_of, land, w, at, sems):
        super().__init__(me, w, at)
        self.src_of, self.land, self.sems = src_of, land, sems

    def swap(self):
        me = self.me
        self.c0 = rcopy(self.src_of(1 - me.c), self.land.at[:, self.at], *self.sems(), me.sib())
        self.c0.start()

    def start(self, ref, to):
        c = rcopy(ref, ref, *self.sems(), to)
        c.start()
        self.sent.append(c)
        return c

    def own(self):
        me = self.me
        self.c0.wait()
        mine = self.src_of(me.c)[...].astype(F32)
        other = self.land[:, self.at].astype(F32)
        flag = (me.c == 0).astype(F32)
        top = flag * mine + (1 - flag) * other
        low = flag * other + (1 - flag) * mine
        own = self.block(me.hi, me.lo, me.y, me.x)
        own[...] = jnp.concatenate([top, low], axis=0).astype(BF16)
        self.sent = []

    def s0(self):
        me = self.me
        self.own()
        self.a = self.start(self.block(me.hi, me.lo, me.y, me.x), me.z2())

    def s1(self):
        me = self.me
        self.a.wait_recv()
        self.b = self.start(self.block(ALL, me.lo, me.y, me.x), me.z1())

    def s2(self):
        me = self.me
        self.b.wait_recv()
        col = self.block(ALL, ALL, me.y, me.x)
        self.e = self.start(col, me.first())
        self.to_sib = [self.start(col, me.sib())]

    def fork(self, ref0, ref1, to, like):
        me, m = self.me, self.sems()

        @pl.when(me.c == 0)
        def _():
            rcopy(ref0, ref0, *m, to).start()

        @pl.when(me.c == 1)
        def _():
            rcopy(ref1, ref1, *m, to).start()

        c = rcopy(like, like, *m, to)
        self.sent.append(c)
        return c

    def s3(self):
        me = self.me
        self.e.wait_recv()
        two, col = self.block(ALL, ALL, me.y, ALL), self.block(ALL, ALL, me.y, me.x)
        self.g = self.fork(
            self.block(ALL, ALL, me.y, ALL, 0), self.block(ALL, ALL, ALL, me.x, 1), me.second(), two
        )
        self.to_sib.append(
            self.fork(
                self.block(ALL, ALL, me.y, 1 - me.x, 0), self.block(ALL, ALL, 1 - me.y, me.x, 1), me.sib(), col
            )
        )

    def s4(self):
        me = self.me
        self.g.wait_recv()
        two = self.block(ALL, ALL, me.y, ALL)
        self.to_sib.append(
            self.fork(
                self.block(ALL, ALL, 1 - me.y, ALL, 0), self.block(ALL, ALL, ALL, 1 - me.x, 1), me.sib(), two
            )
        )

    def s5(self):
        for c in self.to_sib:
            c.wait_recv()

    def drain(self):
        for c in self.sent:
            c.wait_send()


class Reduce(Part):
    def __init__(self, me, w, at, lands, out_of, sems):
        super().__init__(me, w, at)
        self.l0, self.l1, self.l2, self.l3, self.l4 = lands
        self.out_of, self.sems = out_of, sems

    def add(self, n, mine_of, land_of):
        def body(k, _):
            mine = mine_of(k)
            mine[...] = (mine[...].astype(F32) + land_of(k)[...].astype(F32)).astype(BF16)
            return 0

        lax.fori_loop(0, n, body, 0)

    def r0(self):
        me = self.me
        self.c0 = rcopy(
            self.block(ALL, ALL, ALL, ALL, 1 - me.c), self.l0.at[:, :, :, :, :, self.at], *self.sems(), me.sib()
        )
        self.c0.start()

    def r1(self):
        me = self.me
        self.c0.wait()
        self.add(
            16,
            lambda k: self.block(k // 8, k // 4 % 2, k // 2 % 2, k % 2),
            lambda k: self.l0.at[k // 8, k // 4 % 2, k // 2 % 2, k % 2, :, self.at],
        )
        land, m = self.l1.at[:, :, :, :, self.at], self.sems()

        @pl.when(me.c == 0)
        def _():
            rcopy(self.block(ALL, ALL, 1 - me.y, ALL, 0), land, *m, me.second()).start()

        @pl.when(me.c == 1)
        def _():
            rcopy(self.block(ALL, ALL, ALL, 1 - me.x, 1), land, *m, me.second()).start()

        self.c1 = rcopy(land, land, *m, me.sib())

    def r2(self):
        me = self.me
        self.c1.wait()

        def mine(k):
            m = k % 2
            y, x = me.y + me.c * (m - me.y), me.x + (1 - me.c) * (m - me.x)
            return self.block(k // 4, k // 2 % 2, y, x)

        self.add(8, mine, lambda k: self.l1.at[k // 4, k // 2 % 2, k % 2, :, self.at])
        oy = me.y + me.c * (1 - 2 * me.y)
        ox = me.x + (1 - me.c) * (1 - 2 * me.x)
        self.c2 = rcopy(self.block(ALL, ALL, oy, ox), self.l2.at[:, :, :, self.at], *self.sems(), me.first())
        self.c2.start()

    def r3(self):
        me = self.me
        self.c2.wait()
        self.add(
            4, lambda k: self.block(k // 2, k % 2, me.y, me.x), lambda k: self.l2.at[k // 2, k % 2, :, self.at]
        )
        self.c3 = rcopy(
            self.block(ALL, 1 - me.lo, me.y, me.x), self.l3.at[pl.ds(0, 2), :, self.at], *self.sems(), me.z1()
        )
        self.c3.start()

    def r3b(self):
        me = self.me
        self.c3.wait()
        self.add(2, lambda k: self.block(k, me.lo, me.y, me.x), lambda k: self.l3.at[k, :, self.at])
        self.c3 = rcopy(
            self.block(1 - me.hi, me.lo, me.y, me.x), self.l3.at[2, :, self.at], *self.sems(), me.z2()
        )
        self.c3.start()

    def r4(self):
        me = self.me
        self.c3.wait()
        total = self.block(me.hi, me.lo, me.y, me.x)[...].astype(F32) + self.l3[2, :, self.at].astype(F32)
        half = total.shape[0] // 2
        flag = (me.c == 0).astype(F32)
        top, low = total[:half], total[half:]
        self.out_of(me.c)[...] = flag * top + (1 - flag) * low
        self.l4[0, :, self.at] = flag * low + (1 - flag) * top
        self.c4 = rcopy(self.l4.at[0, :, self.at], self.l4.at[1, :, self.at], *self.sems(), me.sib())
        self.c4.start()

    def r5(self):
        self.c4.wait()
        self.out_of(1 - self.me.c)[...] = self.l4[1, :, self.at]


class LastOverX(Gather):
    def s2(self):
        me = self.me
        self.b.wait_recv()
        col = self.block(ALL, ALL, me.y, me.x)
        self.e = self.start(col, me.yn())
        self.to_sib = [self.start(col, me.sib())]

    def s3(self):
        me = self.me
        self.e.wait_recv()
        self.g = self.start(self.block(ALL, ALL, ALL, me.x), me.xn())
        self.to_sib.append(self.start(self.block(ALL, ALL, 1 - me.y, me.x), me.sib()))

    def s4(self):
        me = self.me
        self.g.wait_recv()
        self.to_sib.append(self.start(self.block(ALL, ALL, ALL, 1 - me.x), me.sib()))


class EarlyReduce(Reduce):
    def go(self, src, land, to):
        self.c = rcopy(src, land, *self.sems(), to)
        self.c.start()

    def r1(self):
        me = self.me
        self.c0.wait()
        self.add(
            16,
            lambda k: self.block(k // 8, k // 4 % 2, k // 2 % 2, k % 2),
            lambda k: self.l0.at[k // 8, k // 4 % 2, k // 2 % 2, k % 2, :, self.at],
        )
        self.go(self.block(ALL, 1 - me.lo, ALL, ALL), self.l1.at[:, :, :, :, self.at], me.z1())

    def r2(self):
        me = self.me
        self.c.wait()
        self.add(
            8,
            lambda k: self.block(k // 4, me.lo, k // 2 % 2, k % 2),
            lambda k: self.l1.at[k // 4, k // 2 % 2, k % 2, :, self.at],
        )
        self.go(self.block(1 - me.hi, me.lo, ALL, ALL), self.l2.at[:, :, :, self.at], me.z2())

    def r3(self):
        me = self.me
        self.c.wait()
        self.add(
            4,
            lambda k: self.block(me.hi, me.lo, k // 2, k % 2),
            lambda k: self.l2.at[k // 2, k % 2, :, self.at],
        )
        self.go(self.block(me.hi, me.lo, ALL, 1 - me.x), self.l3.at[pl.ds(0, 2), :, self.at], me.xn())

    def r3b(self):
        me = self.me
        self.c.wait()
        self.add(2, lambda k: self.block(me.hi, me.lo, k, me.x), lambda k: self.l3.at[k, :, self.at])
        self.go(self.block(me.hi, me.lo, 1 - me.y, me.x), self.l3.at[2, :, self.at], me.yn())
        self.c3 = self.c


class Swap:
    def __init__(self, me, ssem, rsem):
        self.me, self.ss, self.rs, self.sent = me, ssem, rsem, []

    def other(self, d):
        return (self.me.f + d) % 4

    def go(self, src_of, dst):
        me = self.me
        for d in (1, 2, 3):
            t = self.other(d)
            c = rcopy(src_of(t), dst, self.ss.at[d - 1], self.rs.at[d - 1], me.dev(me.z, me.y, t // 2, t % 2))
            c.start()
            self.sent.append(c)

    def wait(self):
        for c in self.sent:
            c.wait_send()
            c.wait_recv()


class Slices:
    def __init__(self, me, w, at, l1, l2, sems, early=False):
        self.me, self.w, self.at, self.l1, self.l2, self.sems, self.early = me, w, at, l1, l2, sems, early
        self.sent = []

    def part(self, hi, lo, y):
        return self.w.at[hi, lo, y, :, self.at]

    def steps(self):
        me = self.me
        if self.early:
            return (
                (self.part(me.hi, me.lo, me.y), me.yn()),
                (self.part(me.hi, me.lo, ALL), me.z2()),
                (self.part(ALL, me.lo, ALL), me.z1()),
            )
        return (
            (self.part(me.hi, me.lo, me.y), me.z2()),
            (self.part(ALL, me.lo, me.y), me.z1()),
            (self.part(ALL, ALL, me.y), me.yn()),
        )

    def send(self, n):
        if n:
            self.sent[-1].wait_recv()
        ref, to = self.steps()[n]
        c = rcopy(ref, ref, *self.sems(), to)
        c.start()
        self.sent.append(c)

    def finish(self):
        self.sent[-1].wait_recv()
        for c in self.sent:
            c.wait_send()

    def kept(self, n):
        me = self.me
        if self.early:
            return (
                (4, lambda k: self.part(k // 2, me.lo, k % 2)),
                (2, lambda k: self.part(me.hi, me.lo, k)),
            )[n]
        return (
            (4, lambda k: self.part(k // 2, k % 2, me.y)),
            (2, lambda k: self.part(k, me.lo, me.y)),
        )[n]

    def back(self, n):
        me = self.me
        if n:
            self.c.wait()
            count, mine_of = self.kept(n - 1)

            def body(k, _):
                mine = mine_of(k)
                land = self.l1[k // 2, k % 2, :, self.at] if n == 1 else self.l2[k, :, self.at]
                mine[...] = (mine[...].astype(F32) + land.astype(F32)).astype(BF16)
                return 0

            lax.fori_loop(0, count, body, 0)
        lands = (self.l1.at[:, :, :, self.at], self.l2.at[pl.ds(0, 2), :, self.at], self.l2.at[2, :, self.at])
        if self.early:
            src, to = (
                (self.part(ALL, 1 - me.lo, ALL), me.z1()),
                (self.part(1 - me.hi, me.lo, ALL), me.z2()),
                (self.part(me.hi, me.lo, 1 - me.y), me.yn()),
            )[n]
        else:
            src, to = (
                (self.part(ALL, ALL, 1 - me.y), me.yn()),
                (self.part(ALL, 1 - me.lo, me.y), me.z1()),
                (self.part(1 - me.hi, me.lo, me.y), me.z2()),
            )[n]
        self.c = rcopy(src, lands[n], *self.sems(), to)
        self.c.start()

    def back_sum(self):
        me = self.me
        self.c.wait()
        return self.part(me.hi, me.lo, me.y)[...].astype(F32) + self.l2[2, :, self.at].astype(F32)


class Share:
    def __init__(self, me, whole, sems):
        self.me, self.sems = me, sems
        self.whole = whole

    def send(self):
        me = self.me
        own = self.whole(me.f)
        self.s = rcopy(own, own, *self.sems(), me.sib())
        self.x = rcopy(own, own, *self.sems(), me.xn())
        self.s.start()
        self.x.start()

    def near(self):
        self.s.wait()

    def forward(self):
        me = self.me
        self.x.wait_recv()
        got = self.whole(2 * (1 - me.x) + me.c)
        self.t = rcopy(got, got, *self.sems(), me.sib())
        self.t.start()

    def finish(self):
        self.x.wait_send()
        self.t.wait()


class Collect:
    def __init__(self, me, part_of, lands, sems, pieces=4):
        self.me, self.part_of, self.lands, self.sems, self.pieces = me, part_of, lands, sems, pieces

    def near(self):
        me = self.me
        self.n = rcopy(self.part_of(2 * me.x + 1 - me.c), self.lands.at[0], *self.sems(), me.sib())
        self.n.start()

    def pair(self):
        me = self.me
        self.p = rcopy(self.part_of(2 * (1 - me.x) + 1 - me.c), self.lands.at[1], *self.sems(), me.sib())
        self.p.start()

    def cross(self):
        me = self.me
        self.p.wait()
        part = self.part_of(2 * (1 - me.x) + me.c)

        def add(k, _):
            mine = part.at[k]
            mine[...] = (mine[...].astype(F32) + self.lands[1, k].astype(F32)).astype(BF16)
            return 0

        lax.fori_loop(0, self.pieces, add, 0)
        self.x = rcopy(part, self.lands.at[2], *self.sems(), me.xn())
        self.x.start()

    def finish(self):
        self.n.wait()
        self.x.wait()

    def total(self, k, at):
        own = self.part_of(self.me.f)[k, at].astype(F32) + self.lands[0, k, at].astype(F32)
        return own + self.lands[2, k, at].astype(F32)


def nn(a, b):
    return lax.dot_general(a, b, (((1,), (0,)), ((), ())), preferred_element_type=F32)


def nt(a, b):
    return lax.dot_general(a, b, (((1,), (1,)), ((), ())), preferred_element_type=F32)


def tn(a, b):
    return lax.dot_general(a, b, (((0,), (0,)), ((), ())), preferred_element_type=F32)


def standard(values):
    centred = values - jnp.mean(values, axis=-1, keepdims=True)
    scale = lax.rsqrt(jnp.mean(centred * centred, axis=-1, keepdims=True) + EPSILON)
    return centred * scale, scale


def norm_back(values, gain, grad):
    unit, scale = standard(values)
    inner = grad * gain
    low = jnp.mean(inner, axis=-1, keepdims=True)
    high = jnp.mean(inner * unit, axis=-1, keepdims=True)
    return scale * (inner - low - unit * high)


def softmax(scores):
    e = jnp.exp(scores - jnp.max(scores, axis=-1, keepdims=True))
    return e / jnp.sum(e, axis=-1, keepdims=True)


def low_half(shape):
    return lax.broadcasted_iota(jnp.int32, shape, 1) % 128 < 64


def by_halves(pieces):
    out = []
    for n, piece in enumerate(pieces):
        if piece is None:
            out.append(jnp.zeros_like(pieces[0][0][:, :128]))
            continue
        ref, k = piece
        part = ref[:, k // 2 * 128 : k // 2 * 128 + 128].astype(F32)
        out.append(part if k % 2 == n else pltpu.roll(part, 64, 1))
    return jnp.where(low_half(out[0].shape), out[0], out[1])


def head_order(f):
    q, k, v = (HEADS * n + 3 * f for n in range(3))
    return ((q, q + 1), (q + 2, k + 2), (k, k + 1), (v, v + 1), (v + 2, None))


def spread(parts, shifts):
    lane = lax.broadcasted_iota(jnp.int32, parts[0].shape, 1) // 96
    total = None
    for n in range(4):
        part = pltpu.roll(parts[n], shifts[n] % 4 * 96, 1) if shifts[n] % 4 else parts[n]
        total = part if total is None else jnp.where(lane == n, part, total)
    return total


def upright(row):
    n = row.shape[1]
    i, j = (lax.broadcasted_iota(jnp.int32, (n, n), k) for k in range(2))
    return jnp.sum(jnp.where(i == j, jnp.broadcast_to(row, (n, n)), 0.0), axis=1, keepdims=True)


def level(column):
    n = column.shape[0]
    i, j = (lax.broadcasted_iota(jnp.int32, (n, n), k) for k in range(2))
    return jnp.sum(jnp.where(i == j, jnp.broadcast_to(column, (n, n)), 0.0), axis=0, keepdims=True)


D, FF, ROWS, COLS, HEAD = 768, 3072, 8, 128, 64
HALF = D // 2
OWN = COLS // 4
TOK = ROWS * OWN
WIDE = 640
FACTOR = HEAD**-0.5


def layer_kernel(
    tok, cot, seq, cid, gain_row, r_q, r_o, gain_col, r_c, r_co, gain_ffn, r_u, r_d,
    mixed, igrad, o_q, d_o, d_c, d_co, o_u, d_d,
    i_q, i_u,
    w_q, w_o, w_c, w_u, w_d, f_q, f_o, f_c, f_u,
    l_o0, l_o1, l_o2, l_o3, l_o4,
    l_c0, l_c1, l_c2, l_c3, l_c4,
    l_q1, l_q2, t_q, l_u1, l_u2, t_u, l_d1, l_d2,
    tok_all, e_all, h1, qkv, p_row, o1f, o1c, x1, h2, qkv2, p_col, o2, x2, h3, act, du, yp, l_y, dp, l_p,
    g, do2, dqkv2, dh2, e1, dost, do1, dqkv, e1r, gains, cmask, tmask, ms, mr,
):
    me = Place()
    f = me.f
    scope = jax.named_scope
    sib_f, x_f, diag_f = 2 * me.x + 1 - me.c, 2 * (1 - me.x) + me.c, 2 * (1 - me.x) + 1 - me.c
    diag = me.dev(me.z, me.y, 1 - me.x, 1 - me.c)
    greet([me.sib(), me.xn(), diag, me.yn(), me.z1(), me.z2()])
    used = [0]

    def sems():
        used[0] += 1
        return ms.at[used[0] - 1], mr.at[used[0] - 1]

    def swap():
        used[0] += 3
        at = pl.ds(used[0] - 3, 3)
        return Swap(me, ms.at[at], mr.at[at])

    at_w = pl.ds(0, HALF)
    at_qv, at_k, at_o = pl.ds(0, D), pl.ds(D, HALF), pl.ds(D + HALF, HALF)

    def lanes(ref, start, step, size):
        return lambda h: ref.at[:, pl.ds(pl.multiple_of(start + h * step, 128), size)]

    of_o = lanes(r_o, 0, HALF, HALF)
    of_qv, of_k, of_co = lanes(r_c, 0, 2 * D, D), lanes(r_c, D, HALF, HALF), lanes(r_co, 0, HALF, HALF)
    go = Gather(me, of_o, f_o, w_o, at_w, sems)
    g_qv = Gather(me, of_qv, f_c, w_c, at_qv, sems)
    g_k = Gather(me, of_k, f_c, w_c, at_k, sems)
    g_out = LastOverX(me, of_co, f_c, w_c, at_o, sems)
    ro = Reduce(me, w_o, at_w, (l_o0, l_o1, l_o2, l_o3, l_o4), lanes(d_o, 0, HALF, HALF), sems)
    r_qv, r_k, r_out = (
        kind(me, w_c, at, (l_c0, l_c1, l_c2, l_c3, l_c4), out, sems)
        for kind, at, out in (
            (Reduce, at_qv, lanes(d_c, 0, 2 * D, D)),
            (EarlyReduce, at_k, lanes(d_c, D, HALF, HALF)),
            (Reduce, at_o, lanes(d_co, 0, HALF, HALF)),
        )
    )
    sq = [Slices(me, w_q, pl.ds(*at), l_q1, l_q2, sems, at[0] > 0) for at in ((0, 384), (384, 256))]
    su = [Slices(me, w_u, pl.ds(k * HALF, HALF), l_u1, l_u2, sems, k == 1) for k in range(2)]
    sd = [Slices(me, w_d, pl.ds(k * HALF, HALF), l_d1, l_d2, sems, k == 0) for k in range(2)]

    def cols_of(t):
        return pl.ds(pl.multiple_of(t * OWN, OWN), OWN)

    own_cols = cols_of(f)

    def stacked(land):
        return jnp.concatenate([land[k].astype(F32) for k in range(4)], axis=0).astype(BF16)

    lane = lax.broadcasted_iota(jnp.int32, (r_q.shape[0], 128), 1)
    columns = [upright(v[...].astype(F32)) for v in (gain_row, gain_col, gain_ffn)]
    spare = sum(jnp.where(lane == HEAD + n, v, 0.0) for n, v in enumerate(columns))
    for t in range(4):
        for n, pair in enumerate(head_order(t)):
            part = by_halves([None if k is None else (r_q, k) for k in pair])
            i_q[t, :, n * 128 : (n + 1) * 128] = (part + spare if n == 4 else part).astype(BF16)
    s_q = swap()
    s_q.go(lambda t: i_q.at[t], f_q.at[f])
    for k in (g_k, g_qv, go, g_out):
        k.swap()
    tok_all[pl.ds(2 * f, 2)] = tok[...]
    w_d[me.hi, me.lo, me.y] = r_d[...]
    sd[0].send(0)
    with scope("i_u"):
        for t in range(4):
            for n in range(2):
                parts = [r_u[:, (4 * n + k) * 384 : (4 * n + k + 1) * 384].astype(F32) for k in range(4)]
                i_u[t, :, n * 384 : (n + 1) * 384] = spread(parts, [k - t for k in range(4)]).astype(BF16)
    s_u = swap()
    s_u.go(lambda t: i_u.at[t], f_u.at[f])
    shr_t = Share(me, lambda k: tok_all.at[pl.ds(2 * k, 2)], sems)
    shr_t.send()
    with scope("q_f"):
        f_q[f] = i_q[f]
        s_q.wait()
        w_q[me.hi, me.lo, me.y] = stacked(f_q)
    sq[1].send(0)
    sq[0].send(0)
    with scope("masks"):
        first = seq[0, 0]
        ids = jnp.broadcast_to(cid[...], (COLS, COLS)).astype(F32)
        cmask[...] = jnp.where(ids == ids.T, 1.0, 0.0)
        i, j = (lax.broadcasted_iota(jnp.int32, tmask.shape, n) for n in range(2))
        wide = OWN // 2

        def block_of(k):
            r = k // wide
            return jnp.where(r == 0, first, jnp.where(r == ROWS - 1, 2, 1))

        tmask[...] = jnp.where((i % wide == j % wide) & (block_of(i) == block_of(j)), 1.0, 0.0)
        e_all[pl.ds(2 * f, 2)] = cot[...]
        f_u[f] = i_u[f]
    with scope("q_m1"):
        sq[1].send(1)
    s_u.wait()
    w_u[me.hi, me.lo, me.y] = stacked(f_u)
    su[1].send(0)
    with scope("q_m0"):
        sq[0].send(1)
    g_qv.s0()
    go.s0()
    with scope("q_n1"):
        sq[1].send(2)
    shr_e = Share(me, lambda k: e_all.at[pl.ds(2 * k, 2)], sems)
    shr_e.send()
    with scope("q_n0"):
        sq[0].send(2)
    g_k.s0()
    with scope("qv1"):
        g_qv.s1()
    with scope("tok"):
        shr_t.forward()
    with scope("go1"):
        go.s1()
    with scope("q_fin1"):
        sq[1].finish()
    with scope("gains"):
        wide = w_q[:, :, :, :, WIDE - 128 :].reshape(D, 128)
        for k in range(D // 128):
            part = wide[k * 128 : (k + 1) * 128].astype(F32).T
            gains[:, k * 128 : (k + 1) * 128] = part[HEAD : HEAD + 8]
    with scope("tok2"):
        shr_t.near()
        shr_t.finish()

    with scope("norm_row"):

        def norm_rows(k, _):
            unit, _s = standard(tok_all[k].astype(F32))
            h1[k] = (unit * gains[0:1]).astype(BF16)
            return 0

        lax.fori_loop(0, ROWS, norm_rows, 0)
    with scope("k1"):
        g_k.s1()
    with scope("qv2"):
        g_qv.s2()
    su[0].send(0)
    g_out.s0()
    with scope("go2"):
        go.s2()
    with scope("q_fin0"):
        sq[0].finish()
    with scope("qkv_row"):
        wide = w_q[...].reshape(D, WIDE)

        def project(k, _):
            pair = h1[pl.ds(2 * k, 2)].reshape(2 * COLS, D)
            qkv[pl.ds(2 * k, 2)] = nn(pair, wide).astype(BF16).reshape(2, COLS, WIDE)
            return 0

        lax.fori_loop(0, ROWS // 2, project, 0)
    with scope("k2"):
        g_k.s2()
    with scope("qv3"):
        g_qv.s3()
    with scope("su_m0"):
        su[0].send(1)

    joined = (jnp.full((1, 1), first, jnp.int32) == 1)
    tied = jnp.where(joined, 1.0, 0.0)
    s_mid = jnp.where(joined, FACTOR / 7**0.5, FACTOR / 6**0.5)
    lower = low_half((COLS, 128))
    zero = jnp.zeros((COLS, 128), BF16)

    def tile(ref, r, k):
        return ref[r, :, k * 128 : (k + 1) * 128]

    def head_tiles(r):
        q01, q2k2, k01 = tile(qkv, r, 0), tile(qkv, r, 1), tile(qkv, r, 2)
        k2 = pltpu.roll(q2k2.astype(F32), 64, 1).astype(BF16)
        return (
            (jnp.where(lower, q01, zero), k01),
            (jnp.where(lower, zero, q01), k01),
            (jnp.where(lower, q2k2, zero), k2),
        )

    with scope("go3"):
        go.s3()
    with scope("row_fwd"):
        sums = [[None] * 3 for _ in range(3)]
        for r in range(ROWS):
            for h, (a, b) in enumerate(head_tiles(r)):
                s = nt(a, b)
                t = 0 if r == 0 else 2 if r == ROWS - 1 else 1
                sums[h][t] = s if sums[h][t] is None else sums[h][t] + s
        for h in range(3):
            s0, s1, s2 = sums[h]
            for t, s in enumerate((s0 * FACTOR, (s1 + tied * s0) * s_mid, s2 * FACTOR)):
                p_row[h, t] = softmax(jnp.where(cmask[...] > 0.5, s, NEGATIVE))

    def chances(h, r):
        if r == 0:
            return jnp.where(joined, p_row[h, 1], p_row[h, 0])
        return p_row[h, 2 if r == ROWS - 1 else 1]

    with scope("row_out"):
        for r in range(ROWS):
            v01, v2 = tile(qkv, r, 3), tile(qkv, r, 4)
            p = [chances(h, r).astype(BF16) for h in range(3)]
            o1f[r, :, :128] = jnp.where(lower, nn(p[0], v01), nn(p[1], v01)).astype(BF16)
            o1f[r, :, 128:] = nn(p[2], v2).astype(BF16)
    s_o = swap()
    s_o.go(lambda t: o1f.at[:, cols_of(t)], o1c.at[f])
    o1c[f] = o1f[:, own_cols]
    with scope("out1"):
        g_out.s1()
    su[1].send(1)
    with scope("e_f"):
        shr_e.forward()
    with scope("k3"):
        g_k.s3()
    sd[1].send(0)
    with scope("qv4"):
        g_qv.s4()
    with scope("su_n1"):
        su[1].send(2)
    sd[0].send(1)
    with scope("sd_m1"):
        sd[1].send(1)
    with scope("go4"):
        go.s4()
    with scope("out2"):
        g_out.s2()
    with scope("k4"):
        g_k.s4()
    with scope("su_y0"):
        su[0].send(2)
    with scope("o1"):
        s_o.wait()

    def o1_of(k):
        return o1c[k].reshape(TOK, 256)[:, :192]

    def w_out(h, k):
        return w_o[h, k // 2, k % 2].reshape(192, HALF)

    with scope("go5"):
        go.s5()
    with scope("out_row"):
        for h in range(2):
            cols = slice(h * HALF, (h + 1) * HALF)
            total = tok_all[:, own_cols, cols].reshape(TOK, HALF).astype(F32)
            for k in range(4):
                total = total + nn(o1_of(k), w_out(h, k))
            x1[:, cols] = total

    def in_pieces(step, rows=64, total=TOK):
        def body(k, _):
            step(pl.ds(pl.multiple_of(k * rows, rows), rows))
            return 0

        lax.fori_loop(0, total // rows, body, 0)

    with scope("norm_col"):

        def norm_col(at):
            h2[at] = (standard(x1[at])[0] * gains[1:2]).astype(BF16)

        in_pieces(norm_col)

    def w_col(part, k):
        half, off = ((0, k * HALF), (k, D), (1, k * HALF), (k, D + HALF))[part]
        return w_c.at[half, :, :, :, :, :, off : off + HALF]

    def project2(part):
        for k in range(2):
            at = slice(k * HALF, (k + 1) * HALF)
            one = nn(h2[...], w_col(part, k)[...].reshape(D, HALF))
            qkv2[part, :, :, at] = one.astype(BF16).reshape(ROWS, OWN, HALF)

    with scope("qv5"):
        g_qv.s5()
    with scope("qkv_col"):
        project2(0)
        project2(2)
        g_k.s5()
        project2(1)
    with scope("out3"):
        g_out.s3()
    with scope("sd_n0"):
        sd[0].send(2)
    with scope("sd_n1"):
        sd[1].send(2)
    part_cols = OWN // 2
    part_size = ROWS * part_cols
    lower2 = low_half((part_size, 128))
    zero2 = jnp.zeros((part_size, 128), BF16)

    def some(ref, m, at, *lead):
        return ref[(*lead, ALL, slice(m * part_cols, (m + 1) * part_cols), at)].reshape(part_size, 128)

    def put(ref, m, at, value, *lead):
        value = value.astype(BF16).reshape(ROWS, part_cols, 128)
        ref[(*lead, ALL, slice(m * part_cols, (m + 1) * part_cols), at)] = value

    def pairs(step):
        def body(k, _):
            step([(2 * k + n, m, pl.ds(pl.multiple_of((2 * k + n) * 128, 128), 128)) for n in range(2) for m in range(2)])
            return 0

        lax.fori_loop(0, HEADS // 4, body, 0)

    def one_head(e, value):
        return jnp.where(lower2, value, zero2) if e == 0 else jnp.where(lower2, zero2, value)

    with scope("col_fwd"):

        def col_pair(work):
            scores, chosen = [], []
            for _k, m, at in work:
                q, kk = some(qkv2, m, at, 0), some(qkv2, m, at, 1)
                scores.append([nt(one_head(e, q), kk) * FACTOR for e in range(2)])
            same = tmask[...] > 0.5
            for pair in scores:
                chosen.append([softmax(jnp.where(same, one, NEGATIVE)) for one in pair])
            out = []
            for (_k, m, at), pair in zip(work, chosen):
                v = some(qkv2, m, at, 2)
                out.append([nn(p.astype(BF16), v) for p in pair])
            for (k, m, at), pair, got in zip(work, chosen, out):
                put(o2, m, at, jnp.where(lower2, got[0], got[1]))
                for e in range(2):
                    p_col[2 * k + e, m] = pair[e]

        pairs(col_pair)
    with scope("out4"):
        g_out.s4()
    with scope("out_col"):
        g_out.s5()
        for k in range(2):
            at = slice(k * HALF, (k + 1) * HALF)
            x2[:, at] = x1[:, at] + nn(o2[...].reshape(TOK, D), w_col(3, k)[...].reshape(D, HALF))
    half_size = TOK // 2
    shr_h = [Share(me, lambda k, u=u: h3.at[k, u], sems) for u in range(2)]
    for u in range(2):
        with scope("norm_ffn%d" % u):

            def norm_ffn(k, _, u=u):
                at = pl.ds(pl.multiple_of(k * 64, 64), 64)
                src = pl.ds(pl.multiple_of(u * half_size + k * 64, 64), 64)
                h3[f, u, at] = (standard(x2[src])[0] * gains[2:3]).astype(BF16)
                return 0

            lax.fori_loop(0, half_size // 64, norm_ffn, 0)
        shr_h[u].send()
    for k in (go, g_qv, g_k, g_out):
        k.drain()
    with scope("su_f"):
        for k in su:
            k.finish()
    with scope("e"):
        shr_e.near()
        shr_e.finish()
    with scope("sd_f"):
        for k in sd:
            k.finish()

    def grads_of(b):
        return e_all[:, cols_of(b)].reshape(TOK, D)

    def ffn_block(pair, mine=None):
        grad = jnp.concatenate(
            [e_all[4 * u : 4 * u + 4, cols_of(b)].reshape(half_size, D) for b, u in pair], axis=0
        )
        tokens = jnp.concatenate([h3[b, u] for b, u in pair], axis=0)
        y_sum, d_sum = None, None
        for k in range(2):
            at = slice(k * HALF, (k + 1) * HALF)
            up = w_u[:, :, :, :, at].reshape(D, HALF)
            down = w_d[k].reshape(HALF, D)
            u_k = nn(tokens, up)
            bell = jnp.exp(-0.5 * u_k * u_k) * (1 / (2 * jnp.pi) ** 0.5)
            upper = 0.5 + 0.5 * lax.erf(u_k * 0.5**0.5)
            a = (u_k * upper).astype(BF16)
            d = (nt(grad, down) * (upper + u_k * bell)).astype(BF16)
            for n, (b, u) in enumerate(pair):
                act[b, u, :, at] = a[n * half_size : (n + 1) * half_size]
                du[b, u, :, at] = d[n * half_size : (n + 1) * half_size]
            y, dd = nn(a, down), nt(d, up)
            y_sum = y if y_sum is None else y_sum + y
            d_sum = dd if d_sum is None else d_sum + dd
        if mine is not None:
            y_sum = y_sum + x2[...] * mine
        y_sum = y_sum.astype(BF16).reshape(4, 2 * OWN, D)
        d_sum = d_sum.astype(BF16).reshape(4, 2 * OWN, D)
        for n, (b, u) in enumerate(pair):
            yp[b, 2 * u : 2 * u + 2] = y_sum[2 * n : 2 * n + 2]
            dp[b, 2 * u : 2 * u + 2] = d_sum[2 * n : 2 * n + 2]

    cy = Collect(me, lambda k: yp.at[:, k], l_y, sems)
    cd = [
        Collect(me, lambda k, u=u: dp.at[k, pl.ds(2 * u, 2)], l_p.at[:, pl.ds(2 * u, 2)], sems, 2) for u in range(2)
    ]
    with scope("h3_near"):
        shr_h[0].near()
        shr_h[1].near()
    with scope("ffn1"):

        def near_two(k, _):
            b = jnp.where(k == 0, f, sib_f)
            ffn_block(((b, 0), (b, 1)), (k == 0).astype(F32))
            return 0

        lax.fori_loop(0, 2, near_two, 0)
    cd[0].near()
    cd[1].near()
    with scope("h3_far0"):
        shr_h[0].forward()
    with scope("h3_diag0"):
        shr_h[0].finish()
    with scope("ffn2"):
        ffn_block(((x_f, 0), (diag_f, 0)))
    cd[0].pair()
    with scope("h3_far1"):
        shr_h[1].forward()
    with scope("dh3_0"):
        cd[0].cross()
    with scope("h3_diag1"):
        shr_h[1].finish()
    with scope("ffn3"):
        ffn_block(((x_f, 1), (diag_f, 1)))
    cd[1].pair()
    cy.near()
    cy.pair()
    with scope("dh3_1"):
        cd[1].cross()
    for k in range(2):
        at = slice(k * HALF, (k + 1) * HALF)
        with scope("g_down%d" % k):
            part = sum(tn(act[b].reshape(TOK, D), grads_of(b)[:, at]) for b in range(4))
            w_d[:, :, :, :, at] = part.astype(BF16).reshape(2, 2, 2, 96, HALF)
        sd[k].back(0)
    for k in range(2):
        at = slice(k * HALF, (k + 1) * HALF)
        with scope("g_up%d" % k):
            part = sum(tn(h3[b].reshape(TOK, D), du[b, :, :, at].reshape(TOK, HALF)) for b in range(4))
            w_u[:, :, :, :, at] = part.astype(BF16).reshape(2, 2, 2, 96, HALF)
        su[k].back(0)

    for u in range(2):
        with scope("cd_w%d" % u):
            cd[u].finish()
        with scope("back_ffn%d" % u):

            def back_ffn(k, _, u=u):
                row = 4 * u + k
                at = pl.ds(pl.multiple_of(row * OWN, OWN), OWN)
                grad = cd[u].total(k // 2, pl.ds(pl.multiple_of(k % 2 * OWN, OWN), OWN))
                g[at] = e_all[row, own_cols].astype(F32) + norm_back(x2[at], gains[2:3], grad)
                e1[at] = g[at].astype(BF16)
                return 0

            lax.fori_loop(0, 4, back_ffn, 0)
    with scope("mix"):
        cy.cross()
    with scope("do2"):
        total = sum(nt(e1[:, k * HALF : (k + 1) * HALF], w_col(3, k)[...].reshape(D, HALF)) for k in range(2))
        do2[...] = total.astype(BF16).reshape(ROWS, OWN, D)
        for k in range(2):
            part = tn(o2[...].reshape(TOK, D), e1[:, k * HALF : (k + 1) * HALF])
            w_col(3, k)[...] = part.astype(BF16).reshape(2, 2, 2, 2, 48, HALF)
    r_out.r0()
    with scope("sd_b0"):
        sd[0].back(1)
    with scope("col_bwd"):

        def col_back(work):
            grads, back, out = [], [], []
            for _k, m, at in work:
                d, v = some(do2, m, at), some(qkv2, m, at, 2)
                grads.append([nt(one_head(e, d), v) for e in range(2)])
            for (k, m, at), pair in zip(work, grads):
                for e in range(2):
                    p, dq = p_col[2 * k + e, m], pair[e]
                    ds = p * (dq - jnp.sum(dq * p, axis=-1, keepdims=True))
                    back.append((ds.astype(BF16), ds.T.astype(BF16), p.T.astype(BF16)))
            for n, (_k, m, at) in enumerate(work):
                q, kk, d = some(qkv2, m, at, 0), some(qkv2, m, at, 1), some(do2, m, at)
                got = [
                    (nn(ds, kk) * FACTOR, nn(dst, q) * FACTOR, nn(pt, d)) for ds, dst, pt in back[2 * n : 2 * n + 2]
                ]
                out.append([jnp.where(lower2, got[0][i], got[1][i]) for i in range(3)])
            for (_k, m, at), got in zip(work, out):
                for n in range(3):
                    put(dqkv2, m, at, got[n], n)

        pairs(col_back)
    with scope("dh2"):
        total = None
        for part in range(3):
            for k in range(2):
                one = nt(dqkv2[part, :, :, k * HALF : (k + 1) * HALF].reshape(TOK, HALF), w_col(part, k)[...].reshape(D, HALF))
                total = one if total is None else total + one
        dh2[...] = total

    def grad_col(part):
        for k in range(2):
            one = tn(h2[...], dqkv2[part, :, :, k * HALF : (k + 1) * HALF].reshape(TOK, HALF))
            w_col(part, k)[...] = one.astype(BF16).reshape(2, 2, 2, 2, 48, HALF)

    with scope("back_col"):

        def back_col(at):
            g[at] = g[at] + norm_back(x1[at], gains[1:2], dh2[at])
            e1[at] = g[at].astype(BF16)

        in_pieces(back_col)

    with scope("do1"):
        for k in range(4):
            d = nt(e1[:, :HALF], w_out(0, k)) + nt(e1[:, HALF:], w_out(1, k))
            d = jnp.concatenate([d, jnp.zeros((TOK, 64), F32)], axis=1)
            dost[k] = d.astype(BF16).reshape(ROWS, OWN, 256)
    s_d = swap()
    s_d.go(lambda t: dost.at[t], do1.at[:, own_cols])
    do1[:, own_cols] = dost[f]
    s_g = swap()
    s_g.go(lambda t: e1.at[pl.ds(pl.multiple_of(2 * OWN * t, 2 * OWN), 2 * OWN)], e1r.at[f])
    e1r[f] = e1[pl.ds(pl.multiple_of(2 * OWN * f, 2 * OWN), 2 * OWN)]
    with scope("su_b0"):
        su[0].back(1)
    with scope("out_r1"):
        r_out.r1()
    with scope("sd_b1"):
        sd[1].back(1)
    with scope("g_qv"):
        grad_col(0)
        grad_col(2)
    r_qv.r0()
    with scope("su_b1"):
        su[1].back(1)
    with scope("sd_c0"):
        sd[0].back(2)
    with scope("g_k"):
        grad_col(1)
    r_k.r0()
    with scope("g_out_row"):
        for h in range(2):
            for k in range(4):
                part = tn(o1_of(k), e1[:, h * HALF : (h + 1) * HALF])
                w_o[h, k // 2, k % 2] = part.astype(BF16).reshape(2, 2, 48, HALF)
    ro.r0()
    with scope("qv_r1"):
        r_qv.r1()
    with scope("k_r1"):
        r_k.r1()
    with scope("ro1"):
        ro.r1()
    with scope("su_c0"):
        su[0].back(2)
    with scope("do1w"):
        s_d.wait()
    with scope("row_bwd"):
        d_sum = [[None] * 3 for _ in range(3)]
        for r in range(ROWS):
            d01, d2, v01, v2 = tile(do1, r, 0), tile(do1, r, 1), tile(qkv, r, 3), tile(qkv, r, 4)
            ops = ((jnp.where(lower, d01, zero), v01), (jnp.where(lower, zero, d01), v01), (d2, v2))
            for h, (a, b) in enumerate(ops):
                s = nt(a, b)
                t = 0 if r == 0 else 2 if r == ROWS - 1 else 1
                d_sum[h][t] = s if d_sum[h][t] is None else d_sum[h][t] + s
        da, dat, pt = [], [], []
        for h in range(3):
            s0, s1, s2 = d_sum[h]
            by = []
            for t, s in enumerate((s0, s1 + tied * s0, s2)):
                p = p_row[h, t]
                by.append(p * (s - jnp.sum(s * p, axis=-1, keepdims=True)))
            da.append((jnp.where(joined, by[1], by[0]), by[1], by[2]))
            dat.append([a.T.astype(BF16) for a in da[h]])
            pt.append([chances(h, r).T.astype(BF16) for r in (0, 1, ROWS - 1)])
            da[h] = [a.astype(BF16) for a in da[h]]
        s_first = jnp.where(joined, s_mid, FACTOR)
        for r in range(ROWS):
            t = 0 if r == 0 else 2 if r == ROWS - 1 else 1
            scale = (s_first, s_mid, FACTOR)[t]
            q01, q2k2, k01 = tile(qkv, r, 0), tile(qkv, r, 1), tile(qkv, r, 2)
            d01, d2 = tile(do1, r, 0), tile(do1, r, 1)
            dq = jnp.where(lower, nn(da[0][t], k01), nn(da[1][t], k01)) * scale
            dk = jnp.where(lower, nn(dat[0][t], q01), nn(dat[1][t], q01)) * scale
            mid = jnp.where(lower, nn(dat[2][t], q2k2), nn(da[2][t], q2k2)) * scale
            dv = jnp.where(lower, nn(pt[0][t], d01), nn(pt[1][t], d01))
            for n, val in enumerate((dq, pltpu.roll(mid, 64, 1), dk, dv, nn(pt[2][t], d2))):
                dqkv[r, :, n * 128 : (n + 1) * 128] = val.astype(BF16)
    with scope("dh1"):
        wide = w_q[...].reshape(D, WIDE)

        def partial_dh(k, _):
            pair = dqkv[pl.ds(2 * k, 2)].reshape(2 * COLS, WIDE)
            dp[k] = nt(pair, wide).astype(BF16).reshape(4, 2 * OWN, D)
            return 0

        lax.fori_loop(0, 4, partial_dh, 0)
    ch = Collect(me, lambda k: dp.at[k], l_p, sems)
    ch.pair()
    ch.near()
    for k in range(2):
        at = slice(0, 384) if k == 0 else slice(384, WIDE)
        with scope("g_qkv%d" % k):
            total = tn(h1[...].reshape(ROWS * COLS, D), dqkv[:, :, at].reshape(ROWS * COLS, -1))
            w_q[:, :, :, :, at] = total.astype(BF16).reshape(2, 2, 2, 96, -1)
        sq[k].back(0)
    with scope("out_r2"):
        r_out.r2()
    with scope("sd_c1"):
        sd[1].back(2)
    with scope("su_c1"):
        su[1].back(2)
    with scope("qv_r2"):
        r_qv.r2()
    with scope("k_r2"):
        r_k.r2()
    with scope("q_b1"):
        sq[1].back(1)
    with scope("q_b0"):
        sq[0].back(1)
    with scope("ro2"):
        ro.r2()
    with scope("out_r3"):
        r_out.r3()
    with scope("qv_r3"):
        r_qv.r3()
    with scope("dh1_x"):
        ch.cross()
    with scope("k_r3"):
        r_k.r3()
    with scope("q_c1"):
        sq[1].back(2)
    with scope("q_c0"):
        sq[0].back(2)
    with scope("ro3"):
        ro.r3()
    with scope("out_r3b"):
        r_out.r3b()
    with scope("qv_r3b"):
        r_qv.r3b()
    with scope("ro3b"):
        ro.r3b()
    with scope("k_r3b"):
        r_k.r3b()
    with scope("d_sum"):
        for k in sd:
            d_d[:, k.at] = k.back_sum()
    with scope("u_sum"):
        for k in su:
            t_u[:, :, k.at] = k.back_sum().astype(BF16).reshape(4, -1, HALF)
    s_v = swap()
    s_v.go(lambda t: t_u.at[t], o_u.at[f])
    o_u[f] = t_u[f]
    with scope("mixed"):
        cy.finish()
        for r in range(2):
            for k in range(4):
                mixed[r, k * OWN : (k + 1) * OWN] = cy.total(k, slice(r * OWN, (r + 1) * OWN)).astype(BF16)
    with scope("in_grad"):
        ch.finish()
        s_g.wait()
        for r in range(2):
            for k in range(4):
                at = slice(k * OWN, (k + 1) * OWN)
                grad = ch.total(2 * r + k // 2, slice(k % 2 * OWN, (k % 2 + 1) * OWN))
                back = norm_back(tok[r, at].astype(F32), gains[0:1], grad)
                igrad[r, at] = e1r[k, r * OWN : (r + 1) * OWN].astype(F32) + back
    with scope("out_r4"):
        r_out.r4()
    with scope("qv_r4"):
        r_qv.r4()
    with scope("k_r4"):
        r_k.r4()
    with scope("q_sum"):
        s_t = []
        for k in reversed(sq):
            t_q[:, :, k.at] = k.back_sum().astype(BF16).reshape(4, -1, k.at.size)
            o_q[f, :, k.at] = t_q[f, :, k.at]
            s_t.append(swap())
            s_t[-1].go(lambda t, at=k.at: t_q.at[t, :, at], o_q.at[f, :, k.at])
    with scope("ro4"):
        ro.r4()
    with scope("last"):
        for k in (r_out, r_qv, r_k, ro):
            k.r5()
        s_v.wait()
        for k in s_t:
            k.wait()
    assert used[0] <= SEMS, used[0]


SEMS = 160


def finish_kernel(
    mixed, igrad, o_q, e_o, e_c, e_co, o_u, e_d, gain_row, r_q, gain_col, r_c, gain_ffn, r_u,
    mixed_out, igrad_out, dg_row, d_q, d_o, dg_col, d_c, d_co, dg_ffn, d_u, d_d,
):
    for a, b in ((mixed, mixed_out), (igrad, igrad_out), (e_o, d_o), (e_c, d_c), (e_co, d_co), (e_d, d_d)):
        b[...] = a[...]
    for n in range(8):
        parts = [o_u[t, :, n // 4 * 384 : (n // 4 + 1) * 384].astype(F32) for t in range(4)]
        d_u[:, n * 384 : (n + 1) * 384] = spread(parts, [t - n % 4 for t in range(4)])
    where = {}
    for t in range(4):
        for n, pair in enumerate(head_order(t)):
            for k, piece in enumerate(pair):
                where[piece] = (o_q.at[t], 2 * n + k)
    for n in range(3 * D // 128):
        d_q[:, n * 128 : (n + 1) * 128] = by_halves([where[2 * n], where[2 * n + 1]])

    for out, weight, grad, gain in (
        (dg_row, r_q, d_q, gain_row), (dg_col, r_c, d_c, gain_col), (dg_ffn, r_u, d_u, gain_ffn)
    ):
        total = jnp.sum(weight[...].astype(F32) * grad[...], axis=1, keepdims=True)
        out[...] = level(total / upright(gain[...].astype(F32)))


def run_layer(tok, cot, seq, cid, *weights):
    sds = jax.ShapeDtypeStruct
    rows = weights[1].shape[0]
    i_d = weights[-1]
    first = [sds(tok.shape, BF16), sds(tok.shape, F32)]
    wide_q, wide_u = sds((4, rows, WIDE), BF16), sds((4, rows, D), BF16)
    plain = [sds(w.shape, F32) for w in weights]
    shapes = first + [wide_q, plain[2], plain[4], plain[5], wide_u, plain[8]]

    def vmem(*shape, dtype=BF16):
        return pltpu.VMEM(shape, dtype)

    def lands(r, c):
        return [
            vmem(2, 2, 2, 2, r, c), vmem(2, 2, 2, r, c), vmem(2, 2, r, c), vmem(3, r, c), vmem(2, r // 2, c, dtype=F32)
        ]

    def slices(c):
        return [vmem(2, 2, 4 * rows, c), vmem(3, 4 * rows, c)]

    r2 = 2 * rows
    wo, wc, wu = HALF, 2 * D, D
    scratch = [
        vmem(4, rows, WIDE),
        vmem(4, rows, wu),
        vmem(2, 2, 2, 4 * rows, WIDE),
        vmem(2, 2, 2, 2, 2, r2, wo),
        vmem(2, 2, 2, 2, 2, r2, wc),
        vmem(2, 2, 2, 4 * rows, wu),
        vmem(2, 2, 2, *i_d.shape),
        vmem(4, rows, WIDE),
        vmem(rows, wo),
        vmem(rows, wc),
        vmem(4, rows, wu),
        *lands(r2, wo),
        *lands(r2, wc),
        *slices(WIDE),
        vmem(4, rows, WIDE),
        *slices(wu),
        vmem(4, rows, wu),
        *slices(D),
        vmem(ROWS, COLS, D),
        vmem(ROWS, COLS, D),
        vmem(ROWS, COLS, D),
        vmem(ROWS, COLS, WIDE),
        vmem(3, 3, COLS, COLS, dtype=F32),
        vmem(ROWS, COLS, 256),
        vmem(4, ROWS, OWN, 256),
        vmem(TOK, D, dtype=F32),
        vmem(TOK, D),
        vmem(3, ROWS, OWN, D),
        vmem(HEADS, 2, TOK // 2, TOK // 2, dtype=F32),
        vmem(ROWS, OWN, D),
        vmem(TOK, D, dtype=F32),
        vmem(4, 2, TOK // 2, D),
        vmem(4, 2, TOK // 2, D),
        vmem(4, 2, TOK // 2, D),
        vmem(4, 4, 2 * OWN, D),
        vmem(3, 4, 2 * OWN, D),
        vmem(4, 4, 2 * OWN, D),
        vmem(3, 4, 2 * OWN, D),
        vmem(TOK, D, dtype=F32),
        vmem(ROWS, OWN, D),
        vmem(3, ROWS, OWN, D),
        vmem(TOK, D, dtype=F32),
        vmem(TOK, D),
        vmem(4, ROWS, OWN, 256),
        vmem(ROWS, COLS, 256),
        vmem(ROWS, COLS, WIDE),
        vmem(4, 2 * OWN, D),
        vmem(8, D, dtype=F32),
        vmem(COLS, COLS, dtype=F32),
        vmem(TOK // 2, TOK // 2, dtype=F32),
        pltpu.SemaphoreType.DMA((SEMS,)),
        pltpu.SemaphoreType.DMA((SEMS,)),
    ]
    vm = pl.BlockSpec(memory_space=pltpu.VMEM)
    outs = pl.pallas_call(
        layer_kernel,
        out_shape=shapes,
        in_specs=[vm, vm, pl.BlockSpec(memory_space=pltpu.SMEM)] + [vm] * 10,
        out_specs=[vm] * 8,
        scratch_shapes=scratch,
        name="layer",
        compiler_params=pltpu.CompilerParams(
            collective_id=0, has_side_effects=True, vmem_limit_bytes=VMEM_LIMIT
        ),
    )(tok, cot, seq, cid, *weights)
    return pl.pallas_call(
        finish_kernel,
        out_shape=first + plain,
        in_specs=[vm] * 14,
        out_specs=[vm] * 11,
        name="finish",
        compiler_params=pltpu.CompilerParams(vmem_limit_bytes=VMEM_LIMIT),
    )(*outs, weights[0], weights[1], weights[3], weights[4], weights[6], weights[7])


VMEM_LIMIT = 63 * 2**20


def on_device(
    tokens, cotangent, seq_ids, col_ids,
    gain_row, qkv_row, out_row, gain_col, qkv_col, out_col, gain_ffn, up_ffn, down_ffn,
    cells,
):
    members = CELL * lax.axis_size("fsdp")
    low_index = (lax.axis_index("dp") % CELL) * lax.axis_size("fsdp") + lax.axis_index("fsdp")

    def in_cell(shard):
        if cells == 1:
            return shard
        whole = lax.all_gather(shard, AXES, axis=0, tiled=True)
        rows = whole.shape[0] // members
        return lax.dynamic_slice_in_dim(whole, low_index * rows, rows, 0)

    def from_cell(summed):
        if cells == 1:
            return summed
        rows = summed.shape[0]
        whole = jnp.zeros((rows * members,) + summed.shape[1:], summed.dtype)
        whole = lax.dynamic_update_slice_in_dim(whole, summed, low_index * rows, 0)
        return lax.psum_scatter(whole, AXES, scatter_dimension=0, tiled=True)

    weights = [
        in_cell(w).reshape(1, -1) if w.ndim == 1 else in_cell(w)
        for w in (gain_row, qkv_row, out_row, gain_col, qkv_col, out_col, gain_ffn, up_ffn, down_ffn)
    ]
    mixed, igrad, *grads = run_layer(tokens[0], cotangent[0], seq_ids, col_ids, *weights)
    grads = [from_cell(v.reshape(-1) if v.shape[0] == 1 else v) for v in grads]
    return (mixed[None], igrad[None], *grads)


def solution(mesh):
    rows = P(AXES, None)
    vector = P(AXES)
    grid = P("dp", "fsdp", None, None)
    ids = P("dp", None)
    return jax.shard_map(
        partial(on_device, cells=mesh.shape["dp"] // CELL),
        mesh=mesh,
        in_specs=(grid, grid, ids, ids) + (vector, rows, rows) * 3,
        out_specs=(grid, grid) + (vector, rows, rows) * 3,
        check_vma=False,
    )
```

```python
from functools import partial

import jax
import jax.numpy as jnp
from jax import lax
from jax.experimental import pallas as pl
from jax.experimental.pallas import tpu as pltpu
from jax.sharding import PartitionSpec as P

HEADS = 12
EPSILON = 1e-05
NEGATIVE = -1000000000.0
MESH = pl.DeviceIdType.MESH
BF16 = jnp.bfloat16
F32 = jnp.float32
CELL = 8
AXES = ("dp", "fsdp")


class Place:
    def __init__(self):
        dp = lax.axis_index("dp")
        self.f = lax.axis_index("fsdp")
        self.base = dp // CELL * CELL
        low = dp - self.base
        self.z, self.y = low // 2, low % 2
        self.hi, self.lo = self.z // 2, self.z % 2
        self.x, self.c = self.f // 2, self.f % 2

    def dev(self, z, y, x, c):
        return (self.base + z * 2 + y, x * 2 + c)

    def sib(self):
        return self.dev(self.z, self.y, self.x, 1 - self.c)

    def xn(self):
        return self.dev(self.z, self.y, 1 - self.x, self.c)

    def yn(self):
        return self.dev(self.z, 1 - self.y, self.x, self.c)

    def first(self):
        return self.dev(self.z, self.y + self.c * (1 - 2 * self.y), self.x + (1 - self.c) * (1 - 2 * self.x), self.c)

    def second(self):
        return self.dev(self.z, self.y + (1 - self.c) * (1 - 2 * self.y), self.x + self.c * (1 - 2 * self.x), self.c)

    def z1(self):
        return self.dev(2 * self.hi + 1 - self.lo, self.y, self.x, self.c)

    def z2(self):
        return self.dev(2 * (1 - self.hi) + self.lo, self.y, self.x, self.c)


def greet(partners):
    bar = pltpu.get_barrier_semaphore()
    for t in partners:
        pl.semaphore_signal(bar, inc=1, device_id=t, device_id_type=MESH)
    pl.semaphore_wait(bar, len(partners))


def rcopy(src, dst, ss, rs, to):
    return pltpu.make_async_remote_copy(
        src_ref=src, dst_ref=dst, send_sem=ss, recv_sem=rs, device_id=to, device_id_type=MESH
    )


ALL = slice(None)


class Part:
    def __init__(self, me, w, at):
        self.me, self.w, self.at = me, w, at

    def block(self, hi, lo, y, x, half=None):
        return self.w.at[self.me.c if half is None else half, hi, lo, y, x, :, self.at]


class Gather(Part):
    def __init__(self, me, src_of, land, w, at, sems):
        super().__init__(me, w, at)
        self.src_of, self.land, self.sems = src_of, land, sems

    def swap(self):
        me = self.me
        self.c0 = rcopy(self.src_of(1 - me.c), self.land.at[:, self.at], *self.sems(), me.sib())
        self.c0.start()

    def start(self, ref, to):
        c = rcopy(ref, ref, *self.sems(), to)
        c.start()
        self.sent.append(c)
        return c

    def own(self):
        me = self.me
        self.c0.wait()
        mine = self.src_of(me.c)[...].astype(F32)
        other = self.land[:, self.at].astype(F32)
        flag = (me.c == 0).astype(F32)
        top = flag * mine + (1 - flag) * other
        low = flag * other + (1 - flag) * mine
        own = self.block(me.hi, me.lo, me.y, me.x)
        own[...] = jnp.concatenate([top, low], axis=0).astype(BF16)
        self.sent = []

    def s0(self):
        me = self.me
        self.own()
        self.a = self.start(self.block(me.hi, me.lo, me.y, me.x), me.z2())

    def s1(self):
        me = self.me
        self.a.wait_recv()
        self.b = self.start(self.block(ALL, me.lo, me.y, me.x), me.z1())

    def s2(self):
        me = self.me
        self.b.wait_recv()
        col = self.block(ALL, ALL, me.y, me.x)
        self.e = self.start(col, me.first())
        self.to_sib = [self.start(col, me.sib())]

    def fork(self, ref0, ref1, to, like):
        me, m = self.me, self.sems()

        @pl.when(me.c == 0)
        def _():
            rcopy(ref0, ref0, *m, to).start()

        @pl.when(me.c == 1)
        def _():
            rcopy(ref1, ref1, *m, to).start()

        c = rcopy(like, like, *m, to)
        self.sent.append(c)
        return c

    def s3(self):
        me = self.me
        self.e.wait_recv()
        two, col = self.block(ALL, ALL, me.y, ALL), self.block(ALL, ALL, me.y, me.x)
        self.g = self.fork(
            self.block(ALL, ALL, me.y, ALL, 0), self.block(ALL, ALL, ALL, me.x, 1), me.second(), two
        )
        self.to_sib.append(
            self.fork(
                self.block(ALL, ALL, me.y, 1 - me.x, 0), self.block(ALL, ALL, 1 - me.y, me.x, 1), me.sib(), col
            )
        )

    def s4(self):
        me = self.me
        self.g.wait_recv()
        two = self.block(ALL, ALL, me.y, ALL)
        self.to_sib.append(
            self.fork(
                self.block(ALL, ALL, 1 - me.y, ALL, 0), self.block(ALL, ALL, ALL, 1 - me.x, 1), me.sib(), two
            )
        )

    def s5(self):
        for c in self.to_sib:
            c.wait_recv()

    def drain(self):
        for c in self.sent:
            c.wait_send()


class Reduce(Part):
    def __init__(self, me, w, at, lands, out_of, sems):
        super().__init__(me, w, at)
        self.l0, self.l1, self.l2, self.l3, self.l4 = lands
        self.out_of, self.sems = out_of, sems

    def add(self, n, mine_of, land_of):
        def body(k, _):
            mine = mine_of(k)
            mine[...] = (mine[...].astype(F32) + land_of(k)[...].astype(F32)).astype(BF16)
            return 0

        lax.fori_loop(0, n, body, 0)

    def r0(self):
        me = self.me
        self.c0 = rcopy(
            self.block(ALL, ALL, ALL, ALL, 1 - me.c), self.l0.at[:, :, :, :, :, self.at], *self.sems(), me.sib()
        )
        self.c0.start()

    def r1(self):
        me = self.me
        self.c0.wait()
        self.add(
            16,
            lambda k: self.block(k // 8, k // 4 % 2, k // 2 % 2, k % 2),
            lambda k: self.l0.at[k // 8, k // 4 % 2, k // 2 % 2, k % 2, :, self.at],
        )
        land, m = self.l1.at[:, :, :, :, self.at], self.sems()

        @pl.when(me.c == 0)
        def _():
            rcopy(self.block(ALL, ALL, 1 - me.y, ALL, 0), land, *m, me.second()).start()

        @pl.when(me.c == 1)
        def _():
            rcopy(self.block(ALL, ALL, ALL, 1 - me.x, 1), land, *m, me.second()).start()

        self.c1 = rcopy(land, land, *m, me.sib())

    def r2(self):
        me = self.me
        self.c1.wait()

        def mine(k):
            m = k % 2
            y, x = me.y + me.c * (m - me.y), me.x + (1 - me.c) * (m - me.x)
            return self.block(k // 4, k // 2 % 2, y, x)

        self.add(8, mine, lambda k: self.l1.at[k // 4, k // 2 % 2, k % 2, :, self.at])
        oy = me.y + me.c * (1 - 2 * me.y)
        ox = me.x + (1 - me.c) * (1 - 2 * me.x)
        self.c2 = rcopy(self.block(ALL, ALL, oy, ox), self.l2.at[:, :, :, self.at], *self.sems(), me.first())
        self.c2.start()

    def r3(self):
        me = self.me
        self.c2.wait()
        self.add(
            4, lambda k: self.block(k // 2, k % 2, me.y, me.x), lambda k: self.l2.at[k // 2, k % 2, :, self.at]
        )
        self.c3 = rcopy(
            self.block(ALL, 1 - me.lo, me.y, me.x), self.l3.at[pl.ds(0, 2), :, self.at], *self.sems(), me.z1()
        )
        self.c3.start()

    def r3b(self):
        me = self.me
        self.c3.wait()
        self.add(2, lambda k: self.block(k, me.lo, me.y, me.x), lambda k: self.l3.at[k, :, self.at])
        self.c3 = rcopy(
            self.block(1 - me.hi, me.lo, me.y, me.x), self.l3.at[2, :, self.at], *self.sems(), me.z2()
        )
        self.c3.start()

    def r4(self):
        me = self.me
        self.c3.wait()
        total = self.block(me.hi, me.lo, me.y, me.x)[...].astype(F32) + self.l3[2, :, self.at].astype(F32)
        half = total.shape[0] // 2
        flag = (me.c == 0).astype(F32)
        top, low = total[:half], total[half:]
        self.out_of(me.c)[...] = flag * top + (1 - flag) * low
        self.l4[0, :, self.at] = flag * low + (1 - flag) * top
        self.c4 = rcopy(self.l4.at[0, :, self.at], self.l4.at[1, :, self.at], *self.sems(), me.sib())
        self.c4.start()

    def r5(self):
        self.c4.wait()
        self.out_of(1 - self.me.c)[...] = self.l4[1, :, self.at]


class LastOverX(Gather):
    def s2(self):
        me = self.me
        self.b.wait_recv()
        col = self.block(ALL, ALL, me.y, me.x)
        self.e = self.start(col, me.yn())
        self.to_sib = [self.start(col, me.sib())]

    def s3(self):
        me = self.me
        self.e.wait_recv()
        self.g = self.start(self.block(ALL, ALL, ALL, me.x), me.xn())
        self.to_sib.append(self.start(self.block(ALL, ALL, 1 - me.y, me.x), me.sib()))

    def s4(self):
        me = self.me
        self.g.wait_recv()
        self.to_sib.append(self.start(self.block(ALL, ALL, ALL, 1 - me.x), me.sib()))


class EarlyReduce(Reduce):
    def go(self, src, land, to):
        self.c = rcopy(src, land, *self.sems(), to)
        self.c.start()

    def r1(self):
        me = self.me
        self.c0.wait()
        self.add(
            16,
            lambda k: self.block(k // 8, k // 4 % 2, k // 2 % 2, k % 2),
            lambda k: self.l0.at[k // 8, k // 4 % 2, k // 2 % 2, k % 2, :, self.at],
        )
        self.go(self.block(ALL, 1 - me.lo, ALL, ALL), self.l1.at[:, :, :, :, self.at], me.z1())

    def r2(self):
        me = self.me
        self.c.wait()
        self.add(
            8,
            lambda k: self.block(k // 4, me.lo, k // 2 % 2, k % 2),
            lambda k: self.l1.at[k // 4, k // 2 % 2, k % 2, :, self.at],
        )
        self.go(self.block(1 - me.hi, me.lo, ALL, ALL), self.l2.at[:, :, :, self.at], me.z2())

    def r3(self):
        me = self.me
        self.c.wait()
        self.add(
            4,
            lambda k: self.block(me.hi, me.lo, k // 2, k % 2),
            lambda k: self.l2.at[k // 2, k % 2, :, self.at],
        )
        self.go(self.block(me.hi, me.lo, ALL, 1 - me.x), self.l3.at[pl.ds(0, 2), :, self.at], me.xn())

    def r3b(self):
        me = self.me
        self.c.wait()
        self.add(2, lambda k: self.block(me.hi, me.lo, k, me.x), lambda k: self.l3.at[k, :, self.at])
        self.go(self.block(me.hi, me.lo, 1 - me.y, me.x), self.l3.at[2, :, self.at], me.yn())
        self.c3 = self.c


class Swap:
    def __init__(self, me, ssem, rsem):
        self.me, self.ss, self.rs, self.sent = me, ssem, rsem, []

    def other(self, d):
        return (self.me.f + d) % 4

    def go(self, src_of, dst):
        me = self.me
        for d in (1, 2, 3):
            t = self.other(d)
            c = rcopy(src_of(t), dst, self.ss.at[d - 1], self.rs.at[d - 1], me.dev(me.z, me.y, t // 2, t % 2))
            c.start()
            self.sent.append(c)

    def wait(self):
        for c in self.sent:
            c.wait_send()
            c.wait_recv()


class Slices:
    def __init__(self, me, w, at, l1, l2, sems, early=False):
        self.me, self.w, self.at, self.l1, self.l2, self.sems, self.early = me, w, at, l1, l2, sems, early
        self.sent = []

    def part(self, hi, lo, y):
        return self.w.at[hi, lo, y, :, self.at]

    def steps(self):
        me = self.me
        if self.early:
            return (
                (self.part(me.hi, me.lo, me.y), me.yn()),
                (self.part(me.hi, me.lo, ALL), me.z2()),
                (self.part(ALL, me.lo, ALL), me.z1()),
            )
        return (
            (self.part(me.hi, me.lo, me.y), me.z2()),
            (self.part(ALL, me.lo, me.y), me.z1()),
            (self.part(ALL, ALL, me.y), me.yn()),
        )

    def send(self, n):
        if n:
            self.sent[-1].wait_recv()
        ref, to = self.steps()[n]
        c = rcopy(ref, ref, *self.sems(), to)
        c.start()
        self.sent.append(c)

    def finish(self):
        self.sent[-1].wait_recv()
        for c in self.sent:
            c.wait_send()

    def kept(self, n):
        me = self.me
        if self.early:
            return (
                (4, lambda k: self.part(k // 2, me.lo, k % 2)),
                (2, lambda k: self.part(me.hi, me.lo, k)),
            )[n]
        return (
            (4, lambda k: self.part(k // 2, k % 2, me.y)),
            (2, lambda k: self.part(k, me.lo, me.y)),
        )[n]

    def back(self, n):
        me = self.me
        if n:
            self.c.wait()
            count, mine_of = self.kept(n - 1)

            def body(k, _):
                mine = mine_of(k)
                land = self.l1[k // 2, k % 2, :, self.at] if n == 1 else self.l2[k, :, self.at]
                mine[...] = (mine[...].astype(F32) + land.astype(F32)).astype(BF16)
                return 0

            lax.fori_loop(0, count, body, 0)
        lands = (self.l1.at[:, :, :, self.at], self.l2.at[pl.ds(0, 2), :, self.at], self.l2.at[2, :, self.at])
        if self.early:
            src, to = (
                (self.part(ALL, 1 - me.lo, ALL), me.z1()),
                (self.part(1 - me.hi, me.lo, ALL), me.z2()),
                (self.part(me.hi, me.lo, 1 - me.y), me.yn()),
            )[n]
        else:
            src, to = (
                (self.part(ALL, ALL, 1 - me.y), me.yn()),
                (self.part(ALL, 1 - me.lo, me.y), me.z1()),
                (self.part(1 - me.hi, me.lo, me.y), me.z2()),
            )[n]
        self.c = rcopy(src, lands[n], *self.sems(), to)
        self.c.start()

    def back_sum(self):
        me = self.me
        self.c.wait()
        return self.part(me.hi, me.lo, me.y)[...].astype(F32) + self.l2[2, :, self.at].astype(F32)


class Share:
    def __init__(self, me, whole, sems):
        self.me, self.sems = me, sems
        self.whole = whole

    def send(self):
        me = self.me
        own = self.whole(me.f)
        self.s = rcopy(own, own, *self.sems(), me.sib())
        self.x = rcopy(own, own, *self.sems(), me.xn())
        self.s.start()
        self.x.start()

    def near(self):
        self.s.wait()

    def forward(self):
        me = self.me
        self.x.wait_recv()
        got = self.whole(2 * (1 - me.x) + me.c)
        self.t = rcopy(got, got, *self.sems(), me.sib())
        self.t.start()

    def finish(self):
        self.x.wait_send()
        self.t.wait()


class Collect:
    def __init__(self, me, part_of, lands, sems, pieces=4):
        self.me, self.part_of, self.lands, self.sems, self.pieces = me, part_of, lands, sems, pieces

    def near(self):
        me = self.me
        self.n = rcopy(self.part_of(2 * me.x + 1 - me.c), self.lands.at[0], *self.sems(), me.sib())
        self.n.start()

    def pair(self):
        me = self.me
        self.p = rcopy(self.part_of(2 * (1 - me.x) + 1 - me.c), self.lands.at[1], *self.sems(), me.sib())
        self.p.start()

    def cross(self):
        me = self.me
        self.p.wait()
        part = self.part_of(2 * (1 - me.x) + me.c)

        def add(k, _):
            mine = part.at[k]
            mine[...] = (mine[...].astype(F32) + self.lands[1, k].astype(F32)).astype(BF16)
            return 0

        lax.fori_loop(0, self.pieces, add, 0)
        self.x = rcopy(part, self.lands.at[2], *self.sems(), me.xn())
        self.x.start()

    def finish(self):
        self.n.wait()
        self.x.wait()

    def total(self, k, at):
        own = self.part_of(self.me.f)[k, at].astype(F32) + self.lands[0, k, at].astype(F32)
        return own + self.lands[2, k, at].astype(F32)


def nn(a, b):
    return lax.dot_general(a, b, (((1,), (0,)), ((), ())), preferred_element_type=F32)


def nt(a, b):
    return lax.dot_general(a, b, (((1,), (1,)), ((), ())), preferred_element_type=F32)


def tn(a, b):
    return lax.dot_general(a, b, (((0,), (0,)), ((), ())), preferred_element_type=F32)


def standard(values):
    centred = values - jnp.mean(values, axis=-1, keepdims=True)
    scale = lax.rsqrt(jnp.mean(centred * centred, axis=-1, keepdims=True) + EPSILON)
    return centred * scale, scale


def norm_back(values, gain, grad):
    unit, scale = standard(values)
    inner = grad * gain
    low = jnp.mean(inner, axis=-1, keepdims=True)
    high = jnp.mean(inner * unit, axis=-1, keepdims=True)
    return scale * (inner - low - unit * high)


def softmax(scores):
    e = jnp.exp(scores - jnp.max(scores, axis=-1, keepdims=True))
    return e / jnp.sum(e, axis=-1, keepdims=True)


def low_half(shape):
    return lax.broadcasted_iota(jnp.int32, shape, 1) % 128 < 64


def by_halves(pieces):
    out = []
    for n, piece in enumerate(pieces):
        if piece is None:
            out.append(jnp.zeros_like(pieces[0][0][:, :128]))
            continue
        ref, k = piece
        part = ref[:, k // 2 * 128 : k // 2 * 128 + 128].astype(F32)
        out.append(part if k % 2 == n else pltpu.roll(part, 64, 1))
    return jnp.where(low_half(out[0].shape), out[0], out[1])


def head_order(f):
    q, k, v = (HEADS * n + 3 * f for n in range(3))
    return ((q, q + 1), (q + 2, k + 2), (k, k + 1), (v, v + 1), (v + 2, None))


def spread(parts, shifts):
    lane = lax.broadcasted_iota(jnp.int32, parts[0].shape, 1) // 96
    total = None
    for n in range(4):
        part = pltpu.roll(parts[n], shifts[n] % 4 * 96, 1) if shifts[n] % 4 else parts[n]
        total = part if total is None else jnp.where(lane == n, part, total)
    return total


def upright(row):
    n = row.shape[1]
    i, j = (lax.broadcasted_iota(jnp.int32, (n, n), k) for k in range(2))
    return jnp.sum(jnp.where(i == j, jnp.broadcast_to(row, (n, n)), 0.0), axis=1, keepdims=True)


def level(column):
    n = column.shape[0]
    i, j = (lax.broadcasted_iota(jnp.int32, (n, n), k) for k in range(2))
    return jnp.sum(jnp.where(i == j, jnp.broadcast_to(column, (n, n)), 0.0), axis=0, keepdims=True)


D, FF, ROWS, COLS, HEAD = 768, 3072, 8, 128, 64
HALF = D // 2
OWN = COLS // 4
TOK = ROWS * OWN
WIDE = 640
FACTOR = HEAD**-0.5


def layer_kernel(
    tok_h, cot_h, seq_h, cid_h, gain_row_h, r_q_h, r_o_h, gain_col_h, r_c_h, r_co_h, gain_ffn_h, r_u_h, r_d_h,
    mixed, igrad, o_q, d_o, d_c, d_co, o_u, d_d,
    tok, cot, seq, cid, gain_row, r_q, r_o, gain_col, r_c, r_co, gain_ffn, r_u, r_d, in_sems,
    i_q, i_u,
    w_q, w_o, w_c, w_u, w_d, f_q, f_o, f_c, f_u,
    l_o0, l_o1, l_o2, l_o3, l_o4,
    l_c0, l_c1, l_c2, l_c3, l_c4,
    l_q1, l_q2, t_q, l_u1, l_u2, t_u, l_d1, l_d2,
    tok_all, e_all, h1, qkv, p_row, o1f, o1c, x1, h2, qkv2, p_col, o2, x2, h3, act, du, yp, l_y, dp, l_p,
    g, do2, dqkv2, dh2, e1, dost, do1, dqkv, e1r, gains, cmask, tmask, ms, mr,
):
    me = Place()
    f = me.f
    scope = jax.named_scope
    sib_f, x_f, diag_f = 2 * me.x + 1 - me.c, 2 * (1 - me.x) + me.c, 2 * (1 - me.x) + 1 - me.c
    diag = me.dev(me.z, me.y, 1 - me.x, 1 - me.c)
    names = ("gain_row", "gain_col", "gain_ffn", "q", "o", "co", "c", "u", "d", "tok", "seq", "cid", "cot")
    pairs_in = (
        (gain_row_h, gain_row), (gain_col_h, gain_col), (gain_ffn_h, gain_ffn), (r_q_h, r_q), (r_o_h, r_o),
        (r_co_h, r_co), (r_c_h, r_c), (r_u_h, r_u), (r_d_h, r_d), (tok_h, tok), (seq_h, seq), (cid_h, cid),
        (cot_h, cot),
    )
    loads = {n: pltpu.make_async_copy(a, b, in_sems.at[k]) for k, (n, (a, b)) in enumerate(zip(names, pairs_in))}
    for c in loads.values():
        c.start()

    def loaded(*which):
        for n in which:
            loads[n].wait()

    greet([me.sib(), me.xn(), diag, me.yn(), me.z1(), me.z2()])
    used = [0]

    def sems():
        used[0] += 1
        return ms.at[used[0] - 1], mr.at[used[0] - 1]

    def swap():
        used[0] += 3
        at = pl.ds(used[0] - 3, 3)
        return Swap(me, ms.at[at], mr.at[at])

    at_w = pl.ds(0, HALF)
    at_qv, at_k, at_o = pl.ds(0, D), pl.ds(D, HALF), pl.ds(D + HALF, HALF)

    def lanes(ref, start, step, size):
        return lambda h: ref.at[:, pl.ds(pl.multiple_of(start + h * step, 128), size)]

    of_o = lanes(r_o, 0, HALF, HALF)
    of_qv, of_k, of_co = lanes(r_c, 0, 2 * D, D), lanes(r_c, D, HALF, HALF), lanes(r_co, 0, HALF, HALF)
    go = Gather(me, of_o, f_o, w_o, at_w, sems)
    g_qv = Gather(me, of_qv, f_c, w_c, at_qv, sems)
    g_k = Gather(me, of_k, f_c, w_c, at_k, sems)
    g_out = LastOverX(me, of_co, f_c, w_c, at_o, sems)
    ro = Reduce(me, w_o, at_w, (l_o0, l_o1, l_o2, l_o3, l_o4), lanes(d_o, 0, HALF, HALF), sems)
    r_qv, r_k, r_out = (
        kind(me, w_c, at, (l_c0, l_c1, l_c2, l_c3, l_c4), out, sems)
        for kind, at, out in (
            (Reduce, at_qv, lanes(d_c, 0, 2 * D, D)),
            (EarlyReduce, at_k, lanes(d_c, D, HALF, HALF)),
            (Reduce, at_o, lanes(d_co, 0, HALF, HALF)),
        )
    )
    sq = [Slices(me, w_q, pl.ds(*at), l_q1, l_q2, sems, at[0] > 0) for at in ((0, 384), (384, 256))]
    su = [Slices(me, w_u, pl.ds(k * HALF, HALF), l_u1, l_u2, sems, k == 1) for k in range(2)]
    sd = [Slices(me, w_d, pl.ds(k * HALF, HALF), l_d1, l_d2, sems, k == 0) for k in range(2)]

    def cols_of(t):
        return pl.ds(pl.multiple_of(t * OWN, OWN), OWN)

    own_cols = cols_of(f)

    def stacked(land):
        return jnp.concatenate([land[k].astype(F32) for k in range(4)], axis=0).astype(BF16)

    loaded("gain_row", "gain_col", "gain_ffn", "q")
    lane = lax.broadcasted_iota(jnp.int32, (r_q.shape[0], 128), 1)
    columns = [upright(v[...].astype(F32)) for v in (gain_row, gain_col, gain_ffn)]
    spare = sum(jnp.where(lane == HEAD + n, v, 0.0) for n, v in enumerate(columns))
    for t in range(4):
        for n, pair in enumerate(head_order(t)):
            part = by_halves([None if k is None else (r_q, k) for k in pair])
            i_q[t, :, n * 128 : (n + 1) * 128] = (part + spare if n == 4 else part).astype(BF16)
    s_q = swap()
    s_q.go(lambda t: i_q.at[t], f_q.at[f])
    loaded("o", "co", "c")
    for k in (g_k, g_qv, go, g_out):
        k.swap()
    loaded("tok")
    tok_all[pl.ds(2 * f, 2)] = tok[...]
    loaded("d")
    w_d[me.hi, me.lo, me.y] = r_d[...]
    sd[0].send(0)
    loaded("u")
    with scope("i_u"):
        for t in range(4):
            for n in range(2):
                parts = [r_u[:, (4 * n + k) * 384 : (4 * n + k + 1) * 384].astype(F32) for k in range(4)]
                i_u[t, :, n * 384 : (n + 1) * 384] = spread(parts, [k - t for k in range(4)]).astype(BF16)
    s_u = swap()
    s_u.go(lambda t: i_u.at[t], f_u.at[f])
    shr_t = Share(me, lambda k: tok_all.at[pl.ds(2 * k, 2)], sems)
    shr_t.send()
    with scope("q_f"):
        f_q[f] = i_q[f]
        s_q.wait()
        w_q[me.hi, me.lo, me.y] = stacked(f_q)
    sq[1].send(0)
    sq[0].send(0)
    with scope("masks"):
        loaded("seq", "cid", "cot")
        first = seq[0, 0]
        ids = jnp.broadcast_to(cid[...], (COLS, COLS)).astype(F32)
        cmask[...] = jnp.where(ids == ids.T, 1.0, 0.0)
        i, j = (lax.broadcasted_iota(jnp.int32, tmask.shape, n) for n in range(2))
        wide = OWN // 2

        def block_of(k):
            r = k // wide
            return jnp.where(r == 0, first, jnp.where(r == ROWS - 1, 2, 1))

        tmask[...] = jnp.where((i % wide == j % wide) & (block_of(i) == block_of(j)), 1.0, 0.0)
        e_all[pl.ds(2 * f, 2)] = cot[...]
        f_u[f] = i_u[f]
    with scope("q_m1"):
        sq[1].send(1)
    s_u.wait()
    w_u[me.hi, me.lo, me.y] = stacked(f_u)
    su[1].send(0)
    with scope("q_m0"):
        sq[0].send(1)
    g_qv.s0()
    go.s0()
    with scope("q_n1"):
        sq[1].send(2)
    shr_e = Share(me, lambda k: e_all.at[pl.ds(2 * k, 2)], sems)
    shr_e.send()
    with scope("q_n0"):
        sq[0].send(2)
    g_k.s0()
    with scope("qv1"):
        g_qv.s1()
    with scope("tok"):
        shr_t.forward()
    with scope("go1"):
        go.s1()
    with scope("q_fin1"):
        sq[1].finish()
    with scope("gains"):
        wide = w_q[:, :, :, :, WIDE - 128 :].reshape(D, 128)
        for k in range(D // 128):
            part = wide[k * 128 : (k + 1) * 128].astype(F32).T
            gains[:, k * 128 : (k + 1) * 128] = part[HEAD : HEAD + 8]
    with scope("tok2"):
        shr_t.near()
        shr_t.finish()

    with scope("norm_row"):

        def norm_rows(k, _):
            unit, _s = standard(tok_all[k].astype(F32))
            h1[k] = (unit * gains[0:1]).astype(BF16)
            return 0

        lax.fori_loop(0, ROWS, norm_rows, 0)
    with scope("k1"):
        g_k.s1()
    with scope("qv2"):
        g_qv.s2()
    su[0].send(0)
    g_out.s0()
    with scope("go2"):
        go.s2()
    with scope("q_fin0"):
        sq[0].finish()
    with scope("qkv_row"):
        wide = w_q[...].reshape(D, WIDE)

        def project(k, _):
            pair = h1[pl.ds(2 * k, 2)].reshape(2 * COLS, D)
            qkv[pl.ds(2 * k, 2)] = nn(pair, wide).astype(BF16).reshape(2, COLS, WIDE)
            return 0

        lax.fori_loop(0, ROWS // 2, project, 0)
    with scope("k2"):
        g_k.s2()
    with scope("qv3"):
        g_qv.s3()
    with scope("su_m0"):
        su[0].send(1)

    joined = (jnp.full((1, 1), first, jnp.int32) == 1)
    tied = jnp.where(joined, 1.0, 0.0)
    s_mid = jnp.where(joined, FACTOR / 7**0.5, FACTOR / 6**0.5)
    lower = low_half((COLS, 128))
    zero = jnp.zeros((COLS, 128), BF16)

    def tile(ref, r, k):
        return ref[r, :, k * 128 : (k + 1) * 128]

    def head_tiles(r):
        q01, q2k2, k01 = tile(qkv, r, 0), tile(qkv, r, 1), tile(qkv, r, 2)
        k2 = pltpu.roll(q2k2.astype(F32), 64, 1).astype(BF16)
        return (
            (jnp.where(lower, q01, zero), k01),
            (jnp.where(lower, zero, q01), k01),
            (jnp.where(lower, q2k2, zero), k2),
        )

    with scope("go3"):
        go.s3()
    with scope("row_fwd"):
        sums = [[None] * 3 for _ in range(3)]
        for r in range(ROWS):
            for h, (a, b) in enumerate(head_tiles(r)):
                s = nt(a, b)
                t = 0 if r == 0 else 2 if r == ROWS - 1 else 1
                sums[h][t] = s if sums[h][t] is None else sums[h][t] + s
        for h in range(3):
            s0, s1, s2 = sums[h]
            for t, s in enumerate((s0 * FACTOR, (s1 + tied * s0) * s_mid, s2 * FACTOR)):
                p_row[h, t] = softmax(jnp.where(cmask[...] > 0.5, s, NEGATIVE))

    def chances(h, r):
        if r == 0:
            return jnp.where(joined, p_row[h, 1], p_row[h, 0])
        return p_row[h, 2 if r == ROWS - 1 else 1]

    thirds = []
    with scope("row_out"):
        for r in range(ROWS):
            v01, v2 = tile(qkv, r, 3), tile(qkv, r, 4)
            p = [chances(h, r).astype(BF16) for h in range(3)]
            o1f[r] = jnp.where(lower, nn(p[0], v01), nn(p[1], v01)).astype(BF16)
            thirds.append(nn(p[2], v2))
        for r in range(4):
            o1f[ROWS + r] = jnp.where(lower, thirds[r], pltpu.roll(thirds[r + 4], 64, 1)).astype(BF16)
    s_o = swap()
    s_o.go(lambda t: o1f.at[:, cols_of(t)], o1c.at[f])
    o1c[f] = o1f[:, own_cols]
    with scope("out1"):
        g_out.s1()
    su[1].send(1)
    with scope("e_f"):
        shr_e.forward()
    with scope("k3"):
        g_k.s3()
    sd[1].send(0)
    with scope("su_n1"):
        su[1].send(2)
    sd[0].send(1)
    with scope("sd_m1"):
        sd[1].send(1)
    with scope("qv4"):
        g_qv.s4()
    with scope("go4"):
        go.s4()
    with scope("out2"):
        g_out.s2()
    with scope("k4"):
        g_k.s4()
    with scope("su_y0"):
        su[0].send(2)
    with scope("o1"):
        s_o.wait()

    def o1_of(k):
        packed = o1c[k, ROWS:].reshape(TOK // 2, 128)
        third = jnp.concatenate([packed, pltpu.roll(packed.astype(F32), 64, 1).astype(BF16)], axis=0)
        return jnp.concatenate([o1c[k, :ROWS].reshape(TOK, 128), third[:, :HEAD]], axis=1)

    def w_out(h, k):
        return w_o[h, k // 2, k % 2].reshape(192, HALF)

    with scope("go5"):
        go.s5()
    with scope("out_row"):
        o1_parts = [o1_of(k) for k in range(4)]
        for h in range(2):
            cols = slice(h * HALF, (h + 1) * HALF)
            total = tok_all[:, own_cols, cols].reshape(TOK, HALF).astype(F32)
            for k in range(4):
                total = total + nn(o1_parts[k], w_out(h, k))
            x1[:, cols] = total

    def in_pieces(step, rows=64, total=TOK):
        def body(k, _):
            step(pl.ds(pl.multiple_of(k * rows, rows), rows))
            return 0

        lax.fori_loop(0, total // rows, body, 0)

    with scope("norm_col"):

        def norm_col(at):
            h2[at] = (standard(x1[at])[0] * gains[1:2]).astype(BF16)

        in_pieces(norm_col)

    def w_col(part, k):
        half, off = ((0, k * HALF), (k, D), (1, k * HALF), (k, D + HALF))[part]
        return w_c.at[half, :, :, :, :, :, off : off + HALF]

    def project2(part):
        for k in range(2):
            at = slice(k * HALF, (k + 1) * HALF)
            one = nn(h2[...], w_col(part, k)[...].reshape(D, HALF))
            qkv2[part, :, :, at] = one.astype(BF16).reshape(ROWS, OWN, HALF)

    with scope("qv5"):
        g_qv.s5()
    with scope("qkv_col"):
        project2(0)
        project2(2)
        g_k.s5()
        project2(1)
    with scope("out3"):
        g_out.s3()
    with scope("sd_n0"):
        sd[0].send(2)
    with scope("sd_n1"):
        sd[1].send(2)
    part_cols = OWN // 2
    part_size = ROWS * part_cols
    lower2 = low_half((part_size, 128))
    zero2 = jnp.zeros((part_size, 128), BF16)

    def some(ref, m, at, *lead):
        return ref[(*lead, ALL, slice(m * part_cols, (m + 1) * part_cols), at)].reshape(part_size, 128)

    def put(ref, m, at, value, *lead):
        value = value.astype(BF16).reshape(ROWS, part_cols, 128)
        ref[(*lead, ALL, slice(m * part_cols, (m + 1) * part_cols), at)] = value

    def pairs(step):
        def body(k, _):
            step([(2 * k + n, m, pl.ds(pl.multiple_of((2 * k + n) * 128, 128), 128)) for n in range(2) for m in range(2)])
            return 0

        lax.fori_loop(0, HEADS // 4, body, 0)

    def one_head(e, value):
        return jnp.where(lower2, value, zero2) if e == 0 else jnp.where(lower2, zero2, value)

    with scope("col_fwd"):

        def col_pair(work):
            scores, chosen = [], []
            for _k, m, at in work:
                q, kk = some(qkv2, m, at, 0), some(qkv2, m, at, 1)
                scores.append([nt(one_head(e, q), kk) * FACTOR for e in range(2)])
            same = tmask[...] > 0.5
            for pair in scores:
                chosen.append([softmax(jnp.where(same, one, NEGATIVE)) for one in pair])
            out = []
            for (_k, m, at), pair in zip(work, chosen):
                v = some(qkv2, m, at, 2)
                out.append([nn(p.astype(BF16), v) for p in pair])
            for (k, m, at), pair, got in zip(work, chosen, out):
                put(o2, m, at, jnp.where(lower2, got[0], got[1]))
                for e in range(2):
                    p_col[2 * k + e, m] = pair[e]

        pairs(col_pair)
    with scope("out4"):
        g_out.s4()
    with scope("out_col"):
        g_out.s5()
        for k in range(2):
            at = slice(k * HALF, (k + 1) * HALF)
            x2[:, at] = x1[:, at] + nn(o2[...].reshape(TOK, D), w_col(3, k)[...].reshape(D, HALF))
    half_size = TOK // 2
    shr_h = [Share(me, lambda k, u=u: h3.at[k, u], sems) for u in range(2)]
    for u in range(2):
        with scope("norm_ffn%d" % u):

            def norm_ffn(k, _, u=u):
                at = pl.ds(pl.multiple_of(k * 64, 64), 64)
                src = pl.ds(pl.multiple_of(u * half_size + k * 64, 64), 64)
                h3[f, u, at] = (standard(x2[src])[0] * gains[2:3]).astype(BF16)
                return 0

            lax.fori_loop(0, half_size // 64, norm_ffn, 0)
        shr_h[u].send()
    for k in (go, g_qv, g_k, g_out):
        k.drain()
    with scope("su_f"):
        for k in su:
            k.finish()
    with scope("e"):
        shr_e.near()
        shr_e.finish()
    with scope("sd_f"):
        for k in sd:
            k.finish()

    def grads_of(b):
        return e_all[:, cols_of(b)].reshape(TOK, D)

    def ffn_block(pair, mine=None):
        grad = jnp.concatenate(
            [e_all[4 * u : 4 * u + 4, cols_of(b)].reshape(half_size, D) for b, u in pair], axis=0
        )
        tokens = jnp.concatenate([h3[b, u] for b, u in pair], axis=0)
        y_sum, d_sum = None, None
        for k in range(2):
            at = slice(k * HALF, (k + 1) * HALF)
            up = w_u[:, :, :, :, at].reshape(D, HALF)
            down = w_d[k].reshape(HALF, D)
            u_k = nn(tokens, up)
            bell = jnp.exp(-0.5 * u_k * u_k) * (1 / (2 * jnp.pi) ** 0.5)
            upper = 0.5 + 0.5 * lax.erf(u_k * 0.5**0.5)
            a = (u_k * upper).astype(BF16)
            d = (nt(grad, down) * (upper + u_k * bell)).astype(BF16)
            for n, (b, u) in enumerate(pair):
                act[b, u, :, at] = a[n * half_size : (n + 1) * half_size]
                du[b, u, :, at] = d[n * half_size : (n + 1) * half_size]
            y, dd = nn(a, down), nt(d, up)
            y_sum = y if y_sum is None else y_sum + y
            d_sum = dd if d_sum is None else d_sum + dd
        if mine is not None:
            y_sum = y_sum + x2[...] * mine
        y_sum = y_sum.astype(BF16).reshape(4, 2 * OWN, D)
        d_sum = d_sum.astype(BF16).reshape(4, 2 * OWN, D)
        for n, (b, u) in enumerate(pair):
            yp[b, 2 * u : 2 * u + 2] = y_sum[2 * n : 2 * n + 2]
            dp[b, 2 * u : 2 * u + 2] = d_sum[2 * n : 2 * n + 2]

    cy = Collect(me, lambda k: yp.at[:, k], l_y, sems)
    cd = [
        Collect(me, lambda k, u=u: dp.at[k, pl.ds(2 * u, 2)], l_p.at[:, pl.ds(2 * u, 2)], sems, 2) for u in range(2)
    ]
    with scope("h3_near"):
        shr_h[0].near()
        shr_h[1].near()
    with scope("ffn1"):

        def near_two(k, _):
            b = jnp.where(k == 0, f, sib_f)
            ffn_block(((b, 0), (b, 1)), (k == 0).astype(F32))
            return 0

        lax.fori_loop(0, 2, near_two, 0)
    cd[0].near()
    cd[1].near()
    with scope("h3_far0"):
        shr_h[0].forward()
    with scope("h3_diag0"):
        shr_h[0].finish()
    with scope("ffn2"):
        ffn_block(((x_f, 0), (diag_f, 0)))
    cd[0].pair()
    with scope("h3_far1"):
        shr_h[1].forward()
    with scope("dh3_0"):
        cd[0].cross()
    with scope("h3_diag1"):
        shr_h[1].finish()
    with scope("ffn3"):
        ffn_block(((x_f, 1), (diag_f, 1)))
    cd[1].pair()
    cy.near()
    cy.pair()
    with scope("dh3_1"):
        cd[1].cross()
    for k in range(2):
        at = slice(k * HALF, (k + 1) * HALF)
        with scope("g_down%d" % k):
            part = sum(tn(act[b].reshape(TOK, D), grads_of(b)[:, at]) for b in range(4))
            w_d[:, :, :, :, at] = part.astype(BF16).reshape(2, 2, 2, 96, HALF)
        sd[k].back(0)
    for k in range(2):
        at = slice(k * HALF, (k + 1) * HALF)
        with scope("g_up%d" % k):
            part = sum(tn(h3[b].reshape(TOK, D), du[b, :, :, at].reshape(TOK, HALF)) for b in range(4))
            w_u[:, :, :, :, at] = part.astype(BF16).reshape(2, 2, 2, 96, HALF)
        su[k].back(0)

    for u in range(2):
        with scope("cd_w%d" % u):
            cd[u].finish()
        with scope("back_ffn%d" % u):

            def back_ffn(k, _, u=u):
                row = 4 * u + k
                at = pl.ds(pl.multiple_of(row * OWN, OWN), OWN)
                grad = cd[u].total(k // 2, pl.ds(pl.multiple_of(k % 2 * OWN, OWN), OWN))
                g[at] = e_all[row, own_cols].astype(F32) + norm_back(x2[at], gains[2:3], grad)
                e1[at] = g[at].astype(BF16)
                return 0

            lax.fori_loop(0, 4, back_ffn, 0)
    with scope("mix"):
        cy.cross()
    with scope("do2"):
        total = sum(nt(e1[:, k * HALF : (k + 1) * HALF], w_col(3, k)[...].reshape(D, HALF)) for k in range(2))
        do2[...] = total.astype(BF16).reshape(ROWS, OWN, D)
        for k in range(2):
            part = tn(o2[...].reshape(TOK, D), e1[:, k * HALF : (k + 1) * HALF])
            w_col(3, k)[...] = part.astype(BF16).reshape(2, 2, 2, 2, 48, HALF)
    r_out.r0()
    with scope("sd_b0"):
        sd[0].back(1)
    with scope("col_bwd"):

        def col_back(work):
            grads, back, out = [], [], []
            for _k, m, at in work:
                d, v = some(do2, m, at), some(qkv2, m, at, 2)
                grads.append([nt(one_head(e, d), v) for e in range(2)])
            for (k, m, at), pair in zip(work, grads):
                for e in range(2):
                    p, dq = p_col[2 * k + e, m], pair[e]
                    ds = p * (dq - jnp.sum(dq * p, axis=-1, keepdims=True))
                    back.append((ds.astype(BF16), ds.T.astype(BF16), p.T.astype(BF16)))
            for n, (_k, m, at) in enumerate(work):
                q, kk, d = some(qkv2, m, at, 0), some(qkv2, m, at, 1), some(do2, m, at)
                got = [
                    (nn(ds, kk) * FACTOR, nn(dst, q) * FACTOR, nn(pt, d)) for ds, dst, pt in back[2 * n : 2 * n + 2]
                ]
                out.append([jnp.where(lower2, got[0][i], got[1][i]) for i in range(3)])
            for (_k, m, at), got in zip(work, out):
                for n in range(3):
                    put(dqkv2, m, at, got[n], n)

        pairs(col_back)
    with scope("dh2"):
        total = None
        for part in range(3):
            for k in range(2):
                one = nt(dqkv2[part, :, :, k * HALF : (k + 1) * HALF].reshape(TOK, HALF), w_col(part, k)[...].reshape(D, HALF))
                total = one if total is None else total + one
        dh2[...] = total

    def grad_col(part):
        for k in range(2):
            one = tn(h2[...], dqkv2[part, :, :, k * HALF : (k + 1) * HALF].reshape(TOK, HALF))
            w_col(part, k)[...] = one.astype(BF16).reshape(2, 2, 2, 2, 48, HALF)

    with scope("back_col"):

        def back_col(at):
            g[at] = g[at] + norm_back(x1[at], gains[1:2], dh2[at])
            e1[at] = g[at].astype(BF16)

        in_pieces(back_col)

    with scope("do1"):
        for k in range(4):
            d = nt(e1[:, :HALF], w_out(0, k)) + nt(e1[:, HALF:], w_out(1, k))
            third = jnp.concatenate([d[:, 128:], jnp.zeros((TOK, 64), F32)], axis=1)
            third = third[: TOK // 2] + pltpu.roll(third[TOK // 2 :], 64, 1)
            dost[k, :ROWS] = d[:, :128].astype(BF16).reshape(ROWS, OWN, 128)
            dost[k, ROWS:] = third.astype(BF16).reshape(4, OWN, 128)
    s_d = swap()
    s_d.go(lambda t: dost.at[t], do1.at[:, own_cols])
    do1[:, own_cols] = dost[f]
    s_g = swap()
    s_g.go(lambda t: e1.at[pl.ds(pl.multiple_of(2 * OWN * t, 2 * OWN), 2 * OWN)], e1r.at[f])
    e1r[f] = e1[pl.ds(pl.multiple_of(2 * OWN * f, 2 * OWN), 2 * OWN)]
    with scope("su_b0"):
        su[0].back(1)
    with scope("out_r1"):
        r_out.r1()
    with scope("sd_b1"):
        sd[1].back(1)
    with scope("g_qv"):
        grad_col(0)
        grad_col(2)
    r_qv.r0()
    with scope("su_b1"):
        su[1].back(1)
    with scope("sd_c0"):
        sd[0].back(2)
    with scope("g_k"):
        grad_col(1)
    r_k.r0()
    with scope("g_out_row"):
        o1_parts = [o1_of(k) for k in range(4)]
        for h in range(2):
            for k in range(4):
                part = tn(o1_parts[k], e1[:, h * HALF : (h + 1) * HALF])
                w_o[h, k // 2, k % 2] = part.astype(BF16).reshape(2, 2, 48, HALF)
    ro.r0()
    with scope("qv_r1"):
        r_qv.r1()
    with scope("k_r1"):
        r_k.r1()
    with scope("ro1"):
        ro.r1()
    with scope("su_c0"):
        su[0].back(2)
    with scope("do1w"):
        s_d.wait()
    with scope("row_bwd"):
        d_third = [jnp.where(lower, do1[ROWS + r], zero) for r in range(4)]
        for r in range(4):
            d_third.append(jnp.where(lower, pltpu.roll(do1[ROWS + r].astype(F32), 64, 1).astype(BF16), zero))
        d_sum = [[None] * 3 for _ in range(3)]
        for r in range(ROWS):
            d01, d2, v01, v2 = do1[r], d_third[r], tile(qkv, r, 3), tile(qkv, r, 4)
            ops = ((jnp.where(lower, d01, zero), v01), (jnp.where(lower, zero, d01), v01), (d2, v2))
            for h, (a, b) in enumerate(ops):
                s = nt(a, b)
                t = 0 if r == 0 else 2 if r == ROWS - 1 else 1
                d_sum[h][t] = s if d_sum[h][t] is None else d_sum[h][t] + s
        da, dat, pt = [], [], []
        for h in range(3):
            s0, s1, s2 = d_sum[h]
            by = []
            for t, s in enumerate((s0, s1 + tied * s0, s2)):
                p = p_row[h, t]
                by.append(p * (s - jnp.sum(s * p, axis=-1, keepdims=True)))
            da.append((jnp.where(joined, by[1], by[0]), by[1], by[2]))
            dat.append([a.T.astype(BF16) for a in da[h]])
            pt.append([chances(h, r).T.astype(BF16) for r in (0, 1, ROWS - 1)])
            da[h] = [a.astype(BF16) for a in da[h]]
        s_first = jnp.where(joined, s_mid, FACTOR)
        for r in range(ROWS):
            t = 0 if r == 0 else 2 if r == ROWS - 1 else 1
            scale = (s_first, s_mid, FACTOR)[t]
            q01, q2k2, k01 = tile(qkv, r, 0), tile(qkv, r, 1), tile(qkv, r, 2)
            d01, d2 = do1[r], d_third[r]
            dq = jnp.where(lower, nn(da[0][t], k01), nn(da[1][t], k01)) * scale
            dk = jnp.where(lower, nn(dat[0][t], q01), nn(dat[1][t], q01)) * scale
            mid = jnp.where(lower, nn(dat[2][t], q2k2), nn(da[2][t], q2k2)) * scale
            dv = jnp.where(lower, nn(pt[0][t], d01), nn(pt[1][t], d01))
            for n, val in enumerate((dq, pltpu.roll(mid, 64, 1), dk, dv, nn(pt[2][t], d2))):
                dqkv[r, :, n * 128 : (n + 1) * 128] = val.astype(BF16)
    with scope("dh1"):
        wide = w_q[...].reshape(D, WIDE)

        def partial_dh(k, _):
            pair = dqkv[pl.ds(2 * k, 2)].reshape(2 * COLS, WIDE)
            dp[k] = nt(pair, wide).astype(BF16).reshape(4, 2 * OWN, D)
            return 0

        lax.fori_loop(0, 4, partial_dh, 0)
    ch = Collect(me, lambda k: dp.at[k], l_p, sems)
    ch.pair()
    ch.near()
    for k in range(2):
        at = slice(0, 384) if k == 0 else slice(384, WIDE)
        with scope("g_qkv%d" % k):
            total = tn(h1[...].reshape(ROWS * COLS, D), dqkv[:, :, at].reshape(ROWS * COLS, -1))
            w_q[:, :, :, :, at] = total.astype(BF16).reshape(2, 2, 2, 96, -1)
        sq[k].back(0)
    with scope("out_r2"):
        r_out.r2()
    with scope("sd_c1"):
        sd[1].back(2)
    with scope("su_c1"):
        su[1].back(2)
    with scope("qv_r2"):
        r_qv.r2()
    with scope("k_r2"):
        r_k.r2()
    with scope("q_b1"):
        sq[1].back(1)
    with scope("q_b0"):
        sq[0].back(1)
    with scope("ro2"):
        ro.r2()
    with scope("out_r3"):
        r_out.r3()
    with scope("qv_r3"):
        r_qv.r3()
    with scope("dh1_x"):
        ch.cross()
    with scope("k_r3"):
        r_k.r3()
    with scope("q_c1"):
        sq[1].back(2)
    with scope("q_c0"):
        sq[0].back(2)
    with scope("ro3"):
        ro.r3()
    with scope("out_r3b"):
        r_out.r3b()
    with scope("d_sum"):
        for k in sd:
            d_d[:, k.at] = k.back_sum()
    with scope("u_sum"):
        for k in su:
            t_u[:, :, k.at] = k.back_sum().astype(BF16).reshape(4, -1, HALF)
    s_v = swap()
    s_v.go(lambda t: t_u.at[t], o_u.at[f])
    o_u[f] = t_u[f]
    with scope("qv_r3b"):
        r_qv.r3b()
    with scope("ro3b"):
        ro.r3b()
    with scope("k_r3b"):
        r_k.r3b()
    with scope("q_sum"):
        s_t = []
        for k in reversed(sq):
            t_q[:, :, k.at] = k.back_sum().astype(BF16).reshape(4, -1, k.at.size)
            o_q[f, :, k.at] = t_q[f, :, k.at]
            s_t.append(swap())
            s_t[-1].go(lambda t, at=k.at: t_q.at[t, :, at], o_q.at[f, :, k.at])
    with scope("mixed"):
        cy.finish()
        for r in range(2):
            for k in range(4):
                mixed[r, k * OWN : (k + 1) * OWN] = cy.total(k, slice(r * OWN, (r + 1) * OWN)).astype(BF16)
    with scope("in_grad"):
        ch.finish()
        s_g.wait()
        for r in range(2):
            for k in range(4):
                at = slice(k * OWN, (k + 1) * OWN)
                grad = ch.total(2 * r + k // 2, slice(k % 2 * OWN, (k % 2 + 1) * OWN))
                back = norm_back(tok[r, at].astype(F32), gains[0:1], grad)
                igrad[r, at] = e1r[k, r * OWN : (r + 1) * OWN].astype(F32) + back
    with scope("out_r4"):
        r_out.r4()
    with scope("qv_r4"):
        r_qv.r4()
    with scope("k_r4"):
        r_k.r4()
    with scope("ro4"):
        ro.r4()
    with scope("last"):
        for k in (r_out, r_qv, r_k, ro):
            k.r5()
        s_v.wait()
        for k in s_t:
            k.wait()
    assert used[0] <= SEMS, used[0]


SEMS = 160


def finish_kernel(*refs):
    ins, outs, held, made = refs[:14], refs[14:25], refs[25:39], refs[39:44]
    in_sems, out_sems = refs[44:]
    order = (6, 2, 4, 11, 9, 13, 0, 1, 3, 5, 7, 8, 10, 12)
    loads = [pltpu.make_async_copy(a, b, in_sems.at[k]) for k, (a, b) in enumerate(zip(ins, held))]
    for k in order:
        loads[k].start()
    stores = []

    def store(src, k):
        stores.append(pltpu.make_async_copy(src, outs[k], out_sems.at[k]))
        stores[-1].start()

    _mixed, _igrad, o_q, _o, e_c, _co, o_u, _d, gain_row, r_q, gain_col, r_c, gain_ffn, r_u = held
    dg_row, d_q, dg_col, dg_ffn, d_u = made
    loads[6].wait()
    for n in range(8):
        parts = [o_u[t, :, n // 4 * 384 : (n // 4 + 1) * 384].astype(F32) for t in range(4)]
        d_u[:, n * 384 : (n + 1) * 384] = spread(parts, [t - n % 4 for t in range(4)])
    store(d_u, 9)
    loads[2].wait()
    where = {}
    for t in range(4):
        for n, pair in enumerate(head_order(t)):
            for k, piece in enumerate(pair):
                where[piece] = (o_q.at[t], 2 * n + k)
    for n in range(3 * D // 128):
        d_q[:, n * 128 : (n + 1) * 128] = by_halves([where[2 * n], where[2 * n + 1]])
    store(d_q, 3)
    for k, to in ((0, 0), (1, 1), (3, 4), (4, 6), (5, 7), (7, 10)):
        loads[k].wait()
        store(held[k], to)
    for k in (8, 9, 10, 11, 12, 13):
        loads[k].wait()

    for out, weight, grad, gain, to in (
        (dg_row, r_q, d_q, gain_row, 2), (dg_col, r_c, e_c, gain_col, 5), (dg_ffn, r_u, d_u, gain_ffn, 8)
    ):
        total = jnp.sum(weight[...].astype(F32) * grad[...], axis=1, keepdims=True)
        out[...] = level(total / upright(gain[...].astype(F32)))
        store(out, to)
    for c in stores:
        c.wait()


def run_layer(tok, cot, seq, cid, *weights):
    sds = jax.ShapeDtypeStruct
    rows = weights[1].shape[0]
    i_d = weights[-1]
    first = [sds(tok.shape, BF16), sds(tok.shape, F32)]
    wide_q, wide_u = sds((4, rows, WIDE), BF16), sds((4, rows, D), BF16)
    plain = [sds(w.shape, F32) for w in weights]
    shapes = first + [wide_q, plain[2], plain[4], plain[5], wide_u, plain[8]]

    def vmem(*shape, dtype=BF16):
        return pltpu.VMEM(shape, dtype)

    def lands(r, c):
        return [
            vmem(2, 2, 2, 2, r, c), vmem(2, 2, 2, r, c), vmem(2, 2, r, c), vmem(3, r, c), vmem(2, r // 2, c, dtype=F32)
        ]

    def slices(c):
        return [vmem(2, 2, 4 * rows, c), vmem(3, 4 * rows, c)]

    r2 = 2 * rows
    wo, wc, wu = HALF, 2 * D, D
    scratch = [
        *(pltpu.SMEM(a.shape, a.dtype) if a is seq else pltpu.VMEM(a.shape, a.dtype) for a in (tok, cot, seq, cid, *weights)),
        pltpu.SemaphoreType.DMA((13,)),
        vmem(4, rows, WIDE),
        vmem(4, rows, wu),
        vmem(2, 2, 2, 4 * rows, WIDE),
        vmem(2, 2, 2, 2, 2, r2, wo),
        vmem(2, 2, 2, 2, 2, r2, wc),
        vmem(2, 2, 2, 4 * rows, wu),
        vmem(2, 2, 2, *i_d.shape),
        vmem(4, rows, WIDE),
        vmem(rows, wo),
        vmem(rows, wc),
        vmem(4, rows, wu),
        *lands(r2, wo),
        *lands(r2, wc),
        *slices(WIDE),
        vmem(4, rows, WIDE),
        *slices(wu),
        vmem(4, rows, wu),
        *slices(D),
        vmem(ROWS, COLS, D),
        vmem(ROWS, COLS, D),
        vmem(ROWS, COLS, D),
        vmem(ROWS, COLS, WIDE),
        vmem(3, 3, COLS, COLS, dtype=F32),
        vmem(ROWS + 4, COLS, 128),
        vmem(4, ROWS + 4, OWN, 128),
        vmem(TOK, D, dtype=F32),
        vmem(TOK, D),
        vmem(3, ROWS, OWN, D),
        vmem(HEADS, 2, TOK // 2, TOK // 2, dtype=F32),
        vmem(ROWS, OWN, D),
        vmem(TOK, D, dtype=F32),
        vmem(4, 2, TOK // 2, D),
        vmem(4, 2, TOK // 2, D),
        vmem(4, 2, TOK // 2, D),
        vmem(4, 4, 2 * OWN, D),
        vmem(3, 4, 2 * OWN, D),
        vmem(4, 4, 2 * OWN, D),
        vmem(3, 4, 2 * OWN, D),
        vmem(TOK, D, dtype=F32),
        vmem(ROWS, OWN, D),
        vmem(3, ROWS, OWN, D),
        vmem(TOK, D, dtype=F32),
        vmem(TOK, D),
        vmem(4, ROWS + 4, OWN, 128),
        vmem(ROWS + 4, COLS, 128),
        vmem(ROWS, COLS, WIDE),
        vmem(4, 2 * OWN, D),
        vmem(8, D, dtype=F32),
        vmem(COLS, COLS, dtype=F32),
        vmem(TOK // 2, TOK // 2, dtype=F32),
        pltpu.SemaphoreType.DMA((SEMS,)),
        pltpu.SemaphoreType.DMA((SEMS,)),
    ]
    vm = pl.BlockSpec(memory_space=pltpu.VMEM)
    outs = pl.pallas_call(
        layer_kernel,
        out_shape=shapes,
        in_specs=[pl.BlockSpec(memory_space=pl.ANY)] * 13,
        out_specs=[vm] * 8,
        scratch_shapes=scratch,
        name="layer",
        compiler_params=pltpu.CompilerParams(
            collective_id=0, has_side_effects=True, vmem_limit_bytes=VMEM_LIMIT
        ),
    )(tok, cot, seq, cid, *weights)
    given = (*outs, weights[0], weights[1], weights[3], weights[4], weights[6], weights[7])
    anywhere = pl.BlockSpec(memory_space=pl.ANY)
    made = [plain[k] for k in (0, 1, 3, 6, 7)]
    return pl.pallas_call(
        finish_kernel,
        out_shape=first + plain,
        in_specs=[anywhere] * 14,
        out_specs=[anywhere] * 11,
        scratch_shapes=[pltpu.VMEM(a.shape, a.dtype) for a in (*given, *made)]
        + [pltpu.SemaphoreType.DMA((14,)), pltpu.SemaphoreType.DMA((11,))],
        name="finish",
        compiler_params=pltpu.CompilerParams(vmem_limit_bytes=VMEM_LIMIT),
    )(*given)


VMEM_LIMIT = 63 * 2**20


def on_device(
    tokens, cotangent, seq_ids, col_ids,
    gain_row, qkv_row, out_row, gain_col, qkv_col, out_col, gain_ffn, up_ffn, down_ffn,
    cells,
):
    members = CELL * lax.axis_size("fsdp")
    low_index = (lax.axis_index("dp") % CELL) * lax.axis_size("fsdp") + lax.axis_index("fsdp")

    def in_cell(shard):
        if cells == 1:
            return shard
        whole = lax.all_gather(shard, AXES, axis=0, tiled=True)
        rows = whole.shape[0] // members
        return lax.dynamic_slice_in_dim(whole, low_index * rows, rows, 0)

    def from_cell(summed):
        if cells == 1:
            return summed
        rows = summed.shape[0]
        whole = jnp.zeros((rows * members,) + summed.shape[1:], summed.dtype)
        whole = lax.dynamic_update_slice_in_dim(whole, summed, low_index * rows, 0)
        return lax.psum_scatter(whole, AXES, scatter_dimension=0, tiled=True)

    weights = [
        in_cell(w).reshape(1, -1) if w.ndim == 1 else in_cell(w)
        for w in (gain_row, qkv_row, out_row, gain_col, qkv_col, out_col, gain_ffn, up_ffn, down_ffn)
    ]
    mixed, igrad, *grads = run_layer(tokens[0], cotangent[0], seq_ids, col_ids, *weights)
    grads = [from_cell(v.reshape(-1) if v.shape[0] == 1 else v) for v in grads]
    return (mixed[None], igrad[None], *grads)


def solution(mesh):
    rows = P(AXES, None)
    vector = P(AXES)
    grid = P("dp", "fsdp", None, None)
    ids = P("dp", None)
    return jax.shard_map(
        partial(on_device, cells=mesh.shape["dp"] // CELL),
        mesh=mesh,
        in_specs=(grid, grid, ids, ids) + (vector, rows, rows) * 3,
        out_specs=(grid, grid) + (vector, rows, rows) * 3,
        check_vma=False,
    )
```

```python
from functools import partial

import jax
import jax.numpy as jnp
from jax import lax
from jax.experimental import pallas as pl
from jax.experimental.pallas import tpu as pltpu
from jax.sharding import PartitionSpec as P

HEADS = 12
EPSILON = 1e-05
NEGATIVE = -1000000000.0
MESH = pl.DeviceIdType.MESH
BF16 = jnp.bfloat16
F32 = jnp.float32
CELL = 8
AXES = ("dp", "fsdp")


class Place:
    def __init__(self):
        dp = lax.axis_index("dp")
        self.f = lax.axis_index("fsdp")
        self.base = dp // CELL * CELL
        low = dp - self.base
        self.z, self.y = low // 2, low % 2
        self.hi, self.lo = self.z // 2, self.z % 2
        self.x, self.c = self.f // 2, self.f % 2

    def dev(self, z, y, x, c):
        return (self.base + z * 2 + y, x * 2 + c)

    def sib(self):
        return self.dev(self.z, self.y, self.x, 1 - self.c)

    def xn(self):
        return self.dev(self.z, self.y, 1 - self.x, self.c)

    def yn(self):
        return self.dev(self.z, 1 - self.y, self.x, self.c)

    def first(self):
        return self.dev(self.z, self.y + self.c * (1 - 2 * self.y), self.x + (1 - self.c) * (1 - 2 * self.x), self.c)

    def second(self):
        return self.dev(self.z, self.y + (1 - self.c) * (1 - 2 * self.y), self.x + self.c * (1 - 2 * self.x), self.c)

    def z1(self):
        return self.dev(2 * self.hi + 1 - self.lo, self.y, self.x, self.c)

    def z2(self):
        return self.dev(2 * (1 - self.hi) + self.lo, self.y, self.x, self.c)


def greet(partners):
    bar = pltpu.get_barrier_semaphore()
    for t in partners:
        pl.semaphore_signal(bar, inc=1, device_id=t, device_id_type=MESH)
    pl.semaphore_wait(bar, len(partners))


def rcopy(src, dst, ss, rs, to):
    return pltpu.make_async_remote_copy(
        src_ref=src, dst_ref=dst, send_sem=ss, recv_sem=rs, device_id=to, device_id_type=MESH
    )


ALL = slice(None)


class Part:
    def __init__(self, me, w, at):
        self.me, self.w, self.at = me, w, at

    def block(self, hi, lo, y, x, half=None):
        return self.w.at[self.me.c if half is None else half, hi, lo, y, x, :, self.at]


class Gather(Part):
    def __init__(self, me, src_of, land, w, at, sems):
        super().__init__(me, w, at)
        self.src_of, self.land, self.sems = src_of, land, sems

    def swap(self):
        me = self.me
        self.c0 = rcopy(self.src_of(1 - me.c), self.land.at[:, self.at], *self.sems(), me.sib())
        self.c0.start()

    def start(self, ref, to):
        c = rcopy(ref, ref, *self.sems(), to)
        c.start()
        self.sent.append(c)
        return c

    def own(self):
        me = self.me
        self.c0.wait()
        mine = self.src_of(me.c)[...].astype(F32)
        other = self.land[:, self.at].astype(F32)
        flag = (me.c == 0).astype(F32)
        top = flag * mine + (1 - flag) * other
        low = flag * other + (1 - flag) * mine
        own = self.block(me.hi, me.lo, me.y, me.x)
        own[...] = jnp.concatenate([top, low], axis=0).astype(BF16)
        self.sent = []

    def s0(self):
        me = self.me
        self.own()
        self.a = self.start(self.block(me.hi, me.lo, me.y, me.x), me.z2())

    def s1(self):
        me = self.me
        self.a.wait_recv()
        self.b = self.start(self.block(ALL, me.lo, me.y, me.x), me.z1())

    def s2(self):
        me = self.me
        self.b.wait_recv()
        col = self.block(ALL, ALL, me.y, me.x)
        self.e = self.start(col, me.first())
        self.to_sib = [self.start(col, me.sib())]

    def fork(self, ref0, ref1, to, like):
        me, m = self.me, self.sems()

        @pl.when(me.c == 0)
        def _():
            rcopy(ref0, ref0, *m, to).start()

        @pl.when(me.c == 1)
        def _():
            rcopy(ref1, ref1, *m, to).start()

        c = rcopy(like, like, *m, to)
        self.sent.append(c)
        return c

    def s3(self):
        me = self.me
        self.e.wait_recv()
        two, col = self.block(ALL, ALL, me.y, ALL), self.block(ALL, ALL, me.y, me.x)
        self.g = self.fork(
            self.block(ALL, ALL, me.y, ALL, 0), self.block(ALL, ALL, ALL, me.x, 1), me.second(), two
        )
        self.to_sib.append(
            self.fork(
                self.block(ALL, ALL, me.y, 1 - me.x, 0), self.block(ALL, ALL, 1 - me.y, me.x, 1), me.sib(), col
            )
        )

    def s4(self):
        me = self.me
        self.g.wait_recv()
        two = self.block(ALL, ALL, me.y, ALL)
        self.to_sib.append(
            self.fork(
                self.block(ALL, ALL, 1 - me.y, ALL, 0), self.block(ALL, ALL, ALL, 1 - me.x, 1), me.sib(), two
            )
        )

    def s5(self):
        for c in self.to_sib:
            c.wait_recv()

    def drain(self):
        for c in self.sent:
            c.wait_send()


class Reduce(Part):
    def __init__(self, me, w, at, lands, out_of, sems):
        super().__init__(me, w, at)
        self.l0, self.l1, self.l2, self.l3, self.l4 = lands
        self.out_of, self.sems = out_of, sems

    def add(self, n, mine_of, land_of):
        def body(k, _):
            mine = mine_of(k)
            mine[...] = (mine[...].astype(F32) + land_of(k)[...].astype(F32)).astype(BF16)
            return 0

        lax.fori_loop(0, n, body, 0)

    def r0(self):
        me = self.me
        self.c0 = rcopy(
            self.block(ALL, ALL, ALL, ALL, 1 - me.c), self.l0.at[:, :, :, :, :, self.at], *self.sems(), me.sib()
        )
        self.c0.start()

    def r1(self):
        me = self.me
        self.c0.wait()
        self.add(
            16,
            lambda k: self.block(k // 8, k // 4 % 2, k // 2 % 2, k % 2),
            lambda k: self.l0.at[k // 8, k // 4 % 2, k // 2 % 2, k % 2, :, self.at],
        )
        land, m = self.l1.at[:, :, :, :, self.at], self.sems()

        @pl.when(me.c == 0)
        def _():
            rcopy(self.block(ALL, ALL, 1 - me.y, ALL, 0), land, *m, me.second()).start()

        @pl.when(me.c == 1)
        def _():
            rcopy(self.block(ALL, ALL, ALL, 1 - me.x, 1), land, *m, me.second()).start()

        self.c1 = rcopy(land, land, *m, me.sib())

    def r2(self):
        me = self.me
        self.c1.wait()

        def mine(k):
            m = k % 2
            y, x = me.y + me.c * (m - me.y), me.x + (1 - me.c) * (m - me.x)
            return self.block(k // 4, k // 2 % 2, y, x)

        self.add(8, mine, lambda k: self.l1.at[k // 4, k // 2 % 2, k % 2, :, self.at])
        oy = me.y + me.c * (1 - 2 * me.y)
        ox = me.x + (1 - me.c) * (1 - 2 * me.x)
        self.c2 = rcopy(self.block(ALL, ALL, oy, ox), self.l2.at[:, :, :, self.at], *self.sems(), me.first())
        self.c2.start()

    def r3(self):
        me = self.me
        self.c2.wait()
        self.add(
            4, lambda k: self.block(k // 2, k % 2, me.y, me.x), lambda k: self.l2.at[k // 2, k % 2, :, self.at]
        )
        self.c3 = rcopy(
            self.block(ALL, 1 - me.lo, me.y, me.x), self.l3.at[pl.ds(0, 2), :, self.at], *self.sems(), me.z1()
        )
        self.c3.start()

    def r3b(self):
        me = self.me
        self.c3.wait()
        self.add(2, lambda k: self.block(k, me.lo, me.y, me.x), lambda k: self.l3.at[k, :, self.at])
        self.c3 = rcopy(
            self.block(1 - me.hi, me.lo, me.y, me.x), self.l3.at[2, :, self.at], *self.sems(), me.z2()
        )
        self.c3.start()

    def r4(self):
        me = self.me
        self.c3.wait()
        total = self.block(me.hi, me.lo, me.y, me.x)[...].astype(F32) + self.l3[2, :, self.at].astype(F32)
        half = total.shape[0] // 2
        flag = (me.c == 0).astype(F32)
        top, low = total[:half], total[half:]
        self.out_of(me.c)[...] = flag * top + (1 - flag) * low
        self.l4[0, :, self.at] = flag * low + (1 - flag) * top
        self.c4 = rcopy(self.l4.at[0, :, self.at], self.l4.at[1, :, self.at], *self.sems(), me.sib())
        self.c4.start()

    def r5(self):
        self.c4.wait()
        self.out_of(1 - self.me.c)[...] = self.l4[1, :, self.at]


class LastOverX(Gather):
    def s2(self):
        me = self.me
        self.b.wait_recv()
        col = self.block(ALL, ALL, me.y, me.x)
        self.e = self.start(col, me.yn())
        self.to_sib = [self.start(col, me.sib())]

    def s3(self):
        me = self.me
        self.e.wait_recv()
        self.g = self.start(self.block(ALL, ALL, ALL, me.x), me.xn())
        self.to_sib.append(self.start(self.block(ALL, ALL, 1 - me.y, me.x), me.sib()))

    def s4(self):
        me = self.me
        self.g.wait_recv()
        self.to_sib.append(self.start(self.block(ALL, ALL, ALL, 1 - me.x), me.sib()))


class EarlyReduce(Reduce):
    def go(self, src, land, to):
        self.c = rcopy(src, land, *self.sems(), to)
        self.c.start()

    def r1(self):
        me = self.me
        self.c0.wait()
        self.add(
            16,
            lambda k: self.block(k // 8, k // 4 % 2, k // 2 % 2, k % 2),
            lambda k: self.l0.at[k // 8, k // 4 % 2, k // 2 % 2, k % 2, :, self.at],
        )
        self.go(self.block(ALL, 1 - me.lo, ALL, ALL), self.l1.at[:, :, :, :, self.at], me.z1())

    def r2(self):
        me = self.me
        self.c.wait()
        self.add(
            8,
            lambda k: self.block(k // 4, me.lo, k // 2 % 2, k % 2),
            lambda k: self.l1.at[k // 4, k // 2 % 2, k % 2, :, self.at],
        )
        self.go(self.block(1 - me.hi, me.lo, ALL, ALL), self.l2.at[:, :, :, self.at], me.z2())

    def r3(self):
        me = self.me
        self.c.wait()
        self.add(
            4,
            lambda k: self.block(me.hi, me.lo, k // 2, k % 2),
            lambda k: self.l2.at[k // 2, k % 2, :, self.at],
        )
        self.go(self.block(me.hi, me.lo, ALL, 1 - me.x), self.l3.at[pl.ds(0, 2), :, self.at], me.xn())

    def r3b(self):
        me = self.me
        self.c.wait()
        self.add(2, lambda k: self.block(me.hi, me.lo, k, me.x), lambda k: self.l3.at[k, :, self.at])
        self.go(self.block(me.hi, me.lo, 1 - me.y, me.x), self.l3.at[2, :, self.at], me.yn())
        self.c3 = self.c


class Swap:
    def __init__(self, me, ssem, rsem):
        self.me, self.ss, self.rs, self.sent = me, ssem, rsem, []

    def other(self, d):
        return (self.me.f + d) % 4

    def go(self, src_of, dst):
        me = self.me
        for d in (1, 2, 3):
            t = self.other(d)
            c = rcopy(src_of(t), dst, self.ss.at[d - 1], self.rs.at[d - 1], me.dev(me.z, me.y, t // 2, t % 2))
            c.start()
            self.sent.append(c)

    def wait(self):
        for c in self.sent:
            c.wait_send()
            c.wait_recv()


class Slices:
    def __init__(self, me, w, at, l1, l2, sems, early=False):
        self.me, self.w, self.at, self.l1, self.l2, self.sems, self.early = me, w, at, l1, l2, sems, early
        self.sent = []

    def part(self, hi, lo, y):
        return self.w.at[hi, lo, y, :, self.at]

    def steps(self):
        me = self.me
        if self.early:
            return (
                (self.part(me.hi, me.lo, me.y), me.yn()),
                (self.part(me.hi, me.lo, ALL), me.z2()),
                (self.part(ALL, me.lo, ALL), me.z1()),
            )
        return (
            (self.part(me.hi, me.lo, me.y), me.z2()),
            (self.part(ALL, me.lo, me.y), me.z1()),
            (self.part(ALL, ALL, me.y), me.yn()),
        )

    def send(self, n):
        if n:
            self.sent[-1].wait_recv()
        ref, to = self.steps()[n]
        c = rcopy(ref, ref, *self.sems(), to)
        c.start()
        self.sent.append(c)

    def finish(self):
        self.sent[-1].wait_recv()
        for c in self.sent:
            c.wait_send()

    def kept(self, n):
        me = self.me
        if self.early:
            return (
                (4, lambda k: self.part(k // 2, me.lo, k % 2)),
                (2, lambda k: self.part(me.hi, me.lo, k)),
            )[n]
        return (
            (4, lambda k: self.part(k // 2, k % 2, me.y)),
            (2, lambda k: self.part(k, me.lo, me.y)),
        )[n]

    def back(self, n):
        me = self.me
        if n:
            self.c.wait()
            count, mine_of = self.kept(n - 1)

            def body(k, _):
                mine = mine_of(k)
                land = self.l1[k // 2, k % 2, :, self.at] if n == 1 else self.l2[k, :, self.at]
                mine[...] = (mine[...].astype(F32) + land.astype(F32)).astype(BF16)
                return 0

            lax.fori_loop(0, count, body, 0)
        lands = (self.l1.at[:, :, :, self.at], self.l2.at[pl.ds(0, 2), :, self.at], self.l2.at[2, :, self.at])
        if self.early:
            src, to = (
                (self.part(ALL, 1 - me.lo, ALL), me.z1()),
                (self.part(1 - me.hi, me.lo, ALL), me.z2()),
                (self.part(me.hi, me.lo, 1 - me.y), me.yn()),
            )[n]
        else:
            src, to = (
                (self.part(ALL, ALL, 1 - me.y), me.yn()),
                (self.part(ALL, 1 - me.lo, me.y), me.z1()),
                (self.part(1 - me.hi, me.lo, me.y), me.z2()),
            )[n]
        self.c = rcopy(src, lands[n], *self.sems(), to)
        self.c.start()

    def back_sum(self):
        me = self.me
        self.c.wait()
        return self.part(me.hi, me.lo, me.y)[...].astype(F32) + self.l2[2, :, self.at].astype(F32)


class Share:
    def __init__(self, me, whole, sems):
        self.me, self.sems = me, sems
        self.whole = whole

    def send(self):
        me = self.me
        own = self.whole(me.f)
        self.s = rcopy(own, own, *self.sems(), me.sib())
        self.x = rcopy(own, own, *self.sems(), me.xn())
        self.s.start()
        self.x.start()

    def near(self):
        self.s.wait()

    def forward(self):
        me = self.me
        self.x.wait_recv()
        got = self.whole(2 * (1 - me.x) + me.c)
        self.t = rcopy(got, got, *self.sems(), me.sib())
        self.t.start()

    def finish(self):
        self.x.wait_send()
        self.t.wait()


class Collect:
    def __init__(self, me, part_of, lands, sems, pieces=4):
        self.me, self.part_of, self.lands, self.sems, self.pieces = me, part_of, lands, sems, pieces

    def near(self):
        me = self.me
        self.n = rcopy(self.part_of(2 * me.x + 1 - me.c), self.lands.at[0], *self.sems(), me.sib())
        self.n.start()

    def pair(self):
        me = self.me
        self.p = rcopy(self.part_of(2 * (1 - me.x) + 1 - me.c), self.lands.at[1], *self.sems(), me.sib())
        self.p.start()

    def cross(self):
        me = self.me
        self.p.wait()
        part = self.part_of(2 * (1 - me.x) + me.c)

        def add(k, _):
            mine = part.at[k]
            mine[...] = (mine[...].astype(F32) + self.lands[1, k].astype(F32)).astype(BF16)
            return 0

        lax.fori_loop(0, self.pieces, add, 0)
        self.x = rcopy(part, self.lands.at[2], *self.sems(), me.xn())
        self.x.start()

    def finish(self):
        self.n.wait()
        self.x.wait()

    def total(self, k, at):
        own = self.part_of(self.me.f)[k, at].astype(F32) + self.lands[0, k, at].astype(F32)
        return own + self.lands[2, k, at].astype(F32)


def nn(a, b):
    return lax.dot_general(a, b, (((1,), (0,)), ((), ())), preferred_element_type=F32)


def nt(a, b):
    return lax.dot_general(a, b, (((1,), (1,)), ((), ())), preferred_element_type=F32)


def tn(a, b):
    return lax.dot_general(a, b, (((0,), (0,)), ((), ())), preferred_element_type=F32)


def standard(values):
    centred = values - jnp.mean(values, axis=-1, keepdims=True)
    scale = lax.rsqrt(jnp.mean(centred * centred, axis=-1, keepdims=True) + EPSILON)
    return centred * scale, scale


def norm_back(values, gain, grad):
    unit, scale = standard(values)
    inner = grad * gain
    low = jnp.mean(inner, axis=-1, keepdims=True)
    high = jnp.mean(inner * unit, axis=-1, keepdims=True)
    return scale * (inner - low - unit * high)


def softmax(scores):
    e = jnp.exp(scores - jnp.max(scores, axis=-1, keepdims=True))
    return e / jnp.sum(e, axis=-1, keepdims=True)


def low_half(shape):
    return lax.broadcasted_iota(jnp.int32, shape, 1) % 128 < 64


def by_halves(pieces):
    out = []
    for n, piece in enumerate(pieces):
        if piece is None:
            out.append(jnp.zeros_like(pieces[0][0][:, :128]))
            continue
        ref, k = piece
        part = ref[:, k // 2 * 128 : k // 2 * 128 + 128].astype(F32)
        out.append(part if k % 2 == n else pltpu.roll(part, 64, 1))
    return jnp.where(low_half(out[0].shape), out[0], out[1])


def head_order(f):
    q, k, v = (HEADS * n + 3 * f for n in range(3))
    return ((q, q + 1), (q + 2, k + 2), (k, k + 1), (v, v + 1), (v + 2, None))


def spread(parts, shifts):
    lane = lax.broadcasted_iota(jnp.int32, parts[0].shape, 1) // 96
    total = None
    for n in range(4):
        part = pltpu.roll(parts[n], shifts[n] % 4 * 96, 1) if shifts[n] % 4 else parts[n]
        total = part if total is None else jnp.where(lane == n, part, total)
    return total


def upright(row):
    n = row.shape[1]
    i, j = (lax.broadcasted_iota(jnp.int32, (n, n), k) for k in range(2))
    return jnp.sum(jnp.where(i == j, jnp.broadcast_to(row, (n, n)), 0.0), axis=1, keepdims=True)


def level(column):
    n = column.shape[0]
    i, j = (lax.broadcasted_iota(jnp.int32, (n, n), k) for k in range(2))
    return jnp.sum(jnp.where(i == j, jnp.broadcast_to(column, (n, n)), 0.0), axis=0, keepdims=True)


D, FF, ROWS, COLS, HEAD = 768, 3072, 8, 128, 64
HALF = D // 2
OWN = COLS // 4
TOK = ROWS * OWN
WIDE = 640
FACTOR = HEAD**-0.5


def layer_kernel(
    tok_h, cot_h, seq_h, cid_h, gain_row_h, r_q_h, r_o_h, gain_col_h, r_c_h, r_co_h, gain_ffn_h, r_u_h, r_d_h,
    mixed_h, igrad_h, o_q_h, d_o_h, d_c_h, d_co_h, o_u_h, d_d_h,
    mixed, igrad, o_q, d_o, d_c, d_co, o_u, d_d, out_sems,
    tok, cot, seq, cid, gain_row, r_q, r_o, gain_col, r_c, r_co, gain_ffn, r_u, r_d, in_sems,
    i_q, i_u,
    w_q, w_o, w_c, w_u, w_d, f_q, f_o, f_c, f_u,
    l_o0, l_o1, l_o2, l_o3, l_o4,
    l_c0, l_c1, l_c2, l_c3, l_c4,
    l_q1, l_q2, t_q, l_u1, l_u2, t_u, l_d1, l_d2,
    tok_all, e_all, h1, qkv, p_row, o1f, o1c, x1, h2, qkv2, p_col, o2, x2, h3, act, du, yp, l_y, dp, l_p,
    g, do2, dqkv2, dh2, e1, dost, do1, dqkv, e1r, gains, cmask, tmask, ms, mr,
):
    me = Place()
    f = me.f
    scope = jax.named_scope
    sib_f, x_f, diag_f = 2 * me.x + 1 - me.c, 2 * (1 - me.x) + me.c, 2 * (1 - me.x) + 1 - me.c
    diag = me.dev(me.z, me.y, 1 - me.x, 1 - me.c)
    names = ("gain_row", "gain_col", "gain_ffn", "q", "o", "co", "c", "u", "d", "tok", "seq", "cid", "cot")
    pairs_in = (
        (gain_row_h, gain_row), (gain_col_h, gain_col), (gain_ffn_h, gain_ffn), (r_q_h, r_q), (r_o_h, r_o),
        (r_co_h, r_co), (r_c_h, r_c), (r_u_h, r_u), (r_d_h, r_d), (tok_h, tok), (seq_h, seq), (cid_h, cid),
        (cot_h, cot),
    )
    loads = {n: pltpu.make_async_copy(a, b, in_sems.at[k]) for k, (n, (a, b)) in enumerate(zip(names, pairs_in))}
    for c in loads.values():
        c.start()

    stores = []

    def store(k):
        src = (mixed, igrad, o_q, d_o, d_c, d_co, o_u, d_d)[k]
        dst = (mixed_h, igrad_h, o_q_h, d_o_h, d_c_h, d_co_h, o_u_h, d_d_h)[k]
        stores.append(pltpu.make_async_copy(src, dst, out_sems.at[k]))
        stores[-1].start()

    def loaded(*which):
        for n in which:
            loads[n].wait()

    greet([me.sib(), me.xn(), diag, me.yn(), me.z1(), me.z2()])
    used = [0]

    def sems():
        used[0] += 1
        return ms.at[used[0] - 1], mr.at[used[0] - 1]

    def swap():
        used[0] += 3
        at = pl.ds(used[0] - 3, 3)
        return Swap(me, ms.at[at], mr.at[at])

    at_w = pl.ds(0, HALF)
    at_qv, at_k, at_o = pl.ds(0, D), pl.ds(D, HALF), pl.ds(D + HALF, HALF)

    def lanes(ref, start, step, size):
        return lambda h: ref.at[:, pl.ds(pl.multiple_of(start + h * step, 128), size)]

    of_o = lanes(r_o, 0, HALF, HALF)
    of_qv, of_k, of_co = lanes(r_c, 0, 2 * D, D), lanes(r_c, D, HALF, HALF), lanes(r_co, 0, HALF, HALF)
    go = Gather(me, of_o, f_o, w_o, at_w, sems)
    g_qv = Gather(me, of_qv, f_c, w_c, at_qv, sems)
    g_k = Gather(me, of_k, f_c, w_c, at_k, sems)
    g_out = LastOverX(me, of_co, f_c, w_c, at_o, sems)
    ro = Reduce(me, w_o, at_w, (l_o0, l_o1, l_o2, l_o3, l_o4), lanes(d_o, 0, HALF, HALF), sems)
    r_qv, r_k, r_out = (
        kind(me, w_c, at, (l_c0, l_c1, l_c2, l_c3, l_c4), out, sems)
        for kind, at, out in (
            (Reduce, at_qv, lanes(d_c, 0, 2 * D, D)),
            (EarlyReduce, at_k, lanes(d_c, D, HALF, HALF)),
            (Reduce, at_o, lanes(d_co, 0, HALF, HALF)),
        )
    )
    sq = [Slices(me, w_q, pl.ds(*at), l_q1, l_q2, sems, at[0] > 0) for at in ((0, 384), (384, 256))]
    su = [Slices(me, w_u, pl.ds(k * HALF, HALF), l_u1, l_u2, sems, k == 1) for k in range(2)]
    sd = [Slices(me, w_d, pl.ds(k * HALF, HALF), l_d1, l_d2, sems, k == 0) for k in range(2)]

    def cols_of(t):
        return pl.ds(pl.multiple_of(t * OWN, OWN), OWN)

    own_cols = cols_of(f)

    def stacked(land):
        return jnp.concatenate([land[k].astype(F32) for k in range(4)], axis=0).astype(BF16)

    loaded("gain_row", "gain_col", "gain_ffn", "q")
    lane = lax.broadcasted_iota(jnp.int32, (r_q.shape[0], 128), 1)
    columns = [upright(v[...].astype(F32)) for v in (gain_row, gain_col, gain_ffn)]
    spare = sum(jnp.where(lane == HEAD + n, v, 0.0) for n, v in enumerate(columns))
    for t in range(4):
        for n, pair in enumerate(head_order(t)):
            part = by_halves([None if k is None else (r_q, k) for k in pair])
            i_q[t, :, n * 128 : (n + 1) * 128] = (part + spare if n == 4 else part).astype(BF16)
    s_q = swap()
    s_q.go(lambda t: i_q.at[t], f_q.at[f])
    loaded("o", "co", "c")
    for k in (g_k, g_qv, go, g_out):
        k.swap()
    loaded("tok")
    tok_all[pl.ds(2 * f, 2)] = tok[...]
    loaded("d")
    w_d[me.hi, me.lo, me.y] = r_d[...]
    sd[0].send(0)
    loaded("u")
    with scope("i_u"):
        for t in range(4):
            for n in range(2):
                parts = [r_u[:, (4 * n + k) * 384 : (4 * n + k + 1) * 384].astype(F32) for k in range(4)]
                i_u[t, :, n * 384 : (n + 1) * 384] = spread(parts, [k - t for k in range(4)]).astype(BF16)
    s_u = swap()
    s_u.go(lambda t: i_u.at[t], f_u.at[f])
    shr_t = Share(me, lambda k: tok_all.at[pl.ds(2 * k, 2)], sems)
    shr_t.send()
    with scope("q_f"):
        f_q[f] = i_q[f]
        s_q.wait()
        w_q[me.hi, me.lo, me.y] = stacked(f_q)
    sq[1].send(0)
    sq[0].send(0)
    with scope("masks"):
        loaded("seq", "cid", "cot")
        first = seq[0, 0]
        ids = jnp.broadcast_to(cid[...], (COLS, COLS)).astype(F32)
        cmask[...] = jnp.where(ids == ids.T, 1.0, 0.0)
        i, j = (lax.broadcasted_iota(jnp.int32, tmask.shape, n) for n in range(2))
        wide = OWN // 2

        def block_of(k):
            r = k // wide
            return jnp.where(r == 0, first, jnp.where(r == ROWS - 1, 2, 1))

        tmask[...] = jnp.where((i % wide == j % wide) & (block_of(i) == block_of(j)), 1.0, 0.0)
        e_all[pl.ds(2 * f, 2)] = cot[...]
        f_u[f] = i_u[f]
    with scope("q_m1"):
        sq[1].send(1)
    s_u.wait()
    w_u[me.hi, me.lo, me.y] = stacked(f_u)
    su[1].send(0)
    with scope("q_m0"):
        sq[0].send(1)
    g_qv.s0()
    go.s0()
    with scope("q_n1"):
        sq[1].send(2)
    shr_e = Share(me, lambda k: e_all.at[pl.ds(2 * k, 2)], sems)
    shr_e.send()
    with scope("q_n0"):
        sq[0].send(2)
    g_k.s0()
    with scope("qv1"):
        g_qv.s1()
    with scope("tok"):
        shr_t.forward()
    with scope("go1"):
        go.s1()
    with scope("q_fin1"):
        sq[1].finish()
    with scope("gains"):
        wide = w_q[:, :, :, :, WIDE - 128 :].reshape(D, 128)
        for k in range(D // 128):
            part = wide[k * 128 : (k + 1) * 128].astype(F32).T
            gains[:, k * 128 : (k + 1) * 128] = part[HEAD : HEAD + 8]
    with scope("tok2"):
        shr_t.near()
        shr_t.finish()

    with scope("norm_row"):

        def norm_rows(k, _):
            unit, _s = standard(tok_all[k].astype(F32))
            h1[k] = (unit * gains[0:1]).astype(BF16)
            return 0

        lax.fori_loop(0, ROWS, norm_rows, 0)
    with scope("k1"):
        g_k.s1()
    with scope("qv2"):
        g_qv.s2()
    su[0].send(0)
    g_out.s0()
    with scope("go2"):
        go.s2()
    with scope("q_fin0"):
        sq[0].finish()
    with scope("qkv_row"):
        wide = w_q[...].reshape(D, WIDE)

        def project(k, _):
            pair = h1[pl.ds(2 * k, 2)].reshape(2 * COLS, D)
            qkv[pl.ds(2 * k, 2)] = nn(pair, wide).astype(BF16).reshape(2, COLS, WIDE)
            return 0

        lax.fori_loop(0, ROWS // 2, project, 0)
    with scope("k2"):
        g_k.s2()
    with scope("qv3"):
        g_qv.s3()
    with scope("su_m0"):
        su[0].send(1)

    joined = (jnp.full((1, 1), first, jnp.int32) == 1)
    tied = jnp.where(joined, 1.0, 0.0)
    s_mid = jnp.where(joined, FACTOR / 7**0.5, FACTOR / 6**0.5)
    lower = low_half((COLS, 128))
    zero = jnp.zeros((COLS, 128), BF16)

    def tile(ref, r, k):
        return ref[r, :, k * 128 : (k + 1) * 128]

    def head_tiles(r):
        q01, q2k2, k01 = tile(qkv, r, 0), tile(qkv, r, 1), tile(qkv, r, 2)
        k2 = pltpu.roll(q2k2.astype(F32), 64, 1).astype(BF16)
        return (
            (jnp.where(lower, q01, zero), k01),
            (jnp.where(lower, zero, q01), k01),
            (jnp.where(lower, q2k2, zero), k2),
        )

    with scope("go3"):
        go.s3()
    with scope("row_fwd"):
        sums = [[None] * 3 for _ in range(3)]
        for r in range(ROWS):
            for h, (a, b) in enumerate(head_tiles(r)):
                s = nt(a, b)
                t = 0 if r == 0 else 2 if r == ROWS - 1 else 1
                sums[h][t] = s if sums[h][t] is None else sums[h][t] + s
        for h in range(3):
            s0, s1, s2 = sums[h]
            for t, s in enumerate((s0 * FACTOR, (s1 + tied * s0) * s_mid, s2 * FACTOR)):
                p_row[h, t] = softmax(jnp.where(cmask[...] > 0.5, s, NEGATIVE))

    def chances(h, r):
        if r == 0:
            return jnp.where(joined, p_row[h, 1], p_row[h, 0])
        return p_row[h, 2 if r == ROWS - 1 else 1]

    thirds = []
    with scope("row_out"):
        for r in range(ROWS):
            v01, v2 = tile(qkv, r, 3), tile(qkv, r, 4)
            p = [chances(h, r).astype(BF16) for h in range(3)]
            o1f[r] = jnp.where(lower, nn(p[0], v01), nn(p[1], v01)).astype(BF16)
            thirds.append(nn(p[2], v2))
        for r in range(4):
            o1f[ROWS + r] = jnp.where(lower, thirds[r], pltpu.roll(thirds[r + 4], 64, 1)).astype(BF16)
    s_o = swap()
    s_o.go(lambda t: o1f.at[:, cols_of(t)], o1c.at[f])
    o1c[f] = o1f[:, own_cols]
    with scope("out1"):
        g_out.s1()
    su[1].send(1)
    with scope("e_f"):
        shr_e.forward()
    with scope("k3"):
        g_k.s3()
    sd[1].send(0)
    with scope("su_n1"):
        su[1].send(2)
    sd[0].send(1)
    with scope("sd_m1"):
        sd[1].send(1)
    with scope("qv4"):
        g_qv.s4()
    with scope("go4"):
        go.s4()
    with scope("out2"):
        g_out.s2()
    with scope("k4"):
        g_k.s4()
    with scope("su_y0"):
        su[0].send(2)
    with scope("o1"):
        s_o.wait()

    def o1_of(k):
        packed = o1c[k, ROWS:].reshape(TOK // 2, 128)
        third = jnp.concatenate([packed, pltpu.roll(packed.astype(F32), 64, 1).astype(BF16)], axis=0)
        return jnp.concatenate([o1c[k, :ROWS].reshape(TOK, 128), third[:, :HEAD]], axis=1)

    def w_out(h, k):
        return w_o[h, k // 2, k % 2].reshape(192, HALF)

    with scope("go5"):
        go.s5()
    with scope("out_row"):
        o1_parts = [o1_of(k) for k in range(4)]
        for h in range(2):
            cols = slice(h * HALF, (h + 1) * HALF)
            total = tok_all[:, own_cols, cols].reshape(TOK, HALF).astype(F32)
            for k in range(4):
                total = total + nn(o1_parts[k], w_out(h, k))
            x1[:, cols] = total

    def in_pieces(step, rows=64, total=TOK):
        def body(k, _):
            step(pl.ds(pl.multiple_of(k * rows, rows), rows))
            return 0

        lax.fori_loop(0, total // rows, body, 0)

    with scope("norm_col"):

        def norm_col(at):
            h2[at] = (standard(x1[at])[0] * gains[1:2]).astype(BF16)

        in_pieces(norm_col)

    def w_col(part, k):
        half, off = ((0, k * HALF), (k, D), (1, k * HALF), (k, D + HALF))[part]
        return w_c.at[half, :, :, :, :, :, off : off + HALF]

    def project2(part):
        for k in range(2):
            at = slice(k * HALF, (k + 1) * HALF)
            one = nn(h2[...], w_col(part, k)[...].reshape(D, HALF))
            qkv2[part, :, :, at] = one.astype(BF16).reshape(ROWS, OWN, HALF)

    with scope("qv5"):
        g_qv.s5()
    with scope("qkv_col"):
        project2(0)
        project2(2)
        g_k.s5()
        project2(1)
    with scope("out3"):
        g_out.s3()
    with scope("sd_n0"):
        sd[0].send(2)
    with scope("sd_n1"):
        sd[1].send(2)
    part_cols = OWN // 2
    part_size = ROWS * part_cols
    lower2 = low_half((part_size, 128))
    zero2 = jnp.zeros((part_size, 128), BF16)

    def some(ref, m, at, *lead):
        return ref[(*lead, ALL, slice(m * part_cols, (m + 1) * part_cols), at)].reshape(part_size, 128)

    def put(ref, m, at, value, *lead):
        value = value.astype(BF16).reshape(ROWS, part_cols, 128)
        ref[(*lead, ALL, slice(m * part_cols, (m + 1) * part_cols), at)] = value

    def pairs(step):
        def body(k, _):
            step([(2 * k + n, m, pl.ds(pl.multiple_of((2 * k + n) * 128, 128), 128)) for n in range(2) for m in range(2)])
            return 0

        lax.fori_loop(0, HEADS // 4, body, 0)

    def one_head(e, value):
        return jnp.where(lower2, value, zero2) if e == 0 else jnp.where(lower2, zero2, value)

    with scope("col_fwd"):

        def col_pair(work):
            scores, chosen = [], []
            for _k, m, at in work:
                q, kk = some(qkv2, m, at, 0), some(qkv2, m, at, 1)
                scores.append([nt(one_head(e, q), kk) * FACTOR for e in range(2)])
            same = tmask[...] > 0.5
            for pair in scores:
                chosen.append([softmax(jnp.where(same, one, NEGATIVE)) for one in pair])
            out = []
            for (_k, m, at), pair in zip(work, chosen):
                v = some(qkv2, m, at, 2)
                out.append([nn(p.astype(BF16), v) for p in pair])
            for (k, m, at), pair, got in zip(work, chosen, out):
                put(o2, m, at, jnp.where(lower2, got[0], got[1]))
                for e in range(2):
                    p_col[2 * k + e, m] = pair[e]

        pairs(col_pair)
    with scope("out4"):
        g_out.s4()
    with scope("out_col"):
        g_out.s5()
        for k in range(2):
            at = slice(k * HALF, (k + 1) * HALF)
            x2[:, at] = x1[:, at] + nn(o2[...].reshape(TOK, D), w_col(3, k)[...].reshape(D, HALF))
    half_size = TOK // 2
    shr_h = [Share(me, lambda k, u=u: h3.at[k, u], sems) for u in range(2)]
    for u in range(2):
        with scope("norm_ffn%d" % u):

            def norm_ffn(k, _, u=u):
                at = pl.ds(pl.multiple_of(k * 64, 64), 64)
                src = pl.ds(pl.multiple_of(u * half_size + k * 64, 64), 64)
                h3[f, u, at] = (standard(x2[src])[0] * gains[2:3]).astype(BF16)
                return 0

            lax.fori_loop(0, half_size // 64, norm_ffn, 0)
        shr_h[u].send()
    for k in (go, g_qv, g_k, g_out):
        k.drain()
    with scope("su_f"):
        for k in su:
            k.finish()
    with scope("e"):
        shr_e.near()
        shr_e.finish()
    with scope("sd_f"):
        for k in sd:
            k.finish()

    def grads_of(b):
        return e_all[:, cols_of(b)].reshape(TOK, D)

    def ffn_block(pair, mine=None):
        grad = jnp.concatenate(
            [e_all[4 * u : 4 * u + 4, cols_of(b)].reshape(half_size, D) for b, u in pair], axis=0
        )
        tokens = jnp.concatenate([h3[b, u] for b, u in pair], axis=0)
        y_sum, d_sum = None, None
        for k in range(2):
            at = slice(k * HALF, (k + 1) * HALF)
            up = w_u[:, :, :, :, at].reshape(D, HALF)
            down = w_d[k].reshape(HALF, D)
            u_k = nn(tokens, up)
            bell = jnp.exp(-0.5 * u_k * u_k) * (1 / (2 * jnp.pi) ** 0.5)
            upper = 0.5 + 0.5 * lax.erf(u_k * 0.5**0.5)
            a = (u_k * upper).astype(BF16)
            d = (nt(grad, down) * (upper + u_k * bell)).astype(BF16)
            for n, (b, u) in enumerate(pair):
                act[b, u, :, at] = a[n * half_size : (n + 1) * half_size]
                du[b, u, :, at] = d[n * half_size : (n + 1) * half_size]
            y, dd = nn(a, down), nt(d, up)
            y_sum = y if y_sum is None else y_sum + y
            d_sum = dd if d_sum is None else d_sum + dd
        if mine is not None:
            y_sum = y_sum + x2[...] * mine
        y_sum = y_sum.astype(BF16).reshape(4, 2 * OWN, D)
        d_sum = d_sum.astype(BF16).reshape(4, 2 * OWN, D)
        for n, (b, u) in enumerate(pair):
            yp[b, 2 * u : 2 * u + 2] = y_sum[2 * n : 2 * n + 2]
            dp[b, 2 * u : 2 * u + 2] = d_sum[2 * n : 2 * n + 2]

    cy = Collect(me, lambda k: yp.at[:, k], l_y, sems)
    cd = [
        Collect(me, lambda k, u=u: dp.at[k, pl.ds(2 * u, 2)], l_p.at[:, pl.ds(2 * u, 2)], sems, 2) for u in range(2)
    ]
    with scope("h3_near"):
        shr_h[0].near()
        shr_h[1].near()
    with scope("ffn1"):

        def near_two(k, _):
            b = jnp.where(k == 0, f, sib_f)
            ffn_block(((b, 0), (b, 1)), (k == 0).astype(F32))
            return 0

        lax.fori_loop(0, 2, near_two, 0)
    cd[0].near()
    cd[1].near()
    with scope("h3_far0"):
        shr_h[0].forward()
    with scope("h3_diag0"):
        shr_h[0].finish()
    with scope("ffn2"):
        ffn_block(((x_f, 0), (diag_f, 0)))
    cd[0].pair()
    with scope("h3_far1"):
        shr_h[1].forward()
    with scope("dh3_0"):
        cd[0].cross()
    with scope("h3_diag1"):
        shr_h[1].finish()
    with scope("ffn3"):
        ffn_block(((x_f, 1), (diag_f, 1)))
    cd[1].pair()
    cy.near()
    cy.pair()
    with scope("dh3_1"):
        cd[1].cross()
    for k in range(2):
        at = slice(k * HALF, (k + 1) * HALF)
        with scope("g_down%d" % k):
            part = sum(tn(act[b].reshape(TOK, D), grads_of(b)[:, at]) for b in range(4))
            w_d[:, :, :, :, at] = part.astype(BF16).reshape(2, 2, 2, 96, HALF)
        sd[k].back(0)
    for k in range(2):
        at = slice(k * HALF, (k + 1) * HALF)
        with scope("g_up%d" % k):
            part = sum(tn(h3[b].reshape(TOK, D), du[b, :, :, at].reshape(TOK, HALF)) for b in range(4))
            w_u[:, :, :, :, at] = part.astype(BF16).reshape(2, 2, 2, 96, HALF)
        su[k].back(0)

    for u in range(2):
        with scope("cd_w%d" % u):
            cd[u].finish()
        with scope("back_ffn%d" % u):

            def back_ffn(k, _, u=u):
                row = 4 * u + k
                at = pl.ds(pl.multiple_of(row * OWN, OWN), OWN)
                grad = cd[u].total(k // 2, pl.ds(pl.multiple_of(k % 2 * OWN, OWN), OWN))
                g[at] = e_all[row, own_cols].astype(F32) + norm_back(x2[at], gains[2:3], grad)
                e1[at] = g[at].astype(BF16)
                return 0

            lax.fori_loop(0, 4, back_ffn, 0)
    with scope("mix"):
        cy.cross()
    with scope("do2"):
        total = sum(nt(e1[:, k * HALF : (k + 1) * HALF], w_col(3, k)[...].reshape(D, HALF)) for k in range(2))
        do2[...] = total.astype(BF16).reshape(ROWS, OWN, D)
        for k in range(2):
            part = tn(o2[...].reshape(TOK, D), e1[:, k * HALF : (k + 1) * HALF])
            w_col(3, k)[...] = part.astype(BF16).reshape(2, 2, 2, 2, 48, HALF)
    r_out.r0()
    with scope("col_bwd"):

        def col_back(work):
            grads, back, out = [], [], []
            for _k, m, at in work:
                d, v = some(do2, m, at), some(qkv2, m, at, 2)
                grads.append([nt(one_head(e, d), v) for e in range(2)])
            for (k, m, at), pair in zip(work, grads):
                for e in range(2):
                    p, dq = p_col[2 * k + e, m], pair[e]
                    ds = p * (dq - jnp.sum(dq * p, axis=-1, keepdims=True))
                    back.append((ds.astype(BF16), ds.T.astype(BF16), p.T.astype(BF16)))
            for n, (_k, m, at) in enumerate(work):
                q, kk, d = some(qkv2, m, at, 0), some(qkv2, m, at, 1), some(do2, m, at)
                got = [
                    (nn(ds, kk) * FACTOR, nn(dst, q) * FACTOR, nn(pt, d)) for ds, dst, pt in back[2 * n : 2 * n + 2]
                ]
                out.append([jnp.where(lower2, got[0][i], got[1][i]) for i in range(3)])
            for (_k, m, at), got in zip(work, out):
                for n in range(3):
                    put(dqkv2, m, at, got[n], n)

        pairs(col_back)
    with scope("sd_b0"):
        sd[0].back(1)
    with scope("dh2"):
        total = None
        for part in range(3):
            for k in range(2):
                one = nt(dqkv2[part, :, :, k * HALF : (k + 1) * HALF].reshape(TOK, HALF), w_col(part, k)[...].reshape(D, HALF))
                total = one if total is None else total + one
        dh2[...] = total

    def grad_col(part):
        for k in range(2):
            one = tn(h2[...], dqkv2[part, :, :, k * HALF : (k + 1) * HALF].reshape(TOK, HALF))
            w_col(part, k)[...] = one.astype(BF16).reshape(2, 2, 2, 2, 48, HALF)

    with scope("back_col"):

        def back_col(at):
            g[at] = g[at] + norm_back(x1[at], gains[1:2], dh2[at])
            e1[at] = g[at].astype(BF16)

        in_pieces(back_col)

    with scope("do1"):
        for k in range(4):
            d = nt(e1[:, :HALF], w_out(0, k)) + nt(e1[:, HALF:], w_out(1, k))
            third = jnp.concatenate([d[:, 128:], jnp.zeros((TOK, 64), F32)], axis=1)
            third = third[: TOK // 2] + pltpu.roll(third[TOK // 2 :], 64, 1)
            dost[k, :ROWS] = d[:, :128].astype(BF16).reshape(ROWS, OWN, 128)
            dost[k, ROWS:] = third.astype(BF16).reshape(4, OWN, 128)
    s_d = swap()
    s_d.go(lambda t: dost.at[t], do1.at[:, own_cols])
    do1[:, own_cols] = dost[f]
    s_g = swap()
    s_g.go(lambda t: e1.at[pl.ds(pl.multiple_of(2 * OWN * t, 2 * OWN), 2 * OWN)], e1r.at[f])
    e1r[f] = e1[pl.ds(pl.multiple_of(2 * OWN * f, 2 * OWN), 2 * OWN)]
    with scope("out_r1"):
        r_out.r1()
    with scope("sd_b1"):
        sd[1].back(1)
    with scope("g_qv"):
        grad_col(0)
        grad_col(2)
    r_qv.r0()
    with scope("su_b1"):
        su[1].back(1)
    with scope("sd_c0"):
        sd[0].back(2)
    with scope("su_b0"):
        su[0].back(1)
    with scope("g_k"):
        grad_col(1)
    r_k.r0()
    with scope("g_out_row"):
        o1_parts = [o1_of(k) for k in range(4)]
        for h in range(2):
            for k in range(4):
                part = tn(o1_parts[k], e1[:, h * HALF : (h + 1) * HALF])
                w_o[h, k // 2, k % 2] = part.astype(BF16).reshape(2, 2, 48, HALF)
    ro.r0()
    with scope("qv_r1"):
        r_qv.r1()
    with scope("k_r1"):
        r_k.r1()
    with scope("ro1"):
        ro.r1()
    with scope("su_c0"):
        su[0].back(2)
    with scope("do1w"):
        s_d.wait()
    with scope("row_bwd"):
        d_third = [jnp.where(lower, do1[ROWS + r], zero) for r in range(4)]
        for r in range(4):
            d_third.append(jnp.where(lower, pltpu.roll(do1[ROWS + r].astype(F32), 64, 1).astype(BF16), zero))
        d_sum = [[None] * 3 for _ in range(3)]
        for r in range(ROWS):
            d01, d2, v01, v2 = do1[r], d_third[r], tile(qkv, r, 3), tile(qkv, r, 4)
            ops = ((jnp.where(lower, d01, zero), v01), (jnp.where(lower, zero, d01), v01), (d2, v2))
            for h, (a, b) in enumerate(ops):
                s = nt(a, b)
                t = 0 if r == 0 else 2 if r == ROWS - 1 else 1
                d_sum[h][t] = s if d_sum[h][t] is None else d_sum[h][t] + s
        da, dat, pt = [], [], []
        for h in range(3):
            s0, s1, s2 = d_sum[h]
            by = []
            for t, s in enumerate((s0, s1 + tied * s0, s2)):
                p = p_row[h, t]
                by.append(p * (s - jnp.sum(s * p, axis=-1, keepdims=True)))
            da.append((jnp.where(joined, by[1], by[0]), by[1], by[2]))
            dat.append([a.T.astype(BF16) for a in da[h]])
            pt.append([chances(h, r).T.astype(BF16) for r in (0, 1, ROWS - 1)])
            da[h] = [a.astype(BF16) for a in da[h]]
        s_first = jnp.where(joined, s_mid, FACTOR)
        for r in range(ROWS):
            t = 0 if r == 0 else 2 if r == ROWS - 1 else 1
            scale = (s_first, s_mid, FACTOR)[t]
            q01, q2k2, k01 = tile(qkv, r, 0), tile(qkv, r, 1), tile(qkv, r, 2)
            d01, d2 = do1[r], d_third[r]
            dq = jnp.where(lower, nn(da[0][t], k01), nn(da[1][t], k01)) * scale
            dk = jnp.where(lower, nn(dat[0][t], q01), nn(dat[1][t], q01)) * scale
            mid = jnp.where(lower, nn(dat[2][t], q2k2), nn(da[2][t], q2k2)) * scale
            dv = jnp.where(lower, nn(pt[0][t], d01), nn(pt[1][t], d01))
            for n, val in enumerate((dq, pltpu.roll(mid, 64, 1), dk, dv, nn(pt[2][t], d2))):
                dqkv[r, :, n * 128 : (n + 1) * 128] = val.astype(BF16)
    with scope("dh1"):
        wide = w_q[...].reshape(D, WIDE)

        def partial_dh(k, _):
            pair = dqkv[pl.ds(2 * k, 2)].reshape(2 * COLS, WIDE)
            dp[k] = nt(pair, wide).astype(BF16).reshape(4, 2 * OWN, D)
            return 0

        lax.fori_loop(0, 4, partial_dh, 0)
    ch = Collect(me, lambda k: dp.at[k], l_p, sems)
    ch.pair()
    ch.near()
    for k in range(2):
        at = slice(0, 384) if k == 0 else slice(384, WIDE)
        with scope("g_qkv%d" % k):
            total = tn(h1[...].reshape(ROWS * COLS, D), dqkv[:, :, at].reshape(ROWS * COLS, -1))
            w_q[:, :, :, :, at] = total.astype(BF16).reshape(2, 2, 2, 96, -1)
        sq[k].back(0)
    with scope("out_r2"):
        r_out.r2()
    with scope("sd_c1"):
        sd[1].back(2)
    with scope("su_c1"):
        su[1].back(2)
    with scope("qv_r2"):
        r_qv.r2()
    with scope("k_r2"):
        r_k.r2()
    with scope("q_b1"):
        sq[1].back(1)
    with scope("q_b0"):
        sq[0].back(1)
    with scope("ro2"):
        ro.r2()
    with scope("out_r3"):
        r_out.r3()
    with scope("qv_r3"):
        r_qv.r3()
    with scope("dh1_x"):
        ch.cross()
    with scope("k_r3"):
        r_k.r3()
    with scope("q_c1"):
        sq[1].back(2)
    with scope("q_c0"):
        sq[0].back(2)
    with scope("ro3"):
        ro.r3()
    with scope("out_r3b"):
        r_out.r3b()
    with scope("d_sum"):
        for k in sd:
            d_d[:, k.at] = k.back_sum()
        store(7)
    with scope("u_sum"):
        for k in su:
            t_u[:, :, k.at] = k.back_sum().astype(BF16).reshape(4, -1, HALF)
    s_v = swap()
    s_v.go(lambda t: t_u.at[t], o_u.at[f])
    o_u[f] = t_u[f]
    with scope("qv_r3b"):
        r_qv.r3b()
    with scope("ro3b"):
        ro.r3b()
    with scope("k_r3b"):
        r_k.r3b()
    with scope("q_sum"):
        s_t = []
        for k in reversed(sq):
            t_q[:, :, k.at] = k.back_sum().astype(BF16).reshape(4, -1, k.at.size)
            o_q[f, :, k.at] = t_q[f, :, k.at]
            s_t.append(swap())
            s_t[-1].go(lambda t, at=k.at: t_q.at[t, :, at], o_q.at[f, :, k.at])
    with scope("mixed"):
        cy.finish()
        for r in range(2):
            for k in range(4):
                mixed[r, k * OWN : (k + 1) * OWN] = cy.total(k, slice(r * OWN, (r + 1) * OWN)).astype(BF16)
        store(0)
    with scope("in_grad"):
        ch.finish()
        s_g.wait()
        for r in range(2):
            for k in range(4):
                at = slice(k * OWN, (k + 1) * OWN)
                grad = ch.total(2 * r + k // 2, slice(k % 2 * OWN, (k % 2 + 1) * OWN))
                back = norm_back(tok[r, at].astype(F32), gains[0:1], grad)
                igrad[r, at] = e1r[k, r * OWN : (r + 1) * OWN].astype(F32) + back
        store(1)
    with scope("out_r4"):
        r_out.r4()
    with scope("qv_r4"):
        r_qv.r4()
    with scope("k_r4"):
        r_k.r4()
    with scope("ro4"):
        ro.r4()
    with scope("last"):
        s_v.wait()
        store(6)
        for k in (r_out, r_qv, r_k):
            k.r5()
        store(4)
        store(5)
        ro.r5()
        store(3)
        for k in s_t:
            k.wait()
        store(2)
        for c in stores:
            c.wait()
    assert used[0] <= SEMS, used[0]


SEMS = 160


def finish_kernel(*refs):
    ins, outs, held, made = refs[:14], refs[14:25], refs[25:39], refs[39:44]
    in_sems, out_sems = refs[44:]
    order = (6, 2, 4, 11, 9, 13, 0, 1, 3, 5, 7, 8, 10, 12)
    loads = [pltpu.make_async_copy(a, b, in_sems.at[k]) for k, (a, b) in enumerate(zip(ins, held))]
    for k in order:
        loads[k].start()
    stores = []

    def store(src, k):
        stores.append(pltpu.make_async_copy(src, outs[k], out_sems.at[k]))
        stores[-1].start()

    _mixed, _igrad, o_q, _o, e_c, _co, o_u, _d, gain_row, r_q, gain_col, r_c, gain_ffn, r_u = held
    dg_row, d_q, dg_col, dg_ffn, d_u = made
    loads[6].wait()
    for n in range(8):
        parts = [o_u[t, :, n // 4 * 384 : (n // 4 + 1) * 384].astype(F32) for t in range(4)]
        d_u[:, n * 384 : (n + 1) * 384] = spread(parts, [t - n % 4 for t in range(4)])
    store(d_u, 9)
    loads[2].wait()
    where = {}
    for t in range(4):
        for n, pair in enumerate(head_order(t)):
            for k, piece in enumerate(pair):
                where[piece] = (o_q.at[t], 2 * n + k)
    for n in range(3 * D // 128):
        d_q[:, n * 128 : (n + 1) * 128] = by_halves([where[2 * n], where[2 * n + 1]])
    store(d_q, 3)
    for k, to in ((0, 0), (1, 1), (3, 4), (4, 6), (5, 7), (7, 10)):
        loads[k].wait()
        store(held[k], to)
    for k in (8, 9, 10, 11, 12, 13):
        loads[k].wait()

    for out, weight, grad, gain, to in (
        (dg_row, r_q, d_q, gain_row, 2), (dg_col, r_c, e_c, gain_col, 5), (dg_ffn, r_u, d_u, gain_ffn, 8)
    ):
        total = jnp.sum(weight[...].astype(F32) * grad[...], axis=1, keepdims=True)
        out[...] = level(total / upright(gain[...].astype(F32)))
        store(out, to)
    for c in stores:
        c.wait()


def run_layer(tok, cot, seq, cid, *weights):
    sds = jax.ShapeDtypeStruct
    rows = weights[1].shape[0]
    i_d = weights[-1]
    first = [sds(tok.shape, BF16), sds(tok.shape, F32)]
    wide_q, wide_u = sds((4, rows, WIDE), BF16), sds((4, rows, D), BF16)
    plain = [sds(w.shape, F32) for w in weights]
    shapes = first + [wide_q, plain[2], plain[4], plain[5], wide_u, plain[8]]

    def vmem(*shape, dtype=BF16):
        return pltpu.VMEM(shape, dtype)

    def lands(r, c):
        return [
            vmem(2, 2, 2, 2, r, c), vmem(2, 2, 2, r, c), vmem(2, 2, r, c), vmem(3, r, c), vmem(2, r // 2, c, dtype=F32)
        ]

    def slices(c):
        return [vmem(2, 2, 4 * rows, c), vmem(3, 4 * rows, c)]

    r2 = 2 * rows
    wo, wc, wu = HALF, 2 * D, D
    scratch = [
        *(pltpu.VMEM(a.shape, a.dtype) for a in shapes),
        pltpu.SemaphoreType.DMA((8,)),
        *(pltpu.SMEM(a.shape, a.dtype) if a is seq else pltpu.VMEM(a.shape, a.dtype) for a in (tok, cot, seq, cid, *weights)),
        pltpu.SemaphoreType.DMA((13,)),
        vmem(4, rows, WIDE),
        vmem(4, rows, wu),
        vmem(2, 2, 2, 4 * rows, WIDE),
        vmem(2, 2, 2, 2, 2, r2, wo),
        vmem(2, 2, 2, 2, 2, r2, wc),
        vmem(2, 2, 2, 4 * rows, wu),
        vmem(2, 2, 2, *i_d.shape),
        vmem(4, rows, WIDE),
        vmem(rows, wo),
        vmem(rows, wc),
        vmem(4, rows, wu),
        *lands(r2, wo),
        *lands(r2, wc),
        *slices(WIDE),
        vmem(4, rows, WIDE),
        *slices(wu),
        vmem(4, rows, wu),
        *slices(D),
        vmem(ROWS, COLS, D),
        vmem(ROWS, COLS, D),
        vmem(ROWS, COLS, D),
        vmem(ROWS, COLS, WIDE),
        vmem(3, 3, COLS, COLS, dtype=F32),
        vmem(ROWS + 4, COLS, 128),
        vmem(4, ROWS + 4, OWN, 128),
        vmem(TOK, D, dtype=F32),
        vmem(TOK, D),
        vmem(3, ROWS, OWN, D),
        vmem(HEADS, 2, TOK // 2, TOK // 2, dtype=F32),
        vmem(ROWS, OWN, D),
        vmem(TOK, D, dtype=F32),
        vmem(4, 2, TOK // 2, D),
        vmem(4, 2, TOK // 2, D),
        vmem(4, 2, TOK // 2, D),
        vmem(4, 4, 2 * OWN, D),
        vmem(3, 4, 2 * OWN, D),
        vmem(4, 4, 2 * OWN, D),
        vmem(3, 4, 2 * OWN, D),
        vmem(TOK, D, dtype=F32),
        vmem(ROWS, OWN, D),
        vmem(3, ROWS, OWN, D),
        vmem(TOK, D, dtype=F32),
        vmem(TOK, D),
        vmem(4, ROWS + 4, OWN, 128),
        vmem(ROWS + 4, COLS, 128),
        vmem(ROWS, COLS, WIDE),
        vmem(4, 2 * OWN, D),
        vmem(8, D, dtype=F32),
        vmem(COLS, COLS, dtype=F32),
        vmem(TOK // 2, TOK // 2, dtype=F32),
        pltpu.SemaphoreType.DMA((SEMS,)),
        pltpu.SemaphoreType.DMA((SEMS,)),
    ]
    outs = pl.pallas_call(
        layer_kernel,
        out_shape=shapes,
        in_specs=[pl.BlockSpec(memory_space=pl.ANY)] * 13,
        out_specs=[pl.BlockSpec(memory_space=pl.ANY)] * 8,
        scratch_shapes=scratch,
        name="layer",
        compiler_params=pltpu.CompilerParams(
            collective_id=0, has_side_effects=True, vmem_limit_bytes=VMEM_LIMIT
        ),
    )(tok, cot, seq, cid, *weights)
    given = (*outs, weights[0], weights[1], weights[3], weights[4], weights[6], weights[7])
    anywhere = pl.BlockSpec(memory_space=pl.ANY)
    made = [plain[k] for k in (0, 1, 3, 6, 7)]
    return pl.pallas_call(
        finish_kernel,
        out_shape=first + plain,
        in_specs=[anywhere] * 14,
        out_specs=[anywhere] * 11,
        scratch_shapes=[pltpu.VMEM(a.shape, a.dtype) for a in (*given, *made)]
        + [pltpu.SemaphoreType.DMA((14,)), pltpu.SemaphoreType.DMA((11,))],
        name="finish",
        compiler_params=pltpu.CompilerParams(vmem_limit_bytes=VMEM_LIMIT),
    )(*given)


VMEM_LIMIT = 63 * 2**20


def on_device(
    tokens, cotangent, seq_ids, col_ids,
    gain_row, qkv_row, out_row, gain_col, qkv_col, out_col, gain_ffn, up_ffn, down_ffn,
    cells,
):
    members = CELL * lax.axis_size("fsdp")
    low_index = (lax.axis_index("dp") % CELL) * lax.axis_size("fsdp") + lax.axis_index("fsdp")

    def in_cell(shard):
        if cells == 1:
            return shard
        whole = lax.all_gather(shard, AXES, axis=0, tiled=True)
        rows = whole.shape[0] // members
        return lax.dynamic_slice_in_dim(whole, low_index * rows, rows, 0)

    def from_cell(summed):
        if cells == 1:
            return summed
        rows = summed.shape[0]
        whole = jnp.zeros((rows * members,) + summed.shape[1:], summed.dtype)
        whole = lax.dynamic_update_slice_in_dim(whole, summed, low_index * rows, 0)
        return lax.psum_scatter(whole, AXES, scatter_dimension=0, tiled=True)

    weights = [
        in_cell(w).reshape(1, -1) if w.ndim == 1 else in_cell(w)
        for w in (gain_row, qkv_row, out_row, gain_col, qkv_col, out_col, gain_ffn, up_ffn, down_ffn)
    ]
    mixed, igrad, *grads = run_layer(tokens[0], cotangent[0], seq_ids, col_ids, *weights)
    grads = [from_cell(v.reshape(-1) if v.shape[0] == 1 else v) for v in grads]
    return (mixed[None], igrad[None], *grads)


def solution(mesh):
    rows = P(AXES, None)
    vector = P(AXES)
    grid = P("dp", "fsdp", None, None)
    ids = P("dp", None)
    return jax.shard_map(
        partial(on_device, cells=mesh.shape["dp"] // CELL),
        mesh=mesh,
        in_specs=(grid, grid, ids, ids) + (vector, rows, rows) * 3,
        out_specs=(grid, grid) + (vector, rows, rows) * 3,
        check_vma=False,
    )
```
